32 devices in a mesh: seq: 8 (over z, y), batch: 4 (over x, core).
Axes of the slice: x: 2, y: 2, z: 4, core: 2. Of those that a mesh axis runs over, the one named last changes fastest.
Arguments:
- tokens: bfloat16 [4, 16384, 256], P('batch', 'seq'), may hold values from -6 to 6
- cotangent: bfloat16 [4, 16384, 256], P('batch', 'seq'), may hold values from -3 to 3
- first_factor: bfloat16 [32, 512, 512], P('seq', 'batch'), may hold values from -0.25 to 0.25
- second_factor: bfloat16 [512, 32, 32], P('seq', 'batch'), may hold values from -1 to 1
- gate_source: int32 [256], replicated, may hold values from 0 to 255
- alternate: int32 [512], replicated, may hold values from 0 to 511, each once
Outputs:
- grad_tokens: bfloat16 [4, 16384, 256], P('batch', 'seq')
- grad_first: bfloat16 [32, 512, 512], P('seq', 'batch')
- grad_second: bfloat16 [512, 32, 32], P('seq', 'batch')
The draws below stay inside these ranges and needn't reach their ends.
Inputs may be any that keep to these rules, and one draw needn't show every extreme that they name: `alternate`: a permutation: each of 0 to 511 once.
All inputs are finite; a program needn't handle non-finite values.
Results may differ from the reference program's by a relative error of at most 0.012.
Values may be sent and summed in bfloat16 or wider, within the bound.
No kernel may reach another device: no remote copies, remote signals or barrier semaphores. Data moves between devices by JAX's collectives and lax.ppermute only.
A program may use at most 64 MiB of HBM per device.

```python
import jax
import jax.numpy as jnp
from jax import lax

BLOCK_ORDER = 512
CHANNELS = 256
BLOCKS = 32
SEQ_LEN = 16384
SEQUENCES = 4


def plant(entries, key, least, top_value):
    dims = entries.shape
    place = [jax.random.randint(jax.random.fold_in(key, axis), (), 0, dims[axis]) for axis in range(len(dims))]
    entries = entries.at[tuple(place)].set(least)
    longest = dims.index(max(dims))
    place[longest] = (place[longest] + 1) % dims[longest]
    return entries.at[tuple(place)].set(top_value)


def level_of(own_key, dims, split, smallest, largest):
    gain, own = 1.0, jax.random.fold_in(own_key, 6)
    for position, blocks in split:
        heights = jnp.exp(jax.random.uniform(jax.random.fold_in(own, position), (blocks,), jnp.float32, smallest / len(split), largest / len(split)))
        gain = gain * jnp.repeat(heights, dims[position] // blocks).reshape([-1 if axis == position else 1 for axis in range(len(dims))])
    return gain


def centred(key, extent, width, limit, split=(), kind=jnp.bfloat16):
    array = jax.random.normal(key, extent, jnp.float32) * width
    if len(split) > 0:
        array = level_of(key, extent, split, -0.22, 0.18) * array
    return jnp.clip(array, min=-limit, max=limit).astype(kind)


def setup_inputs(seed: int = 0) -> dict:
    key_of = jax.random.split(jax.random.key(seed), 7)
    tokens = centred(key_of[0], (SEQUENCES, SEQ_LEN, CHANNELS), 1.0, 6.0, ((0, 4), (1, 8)))
    cotangent = centred(key_of[1], (SEQUENCES, SEQ_LEN, CHANNELS), 0.5, 3.0, ((0, 4), (1, 8)))
    first_factor = centred(key_of[2], (BLOCKS, BLOCK_ORDER, BLOCK_ORDER), BLOCK_ORDER ** -0.5, 0.25, ((0, 8), (1, 4)))
    second_factor = centred(key_of[3], (BLOCK_ORDER, BLOCKS, BLOCKS), BLOCKS ** -0.5, 1.0, ((0, 8), (1, 4)))
    gate_source = plant(jax.random.randint(key_of[4], (CHANNELS,), 0, CHANNELS), jax.random.fold_in(key_of[4], 1), 0, CHANNELS - 1).astype(jnp.int32)
    alternate = jax.random.permutation(key_of[5], BLOCK_ORDER).astype(jnp.int32)
    return dict(tokens=tokens, cotangent=cotangent, first_factor=first_factor, second_factor=second_factor, gate_source=gate_source, alternate=alternate)


def reference(tokens, cotangent, first_factor, second_factor, gate_source, alternate):
    first_wide = first_factor.astype(jnp.float32)
    second_wide = second_factor.astype(jnp.float32)
    positions = jnp.arange(BLOCK_ORDER, dtype=jnp.int32)
    inverse = jnp.zeros((BLOCK_ORDER,), jnp.int32).at[alternate].set(positions)
    grad_one = jnp.zeros((BLOCKS, BLOCK_ORDER, BLOCK_ORDER), jnp.float32)
    grad_two = jnp.zeros((BLOCK_ORDER, BLOCKS, BLOCKS), jnp.float32)
    results = []
    for seq_index in range(SEQUENCES):
        inputs = tokens[seq_index]
        gate = jax.nn.sigmoid(inputs[:, gate_source].astype(jnp.float32))
        blocked = inputs.reshape(BLOCKS, BLOCK_ORDER, CHANNELS).astype(jnp.float32)
        mixed = jnp.einsum("ikj,ijc->ikc", first_wide, blocked).astype(jnp.bfloat16)
        regrouped = mixed[:, alternate, :]
        regrouped_wide = regrouped.astype(jnp.float32)
        z_out = jnp.einsum("jmi,ijc->jmc", second_wide, regrouped_wide).reshape(SEQ_LEN, CHANNELS)
        cot = cotangent[seq_index].astype(jnp.float32)
        dz_out = (cot * gate).astype(jnp.bfloat16)
        dgate = cot * z_out * gate * (1.0 - gate)
        dz_wide = dz_out.reshape(BLOCK_ORDER, BLOCKS, CHANNELS).astype(jnp.float32)
        part_two = jnp.einsum("jmc,ijc->jmi", dz_wide, regrouped_wide).astype(jnp.bfloat16)
        grad_two = grad_two + lax.optimization_barrier(part_two).astype(jnp.float32)
        dregrouped = jnp.einsum("jmi,jmc->ijc", second_wide, dz_wide).astype(jnp.bfloat16)
        dmixed = dregrouped[:, inverse, :].astype(jnp.float32)
        part_one = jnp.einsum("ikc,ijc->ikj", dmixed, blocked).astype(jnp.bfloat16)
        grad_one = grad_one + lax.optimization_barrier(part_one).astype(jnp.float32)
        dmix_in = jnp.einsum("ikj,ikc->ijc", first_wide, dmixed).reshape(SEQ_LEN, CHANNELS)
        spread = jax.ops.segment_sum(dgate.T, gate_source, num_segments=CHANNELS).T
        results.append((dmix_in + spread).astype(jnp.bfloat16))
    return jnp.stack(results), grad_one.astype(jnp.bfloat16), grad_two.astype(jnp.bfloat16)
```

```python
import functools

import jax
import jax.numpy as jnp
from jax import lax
from jax.experimental import pallas as pl
from jax.experimental.pallas import tpu as pltpu
from jax.sharding import PartitionSpec as P

BF16 = jnp.bfloat16
F32 = jnp.float32
LANE_GROUP = 16


def iota(shape, dim):
    return lax.broadcasted_iota(jnp.int32, shape, dim)


def one_hot(mask):
    return jnp.where(mask, 1.0, 0.0).astype(BF16)


def dot(a, b, da=1, db=0):
    return lax.dot_general(a, b, (((da,), (db,)), ((), ())), preferred_element_type=F32)


def call(body, outs, ins, scratch=(), flops=0, limit=40 << 20):
    size = sum(o.size * o.dtype.itemsize for o in outs) + sum(v.size * v.dtype.itemsize for v in ins)
    return pl.pallas_call(
        body,
        out_shape=outs,
        in_specs=[pl.BlockSpec(memory_space=pltpu.VMEM)] * len(ins),
        out_specs=[pl.BlockSpec(memory_space=pltpu.VMEM)] * len(outs),
        scratch_shapes=list(scratch),
        compiler_params=pltpu.CompilerParams(vmem_limit_bytes=limit),
        cost_estimate=pl.CostEstimate(flops=int(flops), bytes_accessed=int(size), transcendentals=0),
    )(*ins)


def of(shape, dtype=BF16):
    return jax.ShapeDtypeStruct(shape, dtype)


def swap(value, axis, step, size):
    return lax.ppermute(value, axis, [(p, p ^ step) for p in range(size)])


def pack_body(order, s_ref, out_ref):
    rows, j_here = s_ref.shape
    groups = j_here // LANE_GROUP
    lanes = order * LANE_GROUP
    m_here = rows // order
    s = s_ref[...]
    lane = iota((j_here, lanes), 1)
    keep = (iota((rows, lanes), 0) % order) == (iota((rows, lanes), 1) // LANE_GROUP)
    for g in range(groups):
        place = one_hot(iota((j_here, lanes), 0) == g * LANE_GROUP + lane % LANE_GROUP)
        wide = jnp.where(keep, dot(s, place), 0.0)
        packed = jnp.sum(wide.reshape(m_here, order, lanes), axis=1)
        out_ref[g * m_here : (g + 1) * m_here, :] = packed.astype(BF16)


def gate_body(x_ref, cot_ref, src_ref, dz_ref, h_ref):
    width = x_ref.shape[1]
    select = one_hot(iota((width, width), 0) == src_ref[...])
    step = 512

    @pl.loop(0, x_ref.shape[0] // step)
    def _(n):
        rows = pl.ds(pl.multiple_of(n * step, step), step)
        gate = jax.nn.sigmoid(dot(x_ref[rows, :], select))
        part = cot_ref[rows, :].astype(F32) * gate
        dz_ref[rows, :] = part.astype(BF16)
        h_ref[rows, :] = part * (1.0 - gate)


def regroup_back_body(batch, seq, order, *refs):
    pieces, dz_ref = refs[:batch], refs[batch]
    outs, second_ref, d_scr, r_scr = refs[batch + 1 : -3], refs[-3], refs[-2], refs[-1]
    me, here = lax.axis_index("batch"), lax.axis_index("seq")
    groups = second_ref.shape[0]
    lanes = order * LANE_GROUP
    m_here = order // batch
    for d in range(batch):
        piece = pieces[d][...].astype(F32)
        first = pl.multiple_of((me ^ d) * m_here, m_here)
        for g in range(groups):
            d_scr[g, pl.ds(first, m_here), :] = piece[g * m_here : (g + 1) * m_here]
    width = dz_ref.shape[1]

    @pl.loop(0, groups)
    def _(g):
        packed = d_scr[g].astype(BF16)
        second_ref[g] = packed
        tiled = one_hot((iota((order, lanes), 1) % order) == iota((order, lanes), 0))
        keep = (iota((lanes, lanes), 0) % LANE_GROUP) == (iota((lanes, lanes), 1) // order)
        weights = jnp.where(keep, dot(packed, tiled, 0, 0), 0.0).astype(BF16)
        dz = dz_ref[pl.ds(pl.multiple_of(g * lanes, lanes), lanes), :]
        result = dot(weights, dz).astype(BF16).reshape(order, LANE_GROUP, width)
        r_scr[:, pl.ds(pl.multiple_of(g * LANE_GROUP, LANE_GROUP), LANE_GROUP), :] = result

    blocks = order // seq
    for d in range(seq):
        outs[d][...] = r_scr[pl.ds((here ^ d) * blocks, blocks)]


def mix_body(batch, seq, *refs):
    pieces, x_ref, alt_ref = refs[:batch], refs[batch], refs[batch + 1]
    outs, p_scr, mix_scr, reg_scr = refs[batch + 2 : -3], refs[-3], refs[-2], refs[-1]
    me, here = lax.axis_index("batch"), lax.axis_index("seq")
    blocks, rows, order = pieces[0].shape
    j_here = order // seq
    from_rows = jnp.where(iota((order, order), 0) == alt_ref[...], 1.0, 0.0)
    p_scr[...] = from_rows.T.astype(BF16)

    @pl.loop(0, blocks)
    def _(i):
        x = x_ref[pl.ds(pl.multiple_of(i * order, order), order), :]
        for d in range(batch):
            first = pl.multiple_of((me ^ d) * rows, rows)
            mix_scr[pl.ds(first, rows), :] = dot(pieces[d][i], x).astype(BF16)
        reg_scr[...] = dot(p_scr[...], mix_scr[...]).astype(BF16)
        for d in range(seq):
            first = pl.multiple_of((here ^ d) * j_here, j_here)
            outs[d][i] = reg_scr[pl.ds(first, j_here), :]


def first_grad_body(batch, seq, *refs):
    pieces, x_ref, alt_ref = refs[:seq], refs[seq], refs[seq + 1]
    outs, dmixed_ref = refs[seq + 2 : seq + 2 + batch], refs[seq + 2 + batch]
    p_scr, reg_scr, part_scr = refs[-3:]
    me, here = lax.axis_index("batch"), lax.axis_index("seq")
    blocks, j_here, width = pieces[0].shape
    order = j_here * seq
    rows = order // batch
    p_scr[...] = one_hot(iota((order, order), 0) == alt_ref[...])

    @pl.loop(0, blocks)
    def _(i):
        for d in range(seq):
            first = pl.multiple_of((here ^ d) * j_here, j_here)
            reg_scr[pl.ds(first, j_here), :] = pieces[d][i]
        dmixed = dot(p_scr[...], reg_scr[...]).astype(BF16)
        dmixed_ref[i] = dmixed
        x = x_ref[pl.ds(pl.multiple_of(i * order, order), order), :]
        part_scr[...] = dot(dmixed, x, 1, 1).astype(BF16)
        for d in range(batch):
            first = pl.multiple_of((me ^ d) * rows, rows)
            outs[d][i] = part_scr[pl.ds(first, rows), :]


def mix_back_body(batch, *refs):
    pieces, dmixed_ref, out_ref = refs[:batch], refs[batch], refs[batch + 1]
    me = lax.axis_index("batch")
    blocks, rows, order = pieces[0].shape

    @pl.loop(0, blocks)
    def _(i):
        total = None
        for d in range(batch):
            first = pl.multiple_of((me ^ d) * rows, rows)
            term = dot(pieces[d][i], dmixed_ref[i, pl.ds(first, rows), :], 0, 0)
            total = term if total is None else total + term
        out_ref[pl.ds(pl.multiple_of(i * order, order), order), :] = total


def gather_blocks(seq, pieces, scr):
    here = lax.axis_index("seq")
    blocks = pieces[0].shape[0]
    for d in range(seq):
        scr[pl.ds((here ^ d) * blocks, blocks)] = pieces[d][...]


def second_grad_body(batch, seq, *refs):
    pieces, dz_ref = refs[:seq], refs[seq]
    outs, reg_ref, y_scr = refs[seq + 1 : seq + 1 + batch], refs[-2], refs[-1]
    me = lax.axis_index("batch")
    order, j_here, width = reg_ref.shape
    groups, lanes, m_here = j_here // LANE_GROUP, order * LANE_GROUP, order // batch
    gather_blocks(seq, pieces, reg_ref)

    @pl.loop(0, groups)
    def _(g):
        js = pl.ds(pl.multiple_of(g * LANE_GROUP, LANE_GROUP), LANE_GROUP)
        reg = reg_ref[:, js, :].reshape(lanes, width)
        dz = dz_ref[pl.ds(pl.multiple_of(g * lanes, lanes), lanes), :]
        wide = dot(dz, reg, 1, 1)
        col = iota((order, lanes), 1) % LANE_GROUP
        packed = wide[:order]
        for jj in range(1, LANE_GROUP):
            packed = jnp.where(col == jj, wide[jj * order : (jj + 1) * order], packed)
        y_scr[g] = packed

    for d in range(batch):
        first = pl.multiple_of((me ^ d) * m_here, m_here)
        rows = [y_scr[g, pl.ds(first, m_here), :] for g in range(groups)]
        outs[d][...] = jnp.concatenate(rows, axis=0).astype(BF16)


def tokens_body(reg_ref, second_ref, h_ref, src_ref, back_ref, out_ref):
    order, j_here, width = reg_ref.shape
    groups, lanes = j_here // LANE_GROUP, order * LANE_GROUP
    select = one_hot(iota((width, width), 0) == src_ref[...])

    @pl.loop(0, groups)
    def _(g):
        js = pl.ds(pl.multiple_of(g * LANE_GROUP, LANE_GROUP), LANE_GROUP)
        reg = reg_ref[:, js, :].reshape(lanes, width)
        packed = second_ref[g].astype(F32)
        col = iota((order, lanes), 1) % LANE_GROUP
        weights = jnp.concatenate(
            [jnp.where(col == jj, packed, 0.0).astype(BF16) for jj in range(LANE_GROUP)], axis=0
        )
        rows = pl.ds(pl.multiple_of(g * lanes, lanes), lanes)
        dgate = dot(weights, reg) * h_ref[rows, :]
        high = dgate.astype(BF16)
        low = (dgate - high.astype(F32)).astype(BF16)
        spread = dot(high, select, 1, 1) + dot(low, select, 1, 1)
        out_ref[rows, :] = (back_ref[rows, :] + spread).astype(BF16)


def pair_body(own_a, own_b, got_a, got_b, out_a, out_b):
    out_a[...] = own_a[...].astype(F32) + got_a[...].astype(F32)
    out_b[...] = (own_b[...].astype(F32) + got_b[...].astype(F32)).astype(BF16)


def add_body(own, got, out):
    out[...] = (own[...] + got[...].astype(F32)).astype(BF16)


def unpack_body(order, *refs):
    pieces, out_ref = refs[:-1], refs[-1]
    rows, j_here = out_ref.shape
    groups, lanes, m_here = j_here // LANE_GROUP, order * LANE_GROUP, rows // order
    total = pieces[0][...].astype(F32)
    for piece in pieces[1:]:
        total = total + piece[...].astype(F32)
    lane = iota((j_here, lanes), 1)
    keep = (iota((rows, lanes), 0) % order) == (iota((rows, lanes), 1) // LANE_GROUP)
    result = jnp.zeros((rows, j_here), F32)
    for g in range(groups):
        place = one_hot(iota((j_here, lanes), 0) == g * LANE_GROUP + lane % LANE_GROUP)
        packed = total[g * m_here : (g + 1) * m_here]
        wide = jnp.broadcast_to(packed[:, None, :], (m_here, order, lanes)).reshape(rows, lanes)
        result = result + dot(jnp.where(keep, wide, 0.0).astype(BF16), place, 1, 1)
    out_ref[...] = result.astype(BF16)


def packed_shards(tokens, cotangent, first_factor, second_factor, gate_source, alternate, batch, seq):
    x, cot = tokens[0], cotangent[0]
    rows_here, width = x.shape
    blocks, k_here, order = first_factor.shape
    j_here, m_here, count = second_factor.shape
    groups, lanes = j_here // LANE_GROUP, count * LANE_GROUP
    src = gate_source.reshape(1, width)
    alt = alternate.reshape(1, order)
    big = 2 * rows_here * order * width

    flat = jnp.transpose(second_factor, (1, 2, 0)).reshape(m_here * count, j_here)
    (mine,) = call(functools.partial(pack_body, count), [of((groups * m_here, lanes))], [flat])
    packed = [mine] + [swap(mine, "batch", d, batch) for d in range(1, batch)]
    dz, h = call(
        gate_body, [of((rows_here, width)), of((rows_here, width), F32)], [x, cot, src], flops=big // 2
    )
    piece = of((blocks, j_here, width))
    *back, second = call(
        functools.partial(regroup_back_body, batch, seq, count),
        [piece] * seq + [of((groups, count, lanes))],
        [*packed, dz],
        [pltpu.VMEM((groups, count, lanes), F32), pltpu.VMEM((count, j_here, width), BF16)],
        flops=2 * big,
    )
    order_of = sorted(range(1, seq), key=lambda d: -d)
    back_got = {d: swap(back[d], "seq", d, seq) for d in order_of}
    back_got[0] = back[0]

    first_ready, _ = lax.optimization_barrier((first_factor, packed[1:]))
    across = swap(first_ready, "batch", 2, batch)
    first = [first_ready, swap(first_ready, "batch", 1, batch), across, swap(across, "batch", 1, batch)]
    regrouped = call(
        functools.partial(mix_body, batch, seq),
        [piece] * seq,
        [*first, x, alt],
        [pltpu.VMEM((order, order), BF16), pltpu.VMEM((order, width), BF16), pltpu.VMEM((order, width), BF16)],
        flops=2 * big,
    )
    got = {d: swap(regrouped[d], "seq", d, seq) for d in order_of}
    got[0] = regrouped[0]

    *parts, dmixed = call(
        functools.partial(first_grad_body, batch, seq),
        [of((blocks, k_here, order))] * batch + [of((blocks, order, width))],
        [*[back_got[d] for d in range(seq)], x, alt],
        [pltpu.VMEM((order, order), BF16), pltpu.VMEM((order, width), BF16), pltpu.VMEM((order, order), BF16)],
        flops=2 * big,
    )
    near = swap(parts[1], "batch", 1, batch)
    far = swap(parts[3], "batch", 1, batch)
    (dmix_in,) = call(
        functools.partial(mix_back_body, batch), [of((rows_here, width), F32)], [*first, dmixed], flops=big
    )
    kept, sent = call(
        pair_body, [of(parts[0].shape, F32), of(parts[0].shape)], [parts[0], parts[2], near, far]
    )
    (grad_one,) = call(add_body, [of(parts[0].shape)], [kept, swap(sent, "batch", 2, batch)])

    *terms, gathered = call(
        functools.partial(second_grad_body, batch, seq),
        [of((groups * m_here, lanes))] * batch + [of((count, j_here, width))],
        [*[got[d] for d in range(seq)], dz],
        [pltpu.VMEM((groups, count, lanes), F32)],
        flops=2 * big,
    )
    terms_got = [terms[0]] + [swap(terms[d], "batch", d, batch) for d in range(1, batch)]
    (grad_tokens,) = call(
        tokens_body, [of((rows_here, width))], [gathered, second, h, src, dmix_in], flops=2 * big
    )
    (grad_flat,) = call(
        functools.partial(unpack_body, count), [of((m_here * count, j_here))], terms_got
    )
    grad_two = jnp.transpose(grad_flat.reshape(m_here, count, j_here), (2, 0, 1))
    return (grad_tokens[None], grad_one, grad_two)


def wide_shards(tokens, cotangent, first_factor, second_factor, gate_source, alternate):
    inputs = tokens[0]
    rows_here = inputs.shape[0]
    width = inputs.shape[1]
    order_len = alternate.shape[0]
    blocks_here = rows_here // order_len
    select = one_hot(lax.broadcasted_iota(jnp.int32, (width, width), 0) == gate_source[None, :])
    gate = jax.nn.sigmoid(jnp.dot(inputs, select, preferred_element_type=F32))
    first_full = lax.all_gather(first_factor, "batch", axis=1, tiled=True)
    second_full = lax.all_gather(second_factor, "batch", axis=1, tiled=True)
    blocked = inputs.reshape(blocks_here, order_len, width)
    mixed = jnp.einsum("ikj,ijc->ikc", first_full, blocked, preferred_element_type=F32).astype(BF16)
    shuffled = jnp.take(mixed, alternate, axis=1)
    piece = lax.all_to_all(shuffled, "seq", split_axis=1, concat_axis=0, tiled=True)
    z_blocks = jnp.einsum("jmi,ijc->jmc", second_full, piece, preferred_element_type=F32)
    j_here, count_second = z_blocks.shape[:2]
    z_out = z_blocks.reshape(rows_here, width)
    cot = cotangent[0].astype(F32)
    dz_out = (cot * gate).astype(BF16)
    dgate = cot * z_out * gate * (1.0 - gate)
    dz_blocks = dz_out.reshape(j_here, count_second, width)
    term_second = jnp.einsum("jmc,ijc->jmi", dz_blocks, piece, preferred_element_type=F32)
    grad_two = lax.psum_scatter(term_second.astype(BF16), "batch", scatter_dimension=1, tiled=True)
    dregrouped = jnp.einsum("jmi,jmc->ijc", second_full, dz_blocks, preferred_element_type=F32).astype(BF16)
    positions = lax.iota(jnp.int32, order_len)
    inverse = jnp.zeros((order_len,), jnp.int32).at[alternate].set(positions)
    restored = jnp.take(
        lax.all_to_all(dregrouped, "seq", split_axis=0, concat_axis=1, tiled=True), inverse, axis=1
    )
    dmix_in = jnp.einsum("ikj,ikc->ijc", first_full, restored, preferred_element_type=F32)
    term_first = jnp.einsum("ikc,ijc->ikj", restored, blocked, preferred_element_type=F32)
    grad_one = lax.psum_scatter(term_first.astype(BF16), "batch", scatter_dimension=1, tiled=True)
    spread = jnp.dot(dgate, select.T.astype(F32), precision=lax.Precision.HIGHEST)
    grad_tokens = (dmix_in.reshape(rows_here, width) + spread).astype(BF16)
    return (grad_tokens[None], grad_one, grad_two)


def solution(mesh):
    batch, seq = mesh.shape["batch"], mesh.shape["seq"]

    def shards(*args):
        j_here, m_here, count = args[3].shape
        if batch == 4 and seq & (seq - 1) == 0 and j_here % LANE_GROUP == 0 and m_here % 8 == 0 and count <= 32:
            return packed_shards(*args, batch, seq)
        return wide_shards(*args)

    in_specs = (
        P("batch", "seq", None),
        P("batch", "seq", None),
        P("seq", "batch", None),
        P("seq", "batch", None),
        P(),
        P(),
    )
    out_specs = (P("batch", "seq", None), P("seq", "batch", None), P("seq", "batch", None))
    return jax.shard_map(shards, mesh=mesh, in_specs=in_specs, out_specs=out_specs, check_vma=False)
```

```python
import functools

import jax
import jax.numpy as jnp
from jax import lax
from jax.experimental import pallas as pl
from jax.experimental.pallas import tpu as pltpu
from jax.sharding import PartitionSpec as P

BF16 = jnp.bfloat16
F32 = jnp.float32
LANE_GROUP = 16


def iota(shape, dim):
    return lax.broadcasted_iota(jnp.int32, shape, dim)


def one_hot(mask):
    return jnp.where(mask, 1.0, 0.0).astype(BF16)


def dot(a, b, da=1, db=0):
    return lax.dot_general(a, b, (((da,), (db,)), ((), ())), preferred_element_type=F32)


def call(body, outs, ins, scratch=(), flops=0, limit=40 << 20, cost=None):
    size = sum(o.size * o.dtype.itemsize for o in outs) + sum(v.size * v.dtype.itemsize for v in ins)
    return pl.pallas_call(
        body,
        out_shape=outs,
        in_specs=[pl.BlockSpec(memory_space=pltpu.VMEM)] * len(ins),
        out_specs=[pl.BlockSpec(memory_space=pltpu.VMEM)] * len(outs),
        scratch_shapes=list(scratch),
        compiler_params=pltpu.CompilerParams(vmem_limit_bytes=limit),
        cost_estimate=pl.CostEstimate(flops=0, bytes_accessed=0, transcendentals=0),
    )(*ins)


def of(shape, dtype=BF16):
    return jax.ShapeDtypeStruct(shape, dtype)


def swap(value, axis, step, size):
    return lax.ppermute(value, axis, [(p, p ^ step) for p in range(size)])


def after(value, *earlier):
    return lax.optimization_barrier((value, *earlier))[0]


def pack_body(order, s_hbm, out_ref, s_scr, sem):
    copy = pltpu.make_async_copy(s_hbm, s_scr, sem)
    copy.start()
    copy.wait()
    rows, j_here = s_scr.shape
    groups = j_here // LANE_GROUP
    lanes = order * LANE_GROUP
    m_here = rows // order
    s = s_scr[...]
    lane = iota((j_here, lanes), 1)
    keep = (iota((rows, lanes), 0) % order) == (iota((rows, lanes), 1) // LANE_GROUP)
    for g in range(groups):
        place = one_hot(iota((j_here, lanes), 0) == g * LANE_GROUP + lane % LANE_GROUP)
        wide = jnp.where(keep, dot(s, place), 0.0)
        packed = jnp.sum(wide.reshape(m_here, order, lanes), axis=1)
        out_ref[g * m_here : (g + 1) * m_here, :] = packed.astype(BF16)


def gate_body(step, x_hbm, cot_hbm, src_ref, dz_ref, h_ref, x_scr, cot_scr, sems):
    rows, width = dz_ref.shape
    parts = rows // step
    copies = []
    for n in range(parts):
        part = pl.ds(n * step, step)
        copies.append(
            (
                pltpu.make_async_copy(x_hbm.at[part, :], x_scr.at[part, :], sems.at[0, n]),
                pltpu.make_async_copy(cot_hbm.at[part, :], cot_scr.at[part, :], sems.at[1, n]),
            )
        )
    for pair in copies:
        for copy in pair:
            copy.start()
    select = one_hot(iota((width, width), 0) == src_ref[...])
    for n in range(parts):
        for copy in copies[n]:
            copy.wait()
        part = slice(n * step, (n + 1) * step)
        gate = jax.nn.sigmoid(dot(x_scr[part, :], select))
        scaled = cot_scr[part, :].astype(F32) * gate
        dz_ref[part, :] = scaled.astype(BF16)
        h_ref[part, :] = scaled * (1.0 - gate)


def gate_call(x, cot, src):
    rows, width = x.shape
    step = min(rows, 512)
    whole = pl.BlockSpec(memory_space=pltpu.VMEM)
    left = pl.BlockSpec(memory_space=pltpu.HBM)
    return pl.pallas_call(
        functools.partial(gate_body, step),
        out_shape=[of((rows, width)), of((rows, width), F32)],
        in_specs=[left, left, whole],
        out_specs=[whole, whole],
        scratch_shapes=[
            pltpu.VMEM((rows, width), BF16),
            pltpu.VMEM((rows, width), BF16),
            pltpu.SemaphoreType.DMA((2, rows // step)),
        ],
        compiler_params=pltpu.CompilerParams(vmem_limit_bytes=60 << 20),
        cost_estimate=pl.CostEstimate(
            flops=2 * rows * width * width, bytes_accessed=10 * rows * width, transcendentals=rows * width
        ),
    )(x, cot, src)


def regroup_back_body(batch, seq, order, *refs):
    pieces, dz_ref = refs[:batch], refs[batch]
    outs, second_ref, d_scr, r_scr = refs[batch + 1 : -3], refs[-3], refs[-2], refs[-1]
    me, here = lax.axis_index("batch"), lax.axis_index("seq")
    groups = second_ref.shape[0]
    lanes = order * LANE_GROUP
    m_here = order // batch
    for d in range(batch):
        piece = pieces[d][...].astype(F32)
        first = pl.multiple_of((me ^ d) * m_here, m_here)
        for g in range(groups):
            d_scr[g, pl.ds(first, m_here), :] = piece[g * m_here : (g + 1) * m_here]
    width = dz_ref.shape[1]

    @pl.loop(0, groups)
    def _(g):
        packed = d_scr[g].astype(BF16)
        second_ref[g] = packed
        tiled = one_hot((iota((order, lanes), 1) % order) == iota((order, lanes), 0))
        keep = (iota((lanes, lanes), 0) % LANE_GROUP) == (iota((lanes, lanes), 1) // order)
        weights = jnp.where(keep, dot(packed, tiled, 0, 0), 0.0).astype(BF16)
        dz = dz_ref[pl.ds(pl.multiple_of(g * lanes, lanes), lanes), :]
        result = dot(weights, dz).astype(BF16).reshape(order, LANE_GROUP, width)
        r_scr[:, pl.ds(pl.multiple_of(g * LANE_GROUP, LANE_GROUP), LANE_GROUP), :] = result

    blocks = order // seq
    for d in range(seq):
        outs[d][...] = r_scr[pl.ds((here ^ d) * blocks, blocks)]


def mix_body(batch, seq, *refs):
    pieces, x_ref, alt_ref = refs[:batch], refs[batch], refs[batch + 1]
    outs, p_scr, mix_scr, reg_scr = refs[batch + 2 : -3], refs[-3], refs[-2], refs[-1]
    me, here = lax.axis_index("batch"), lax.axis_index("seq")
    blocks, rows, order = pieces[0].shape
    j_here = order // seq
    from_rows = jnp.where(iota((order, order), 0) == alt_ref[...], 1.0, 0.0)
    p_scr[...] = from_rows.T.astype(BF16)

    @pl.loop(0, blocks)
    def _(i):
        x = x_ref[pl.ds(pl.multiple_of(i * order, order), order), :]
        for d in range(batch):
            first = pl.multiple_of((me ^ d) * rows, rows)
            mix_scr[pl.ds(first, rows), :] = dot(pieces[d][i], x).astype(BF16)
        reg_scr[...] = dot(p_scr[...], mix_scr[...]).astype(BF16)
        for d in range(seq):
            first = pl.multiple_of((here ^ d) * j_here, j_here)
            outs[d][i] = reg_scr[pl.ds(first, j_here), :]


def first_grad_body(batch, seq, *refs):
    pieces, x_ref, alt_ref = refs[:seq], refs[seq], refs[seq + 1]
    outs, dmixed_ref = refs[seq + 2 : seq + 2 + batch], refs[seq + 2 + batch]
    p_scr, reg_scr, part_scr = refs[-3:]
    me, here = lax.axis_index("batch"), lax.axis_index("seq")
    blocks, j_here, width = pieces[0].shape
    order = j_here * seq
    rows = order // batch
    p_scr[...] = one_hot(iota((order, order), 0) == alt_ref[...])

    @pl.loop(0, blocks)
    def _(i):
        for d in range(seq):
            first = pl.multiple_of((here ^ d) * j_here, j_here)
            reg_scr[pl.ds(first, j_here), :] = pieces[d][i]
        dmixed = dot(p_scr[...], reg_scr[...]).astype(BF16)
        dmixed_ref[i] = dmixed
        x = x_ref[pl.ds(pl.multiple_of(i * order, order), order), :]
        part_scr[...] = dot(dmixed, x, 1, 1).astype(BF16)
        for d in range(batch):
            first = pl.multiple_of((me ^ d) * rows, rows)
            outs[d][i] = part_scr[pl.ds(first, rows), :]


def mix_back_body(batch, *refs):
    pieces, dmixed_ref, second_ref, out_ref, weights_ref = refs[:batch], *refs[batch:]
    me = lax.axis_index("batch")
    blocks, rows, order = pieces[0].shape
    groups, count, lanes = second_ref.shape

    @pl.loop(0, blocks)
    def _(i):
        total = None
        for d in range(batch):
            first = pl.multiple_of((me ^ d) * rows, rows)
            term = dot(pieces[d][i], dmixed_ref[i, pl.ds(first, rows), :], 0, 0)
            total = term if total is None else total + term
        out_ref[pl.ds(pl.multiple_of(i * order, order), order), :] = total

    @pl.loop(0, groups)
    def _(g):
        packed = second_ref[g].astype(F32)
        col = iota((count, lanes), 1) % LANE_GROUP
        for jj in range(LANE_GROUP):
            weights_ref[g, jj * count : (jj + 1) * count, :] = jnp.where(col == jj, packed, 0.0).astype(BF16)


def gather_blocks(seq, pieces, scr):
    here = lax.axis_index("seq")
    blocks = pieces[0].shape[0]
    for d in range(seq):
        scr[pl.ds((here ^ d) * blocks, blocks)] = pieces[d][...]


def second_grad_body(batch, seq, *refs):
    pieces, dz_ref = refs[:seq], refs[seq]
    outs, reg_ref, y_scr = refs[seq + 1 : seq + 1 + batch], refs[-2], refs[-1]
    me = lax.axis_index("batch")
    order, j_here, width = reg_ref.shape
    groups, lanes, m_here = j_here // LANE_GROUP, order * LANE_GROUP, order // batch
    gather_blocks(seq, pieces, reg_ref)

    @pl.loop(0, groups)
    def _(g):
        js = pl.ds(pl.multiple_of(g * LANE_GROUP, LANE_GROUP), LANE_GROUP)
        reg = reg_ref[:, js, :].reshape(lanes, width)
        dz = dz_ref[pl.ds(pl.multiple_of(g * lanes, lanes), lanes), :]
        wide = dot(dz, reg, 1, 1)
        col = iota((order, lanes), 1) % LANE_GROUP
        packed = wide[:order]
        for jj in range(1, LANE_GROUP):
            packed = jnp.where(col == jj, wide[jj * order : (jj + 1) * order], packed)
        y_scr[g] = packed

    for d in range(batch):
        first = pl.multiple_of((me ^ d) * m_here, m_here)
        rows = [y_scr[g, pl.ds(first, m_here), :] for g in range(groups)]
        outs[d][...] = jnp.concatenate(rows, axis=0).astype(BF16)


def tokens_body(reg_ref, weights_ref, h_ref, src_ref, back_ref, out_ref):
    order, j_here, width = reg_ref.shape
    groups, lanes = j_here // LANE_GROUP, order * LANE_GROUP
    select = one_hot(iota((width, width), 0) == src_ref[...])
    for g in range(groups):
        reg = reg_ref[:, g * LANE_GROUP : (g + 1) * LANE_GROUP, :].reshape(lanes, width)
        rows = slice(g * lanes, (g + 1) * lanes)
        dgate = (dot(weights_ref[g], reg) * h_ref[rows, :]).astype(BF16)
        out_ref[rows, :] = (back_ref[rows, :] + dot(dgate, select, 1, 1)).astype(BF16)


def pair_body(own_a, own_b, got_a, got_b, out_a, out_b):
    out_a[...] = own_a[...].astype(F32) + got_a[...].astype(F32)
    out_b[...] = (own_b[...].astype(F32) + got_b[...].astype(F32)).astype(BF16)


def add_body(own, got, out):
    out[...] = (own[...] + got[...].astype(F32)).astype(BF16)


def unpack_body(order, *refs):
    pieces, out_ref = refs[:-1], refs[-1]
    rows, j_here = out_ref.shape
    groups, lanes, m_here = j_here // LANE_GROUP, order * LANE_GROUP, rows // order
    total = pieces[0][...].astype(F32)
    for piece in pieces[1:]:
        total = total + piece[...].astype(F32)
    lane = iota((j_here, lanes), 1)
    keep = (iota((rows, lanes), 0) % order) == (iota((rows, lanes), 1) // LANE_GROUP)
    result = jnp.zeros((rows, j_here), F32)
    for g in range(groups):
        place = one_hot(iota((j_here, lanes), 0) == g * LANE_GROUP + lane % LANE_GROUP)
        packed = total[g * m_here : (g + 1) * m_here]
        wide = jnp.broadcast_to(packed[:, None, :], (m_here, order, lanes)).reshape(rows, lanes)
        result = result + dot(jnp.where(keep, wide, 0.0).astype(BF16), place, 1, 1)
    out_ref[...] = result.astype(BF16)


def packed_shards(tokens, cotangent, first_factor, second_factor, gate_source, alternate, batch, seq):
    x, cot = tokens[0], cotangent[0]
    rows_here, width = x.shape
    blocks, k_here, order = first_factor.shape
    j_here, m_here, count = second_factor.shape
    groups, lanes = j_here // LANE_GROUP, count * LANE_GROUP
    src = gate_source.reshape(1, width)
    alt = alternate.reshape(1, order)
    big = 2 * rows_here * order * width

    flat = jnp.transpose(second_factor, (1, 2, 0)).reshape(m_here * count, j_here)
    mine = pl.pallas_call(
        functools.partial(pack_body, count),
        out_shape=of((groups * m_here, lanes)),
        in_specs=[pl.BlockSpec(memory_space=pltpu.HBM)],
        out_specs=pl.BlockSpec(memory_space=pltpu.VMEM),
        scratch_shapes=[pltpu.VMEM(flat.shape, BF16), pltpu.SemaphoreType.DMA],
        compiler_params=pltpu.CompilerParams(vmem_limit_bytes=60 << 20),
        cost_estimate=pl.CostEstimate(flops=4 * flat.size * lanes, bytes_accessed=4 * flat.size, transcendentals=0),
    )(flat)
    packed = [mine] + [swap(mine, "batch", d, batch) for d in (2, 3, 1)]
    packed = [packed[0], packed[3], packed[1], packed[2]]
    dz, h = gate_call(x, cot, src)

    across = swap(after(first_factor, mine), "batch", 2, batch)
    beside = swap(after(first_factor, dz, *packed[1:]), "batch", 1, batch)
    piece = of((blocks, j_here, width))
    *back, second = call(
        functools.partial(regroup_back_body, batch, seq, count),
        [piece] * seq + [of((groups, count, lanes))],
        [*packed, dz],
        [pltpu.VMEM((groups, count, lanes), F32), pltpu.VMEM((count, j_here, width), BF16)],
        flops=2 * big,
    )
    far_first = sorted(range(1, seq), key=lambda d: -d)

    def exchange(blocks_out):
        got = {0: blocks_out[0]}
        for d in far_first:
            ready = after(blocks_out[d], got[far_first[0]]) if d < seq // 2 else blocks_out[d]
            got[d] = swap(ready, "seq", d, seq)
        return [got[d] for d in range(seq)]

    back_got = exchange(back)
    first = [first_factor, beside, across, swap(after(across, back[0]), "batch", 1, batch)]
    regrouped = call(
        functools.partial(mix_body, batch, seq),
        [piece] * seq,
        [*first, x, alt],
        [pltpu.VMEM((order, order), BF16), pltpu.VMEM((order, width), BF16), pltpu.VMEM((order, width), BF16)],
        flops=2 * big,
    )
    got = exchange(regrouped)

    back_got[0] = after(back_got[0], regrouped[0], got[far_first[0]])
    *parts, dmixed = call(
        functools.partial(first_grad_body, batch, seq),
        [of((blocks, k_here, order))] * batch + [of((blocks, order, width))],
        [*back_got, x, alt],
        [pltpu.VMEM((order, order), BF16), pltpu.VMEM((order, width), BF16), pltpu.VMEM((order, order), BF16)],
        flops=2 * big,
    )
    near = swap(after(parts[1], got[far_first[1]]), "batch", 1, batch)
    far = swap(after(parts[3], got[far_first[1]]), "batch", 1, batch)
    dmix_in, weights = call(
        functools.partial(mix_back_body, batch),
        [of((rows_here, width), F32), of((groups, lanes, lanes))],
        [*first, dmixed, second],
        flops=big,
    )
    kept, summed = call(
        pair_body, [of(parts[0].shape, F32), of(parts[0].shape)], [parts[0], parts[2], near, far]
    )
    (grad_one,) = call(add_body, [of(parts[0].shape)], [kept, swap(summed, "batch", 2, batch)])

    *terms, gathered = call(
        functools.partial(second_grad_body, batch, seq),
        [of((groups * m_here, lanes))] * batch + [of((count, j_here, width))],
        [*got, dz],
        [pltpu.VMEM((groups, count, lanes), F32)],
        flops=2 * big,
    )
    terms_got = [terms[0]] + [swap(terms[d], "batch", d, batch) for d in range(1, batch)]
    (grad_tokens,) = call(
        tokens_body, [of((rows_here, width))], [gathered, weights, h, src, dmix_in], flops=2 * big
    )
    (grad_flat,) = call(
        functools.partial(unpack_body, count), [of((m_here * count, j_here))], terms_got
    )
    grad_two = jnp.transpose(grad_flat.reshape(m_here, count, j_here), (2, 0, 1))
    return (grad_tokens[None], grad_one, grad_two)


def wide_shards(tokens, cotangent, first_factor, second_factor, gate_source, alternate):
    inputs = tokens[0]
    rows_here = inputs.shape[0]
    width = inputs.shape[1]
    order_len = alternate.shape[0]
    blocks_here = rows_here // order_len
    select = one_hot(lax.broadcasted_iota(jnp.int32, (width, width), 0) == gate_source[None, :])
    gate = jax.nn.sigmoid(jnp.dot(inputs, select, preferred_element_type=F32))
    first_full = lax.all_gather(first_factor, "batch", axis=1, tiled=True)
    second_full = lax.all_gather(second_factor, "batch", axis=1, tiled=True)
    blocked = inputs.reshape(blocks_here, order_len, width)
    mixed = jnp.einsum("ikj,ijc->ikc", first_full, blocked, preferred_element_type=F32).astype(BF16)
    shuffled = jnp.take(mixed, alternate, axis=1)
    piece = lax.all_to_all(shuffled, "seq", split_axis=1, concat_axis=0, tiled=True)
    z_blocks = jnp.einsum("jmi,ijc->jmc", second_full, piece, preferred_element_type=F32)
    j_here, count_second = z_blocks.shape[:2]
    z_out = z_blocks.reshape(rows_here, width)
    cot = cotangent[0].astype(F32)
    dz_out = (cot * gate).astype(BF16)
    dgate = cot * z_out * gate * (1.0 - gate)
    dz_blocks = dz_out.reshape(j_here, count_second, width)
    term_second = jnp.einsum("jmc,ijc->jmi", dz_blocks, piece, preferred_element_type=F32)
    grad_two = lax.psum_scatter(term_second.astype(BF16), "batch", scatter_dimension=1, tiled=True)
    dregrouped = jnp.einsum("jmi,jmc->ijc", second_full, dz_blocks, preferred_element_type=F32).astype(BF16)
    positions = lax.iota(jnp.int32, order_len)
    inverse = jnp.zeros((order_len,), jnp.int32).at[alternate].set(positions)
    restored = jnp.take(
        lax.all_to_all(dregrouped, "seq", split_axis=0, concat_axis=1, tiled=True), inverse, axis=1
    )
    dmix_in = jnp.einsum("ikj,ikc->ijc", first_full, restored, preferred_element_type=F32)
    term_first = jnp.einsum("ikc,ijc->ikj", restored, blocked, preferred_element_type=F32)
    grad_one = lax.psum_scatter(term_first.astype(BF16), "batch", scatter_dimension=1, tiled=True)
    spread = jnp.dot(dgate, select.T.astype(F32), precision=lax.Precision.HIGHEST)
    grad_tokens = (dmix_in.reshape(rows_here, width) + spread).astype(BF16)
    return (grad_tokens[None], grad_one, grad_two)


def solution(mesh):
    batch, seq = mesh.shape["batch"], mesh.shape["seq"]

    def shards(*args):
        j_here, m_here, count = args[3].shape
        if batch == 4 and seq & (seq - 1) == 0 and j_here % LANE_GROUP == 0 and m_here % 8 == 0 and count <= 32:
            return packed_shards(*args, batch, seq)
        return wide_shards(*args)

    in_specs = (
        P("batch", "seq", None),
        P("batch", "seq", None),
        P("seq", "batch", None),
        P("seq", "batch", None),
        P(),
        P(),
    )
    out_specs = (P("batch", "seq", None), P("seq", "batch", None), P("seq", "batch", None))
    return jax.shard_map(shards, mesh=mesh, in_specs=in_specs, out_specs=out_specs, check_vma=False)
```

```python
import functools

import jax
import jax.numpy as jnp
from jax import lax
from jax.experimental import pallas as pl
from jax.experimental.pallas import tpu as pltpu
from jax.sharding import PartitionSpec as P

BF16 = jnp.bfloat16
F32 = jnp.float32
LANE_GROUP = 16
CFG = {'cost': {}, 'direct': False, 'rsdirect': False, 'f2early': False, 'order': [[7, 6, 5, 4, 3, 2, 1], [7, 6, 5, 4, 3, 2, 1]], 'deps': {'h3': ['h7'], 'h2': ['h7'], 'h1': ['h7'], 'fx': ['h7', 'h4'], 'F1': ['M', 'H1', 'H2', 'H3', 'fx'], 'near': ['H7', 'H6'], 'far': ['H7', 'H6'], 'pair': ['F2'], 'unpack': ['add'], 'H1': ['h3'], 'H2': ['M']}}


def iota(shape, dim):
    return lax.broadcasted_iota(jnp.int32, shape, dim)


def one_hot(mask):
    return jnp.where(mask, 1.0, 0.0).astype(BF16)


def dot(a, b, da=1, db=0):
    return lax.dot_general(a, b, (((da,), (db,)), ((), ())), preferred_element_type=F32)


def call(body, outs, ins, scratch=(), spaces={}, limit=40 << 20, weight=0):
    name = getattr(body, "func", body).__name__
    weight = CFG['cost'].get(name, 0)
    return pl.pallas_call(
        body,
        name=name,
        out_shape=outs,
        in_specs=[pl.BlockSpec(memory_space=spaces.get(n, pltpu.VMEM)) for n in range(len(ins))],
        out_specs=[pl.BlockSpec(memory_space=pltpu.VMEM)] * len(outs),
        scratch_shapes=list(scratch),
        compiler_params=pltpu.CompilerParams(vmem_limit_bytes=limit),
        cost_estimate=pl.CostEstimate(flops=0, bytes_accessed=weight, transcendentals=0),
    )(*ins)


def of(shape, dtype=BF16):
    return jax.ShapeDtypeStruct(shape, dtype)


def swap(value, axis, step, size):
    return lax.ppermute(value, axis, [(p, p ^ step) for p in range(size)])


def after(value, *earlier):
    return lax.optimization_barrier((value, *earlier))[0]


def pack_body(order, s_ref, out_ref):
    rows, j_here = s_ref.shape
    groups = j_here // LANE_GROUP
    lanes = order * LANE_GROUP
    m_here = rows // order
    s = s_ref[...]
    lane = iota((j_here, lanes), 1)
    keep = (iota((rows, lanes), 0) % order) == (iota((rows, lanes), 1) // LANE_GROUP)
    for g in range(groups):
        place = one_hot(iota((j_here, lanes), 0) == g * LANE_GROUP + lane % LANE_GROUP)
        wide = jnp.where(keep, dot(s, place), 0.0)
        packed = jnp.sum(wide.reshape(m_here, order, lanes), axis=1)
        out_ref[g * m_here : (g + 1) * m_here, :] = packed.astype(BF16)


def gate_body(step, x_hbm, cot_hbm, src_ref, dz_hbm, x_scr, cot_scr, dz_scr, sems):
    rows, width = x_scr.shape
    parts = rows // step
    reads, writes = [], []
    for n in range(parts):
        part = pl.ds(n * step, step)
        reads.append(pltpu.make_async_copy(x_hbm.at[part, :], x_scr.at[part, :], sems.at[0, n]))
        reads.append(pltpu.make_async_copy(cot_hbm.at[part, :], cot_scr.at[part, :], sems.at[1, n]))
        writes.append(pltpu.make_async_copy(dz_scr.at[part, :], dz_hbm.at[part, :], sems.at[2, n]))
    for copy in reads:
        copy.start()
    select = one_hot(iota((width, width), 0) == src_ref[...])
    for n in range(parts):
        reads[2 * n].wait()
        reads[2 * n + 1].wait()
        part = slice(n * step, (n + 1) * step)
        gate = jax.nn.sigmoid(dot(x_scr[part, :], select))
        dz_scr[part, :] = (cot_scr[part, :].astype(F32) * gate).astype(BF16)
        writes[n].start()
    for copy in writes:
        copy.wait()


def gate_call(x, cot, src):
    rows, width = x.shape
    step = min(rows, 256)
    left = pl.BlockSpec(memory_space=pltpu.HBM)
    return pl.pallas_call(
        functools.partial(gate_body, step),
        name="gate_body",
        out_shape=of((rows, width)),
        in_specs=[left, left, pl.BlockSpec(memory_space=pltpu.VMEM)],
        out_specs=left,
        scratch_shapes=[pltpu.VMEM((rows, width), BF16)] * 3 + [pltpu.SemaphoreType.DMA((3, rows // step))],
        compiler_params=pltpu.CompilerParams(vmem_limit_bytes=60 << 20),
        cost_estimate=pl.CostEstimate(flops=0, bytes_accessed=0, transcendentals=0),
    )(x, cot, src)


def regroup_back_body(batch, seq, order, *refs):
    pieces, dz_hbm = refs[:batch], refs[batch]
    outs, second_ref, d_scr, r_scr, dz_ref, sems = refs[batch + 1 : -5], *refs[-5:]
    me, here = lax.axis_index("batch"), lax.axis_index("seq")
    groups = second_ref.shape[0]
    lanes = order * LANE_GROUP
    m_here = order // batch
    reads = []
    for g in range(groups):
        part = pl.ds(g * lanes, lanes)
        reads.append(pltpu.make_async_copy(dz_hbm.at[part, :], dz_ref.at[part, :], sems.at[g]))
        reads[g].start()
    for d in range(batch):
        piece = pieces[d][...].astype(F32)
        first = pl.multiple_of((me ^ d) * m_here, m_here)
        for g in range(groups):
            d_scr[g, pl.ds(first, m_here), :] = piece[g * m_here : (g + 1) * m_here]
    width = dz_ref.shape[1]
    tiled = one_hot((iota((order, lanes), 1) % order) == iota((order, lanes), 0))
    keep = (iota((lanes, lanes), 0) % LANE_GROUP) == (iota((lanes, lanes), 1) // order)
    for g in range(groups):
        packed = d_scr[g].astype(BF16)
        second_ref[g] = packed
        weights = jnp.where(keep, dot(packed, tiled, 0, 0), 0.0).astype(BF16)
        reads[g].wait()
        result = dot(weights, dz_ref[g * lanes : (g + 1) * lanes, :]).astype(BF16)
        r_scr[:, g * LANE_GROUP : (g + 1) * LANE_GROUP, :] = result.reshape(order, LANE_GROUP, width)

    blocks = order // seq
    for d in range(seq):
        outs[d][...] = r_scr[pl.ds((here ^ d) * blocks, blocks)]


def mix_body(batch, seq, *refs):
    pieces, x_ref, alt_ref = refs[:batch], refs[batch], refs[batch + 1]
    outs, p_scr, mix_scr, reg_scr = refs[batch + 2 : -3], refs[-3], refs[-2], refs[-1]
    me, here = lax.axis_index("batch"), lax.axis_index("seq")
    blocks, rows, order = pieces[0].shape
    j_here = order // seq
    from_rows = jnp.where(iota((order, order), 0) == alt_ref[...], 1.0, 0.0)
    p_scr[...] = from_rows.T.astype(BF16)

    @pl.loop(0, blocks)
    def _(i):
        x = x_ref[pl.ds(pl.multiple_of(i * order, order), order), :]
        for d in range(batch):
            first = pl.multiple_of((me ^ d) * rows, rows)
            mix_scr[pl.ds(first, rows), :] = dot(pieces[d][i], x).astype(BF16)
        reg_scr[...] = dot(p_scr[...], mix_scr[...]).astype(BF16)
        for d in range(seq):
            first = pl.multiple_of((here ^ d) * j_here, j_here)
            outs[d][i] = reg_scr[pl.ds(first, j_here), :]


def first_grad_body(batch, seq, *refs):
    pieces, x_ref, alt_ref = refs[:seq], refs[seq], refs[seq + 1]
    outs, dmixed_ref = refs[seq + 2 : seq + 2 + batch], refs[seq + 2 + batch]
    p_scr, reg_scr, part_scr = refs[-3:]
    me, here = lax.axis_index("batch"), lax.axis_index("seq")
    blocks, j_here, width = pieces[0].shape
    order = j_here * seq
    rows = order // batch
    p_scr[...] = one_hot(iota((order, order), 0) == alt_ref[...])

    @pl.loop(0, blocks)
    def _(i):
        for d in range(seq):
            first = pl.multiple_of((here ^ d) * j_here, j_here)
            reg_scr[pl.ds(first, j_here), :] = pieces[d][i]
        dmixed = dot(p_scr[...], reg_scr[...]).astype(BF16)
        dmixed_ref[i] = dmixed
        x = x_ref[pl.ds(pl.multiple_of(i * order, order), order), :]
        part_scr[...] = dot(dmixed, x, 1, 1).astype(BF16)
        for d in range(batch):
            first = pl.multiple_of((me ^ d) * rows, rows)
            outs[d][i] = part_scr[pl.ds(first, rows), :]


def mix_back_body(batch, *refs):
    pieces, dmixed_ref, second_ref, x_ref, cot_ref, src_ref = refs[:batch], *refs[batch:-3]
    out_ref, weights_ref, h_ref = refs[-3:]
    me = lax.axis_index("batch")
    blocks, rows, order = pieces[0].shape
    groups, count, lanes = second_ref.shape

    @pl.loop(0, blocks)
    def _(i):
        total = None
        for d in range(batch):
            first = pl.multiple_of((me ^ d) * rows, rows)
            term = dot(pieces[d][i], dmixed_ref[i, pl.ds(first, rows), :], 0, 0)
            total = term if total is None else total + term
        out_ref[pl.ds(pl.multiple_of(i * order, order), order), :] = total

    width = x_ref.shape[1]
    select = one_hot(iota((width, width), 0) == src_ref[...])

    @pl.loop(0, blocks)
    def _(i):
        part = pl.ds(pl.multiple_of(i * order, order), order)
        gate = jax.nn.sigmoid(dot(x_ref[part, :], select))
        h_ref[part, :] = cot_ref[part, :].astype(F32) * gate * (1.0 - gate)

    @pl.loop(0, groups)
    def _(g):
        packed = second_ref[g].astype(F32)
        col = iota((count, lanes), 1) % LANE_GROUP
        for jj in range(LANE_GROUP):
            weights_ref[g, jj * count : (jj + 1) * count, :] = jnp.where(col == jj, packed, 0.0).astype(BF16)


def gather_blocks(seq, pieces, scr):
    here = lax.axis_index("seq")
    blocks = pieces[0].shape[0]
    for d in range(seq):
        scr[pl.ds((here ^ d) * blocks, blocks)] = pieces[d][...]


def second_grad_body(batch, seq, *refs):
    pieces, dz_ref = refs[:seq], refs[seq]
    outs, reg_ref, y_scr = refs[seq + 1 : seq + 1 + batch], refs[-2], refs[-1]
    me = lax.axis_index("batch")
    order, j_here, width = reg_ref.shape
    groups, lanes, m_here = j_here // LANE_GROUP, order * LANE_GROUP, order // batch
    gather_blocks(seq, pieces, reg_ref)

    @pl.loop(0, groups)
    def _(g):
        js = pl.ds(pl.multiple_of(g * LANE_GROUP, LANE_GROUP), LANE_GROUP)
        reg = reg_ref[:, js, :].reshape(lanes, width)
        dz = dz_ref[pl.ds(pl.multiple_of(g * lanes, lanes), lanes), :]
        wide = dot(dz, reg, 1, 1)
        col = iota((order, lanes), 1) % LANE_GROUP
        packed = wide[:order]
        for jj in range(1, LANE_GROUP):
            packed = jnp.where(col == jj, wide[jj * order : (jj + 1) * order], packed)
        y_scr[g] = packed

    for d in range(batch):
        first = pl.multiple_of((me ^ d) * m_here, m_here)
        rows = [y_scr[g, pl.ds(first, m_here), :] for g in range(groups)]
        outs[d][...] = jnp.concatenate(rows, axis=0).astype(BF16)


def tokens_body(reg_ref, weights_ref, h_ref, src_ref, back_ref, out_ref):
    order, j_here, width = reg_ref.shape
    groups, lanes = j_here // LANE_GROUP, order * LANE_GROUP
    select = one_hot(iota((width, width), 0) == src_ref[...])
    for g in range(groups):
        reg = reg_ref[:, g * LANE_GROUP : (g + 1) * LANE_GROUP, :].reshape(lanes, width)
        rows = slice(g * lanes, (g + 1) * lanes)
        dgate = (dot(weights_ref[g], reg) * h_ref[rows, :]).astype(BF16)
        out_ref[rows, :] = (back_ref[rows, :] + dot(dgate, select, 1, 1)).astype(BF16)


def pair_body(own_a, own_b, got_a, got_b, out_a, out_b):
    out_a[...] = own_a[...].astype(F32) + got_a[...].astype(F32)
    out_b[...] = (own_b[...].astype(F32) + got_b[...].astype(F32)).astype(BF16)


def sum_body(own, *refs):
    total = own[...].astype(F32)
    for got in refs[:-1]:
        total = total + got[...].astype(F32)
    refs[-1][...] = total.astype(BF16)


def add_body(own, got, out):
    out[...] = (own[...] + got[...].astype(F32)).astype(BF16)


def unpack_body(order, *refs):
    pieces, out_ref = refs[:-1], refs[-1]
    rows, j_here = out_ref.shape
    groups, lanes, m_here = j_here // LANE_GROUP, order * LANE_GROUP, rows // order
    total = pieces[0][...].astype(F32)
    for piece in pieces[1:]:
        total = total + piece[...].astype(F32)
    lane = iota((j_here, lanes), 1)
    keep = (iota((rows, lanes), 0) % order) == (iota((rows, lanes), 1) // LANE_GROUP)
    result = jnp.zeros((rows, j_here), F32)
    for g in range(groups):
        place = one_hot(iota((j_here, lanes), 0) == g * LANE_GROUP + lane % LANE_GROUP)
        packed = total[g * m_here : (g + 1) * m_here]
        wide = jnp.broadcast_to(packed[:, None, :], (m_here, order, lanes)).reshape(rows, lanes)
        result = result + dot(jnp.where(keep, wide, 0.0).astype(BF16), place, 1, 1)
    out_ref[...] = result.astype(BF16)


def packed_shards(tokens, cotangent, first_factor, second_factor, gate_source, alternate, batch, seq):
    x, cot = tokens[0], cotangent[0]
    rows_here, width = x.shape
    blocks, k_here, order = first_factor.shape
    j_here, m_here, count = second_factor.shape
    groups, lanes = j_here // LANE_GROUP, count * LANE_GROUP
    src = gate_source.reshape(1, width)
    alt = alternate.reshape(1, order)

    flat = jnp.transpose(second_factor, (1, 2, 0)).reshape(m_here * count, j_here)
    vals = {}

    def dep(name, value):
        earlier = [vals[n] for n in CFG['deps'].get(name, ()) if n in vals]
        return after(value, *earlier) if earlier else value

    def keep(name, value):
        vals[name] = value
        return value

    def move(name, value, axis, step, size):
        return keep(name, swap(dep(name, value), axis, step, size))

    (mine,) = call(functools.partial(pack_body, count), [of((groups * m_here, lanes))], [flat])
    packed = {0: mine}
    for d in (3, 2, 1):
        packed[d] = move(f"D{d}", mine, "batch", d, batch)
    dz = keep("gate", gate_call(x, cot, src))
    first_ready = after(first_factor, dz) if CFG['f2early'] else after(first_factor, dz, *[packed[d] for d in (1, 2, 3)])
    across = move("f2", first_ready, "batch", 2, batch)
    beside = move("f1", first_ready, "batch", 1, batch)
    direct = move("f3", first_ready, "batch", 3, batch) if CFG['direct'] else None
    piece = of((blocks, j_here, width))
    *back, second = call(
        functools.partial(regroup_back_body, batch, seq, count),
        [piece] * seq + [of((groups, count, lanes))],
        [*[packed[d] for d in range(batch)], dz],
        [
            pltpu.VMEM((groups, count, lanes), F32),
            pltpu.VMEM((count, j_here, width), BF16),
            pltpu.VMEM((rows_here, width), BF16),
            pltpu.SemaphoreType.DMA((groups,)),
        ],
        spaces={batch: pltpu.HBM},
        limit=56 << 20,
    )
    keep("A2", back[0])
    back_got = {0: back[0]}
    for d in CFG['order'][0]:
        back_got[d] = move(f"h{d}", back[d], "seq", d, seq)
    if direct is None:
        direct = move("fx", across, "batch", 1, batch)
    first = [first_factor, beside, across, direct]
    regrouped = call(
        functools.partial(mix_body, batch, seq),
        [piece] * seq,
        [dep("M", first_factor), *first[1:], x, alt],
        [pltpu.VMEM((order, order), BF16), pltpu.VMEM((order, width), BF16), pltpu.VMEM((order, width), BF16)],
    )
    keep("M", regrouped[0])
    got = {0: regrouped[0]}
    for d in CFG['order'][1]:
        got[d] = move(f"H{d}", regrouped[d], "seq", d, seq)
    *parts, dmixed = call(
        functools.partial(first_grad_body, batch, seq),
        [of((blocks, k_here, order))] * batch + [of((blocks, order, width))],
        [dep("F1", back_got[0]), *[back_got[d] for d in range(1, seq)], x, alt],
        [pltpu.VMEM((order, order), BF16), pltpu.VMEM((order, width), BF16), pltpu.VMEM((order, order), BF16)],
    )
    keep("F1", dmixed)
    if CFG['rsdirect']:
        others = [move(f"rs{d}", parts[d], "batch", d, batch) for d in (3, 2, 1)]
    else:
        near = move("near", parts[1], "batch", 1, batch)
        far = move("far", parts[3], "batch", 1, batch)
    dmix_in, weights, h = call(
        functools.partial(mix_back_body, batch),
        [of((rows_here, width), F32), of((groups, lanes, lanes)), of((rows_here, width), F32)],
        [dep("F2", first_factor), *first[1:], dmixed, second, x, cot, src],
    )
    keep("F2", dmix_in)
    if CFG['rsdirect']:
        (grad_one,) = call(sum_body, [of(parts[0].shape)], [dep("sum", parts[0]), *others])
    else:
        kept, summed = call(
            pair_body, [of(parts[0].shape, F32), of(parts[0].shape)], [dep("pair", parts[0]), parts[2], near, far]
        )
        keep("pair", summed)
        rx = move("rx", summed, "batch", 2, batch)
        (grad_one,) = call(add_body, [of(parts[0].shape)], [kept, rx])
    keep("add", grad_one)
    *terms, gathered = call(
        functools.partial(second_grad_body, batch, seq),
        [of((groups * m_here, lanes))] * batch + [of((count, j_here, width))],
        [after(got[0], dmix_in), *[got[d] for d in range(1, seq)], dz],
        [pltpu.VMEM((groups, count, lanes), F32)],
    )
    terms_got = [dep("unpack", terms[0])] + [move(f"R{d}", terms[d], "batch", d, batch) for d in (1, 2, 3)]
    (grad_tokens,) = call(
        tokens_body, [of((rows_here, width))], [gathered, weights, h, src, dmix_in]
    )
    (grad_flat,) = call(
        functools.partial(unpack_body, count), [of((m_here * count, j_here))], terms_got
    )
    grad_two = jnp.transpose(grad_flat.reshape(m_here, count, j_here), (2, 0, 1))
    return (grad_tokens[None], grad_one, grad_two)


def wide_shards(tokens, cotangent, first_factor, second_factor, gate_source, alternate):
    inputs = tokens[0]
    rows_here = inputs.shape[0]
    width = inputs.shape[1]
    order_len = alternate.shape[0]
    blocks_here = rows_here // order_len
    select = one_hot(lax.broadcasted_iota(jnp.int32, (width, width), 0) == gate_source[None, :])
    gate = jax.nn.sigmoid(jnp.dot(inputs, select, preferred_element_type=F32))
    first_full = lax.all_gather(first_factor, "batch", axis=1, tiled=True)
    second_full = lax.all_gather(second_factor, "batch", axis=1, tiled=True)
    blocked = inputs.reshape(blocks_here, order_len, width)
    mixed = jnp.einsum("ikj,ijc->ikc", first_full, blocked, preferred_element_type=F32).astype(BF16)
    shuffled = jnp.take(mixed, alternate, axis=1)
    piece = lax.all_to_all(shuffled, "seq", split_axis=1, concat_axis=0, tiled=True)
    z_blocks = jnp.einsum("jmi,ijc->jmc", second_full, piece, preferred_element_type=F32)
    j_here, count_second = z_blocks.shape[:2]
    z_out = z_blocks.reshape(rows_here, width)
    cot = cotangent[0].astype(F32)
    dz_out = (cot * gate).astype(BF16)
    dgate = cot * z_out * gate * (1.0 - gate)
    dz_blocks = dz_out.reshape(j_here, count_second, width)
    term_second = jnp.einsum("jmc,ijc->jmi", dz_blocks, piece, preferred_element_type=F32)
    grad_two = lax.psum_scatter(term_second.astype(BF16), "batch", scatter_dimension=1, tiled=True)
    dregrouped = jnp.einsum("jmi,jmc->ijc", second_full, dz_blocks, preferred_element_type=F32).astype(BF16)
    positions = lax.iota(jnp.int32, order_len)
    inverse = jnp.zeros((order_len,), jnp.int32).at[alternate].set(positions)
    restored = jnp.take(
        lax.all_to_all(dregrouped, "seq", split_axis=0, concat_axis=1, tiled=True), inverse, axis=1
    )
    dmix_in = jnp.einsum("ikj,ikc->ijc", first_full, restored, preferred_element_type=F32)
    term_first = jnp.einsum("ikc,ijc->ikj", restored, blocked, preferred_element_type=F32)
    grad_one = lax.psum_scatter(term_first.astype(BF16), "batch", scatter_dimension=1, tiled=True)
    spread = jnp.dot(dgate, select.T.astype(F32), precision=lax.Precision.HIGHEST)
    grad_tokens = (dmix_in.reshape(rows_here, width) + spread).astype(BF16)
    return (grad_tokens[None], grad_one, grad_two)


def solution(mesh):
    batch, seq = mesh.shape["batch"], mesh.shape["seq"]

    def shards(*args):
        j_here, m_here, count = args[3].shape
        if batch == 4 and seq & (seq - 1) == 0 and j_here % LANE_GROUP == 0 and m_here % 8 == 0 and count <= 32:
            return packed_shards(*args, batch, seq)
        return wide_shards(*args)

    in_specs = (
        P("batch", "seq", None),
        P("batch", "seq", None),
        P("seq", "batch", None),
        P("seq", "batch", None),
        P(),
        P(),
    )
    out_specs = (P("batch", "seq", None), P("seq", "batch", None), P("seq", "batch", None))
    return jax.shard_map(shards, mesh=mesh, in_specs=in_specs, out_specs=out_specs, check_vma=False)
```

```python
import functools

import jax
import jax.numpy as jnp
from jax import lax
from jax.experimental import pallas as pl
from jax.experimental.pallas import tpu as pltpu
from jax.sharding import PartitionSpec as P

BF16 = jnp.bfloat16
F32 = jnp.float32
LANE_GROUP = 16
CFG = {'cost': {}, 'direct': False, 'rsdirect': False, 'f2early': False, 'order': [[7, 6, 5, 4, 3, 2, 1], [7, 6, 5, 4, 3, 2, 1]], 'deps': {'h3': ['h7'], 'h2': ['h7'], 'h1': ['h7'], 'fx': ['A2'], 'F1': ['M'], 'pair': ['F2'], 'unpack': ['add']}, 'a2a': [True, True]}


def iota(shape, dim):
    return lax.broadcasted_iota(jnp.int32, shape, dim)


def one_hot(mask):
    return jnp.where(mask, 1.0, 0.0).astype(BF16)


def dot(a, b, da=1, db=0):
    return lax.dot_general(a, b, (((da,), (db,)), ((), ())), preferred_element_type=F32)


def call(body, outs, ins, scratch=(), spaces={}, limit=40 << 20, weight=0):
    name = getattr(body, "func", body).__name__
    weight = CFG['cost'].get(name, 0)
    return pl.pallas_call(
        body,
        name=name,
        out_shape=outs,
        in_specs=[pl.BlockSpec(memory_space=spaces.get(n, pltpu.VMEM)) for n in range(len(ins))],
        out_specs=[pl.BlockSpec(memory_space=pltpu.VMEM)] * len(outs),
        scratch_shapes=list(scratch),
        compiler_params=pltpu.CompilerParams(vmem_limit_bytes=limit),
        cost_estimate=pl.CostEstimate(flops=0, bytes_accessed=weight, transcendentals=0),
    )(*ins)


def of(shape, dtype=BF16):
    return jax.ShapeDtypeStruct(shape, dtype)


def swap(value, axis, step, size):
    return lax.ppermute(value, axis, [(p, p ^ step) for p in range(size)])


def after(value, *earlier):
    return lax.optimization_barrier((value, *earlier))[0]


def pack_body(order, s_ref, out_ref):
    rows, j_here = s_ref.shape
    groups = j_here // LANE_GROUP
    lanes = order * LANE_GROUP
    m_here = rows // order
    s = s_ref[...]
    lane = iota((j_here, lanes), 1)
    keep = (iota((rows, lanes), 0) % order) == (iota((rows, lanes), 1) // LANE_GROUP)
    for g in range(groups):
        place = one_hot(iota((j_here, lanes), 0) == g * LANE_GROUP + lane % LANE_GROUP)
        wide = jnp.where(keep, dot(s, place), 0.0)
        packed = jnp.sum(wide.reshape(m_here, order, lanes), axis=1)
        out_ref[g * m_here : (g + 1) * m_here, :] = packed.astype(BF16)


def gate_body(x_ref, cot_ref, src_ref, dz_ref):
    rows, width = x_ref.shape
    step = min(rows, 512)
    select = one_hot(iota((width, width), 0) == src_ref[...])
    for n in range(rows // step):
        part = slice(n * step, (n + 1) * step)
        gate = jax.nn.sigmoid(dot(x_ref[part, :], select))
        dz_ref[part, :] = (cot_ref[part, :].astype(F32) * gate).astype(BF16)


def regroup_back_body(batch, seq, order, *refs):
    pieces, dz_ref = refs[:batch], refs[batch]
    outs, second_ref, d_scr, r_scr = refs[batch + 1 : -3], *refs[-3:]
    me, here = lax.axis_index("batch"), lax.axis_index("seq")
    groups = second_ref.shape[0]
    lanes = order * LANE_GROUP
    m_here = order // batch
    for d in range(batch):
        piece = pieces[d][...].astype(F32)
        first = pl.multiple_of((me ^ d) * m_here, m_here)
        for g in range(groups):
            d_scr[g, pl.ds(first, m_here), :] = piece[g * m_here : (g + 1) * m_here]
    width = dz_ref.shape[1]
    tiled = one_hot((iota((order, lanes), 1) % order) == iota((order, lanes), 0))
    keep = (iota((lanes, lanes), 0) % LANE_GROUP) == (iota((lanes, lanes), 1) // order)
    for g in range(groups):
        packed = d_scr[g].astype(BF16)
        second_ref[g] = packed
        weights = jnp.where(keep, dot(packed, tiled, 0, 0), 0.0).astype(BF16)
        result = dot(weights, dz_ref[g * lanes : (g + 1) * lanes, :]).astype(BF16)
        r_scr[:, g * LANE_GROUP : (g + 1) * LANE_GROUP, :] = result.reshape(order, LANE_GROUP, width)

    blocks = order // seq
    if len(outs) == 1:
        outs[0][...] = r_scr[...].reshape(outs[0].shape)
    else:
        for d in range(seq):
            outs[d][...] = r_scr[pl.ds((here ^ d) * blocks, blocks)]


def mix_body(batch, seq, *refs):
    pieces, x_ref, alt_ref = refs[:batch], refs[batch], refs[batch + 1]
    outs, p_scr, mix_scr, reg_scr = refs[batch + 2 : -3], refs[-3], refs[-2], refs[-1]
    me, here = lax.axis_index("batch"), lax.axis_index("seq")
    blocks, rows, order = pieces[0].shape
    j_here = order // seq
    from_rows = jnp.where(iota((order, order), 0) == alt_ref[...], 1.0, 0.0)
    p_scr[...] = from_rows.T.astype(BF16)

    @pl.loop(0, blocks)
    def _(i):
        x = x_ref[pl.ds(pl.multiple_of(i * order, order), order), :]
        for d in range(batch):
            first = pl.multiple_of((me ^ d) * rows, rows)
            mix_scr[pl.ds(first, rows), :] = dot(pieces[d][i], x).astype(BF16)
        reg_scr[...] = dot(p_scr[...], mix_scr[...]).astype(BF16)
        if len(outs) == 1:
            outs[0][:, i] = reg_scr[...].reshape(seq, j_here, x.shape[1])
        else:
            for d in range(seq):
                first = pl.multiple_of((here ^ d) * j_here, j_here)
                outs[d][i] = reg_scr[pl.ds(first, j_here), :]


def first_grad_body(batch, seq, *refs):
    count = len(refs) - batch - 6
    pieces, x_ref, alt_ref = refs[:count], refs[count], refs[count + 1]
    outs, dmixed_ref = refs[count + 2 : count + 2 + batch], refs[count + 2 + batch]
    p_scr, reg_scr, part_scr = refs[-3:]
    me, here = lax.axis_index("batch"), lax.axis_index("seq")
    blocks, j_here, width = pieces[0].shape[-3:]
    order = j_here * seq
    rows = order // batch
    p_scr[...] = one_hot(iota((order, order), 0) == alt_ref[...])

    @pl.loop(0, blocks)
    def _(i):
        if count == 1:
            reg_scr[...] = pieces[0][:, i].reshape(order, width)
        else:
            for d in range(seq):
                first = pl.multiple_of((here ^ d) * j_here, j_here)
                reg_scr[pl.ds(first, j_here), :] = pieces[d][i]
        dmixed = dot(p_scr[...], reg_scr[...]).astype(BF16)
        dmixed_ref[i] = dmixed
        x = x_ref[pl.ds(pl.multiple_of(i * order, order), order), :]
        part_scr[...] = dot(dmixed, x, 1, 1).astype(BF16)
        for d in range(batch):
            first = pl.multiple_of((me ^ d) * rows, rows)
            outs[d][i] = part_scr[pl.ds(first, rows), :]


def mix_back_body(batch, *refs):
    pieces, dmixed_ref, second_ref, x_ref, cot_ref, src_ref = refs[:batch], *refs[batch:-3]
    out_ref, weights_ref, h_ref = refs[-3:]
    me = lax.axis_index("batch")
    blocks, rows, order = pieces[0].shape
    groups, count, lanes = second_ref.shape

    @pl.loop(0, blocks)
    def _(i):
        total = None
        for d in range(batch):
            first = pl.multiple_of((me ^ d) * rows, rows)
            term = dot(pieces[d][i], dmixed_ref[i, pl.ds(first, rows), :], 0, 0)
            total = term if total is None else total + term
        out_ref[pl.ds(pl.multiple_of(i * order, order), order), :] = total

    width = x_ref.shape[1]
    select = one_hot(iota((width, width), 0) == src_ref[...])

    @pl.loop(0, blocks)
    def _(i):
        part = pl.ds(pl.multiple_of(i * order, order), order)
        gate = jax.nn.sigmoid(dot(x_ref[part, :], select))
        h_ref[part, :] = cot_ref[part, :].astype(F32) * gate * (1.0 - gate)

    @pl.loop(0, groups)
    def _(g):
        packed = second_ref[g].astype(F32)
        col = iota((count, lanes), 1) % LANE_GROUP
        for jj in range(LANE_GROUP):
            weights_ref[g, jj * count : (jj + 1) * count, :] = jnp.where(col == jj, packed, 0.0).astype(BF16)


def gather_blocks(seq, pieces, scr):
    here = lax.axis_index("seq")
    blocks = pieces[0].shape[0]
    for d in range(seq):
        scr[pl.ds((here ^ d) * blocks, blocks)] = pieces[d][...]


def second_grad_body(batch, seq, *refs):
    count = len(refs) - batch - 3 if len(refs) > batch + 4 else 1
    if count == 1:
        pieces, dz_ref = refs[:1], refs[1]
        outs, reg_ref, y_scr = refs[2 : 2 + batch], refs[0], refs[-1]
    else:
        pieces, dz_ref = refs[:seq], refs[seq]
        outs, reg_ref, y_scr = refs[seq + 1 : seq + 1 + batch], refs[-2], refs[-1]
    me = lax.axis_index("batch")
    order, j_here, width = reg_ref.shape
    groups, lanes, m_here = j_here // LANE_GROUP, order * LANE_GROUP, order // batch
    if count > 1:
        gather_blocks(seq, pieces, reg_ref)

    @pl.loop(0, groups)
    def _(g):
        js = pl.ds(pl.multiple_of(g * LANE_GROUP, LANE_GROUP), LANE_GROUP)
        reg = reg_ref[:, js, :].reshape(lanes, width)
        dz = dz_ref[pl.ds(pl.multiple_of(g * lanes, lanes), lanes), :]
        wide = dot(dz, reg, 1, 1)
        col = iota((order, lanes), 1) % LANE_GROUP
        packed = wide[:order]
        for jj in range(1, LANE_GROUP):
            packed = jnp.where(col == jj, wide[jj * order : (jj + 1) * order], packed)
        y_scr[g] = packed

    for d in range(batch):
        first = pl.multiple_of((me ^ d) * m_here, m_here)
        rows = [y_scr[g, pl.ds(first, m_here), :] for g in range(groups)]
        outs[d][...] = jnp.concatenate(rows, axis=0).astype(BF16)


def tokens_body(reg_ref, weights_ref, h_ref, src_ref, back_ref, out_ref):
    order, j_here, width = reg_ref.shape
    groups, lanes = j_here // LANE_GROUP, order * LANE_GROUP
    select = one_hot(iota((width, width), 0) == src_ref[...])
    for g in range(groups):
        reg = reg_ref[:, g * LANE_GROUP : (g + 1) * LANE_GROUP, :].reshape(lanes, width)
        rows = slice(g * lanes, (g + 1) * lanes)
        dgate = (dot(weights_ref[g], reg) * h_ref[rows, :]).astype(BF16)
        out_ref[rows, :] = (back_ref[rows, :] + dot(dgate, select, 1, 1)).astype(BF16)


def pair_body(own_a, own_b, got_a, got_b, out_a, out_b):
    out_a[...] = own_a[...].astype(F32) + got_a[...].astype(F32)
    out_b[...] = (own_b[...].astype(F32) + got_b[...].astype(F32)).astype(BF16)


def sum_body(own, *refs):
    total = own[...].astype(F32)
    for got in refs[:-1]:
        total = total + got[...].astype(F32)
    refs[-1][...] = total.astype(BF16)


def add_body(own, got, out):
    out[...] = (own[...] + got[...].astype(F32)).astype(BF16)


def unpack_body(order, *refs):
    pieces, out_ref = refs[:-1], refs[-1]
    rows, j_here = out_ref.shape
    groups, lanes, m_here = j_here // LANE_GROUP, order * LANE_GROUP, rows // order
    total = pieces[0][...].astype(F32)
    for piece in pieces[1:]:
        total = total + piece[...].astype(F32)
    lane = iota((j_here, lanes), 1)
    keep = (iota((rows, lanes), 0) % order) == (iota((rows, lanes), 1) // LANE_GROUP)
    result = jnp.zeros((rows, j_here), F32)
    for g in range(groups):
        place = one_hot(iota((j_here, lanes), 0) == g * LANE_GROUP + lane % LANE_GROUP)
        packed = total[g * m_here : (g + 1) * m_here]
        wide = jnp.broadcast_to(packed[:, None, :], (m_here, order, lanes)).reshape(rows, lanes)
        result = result + dot(jnp.where(keep, wide, 0.0).astype(BF16), place, 1, 1)
    out_ref[...] = result.astype(BF16)


def packed_shards(tokens, cotangent, first_factor, second_factor, gate_source, alternate, batch, seq):
    x, cot = tokens[0], cotangent[0]
    rows_here, width = x.shape
    blocks, k_here, order = first_factor.shape
    j_here, m_here, count = second_factor.shape
    groups, lanes = j_here // LANE_GROUP, count * LANE_GROUP
    src = gate_source.reshape(1, width)
    alt = alternate.reshape(1, order)

    flat = jnp.transpose(second_factor, (1, 2, 0)).reshape(m_here * count, j_here)
    vals = {}

    def dep(name, value):
        earlier = [vals[n] for n in CFG['deps'].get(name, ()) if n in vals]
        return after(value, *earlier) if earlier else value

    def keep(name, value):
        vals[name] = value
        return value

    def move(name, value, axis, step, size):
        return keep(name, swap(dep(name, value), axis, step, size))

    (mine,) = call(functools.partial(pack_body, count), [of((groups * m_here, lanes))], [flat])
    packed = {0: mine}
    for d in (3, 2, 1):
        packed[d] = move(f"D{d}", mine, "batch", d, batch)
    (dz,) = call(gate_body, [of((rows_here, width))], [x, cot, src], limit=16 << 20)
    keep("gate", dz)
    first_ready = after(first_factor, dz) if CFG['f2early'] else after(first_factor, dz, *[packed[d] for d in (1, 2, 3)])
    across = move("f2", first_ready, "batch", 2, batch)
    beside = move("f1", first_ready, "batch", 1, batch)
    direct = move("f3", first_ready, "batch", 3, batch) if CFG['direct'] else None
    piece = of((blocks, j_here, width))
    *back, second = call(
        functools.partial(regroup_back_body, batch, seq, count),
        ([of((seq, blocks, j_here, width))] if CFG['a2a'][0] else [piece] * seq) + [of((groups, count, lanes))],
        [*[packed[d] for d in range(batch)], dz],
        [
            pltpu.VMEM((groups, count, lanes), F32),
            pltpu.VMEM((count, j_here, width), BF16),
        ],
    )
    keep("A2", back[0])
    back_got = {0: back[0]}
    if CFG['a2a'][0]:
        back_got[0] = keep("h0", lax.all_to_all(dep("h0", back[0]), "seq", 0, 0, tiled=True))
    else:
        for d in CFG['order'][0]:
            back_got[d] = move(f"h{d}", back[d], "seq", d, seq)
    if direct is None:
        direct = move("fx", across, "batch", 1, batch)
    first = [first_factor, beside, across, direct]
    regrouped = call(
        functools.partial(mix_body, batch, seq),
        [of((seq, blocks, j_here, width))] if CFG['a2a'][1] else [piece] * seq,
        [dep("M", first_factor), *first[1:], x, alt],
        [pltpu.VMEM((order, order), BF16), pltpu.VMEM((order, width), BF16), pltpu.VMEM((order, width), BF16)],
    )
    keep("M", regrouped[0])
    got = {0: regrouped[0]}
    if CFG['a2a'][1]:
        got[0] = keep("H0", lax.all_to_all(dep("H0", regrouped[0]), "seq", 0, 0, tiled=True))
    else:
        for d in CFG['order'][1]:
            got[d] = move(f"H{d}", regrouped[d], "seq", d, seq)
    *parts, dmixed = call(
        functools.partial(first_grad_body, batch, seq),
        [of((blocks, k_here, order))] * batch + [of((blocks, order, width))],
        [dep("F1", back_got[0]), *[back_got[d] for d in range(1, seq) if d in back_got], x, alt],
        [pltpu.VMEM((order, order), BF16), pltpu.VMEM((order, width), BF16), pltpu.VMEM((order, order), BF16)],
    )
    keep("F1", dmixed)
    if CFG['rsdirect']:
        others = [move(f"rs{d}", parts[d], "batch", d, batch) for d in (3, 2, 1)]
    else:
        near = move("near", parts[1], "batch", 1, batch)
        far = move("far", parts[3], "batch", 1, batch)
    dmix_in, weights, h = call(
        functools.partial(mix_back_body, batch),
        [of((rows_here, width), F32), of((groups, lanes, lanes)), of((rows_here, width), F32)],
        [dep("F2", first_factor), *first[1:], dmixed, second, x, cot, src],
    )
    keep("F2", dmix_in)
    if CFG['rsdirect']:
        (grad_one,) = call(sum_body, [of(parts[0].shape)], [dep("sum", parts[0]), *others])
    else:
        kept, summed = call(
            pair_body, [of(parts[0].shape, F32), of(parts[0].shape)], [dep("pair", parts[0]), parts[2], near, far]
        )
        keep("pair", summed)
        rx = move("rx", summed, "batch", 2, batch)
        (grad_one,) = call(add_body, [of(parts[0].shape)], [kept, rx])
    keep("add", grad_one)
    received = [after(got[0], dmix_in), *[got[d] for d in range(1, seq) if d in got]]
    if len(received) == 1:
        received = [received[0].reshape(count, j_here, width)]
    *terms, gathered = call(
        functools.partial(second_grad_body, batch, seq),
        [of((groups * m_here, lanes))] * batch + ([of((count, j_here, width))] if len(received) > 1 else []),
        [*received, dz],
        [pltpu.VMEM((groups, count, lanes), F32)],
    )
    if len(received) == 1:
        terms, gathered = [*terms, gathered], received[0]
    terms_got = [dep("unpack", terms[0])] + [move(f"R{d}", terms[d], "batch", d, batch) for d in (1, 2, 3)]
    (grad_tokens,) = call(
        tokens_body, [of((rows_here, width))], [gathered, weights, h, src, dmix_in]
    )
    (grad_flat,) = call(
        functools.partial(unpack_body, count), [of((m_here * count, j_here))], terms_got
    )
    grad_two = jnp.transpose(grad_flat.reshape(m_here, count, j_here), (2, 0, 1))
    return (grad_tokens[None], grad_one, grad_two)


def wide_shards(tokens, cotangent, first_factor, second_factor, gate_source, alternate):
    inputs = tokens[0]
    rows_here = inputs.shape[0]
    width = inputs.shape[1]
    order_len = alternate.shape[0]
    blocks_here = rows_here // order_len
    select = one_hot(lax.broadcasted_iota(jnp.int32, (width, width), 0) == gate_source[None, :])
    gate = jax.nn.sigmoid(jnp.dot(inputs, select, preferred_element_type=F32))
    first_full = lax.all_gather(first_factor, "batch", axis=1, tiled=True)
    second_full = lax.all_gather(second_factor, "batch", axis=1, tiled=True)
    blocked = inputs.reshape(blocks_here, order_len, width)
    mixed = jnp.einsum("ikj,ijc->ikc", first_full, blocked, preferred_element_type=F32).astype(BF16)
    shuffled = jnp.take(mixed, alternate, axis=1)
    piece = lax.all_to_all(shuffled, "seq", split_axis=1, concat_axis=0, tiled=True)
    z_blocks = jnp.einsum("jmi,ijc->jmc", second_full, piece, preferred_element_type=F32)
    j_here, count_second = z_blocks.shape[:2]
    z_out = z_blocks.reshape(rows_here, width)
    cot = cotangent[0].astype(F32)
    dz_out = (cot * gate).astype(BF16)
    dgate = cot * z_out * gate * (1.0 - gate)
    dz_blocks = dz_out.reshape(j_here, count_second, width)
    term_second = jnp.einsum("jmc,ijc->jmi", dz_blocks, piece, preferred_element_type=F32)
    grad_two = lax.psum_scatter(term_second.astype(BF16), "batch", scatter_dimension=1, tiled=True)
    dregrouped = jnp.einsum("jmi,jmc->ijc", second_full, dz_blocks, preferred_element_type=F32).astype(BF16)
    positions = lax.iota(jnp.int32, order_len)
    inverse = jnp.zeros((order_len,), jnp.int32).at[alternate].set(positions)
    restored = jnp.take(
        lax.all_to_all(dregrouped, "seq", split_axis=0, concat_axis=1, tiled=True), inverse, axis=1
    )
    dmix_in = jnp.einsum("ikj,ikc->ijc", first_full, restored, preferred_element_type=F32)
    term_first = jnp.einsum("ikc,ijc->ikj", restored, blocked, preferred_element_type=F32)
    grad_one = lax.psum_scatter(term_first.astype(BF16), "batch", scatter_dimension=1, tiled=True)
    spread = jnp.dot(dgate, select.T.astype(F32), precision=lax.Precision.HIGHEST)
    grad_tokens = (dmix_in.reshape(rows_here, width) + spread).astype(BF16)
    return (grad_tokens[None], grad_one, grad_two)


def solution(mesh):
    batch, seq = mesh.shape["batch"], mesh.shape["seq"]

    def shards(*args):
        j_here, m_here, count = args[3].shape
        if batch == 4 and seq & (seq - 1) == 0 and j_here % LANE_GROUP == 0 and m_here % 8 == 0 and count <= 32:
            return packed_shards(*args, batch, seq)
        return wide_shards(*args)

    in_specs = (
        P("batch", "seq", None),
        P("batch", "seq", None),
        P("seq", "batch", None),
        P("seq", "batch", None),
        P(),
        P(),
    )
    out_specs = (P("batch", "seq", None), P("seq", "batch", None), P("seq", "batch", None))
    return jax.shard_map(shards, mesh=mesh, in_specs=in_specs, out_specs=out_specs, check_vma=False)
```

```python
import functools

import jax
import jax.numpy as jnp
from jax import lax
from jax.experimental import pallas as pl
from jax.experimental.pallas import tpu as pltpu
from jax.sharding import PartitionSpec as P

BF16 = jnp.bfloat16
F32 = jnp.float32
LANE_GROUP = 16
CFG = {'cost': {}, 'direct': False, 'rsdirect': False, 'f2early': False, 'order': [[7, 4, 6, 5, 3, 2, 1], [7, 6, 5, 4, 3, 2, 1]], 'deps': {'h3': ['h7'], 'h2': ['h7'], 'h1': ['h7'], 'fx': ['h7', 'h4'], 'F1': ['M'], 'pair': ['F2'], 'unpack': ['add']}, 'a2a': [False, True]}


def iota(shape, dim):
    return lax.broadcasted_iota(jnp.int32, shape, dim)


def one_hot(mask):
    return jnp.where(mask, 1.0, 0.0).astype(BF16)


def dot(a, b, da=1, db=0):
    return lax.dot_general(a, b, (((da,), (db,)), ((), ())), preferred_element_type=F32)


def call(body, outs, ins, scratch=(), spaces={}, limit=40 << 20, weight=0):
    name = getattr(body, "func", body).__name__
    weight = CFG['cost'].get(name, 0)
    return pl.pallas_call(
        body,
        name=name,
        out_shape=outs,
        in_specs=[pl.BlockSpec(memory_space=spaces.get(n, pltpu.VMEM)) for n in range(len(ins))],
        out_specs=[pl.BlockSpec(memory_space=pltpu.VMEM)] * len(outs),
        scratch_shapes=list(scratch),
        compiler_params=pltpu.CompilerParams(vmem_limit_bytes=limit),
        cost_estimate=pl.CostEstimate(flops=0, bytes_accessed=weight, transcendentals=0),
    )(*ins)


def of(shape, dtype=BF16):
    return jax.ShapeDtypeStruct(shape, dtype)


def swap(value, axis, step, size):
    return lax.ppermute(value, axis, [(p, p ^ step) for p in range(size)])


def after(value, *earlier):
    return lax.optimization_barrier((value, *earlier))[0]


def pack_body(order, s_ref, out_ref):
    rows, j_here = s_ref.shape
    groups = j_here // LANE_GROUP
    lanes = order * LANE_GROUP
    m_here = rows // order
    s = s_ref[...]
    lane = iota((j_here, lanes), 1)
    keep = (iota((rows, lanes), 0) % order) == (iota((rows, lanes), 1) // LANE_GROUP)
    for g in range(groups):
        place = one_hot(iota((j_here, lanes), 0) == g * LANE_GROUP + lane % LANE_GROUP)
        wide = jnp.where(keep, dot(s, place), 0.0)
        packed = jnp.sum(wide.reshape(m_here, order, lanes), axis=1)
        out_ref[g * m_here : (g + 1) * m_here, :] = packed.astype(BF16)


def gate_body(x_ref, cot_ref, src_ref, dz_ref):
    rows, width = x_ref.shape
    step = min(rows, 512)
    select = one_hot(iota((width, width), 0) == src_ref[...])
    for n in range(rows // step):
        part = slice(n * step, (n + 1) * step)
        gate = jax.nn.sigmoid(dot(x_ref[part, :], select))
        dz_ref[part, :] = (cot_ref[part, :].astype(F32) * gate).astype(BF16)


def regroup_back_body(batch, seq, order, *refs):
    pieces, dz_ref = refs[:batch], refs[batch]
    outs, second_ref, d_scr, r_scr = refs[batch + 1 : -3], *refs[-3:]
    me, here = lax.axis_index("batch"), lax.axis_index("seq")
    groups = second_ref.shape[0]
    lanes = order * LANE_GROUP
    m_here = order // batch
    for d in range(batch):
        piece = pieces[d][...].astype(F32)
        first = pl.multiple_of((me ^ d) * m_here, m_here)
        for g in range(groups):
            d_scr[g, pl.ds(first, m_here), :] = piece[g * m_here : (g + 1) * m_here]
    width = dz_ref.shape[1]
    tiled = one_hot((iota((order, lanes), 1) % order) == iota((order, lanes), 0))
    keep = (iota((lanes, lanes), 0) % LANE_GROUP) == (iota((lanes, lanes), 1) // order)
    for g in range(groups):
        packed = d_scr[g].astype(BF16)
        second_ref[g] = packed
        weights = jnp.where(keep, dot(packed, tiled, 0, 0), 0.0).astype(BF16)
        result = dot(weights, dz_ref[g * lanes : (g + 1) * lanes, :]).astype(BF16)
        r_scr[:, g * LANE_GROUP : (g + 1) * LANE_GROUP, :] = result.reshape(order, LANE_GROUP, width)

    blocks = order // seq
    if len(outs) == 1:
        outs[0][...] = r_scr[...].reshape(outs[0].shape)
    else:
        for d in range(seq):
            outs[d][...] = r_scr[pl.ds((here ^ d) * blocks, blocks)]


def mix_body(batch, seq, *refs):
    pieces, x_ref, alt_ref = refs[:batch], refs[batch], refs[batch + 1]
    outs, p_scr, mix_scr, reg_scr = refs[batch + 2 : -3], refs[-3], refs[-2], refs[-1]
    me, here = lax.axis_index("batch"), lax.axis_index("seq")
    blocks, rows, order = pieces[0].shape
    j_here = order // seq
    from_rows = jnp.where(iota((order, order), 0) == alt_ref[...], 1.0, 0.0)
    p_scr[...] = from_rows.T.astype(BF16)

    @pl.loop(0, blocks)
    def _(i):
        x = x_ref[pl.ds(pl.multiple_of(i * order, order), order), :]
        for d in range(batch):
            first = pl.multiple_of((me ^ d) * rows, rows)
            mix_scr[pl.ds(first, rows), :] = dot(pieces[d][i], x).astype(BF16)
        reg_scr[...] = dot(p_scr[...], mix_scr[...]).astype(BF16)
        if len(outs) == 1:
            outs[0][:, i] = reg_scr[...].reshape(seq, j_here, x.shape[1])
        else:
            for d in range(seq):
                first = pl.multiple_of((here ^ d) * j_here, j_here)
                outs[d][i] = reg_scr[pl.ds(first, j_here), :]


def first_grad_body(batch, seq, *refs):
    count = len(refs) - batch - 6
    pieces, x_ref, alt_ref = refs[:count], refs[count], refs[count + 1]
    outs, dmixed_ref = refs[count + 2 : count + 2 + batch], refs[count + 2 + batch]
    p_scr, reg_scr, part_scr = refs[-3:]
    me, here = lax.axis_index("batch"), lax.axis_index("seq")
    blocks, j_here, width = pieces[0].shape[-3:]
    order = j_here * seq
    rows = order // batch
    p_scr[...] = one_hot(iota((order, order), 0) == alt_ref[...])

    @pl.loop(0, blocks)
    def _(i):
        if count == 1:
            reg_scr[...] = pieces[0][:, i].reshape(order, width)
        else:
            for d in range(seq):
                first = pl.multiple_of((here ^ d) * j_here, j_here)
                reg_scr[pl.ds(first, j_here), :] = pieces[d][i]
        dmixed = dot(p_scr[...], reg_scr[...]).astype(BF16)
        dmixed_ref[i] = dmixed
        x = x_ref[pl.ds(pl.multiple_of(i * order, order), order), :]
        part_scr[...] = dot(dmixed, x, 1, 1).astype(BF16)
        for d in range(batch):
            first = pl.multiple_of((me ^ d) * rows, rows)
            outs[d][i] = part_scr[pl.ds(first, rows), :]


def mix_back_body(batch, *refs):
    pieces, dmixed_ref, second_ref, x_ref, cot_ref, src_ref = refs[:batch], *refs[batch:-3]
    out_ref, weights_ref, h_ref = refs[-3:]
    me = lax.axis_index("batch")
    blocks, rows, order = pieces[0].shape
    groups, count, lanes = second_ref.shape

    @pl.loop(0, blocks)
    def _(i):
        total = None
        for d in range(batch):
            first = pl.multiple_of((me ^ d) * rows, rows)
            term = dot(pieces[d][i], dmixed_ref[i, pl.ds(first, rows), :], 0, 0)
            total = term if total is None else total + term
        out_ref[pl.ds(pl.multiple_of(i * order, order), order), :] = total

    width = x_ref.shape[1]
    select = one_hot(iota((width, width), 0) == src_ref[...])

    @pl.loop(0, blocks)
    def _(i):
        part = pl.ds(pl.multiple_of(i * order, order), order)
        gate = jax.nn.sigmoid(dot(x_ref[part, :], select))
        h_ref[part, :] = cot_ref[part, :].astype(F32) * gate * (1.0 - gate)

    @pl.loop(0, groups)
    def _(g):
        packed = second_ref[g].astype(F32)
        col = iota((count, lanes), 1) % LANE_GROUP
        for jj in range(LANE_GROUP):
            weights_ref[g, jj * count : (jj + 1) * count, :] = jnp.where(col == jj, packed, 0.0).astype(BF16)


def gather_blocks(seq, pieces, scr):
    here = lax.axis_index("seq")
    blocks = pieces[0].shape[0]
    for d in range(seq):
        scr[pl.ds((here ^ d) * blocks, blocks)] = pieces[d][...]


def second_grad_body(batch, seq, *refs):
    count = len(refs) - batch - 3 if len(refs) > batch + 4 else 1
    if count == 1:
        pieces, dz_ref = refs[:1], refs[1]
        outs, reg_ref, y_scr = refs[2 : 2 + batch], refs[0], refs[-1]
    else:
        pieces, dz_ref = refs[:seq], refs[seq]
        outs, reg_ref, y_scr = refs[seq + 1 : seq + 1 + batch], refs[-2], refs[-1]
    me = lax.axis_index("batch")
    order, j_here, width = reg_ref.shape
    groups, lanes, m_here = j_here // LANE_GROUP, order * LANE_GROUP, order // batch
    if count > 1:
        gather_blocks(seq, pieces, reg_ref)

    @pl.loop(0, groups)
    def _(g):
        js = pl.ds(pl.multiple_of(g * LANE_GROUP, LANE_GROUP), LANE_GROUP)
        reg = reg_ref[:, js, :].reshape(lanes, width)
        dz = dz_ref[pl.ds(pl.multiple_of(g * lanes, lanes), lanes), :]
        wide = dot(dz, reg, 1, 1)
        col = iota((order, lanes), 1) % LANE_GROUP
        packed = wide[:order]
        for jj in range(1, LANE_GROUP):
            packed = jnp.where(col == jj, wide[jj * order : (jj + 1) * order], packed)
        y_scr[g] = packed

    for d in range(batch):
        first = pl.multiple_of((me ^ d) * m_here, m_here)
        rows = [y_scr[g, pl.ds(first, m_here), :] for g in range(groups)]
        outs[d][...] = jnp.concatenate(rows, axis=0).astype(BF16)


def tokens_body(reg_ref, weights_ref, h_ref, src_ref, back_ref, out_ref):
    order, j_here, width = reg_ref.shape
    groups, lanes = j_here // LANE_GROUP, order * LANE_GROUP
    select = one_hot(iota((width, width), 0) == src_ref[...])
    for g in range(groups):
        reg = reg_ref[:, g * LANE_GROUP : (g + 1) * LANE_GROUP, :].reshape(lanes, width)
        rows = slice(g * lanes, (g + 1) * lanes)
        dgate = (dot(weights_ref[g], reg) * h_ref[rows, :]).astype(BF16)
        out_ref[rows, :] = (back_ref[rows, :] + dot(dgate, select, 1, 1)).astype(BF16)


def pair_body(own_a, own_b, got_a, got_b, out_a, out_b):
    out_a[...] = own_a[...].astype(F32) + got_a[...].astype(F32)
    out_b[...] = (own_b[...].astype(F32) + got_b[...].astype(F32)).astype(BF16)


def sum_body(own, *refs):
    total = own[...].astype(F32)
    for got in refs[:-1]:
        total = total + got[...].astype(F32)
    refs[-1][...] = total.astype(BF16)


def add_body(own, got, out):
    out[...] = (own[...] + got[...].astype(F32)).astype(BF16)


def unpack_body(order, *refs):
    pieces, out_ref = refs[:-1], refs[-1]
    rows, j_here = out_ref.shape
    groups, lanes, m_here = j_here // LANE_GROUP, order * LANE_GROUP, rows // order
    total = pieces[0][...].astype(F32)
    for piece in pieces[1:]:
        total = total + piece[...].astype(F32)
    lane = iota((j_here, lanes), 1)
    keep = (iota((rows, lanes), 0) % order) == (iota((rows, lanes), 1) // LANE_GROUP)
    result = jnp.zeros((rows, j_here), F32)
    for g in range(groups):
        place = one_hot(iota((j_here, lanes), 0) == g * LANE_GROUP + lane % LANE_GROUP)
        packed = total[g * m_here : (g + 1) * m_here]
        wide = jnp.broadcast_to(packed[:, None, :], (m_here, order, lanes)).reshape(rows, lanes)
        result = result + dot(jnp.where(keep, wide, 0.0).astype(BF16), place, 1, 1)
    out_ref[...] = result.astype(BF16)


def packed_shards(tokens, cotangent, first_factor, second_factor, gate_source, alternate, batch, seq):
    x, cot = tokens[0], cotangent[0]
    rows_here, width = x.shape
    blocks, k_here, order = first_factor.shape
    j_here, m_here, count = second_factor.shape
    groups, lanes = j_here // LANE_GROUP, count * LANE_GROUP
    src = gate_source.reshape(1, width)
    alt = alternate.reshape(1, order)

    flat = jnp.transpose(second_factor, (1, 2, 0)).reshape(m_here * count, j_here)
    vals = {}

    def dep(name, value):
        earlier = [vals[n] for n in CFG['deps'].get(name, ()) if n in vals]
        return after(value, *earlier) if earlier else value

    def keep(name, value):
        vals[name] = value
        return value

    def move(name, value, axis, step, size):
        return keep(name, swap(dep(name, value), axis, step, size))

    (mine,) = call(functools.partial(pack_body, count), [of((groups * m_here, lanes))], [flat])
    packed = {0: mine}
    for d in (3, 2, 1):
        packed[d] = move(f"D{d}", mine, "batch", d, batch)
    (dz,) = call(gate_body, [of((rows_here, width))], [x, cot, src], limit=16 << 20)
    keep("gate", dz)
    first_ready = after(first_factor, dz) if CFG['f2early'] else after(first_factor, dz, *[packed[d] for d in (1, 2, 3)])
    across = move("f2", first_ready, "batch", 2, batch)
    beside = move("f1", first_ready, "batch", 1, batch)
    direct = move("f3", first_ready, "batch", 3, batch) if CFG['direct'] else None
    piece = of((blocks, j_here, width))
    *back, second = call(
        functools.partial(regroup_back_body, batch, seq, count),
        ([of((seq, blocks, j_here, width))] if CFG['a2a'][0] else [piece] * seq) + [of((groups, count, lanes))],
        [*[packed[d] for d in range(batch)], dz],
        [
            pltpu.VMEM((groups, count, lanes), F32),
            pltpu.VMEM((count, j_here, width), BF16),
        ],
    )
    keep("A2", back[0])
    back_got = {0: back[0]}
    if CFG['a2a'][0]:
        back_got[0] = keep("h0", lax.all_to_all(dep("h0", back[0]), "seq", 0, 0, tiled=True))
    else:
        for d in CFG['order'][0]:
            back_got[d] = move(f"h{d}", back[d], "seq", d, seq)
    if direct is None:
        direct = move("fx", across, "batch", 1, batch)
    first = [first_factor, beside, across, direct]
    regrouped = call(
        functools.partial(mix_body, batch, seq),
        [of((seq, blocks, j_here, width))] if CFG['a2a'][1] else [piece] * seq,
        [dep("M", first_factor), *first[1:], x, alt],
        [pltpu.VMEM((order, order), BF16), pltpu.VMEM((order, width), BF16), pltpu.VMEM((order, width), BF16)],
    )
    keep("M", regrouped[0])
    got = {0: regrouped[0]}
    if CFG['a2a'][1]:
        got[0] = keep("H0", lax.all_to_all(dep("H0", regrouped[0]), "seq", 0, 0, tiled=True))
    else:
        for d in CFG['order'][1]:
            got[d] = move(f"H{d}", regrouped[d], "seq", d, seq)
    *parts, dmixed = call(
        functools.partial(first_grad_body, batch, seq),
        [of((blocks, k_here, order))] * batch + [of((blocks, order, width))],
        [dep("F1", back_got[0]), *[back_got[d] for d in range(1, seq) if d in back_got], x, alt],
        [pltpu.VMEM((order, order), BF16), pltpu.VMEM((order, width), BF16), pltpu.VMEM((order, order), BF16)],
    )
    keep("F1", dmixed)
    if CFG['rsdirect']:
        others = [move(f"rs{d}", parts[d], "batch", d, batch) for d in (3, 2, 1)]
    else:
        near = move("near", parts[1], "batch", 1, batch)
        far = move("far", parts[3], "batch", 1, batch)
    dmix_in, weights, h = call(
        functools.partial(mix_back_body, batch),
        [of((rows_here, width), F32), of((groups, lanes, lanes)), of((rows_here, width), F32)],
        [dep("F2", first_factor), *first[1:], dmixed, second, x, cot, src],
    )
    keep("F2", dmix_in)
    if CFG['rsdirect']:
        (grad_one,) = call(sum_body, [of(parts[0].shape)], [dep("sum", parts[0]), *others])
    else:
        kept, summed = call(
            pair_body, [of(parts[0].shape, F32), of(parts[0].shape)], [dep("pair", parts[0]), parts[2], near, far]
        )
        keep("pair", summed)
        rx = move("rx", summed, "batch", 2, batch)
        (grad_one,) = call(add_body, [of(parts[0].shape)], [kept, rx])
    keep("add", grad_one)
    received = [after(got[0], dmix_in), *[got[d] for d in range(1, seq) if d in got]]
    if len(received) == 1:
        received = [received[0].reshape(count, j_here, width)]
    *terms, gathered = call(
        functools.partial(second_grad_body, batch, seq),
        [of((groups * m_here, lanes))] * batch + ([of((count, j_here, width))] if len(received) > 1 else []),
        [*received, dz],
        [pltpu.VMEM((groups, count, lanes), F32)],
    )
    if len(received) == 1:
        terms, gathered = [*terms, gathered], received[0]
    terms_got = [dep("unpack", terms[0])] + [move(f"R{d}", terms[d], "batch", d, batch) for d in (1, 2, 3)]
    (grad_tokens,) = call(
        tokens_body, [of((rows_here, width))], [gathered, weights, h, src, dmix_in]
    )
    (grad_flat,) = call(
        functools.partial(unpack_body, count), [of((m_here * count, j_here))], terms_got
    )
    grad_two = jnp.transpose(grad_flat.reshape(m_here, count, j_here), (2, 0, 1))
    return (grad_tokens[None], grad_one, grad_two)


def wide_shards(tokens, cotangent, first_factor, second_factor, gate_source, alternate):
    inputs = tokens[0]
    rows_here = inputs.shape[0]
    width = inputs.shape[1]
    order_len = alternate.shape[0]
    blocks_here = rows_here // order_len
    select = one_hot(lax.broadcasted_iota(jnp.int32, (width, width), 0) == gate_source[None, :])
    gate = jax.nn.sigmoid(jnp.dot(inputs, select, preferred_element_type=F32))
    first_full = lax.all_gather(first_factor, "batch", axis=1, tiled=True)
    second_full = lax.all_gather(second_factor, "batch", axis=1, tiled=True)
    blocked = inputs.reshape(blocks_here, order_len, width)
    mixed = jnp.einsum("ikj,ijc->ikc", first_full, blocked, preferred_element_type=F32).astype(BF16)
    shuffled = jnp.take(mixed, alternate, axis=1)
    piece = lax.all_to_all(shuffled, "seq", split_axis=1, concat_axis=0, tiled=True)
    z_blocks = jnp.einsum("jmi,ijc->jmc", second_full, piece, preferred_element_type=F32)
    j_here, count_second = z_blocks.shape[:2]
    z_out = z_blocks.reshape(rows_here, width)
    cot = cotangent[0].astype(F32)
    dz_out = (cot * gate).astype(BF16)
    dgate = cot * z_out * gate * (1.0 - gate)
    dz_blocks = dz_out.reshape(j_here, count_second, width)
    term_second = jnp.einsum("jmc,ijc->jmi", dz_blocks, piece, preferred_element_type=F32)
    grad_two = lax.psum_scatter(term_second.astype(BF16), "batch", scatter_dimension=1, tiled=True)
    dregrouped = jnp.einsum("jmi,jmc->ijc", second_full, dz_blocks, preferred_element_type=F32).astype(BF16)
    positions = lax.iota(jnp.int32, order_len)
    inverse = jnp.zeros((order_len,), jnp.int32).at[alternate].set(positions)
    restored = jnp.take(
        lax.all_to_all(dregrouped, "seq", split_axis=0, concat_axis=1, tiled=True), inverse, axis=1
    )
    dmix_in = jnp.einsum("ikj,ikc->ijc", first_full, restored, preferred_element_type=F32)
    term_first = jnp.einsum("ikc,ijc->ikj", restored, blocked, preferred_element_type=F32)
    grad_one = lax.psum_scatter(term_first.astype(BF16), "batch", scatter_dimension=1, tiled=True)
    spread = jnp.dot(dgate, select.T.astype(F32), precision=lax.Precision.HIGHEST)
    grad_tokens = (dmix_in.reshape(rows_here, width) + spread).astype(BF16)
    return (grad_tokens[None], grad_one, grad_two)


def solution(mesh):
    batch, seq = mesh.shape["batch"], mesh.shape["seq"]

    def shards(*args):
        j_here, m_here, count = args[3].shape
        if batch == 4 and seq & (seq - 1) == 0 and j_here % LANE_GROUP == 0 and m_here % 8 == 0 and count <= 32:
            return packed_shards(*args, batch, seq)
        return wide_shards(*args)

    in_specs = (
        P("batch", "seq", None),
        P("batch", "seq", None),
        P("seq", "batch", None),
        P("seq", "batch", None),
        P(),
        P(),
    )
    out_specs = (P("batch", "seq", None), P("seq", "batch", None), P("seq", "batch", None))
    return jax.shard_map(shards, mesh=mesh, in_specs=in_specs, out_specs=out_specs, check_vma=False)
```

```python
import functools

import jax
import jax.numpy as jnp
from jax import lax
from jax.experimental import pallas as pl
from jax.experimental.pallas import tpu as pltpu
from jax.sharding import PartitionSpec as P

BF16 = jnp.bfloat16
F32 = jnp.float32
LANE_GROUP = 16
CFG = {'cost': {}, 'direct': False, 'rsdirect': False, 'f2early': False, 'order': [[7, 4, 6, 5, 3, 2, 1], [7, 6, 5, 4, 3, 2, 1]], 'deps': {'F1': ['M'], 'pair': ['F2'], 'H0': ['h1', 'h2', 'h3', 'h4', 'h5', 'h6', 'h7'], 'Z1': ['add'], 'h3': ['h7'], 'h2': ['h7'], 'h1': ['h7'], 'fx': ['h7', 'h4']}, 'a2a': [False, True]}


def iota(shape, dim):
    return lax.broadcasted_iota(jnp.int32, shape, dim)


def one_hot(mask):
    return jnp.where(mask, 1.0, 0.0).astype(BF16)


def dot(a, b, da=1, db=0):
    return lax.dot_general(a, b, (((da,), (db,)), ((), ())), preferred_element_type=F32)


def call(body, outs, ins, scratch=(), spaces={}, limit=40 << 20, weight=0, out_space=pltpu.VMEM):
    name = getattr(body, "func", body).__name__
    weight = CFG['cost'].get(name, 0)
    return pl.pallas_call(
        body,
        name=name,
        out_shape=outs,
        in_specs=[pl.BlockSpec(memory_space=spaces.get(n, pltpu.VMEM)) for n in range(len(ins))],
        out_specs=[pl.BlockSpec(memory_space=out_space)] * len(outs),
        scratch_shapes=list(scratch),
        compiler_params=pltpu.CompilerParams(vmem_limit_bytes=limit),
        cost_estimate=pl.CostEstimate(flops=0, bytes_accessed=weight, transcendentals=0),
    )(*ins)


def of(shape, dtype=BF16):
    return jax.ShapeDtypeStruct(shape, dtype)


def swap(value, axis, step, size):
    return lax.ppermute(value, axis, [(p, p ^ step) for p in range(size)])


def after(value, *earlier):
    return lax.optimization_barrier((value, *earlier))[0]


def pack_body(order, s_ref, out_ref):
    rows, j_here = s_ref.shape
    groups = j_here // LANE_GROUP
    lanes = order * LANE_GROUP
    m_here = rows // order
    s = s_ref[...]
    lane = iota((j_here, lanes), 1)
    keep = (iota((rows, lanes), 0) % order) == (iota((rows, lanes), 1) // LANE_GROUP)
    for g in range(groups):
        place = one_hot(iota((j_here, lanes), 0) == g * LANE_GROUP + lane % LANE_GROUP)
        wide = jnp.where(keep, dot(s, place), 0.0)
        packed = jnp.sum(wide.reshape(m_here, order, lanes), axis=1)
        out_ref[g * m_here : (g + 1) * m_here, :] = packed.astype(BF16)


def gate_body(x_ref, cot_ref, src_ref, dz_ref):
    rows, width = x_ref.shape
    step = min(rows, 512)
    select = one_hot(iota((width, width), 0) == src_ref[...])
    for n in range(rows // step):
        part = slice(n * step, (n + 1) * step)
        gate = jax.nn.sigmoid(dot(x_ref[part, :], select))
        dz_ref[part, :] = (cot_ref[part, :].astype(F32) * gate).astype(BF16)


def regroup_back_body(batch, seq, order, *refs):
    pieces, dz_ref = refs[:batch], refs[batch]
    outs, second_ref, d_scr, r_scr = refs[batch + 1 : -3], *refs[-3:]
    me, here = lax.axis_index("batch"), lax.axis_index("seq")
    groups = second_ref.shape[0]
    lanes = order * LANE_GROUP
    m_here = order // batch
    for d in range(batch):
        piece = pieces[d][...].astype(F32)
        first = pl.multiple_of((me ^ d) * m_here, m_here)
        for g in range(groups):
            d_scr[g, pl.ds(first, m_here), :] = piece[g * m_here : (g + 1) * m_here]
    width = dz_ref.shape[1]
    tiled = one_hot((iota((order, lanes), 1) % order) == iota((order, lanes), 0))
    keep = (iota((lanes, lanes), 0) % LANE_GROUP) == (iota((lanes, lanes), 1) // order)
    for g in range(groups):
        packed = d_scr[g].astype(BF16)
        second_ref[g] = packed
        weights = jnp.where(keep, dot(packed, tiled, 0, 0), 0.0).astype(BF16)
        result = dot(weights, dz_ref[g * lanes : (g + 1) * lanes, :]).astype(BF16)
        r_scr[:, g * LANE_GROUP : (g + 1) * LANE_GROUP, :] = result.reshape(order, LANE_GROUP, width)

    blocks = order // seq
    if len(outs) == 1:
        outs[0][...] = r_scr[...].reshape(outs[0].shape)
    else:
        for d in range(seq):
            outs[d][...] = r_scr[pl.ds((here ^ d) * blocks, blocks)]


def mix_body(batch, seq, *refs):
    pieces, x_ref, alt_ref = refs[:batch], refs[batch], refs[batch + 1]
    outs, p_scr, mix_scr, reg_scr, sems = refs[batch + 2 : -4], *refs[-4:]
    me, here = lax.axis_index("batch"), lax.axis_index("seq")
    blocks, rows, order = pieces[0].shape
    j_here = order // seq
    width = x_ref.shape[1]
    from_rows = jnp.where(iota((order, order), 0) == alt_ref[...], 1.0, 0.0)
    p_scr[...] = from_rows.T.astype(BF16)

    writes = []
    for i in range(blocks):
        x = x_ref[i * order : (i + 1) * order, :]
        for d in range(batch):
            first = pl.multiple_of((me ^ d) * rows, rows)
            mix_scr[pl.ds(first, rows), :] = dot(pieces[d][i], x).astype(BF16)
        result = dot(p_scr[...], mix_scr[...]).astype(BF16)
        if len(outs) == 1:
            reg_scr[i] = result.reshape(seq, j_here, width)
            writes.append(pltpu.make_async_copy(reg_scr.at[i], outs[0].at[:, i], sems.at[i]))
            writes[i].start()
        else:
            reg_scr[i] = result.reshape(seq, j_here, width)
            for d in range(seq):
                outs[d][i] = reg_scr[i, here ^ d]
    for write in writes:
        write.wait()


def first_grad_body(batch, seq, *refs):
    count = len(refs) - batch - 6
    pieces, x_ref, alt_ref = refs[:count], refs[count], refs[count + 1]
    outs, dmixed_ref = refs[count + 2 : count + 2 + batch], refs[count + 2 + batch]
    p_scr, reg_scr, part_scr = refs[-3:]
    me, here = lax.axis_index("batch"), lax.axis_index("seq")
    blocks, j_here, width = pieces[0].shape[-3:]
    order = j_here * seq
    rows = order // batch
    p_scr[...] = one_hot(iota((order, order), 0) == alt_ref[...])

    @pl.loop(0, blocks)
    def _(i):
        if count == 1:
            reg_scr[...] = pieces[0][:, i].reshape(order, width)
        else:
            for d in range(seq):
                first = pl.multiple_of((here ^ d) * j_here, j_here)
                reg_scr[pl.ds(first, j_here), :] = pieces[d][i]
        dmixed = dot(p_scr[...], reg_scr[...]).astype(BF16)
        dmixed_ref[i] = dmixed
        x = x_ref[pl.ds(pl.multiple_of(i * order, order), order), :]
        part_scr[...] = dot(dmixed, x, 1, 1).astype(BF16)
        for d in range(batch):
            first = pl.multiple_of((me ^ d) * rows, rows)
            outs[d][i] = part_scr[pl.ds(first, rows), :]


def mix_back_body(batch, *refs):
    pieces, dmixed_ref, x_ref, cot_ref, src_ref = refs[:batch], *refs[batch:-2]
    out_ref, h_ref = refs[-2:]
    me = lax.axis_index("batch")
    blocks, rows, order = pieces[0].shape

    @pl.loop(0, blocks)
    def _(i):
        total = None
        for d in range(batch):
            first = pl.multiple_of((me ^ d) * rows, rows)
            term = dot(pieces[d][i], dmixed_ref[i, pl.ds(first, rows), :], 0, 0)
            total = term if total is None else total + term
        out_ref[pl.ds(pl.multiple_of(i * order, order), order), :] = total.astype(BF16)

    width = x_ref.shape[1]
    select = one_hot(iota((width, width), 0) == src_ref[...])

    @pl.loop(0, blocks)
    def _(i):
        part = pl.ds(pl.multiple_of(i * order, order), order)
        gate = jax.nn.sigmoid(dot(x_ref[part, :], select))
        h_ref[part, :] = (cot_ref[part, :].astype(F32) * gate * (1.0 - gate)).astype(BF16)


def gather_blocks(seq, pieces, scr):
    here = lax.axis_index("seq")
    blocks = pieces[0].shape[0]
    for d in range(seq):
        scr[pl.ds((here ^ d) * blocks, blocks)] = pieces[d][...]


def second_grad_body(batch, seq, *refs):
    count = len(refs) - batch - 3 if len(refs) > batch + 4 else 1
    if count == 1:
        pieces, dz_ref = refs[:1], refs[1]
        outs, reg_ref, y_scr = refs[2 : 2 + batch], refs[0], refs[-1]
    else:
        pieces, dz_ref = refs[:seq], refs[seq]
        outs, reg_ref, y_scr = refs[seq + 1 : seq + 1 + batch], refs[-2], refs[-1]
    me = lax.axis_index("batch")
    order, j_here, width = reg_ref.shape
    groups, lanes, m_here = j_here // LANE_GROUP, order * LANE_GROUP, order // batch
    if count > 1:
        gather_blocks(seq, pieces, reg_ref)

    @pl.loop(0, groups)
    def _(g):
        js = pl.ds(pl.multiple_of(g * LANE_GROUP, LANE_GROUP), LANE_GROUP)
        reg = reg_ref[:, js, :].reshape(lanes, width)
        dz = dz_ref[pl.ds(pl.multiple_of(g * lanes, lanes), lanes), :]
        wide = dot(dz, reg, 1, 1)
        col = iota((order, lanes), 1) % LANE_GROUP
        packed = wide[:order]
        for jj in range(1, LANE_GROUP):
            packed = jnp.where(col == jj, wide[jj * order : (jj + 1) * order], packed)
        y_scr[g] = packed

    for d in range(batch):
        first = pl.multiple_of((me ^ d) * m_here, m_here)
        rows = [y_scr[g, pl.ds(first, m_here), :] for g in range(groups)]
        outs[d][...] = jnp.concatenate(rows, axis=0).astype(BF16)


def tokens_body(reg_ref, second_ref, h_ref, src_ref, back_ref, out_ref):
    order, j_here, width = reg_ref.shape
    groups, lanes = j_here // LANE_GROUP, order * LANE_GROUP
    select = one_hot(iota((width, width), 0) == src_ref[...])
    col = iota((order, lanes), 1) % LANE_GROUP
    for g in range(groups):
        reg = reg_ref[:, g * LANE_GROUP : (g + 1) * LANE_GROUP, :].reshape(lanes, width)
        packed = second_ref[g].astype(F32)
        weights = jnp.concatenate(
            [jnp.where(col == jj, packed, 0.0).astype(BF16) for jj in range(LANE_GROUP)], axis=0
        )
        rows = slice(g * lanes, (g + 1) * lanes)
        dgate = (dot(weights, reg) * h_ref[rows, :].astype(F32)).astype(BF16)
        out_ref[rows, :] = (back_ref[rows, :].astype(F32) + dot(dgate, select, 1, 1)).astype(BF16)


def pair_body(own_a, own_b, got_a, got_b, out_a, out_b):
    out_a[...] = own_a[...].astype(F32) + got_a[...].astype(F32)
    out_b[...] = (own_b[...].astype(F32) + got_b[...].astype(F32)).astype(BF16)


def sum_body(own, *refs):
    total = own[...].astype(F32)
    for got in refs[:-1]:
        total = total + got[...].astype(F32)
    refs[-1][...] = total.astype(BF16)


def add_body(own, got, out):
    out[...] = (own[...] + got[...].astype(F32)).astype(BF16)


def unpack_body(order, *refs):
    pieces, out_ref = refs[:-1], refs[-1]
    rows, j_here = out_ref.shape
    groups, lanes, m_here = j_here // LANE_GROUP, order * LANE_GROUP, rows // order
    total = pieces[0][...].astype(F32)
    for piece in pieces[1:]:
        total = total + piece[...].astype(F32)
    lane = iota((j_here, lanes), 1)
    keep = (iota((rows, lanes), 0) % order) == (iota((rows, lanes), 1) // LANE_GROUP)
    result = jnp.zeros((rows, j_here), F32)
    for g in range(groups):
        place = one_hot(iota((j_here, lanes), 0) == g * LANE_GROUP + lane % LANE_GROUP)
        packed = total[g * m_here : (g + 1) * m_here]
        wide = jnp.broadcast_to(packed[:, None, :], (m_here, order, lanes)).reshape(rows, lanes)
        result = result + dot(jnp.where(keep, wide, 0.0).astype(BF16), place, 1, 1)
    out_ref[...] = result.astype(BF16)


def packed_shards(tokens, cotangent, first_factor, second_factor, gate_source, alternate, batch, seq):
    x, cot = tokens[0], cotangent[0]
    rows_here, width = x.shape
    blocks, k_here, order = first_factor.shape
    j_here, m_here, count = second_factor.shape
    groups, lanes = j_here // LANE_GROUP, count * LANE_GROUP
    src = gate_source.reshape(1, width)
    alt = alternate.reshape(1, order)

    flat = jnp.transpose(second_factor, (1, 2, 0)).reshape(m_here * count, j_here)
    vals = {}

    def dep(name, value):
        earlier = [vals[n] for n in CFG['deps'].get(name, ()) if n in vals]
        return after(value, *earlier) if earlier else value

    def keep(name, value):
        vals[name] = value
        return value

    def move(name, value, axis, step, size):
        return keep(name, swap(dep(name, value), axis, step, size))

    (mine,) = call(functools.partial(pack_body, count), [of((groups * m_here, lanes))], [flat])
    packed = {0: mine}
    for d in (3, 2, 1):
        packed[d] = move(f"D{d}", mine, "batch", d, batch)
    (dz,) = call(gate_body, [of((rows_here, width))], [x, cot, src], limit=16 << 20)
    keep("gate", dz)
    first_ready = after(first_factor, dz) if CFG['f2early'] else after(first_factor, dz, *[packed[d] for d in (1, 2, 3)])
    across = move("f2", first_ready, "batch", 2, batch)
    beside = move("f1", first_ready, "batch", 1, batch)
    direct = move("f3", first_ready, "batch", 3, batch) if CFG['direct'] else None
    piece = of((blocks, j_here, width))
    *back, second = call(
        functools.partial(regroup_back_body, batch, seq, count),
        ([of((seq, blocks, j_here, width))] if CFG['a2a'][0] else [piece] * seq) + [of((groups, count, lanes))],
        [*[packed[d] for d in range(batch)], dz],
        [
            pltpu.VMEM((groups, count, lanes), F32),
            pltpu.VMEM((count, j_here, width), BF16),
        ],
    )
    keep("A2", back[0])
    back_got = {0: back[0]}
    if CFG['a2a'][0]:
        back_got[0] = keep("h0", lax.all_to_all(dep("h0", back[0]), "seq", 0, 0, tiled=True))
    else:
        for d in CFG['order'][0]:
            back_got[d] = move(f"h{d}", back[d], "seq", d, seq)
    if direct is None:
        direct = move("fx", across, "batch", 1, batch)
    first = [first_factor, beside, across, direct]
    regrouped = call(
        functools.partial(mix_body, batch, seq),
        [of((seq, blocks, j_here, width))] if CFG['a2a'][1] else [piece] * seq,
        [dep("M", first_factor), *first[1:], x, alt],
        [
            pltpu.VMEM((order, order), BF16),
            pltpu.VMEM((order, width), BF16),
            pltpu.VMEM((blocks, seq, j_here, width), BF16),
            pltpu.SemaphoreType.DMA((blocks,)),
        ],
        out_space=pltpu.HBM if CFG['a2a'][1] else pltpu.VMEM,
    )
    keep("M", regrouped[0])
    got = {0: regrouped[0]}
    if CFG['a2a'][1]:
        got[0] = keep("H0", lax.all_to_all(dep("H0", regrouped[0]), "seq", 0, 0, tiled=True))
    else:
        for d in CFG['order'][1]:
            got[d] = move(f"H{d}", regrouped[d], "seq", d, seq)
    *parts, dmixed = call(
        functools.partial(first_grad_body, batch, seq),
        [of((blocks, k_here, order))] * batch + [of((blocks, order, width))],
        [dep("F1", back_got[0]), *[back_got[d] for d in range(1, seq) if d in back_got], x, alt],
        [pltpu.VMEM((order, order), BF16), pltpu.VMEM((order, width), BF16), pltpu.VMEM((order, order), BF16)],
    )
    keep("F1", dmixed)
    if CFG['rsdirect']:
        others = [move(f"rs{d}", parts[d], "batch", d, batch) for d in (3, 2, 1)]
    else:
        near = move("near", parts[1], "batch", 1, batch)
        far = move("far", parts[3], "batch", 1, batch)
    dmix_in, h = call(
        functools.partial(mix_back_body, batch),
        [of((rows_here, width))] * 2,
        [dep("F2", first_factor), *first[1:], dmixed, x, cot, src],
    )
    keep("F2", dmix_in)
    if CFG['rsdirect']:
        (grad_one,) = call(sum_body, [of(parts[0].shape)], [dep("sum", parts[0]), *others])
    else:
        kept, summed = call(
            pair_body, [of(parts[0].shape, F32), of(parts[0].shape)], [dep("pair", parts[0]), parts[2], near, far]
        )
        keep("pair", summed)
        rx = move("rx", summed, "batch", 2, batch)
        (grad_one,) = call(add_body, [of(parts[0].shape)], [kept, rx])
    keep("add", grad_one)
    received = [dep("Z1", after(got[0], dmix_in)), *[got[d] for d in range(1, seq) if d in got]]
    if len(received) == 1:
        received = [received[0].reshape(count, j_here, width)]
    *terms, gathered = call(
        functools.partial(second_grad_body, batch, seq),
        [of((groups * m_here, lanes))] * batch + ([of((count, j_here, width))] if len(received) > 1 else []),
        [*received, dz],
        [pltpu.VMEM((groups, count, lanes), F32)],
    )
    if len(received) == 1:
        terms, gathered = [*terms, gathered], received[0]
    terms_got = [dep("unpack", terms[0])] + [move(f"R{d}", terms[d], "batch", d, batch) for d in (1, 2, 3)]
    (grad_tokens,) = call(
        tokens_body, [of((rows_here, width))], [gathered, second, h, src, dmix_in]
    )
    (grad_flat,) = call(
        functools.partial(unpack_body, count), [of((m_here * count, j_here))], terms_got
    )
    grad_two = jnp.transpose(grad_flat.reshape(m_here, count, j_here), (2, 0, 1))
    return (grad_tokens[None], grad_one, grad_two)


def wide_shards(tokens, cotangent, first_factor, second_factor, gate_source, alternate):
    inputs = tokens[0]
    rows_here = inputs.shape[0]
    width = inputs.shape[1]
    order_len = alternate.shape[0]
    blocks_here = rows_here // order_len
    select = one_hot(lax.broadcasted_iota(jnp.int32, (width, width), 0) == gate_source[None, :])
    gate = jax.nn.sigmoid(jnp.dot(inputs, select, preferred_element_type=F32))
    first_full = lax.all_gather(first_factor, "batch", axis=1, tiled=True)
    second_full = lax.all_gather(second_factor, "batch", axis=1, tiled=True)
    blocked = inputs.reshape(blocks_here, order_len, width)
    mixed = jnp.einsum("ikj,ijc->ikc", first_full, blocked, preferred_element_type=F32).astype(BF16)
    shuffled = jnp.take(mixed, alternate, axis=1)
    piece = lax.all_to_all(shuffled, "seq", split_axis=1, concat_axis=0, tiled=True)
    z_blocks = jnp.einsum("jmi,ijc->jmc", second_full, piece, preferred_element_type=F32)
    j_here, count_second = z_blocks.shape[:2]
    z_out = z_blocks.reshape(rows_here, width)
    cot = cotangent[0].astype(F32)
    dz_out = (cot * gate).astype(BF16)
    dgate = cot * z_out * gate * (1.0 - gate)
    dz_blocks = dz_out.reshape(j_here, count_second, width)
    term_second = jnp.einsum("jmc,ijc->jmi", dz_blocks, piece, preferred_element_type=F32)
    grad_two = lax.psum_scatter(term_second.astype(BF16), "batch", scatter_dimension=1, tiled=True)
    dregrouped = jnp.einsum("jmi,jmc->ijc", second_full, dz_blocks, preferred_element_type=F32).astype(BF16)
    positions = lax.iota(jnp.int32, order_len)
    inverse = jnp.zeros((order_len,), jnp.int32).at[alternate].set(positions)
    restored = jnp.take(
        lax.all_to_all(dregrouped, "seq", split_axis=0, concat_axis=1, tiled=True), inverse, axis=1
    )
    dmix_in = jnp.einsum("ikj,ikc->ijc", first_full, restored, preferred_element_type=F32)
    term_first = jnp.einsum("ikc,ijc->ikj", restored, blocked, preferred_element_type=F32)
    grad_one = lax.psum_scatter(term_first.astype(BF16), "batch", scatter_dimension=1, tiled=True)
    spread = jnp.dot(dgate, select.T.astype(F32), precision=lax.Precision.HIGHEST)
    grad_tokens = (dmix_in.reshape(rows_here, width) + spread).astype(BF16)
    return (grad_tokens[None], grad_one, grad_two)


def solution(mesh):
    batch, seq = mesh.shape["batch"], mesh.shape["seq"]

    def shards(*args):
        j_here, m_here, count = args[3].shape
        if batch == 4 and seq & (seq - 1) == 0 and j_here % LANE_GROUP == 0 and m_here % 8 == 0 and count <= 32:
            return packed_shards(*args, batch, seq)
        return wide_shards(*args)

    in_specs = (
        P("batch", "seq", None),
        P("batch", "seq", None),
        P("seq", "batch", None),
        P("seq", "batch", None),
        P(),
        P(),
    )
    out_specs = (P("batch", "seq", None), P("seq", "batch", None), P("seq", "batch", None))
    return jax.shard_map(shards, mesh=mesh, in_specs=in_specs, out_specs=out_specs, check_vma=False)
```

```python
import functools

import jax
import jax.numpy as jnp
from jax import lax
from jax.experimental import pallas as pl
from jax.experimental.pallas import tpu as pltpu
from jax.sharding import PartitionSpec as P

BF16 = jnp.bfloat16
F32 = jnp.float32
LANE_GROUP = 16
CFG = {'a2a': [False, False], 'cost': {}, 'direct': False, 'rsdirect': False, 'f2early': False, 'order': [[7, 6, 5, 4, 3, 2, 1], [7, 6, 5, 4, 3, 2, 1]], 'deps': {'h3': ['h7'], 'h2': ['h7'], 'h1': ['h7'], 'fx': ['h7', 'h4'], 'F1': ['M', 'H1', 'H2', 'H3', 'fx'], 'near': ['H7', 'H6'], 'far': ['H7', 'H6'], 'pair': ['F2'], 'Z1': ['add'], 'H1': ['h3'], 'H2': ['M']}}


def iota(shape, dim):
    return lax.broadcasted_iota(jnp.int32, shape, dim)


def one_hot(mask):
    return jnp.where(mask, 1.0, 0.0).astype(BF16)


def dot(a, b, da=1, db=0):
    return lax.dot_general(a, b, (((da,), (db,)), ((), ())), preferred_element_type=F32)


def call(body, outs, ins, scratch=(), spaces={}, limit=40 << 20, weight=0, out_space=pltpu.VMEM):
    name = getattr(body, "func", body).__name__
    weight = CFG['cost'].get(name, 0)
    return pl.pallas_call(
        body,
        name=name,
        out_shape=outs,
        in_specs=[pl.BlockSpec(memory_space=spaces.get(n, pltpu.VMEM)) for n in range(len(ins))],
        out_specs=[pl.BlockSpec(memory_space=out_space)] * len(outs),
        scratch_shapes=list(scratch),
        compiler_params=pltpu.CompilerParams(vmem_limit_bytes=limit),
        cost_estimate=pl.CostEstimate(flops=0, bytes_accessed=weight, transcendentals=0),
    )(*ins)


def of(shape, dtype=BF16):
    return jax.ShapeDtypeStruct(shape, dtype)


def swap(value, axis, step, size):
    return lax.ppermute(value, axis, [(p, p ^ step) for p in range(size)])


def after(value, *earlier):
    return lax.optimization_barrier((value, *earlier))[0]


def pack_body(order, s_ref, out_ref):
    rows, j_here = s_ref.shape
    groups = j_here // LANE_GROUP
    lanes = order * LANE_GROUP
    m_here = rows // order
    s = s_ref[...]
    lane = iota((j_here, lanes), 1)
    keep = (iota((rows, lanes), 0) % order) == (iota((rows, lanes), 1) // LANE_GROUP)
    for g in range(groups):
        place = one_hot(iota((j_here, lanes), 0) == g * LANE_GROUP + lane % LANE_GROUP)
        wide = jnp.where(keep, dot(s, place), 0.0)
        packed = jnp.sum(wide.reshape(m_here, order, lanes), axis=1)
        out_ref[g * m_here : (g + 1) * m_here, :] = packed.astype(BF16)


def gate_body(x_ref, cot_ref, src_ref, dz_ref):
    rows, width = x_ref.shape
    step = min(rows, 512)
    select = one_hot(iota((width, width), 0) == src_ref[...])
    for n in range(rows // step):
        part = slice(n * step, (n + 1) * step)
        gate = jax.nn.sigmoid(dot(x_ref[part, :], select))
        dz_ref[part, :] = (cot_ref[part, :].astype(F32) * gate).astype(BF16)


def regroup_back_body(batch, seq, order, *refs):
    pieces, dz_ref = refs[:batch], refs[batch]
    outs, second_ref, d_scr, r_scr = refs[batch + 1 : -3], *refs[-3:]
    me, here = lax.axis_index("batch"), lax.axis_index("seq")
    groups = second_ref.shape[0]
    lanes = order * LANE_GROUP
    m_here = order // batch
    for d in range(batch):
        piece = pieces[d][...].astype(F32)
        first = pl.multiple_of((me ^ d) * m_here, m_here)
        for g in range(groups):
            d_scr[g, pl.ds(first, m_here), :] = piece[g * m_here : (g + 1) * m_here]
    width = dz_ref.shape[1]
    tiled = one_hot((iota((order, lanes), 1) % order) == iota((order, lanes), 0))
    keep = (iota((lanes, lanes), 0) % LANE_GROUP) == (iota((lanes, lanes), 1) // order)
    for g in range(groups):
        packed = d_scr[g].astype(BF16)
        second_ref[g] = packed
        weights = jnp.where(keep, dot(packed, tiled, 0, 0), 0.0).astype(BF16)
        result = dot(weights, dz_ref[g * lanes : (g + 1) * lanes, :]).astype(BF16)
        r_scr[:, g * LANE_GROUP : (g + 1) * LANE_GROUP, :] = result.reshape(order, LANE_GROUP, width)

    blocks = order // seq
    if len(outs) == 1:
        outs[0][...] = r_scr[...].reshape(outs[0].shape)
    else:
        for d in range(seq):
            outs[d][...] = r_scr[pl.ds((here ^ d) * blocks, blocks)]


def mix_body(batch, seq, *refs):
    pieces, x_ref, alt_ref, cot_ref, src_ref = refs[:batch], *refs[batch : batch + 4]
    outs, h_ref, p_scr, mix_scr, reg_scr, sems = refs[batch + 4 : -5], *refs[-5:]
    me, here = lax.axis_index("batch"), lax.axis_index("seq")
    blocks, rows, order = pieces[0].shape
    j_here = order // seq
    width = x_ref.shape[1]
    from_rows = jnp.where(iota((order, order), 0) == alt_ref[...], 1.0, 0.0)
    p_scr[...] = from_rows.T.astype(BF16)
    select = one_hot(iota((width, width), 0) == src_ref[...])

    writes = []
    for i in range(blocks):
        x = x_ref[i * order : (i + 1) * order, :]
        for d in range(batch):
            first = pl.multiple_of((me ^ d) * rows, rows)
            mix_scr[pl.ds(first, rows), :] = dot(pieces[d][i], x).astype(BF16)
        result = dot(p_scr[...], mix_scr[...]).astype(BF16)
        if len(outs) == 1:
            reg_scr[i] = result.reshape(seq, j_here, width)
            writes.append(pltpu.make_async_copy(reg_scr.at[i], outs[0].at[:, i], sems.at[i]))
            writes[i].start()
        else:
            reg_scr[i] = result.reshape(seq, j_here, width)
            for d in range(seq):
                outs[d][i] = reg_scr[i, here ^ d]
        gate = jax.nn.sigmoid(dot(x, select))
        cot = cot_ref[i * order : (i + 1) * order, :].astype(F32)
        h_ref[i * order : (i + 1) * order, :] = (cot * gate * (1.0 - gate)).astype(BF16)
    for write in writes:
        write.wait()


def first_grad_body(batch, seq, *refs):
    count = len(refs) - batch - 6
    pieces, x_ref, alt_ref = refs[:count], refs[count], refs[count + 1]
    outs, dmixed_ref = refs[count + 2 : count + 2 + batch], refs[count + 2 + batch]
    p_scr, reg_scr, part_scr = refs[-3:]
    me, here = lax.axis_index("batch"), lax.axis_index("seq")
    blocks, j_here, width = pieces[0].shape[-3:]
    order = j_here * seq
    rows = order // batch
    p_scr[...] = one_hot(iota((order, order), 0) == alt_ref[...])

    @pl.loop(0, blocks)
    def _(i):
        if count == 1:
            reg_scr[...] = pieces[0][:, i].reshape(order, width)
        else:
            for d in range(seq):
                first = pl.multiple_of((here ^ d) * j_here, j_here)
                reg_scr[pl.ds(first, j_here), :] = pieces[d][i]
        dmixed = dot(p_scr[...], reg_scr[...]).astype(BF16)
        dmixed_ref[i] = dmixed
        x = x_ref[pl.ds(pl.multiple_of(i * order, order), order), :]
        part_scr[...] = dot(dmixed, x, 1, 1).astype(BF16)
        for d in range(batch):
            first = pl.multiple_of((me ^ d) * rows, rows)
            outs[d][i] = part_scr[pl.ds(first, rows), :]


def mix_back_body(batch, *refs):
    pieces, dmixed_ref, out_ref = refs[:batch], *refs[batch:]
    me = lax.axis_index("batch")
    blocks, rows, order = pieces[0].shape

    @pl.loop(0, blocks)
    def _(i):
        total = None
        for d in range(batch):
            first = pl.multiple_of((me ^ d) * rows, rows)
            term = dot(pieces[d][i], dmixed_ref[i, pl.ds(first, rows), :], 0, 0)
            total = term if total is None else total + term
        out_ref[pl.ds(pl.multiple_of(i * order, order), order), :] = total.astype(BF16)


def gather_blocks(seq, pieces, scr):
    here = lax.axis_index("seq")
    blocks = pieces[0].shape[0]
    for d in range(seq):
        scr[pl.ds((here ^ d) * blocks, blocks)] = pieces[d][...]


def second_grad_body(batch, seq, *refs):
    count = len(refs) - batch - 3 if len(refs) > batch + 4 else 1
    if count == 1:
        pieces, dz_ref = refs[:1], refs[1]
        outs, reg_ref, y_scr = refs[2 : 2 + batch], refs[0], refs[-1]
    else:
        pieces, dz_ref = refs[:seq], refs[seq]
        outs, reg_ref, y_scr = refs[seq + 1 : seq + 1 + batch], refs[-2], refs[-1]
    me = lax.axis_index("batch")
    order, j_here, width = reg_ref.shape
    groups, lanes, m_here = j_here // LANE_GROUP, order * LANE_GROUP, order // batch
    if count > 1:
        gather_blocks(seq, pieces, reg_ref)

    @pl.loop(0, groups)
    def _(g):
        js = pl.ds(pl.multiple_of(g * LANE_GROUP, LANE_GROUP), LANE_GROUP)
        reg = reg_ref[:, js, :].reshape(lanes, width)
        dz = dz_ref[pl.ds(pl.multiple_of(g * lanes, lanes), lanes), :]
        wide = dot(dz, reg, 1, 1)
        col = iota((order, lanes), 1) % LANE_GROUP
        packed = wide[:order]
        for jj in range(1, LANE_GROUP):
            packed = jnp.where(col == jj, wide[jj * order : (jj + 1) * order], packed)
        y_scr[g] = packed

    for d in range(batch):
        first = pl.multiple_of((me ^ d) * m_here, m_here)
        rows = [y_scr[g, pl.ds(first, m_here), :] for g in range(groups)]
        outs[d][...] = jnp.concatenate(rows, axis=0).astype(BF16)


def tokens_body(reg_ref, second_ref, h_ref, src_ref, back_ref, out_ref):
    order, j_here, width = reg_ref.shape
    groups, lanes = j_here // LANE_GROUP, order * LANE_GROUP
    select = one_hot(iota((width, width), 0) == src_ref[...])
    col = iota((order, lanes), 1) % LANE_GROUP
    for g in range(groups):
        reg = reg_ref[:, g * LANE_GROUP : (g + 1) * LANE_GROUP, :].reshape(lanes, width)
        packed = second_ref[g].astype(F32)
        weights = jnp.concatenate(
            [jnp.where(col == jj, packed, 0.0).astype(BF16) for jj in range(LANE_GROUP)], axis=0
        )
        rows = slice(g * lanes, (g + 1) * lanes)
        dgate = (dot(weights, reg) * h_ref[rows, :].astype(F32)).astype(BF16)
        out_ref[rows, :] = (back_ref[rows, :].astype(F32) + dot(dgate, select, 1, 1)).astype(BF16)


def pair_body(own_a, own_b, got_a, got_b, out_a, out_b):
    out_a[...] = own_a[...].astype(F32) + got_a[...].astype(F32)
    out_b[...] = (own_b[...].astype(F32) + got_b[...].astype(F32)).astype(BF16)


def sum_body(own, *refs):
    total = own[...].astype(F32)
    for got in refs[:-1]:
        total = total + got[...].astype(F32)
    refs[-1][...] = total.astype(BF16)


def add_body(own, got, out):
    out[...] = (own[...] + got[...].astype(F32)).astype(BF16)


def unpack_body(order, *refs):
    pieces, out_ref = refs[:-1], refs[-1]
    rows, j_here = out_ref.shape
    groups, lanes, m_here = j_here // LANE_GROUP, order * LANE_GROUP, rows // order
    total = pieces[0][...].astype(F32)
    for piece in pieces[1:]:
        total = total + piece[...].astype(F32)
    lane = iota((j_here, lanes), 1)
    keep = (iota((rows, lanes), 0) % order) == (iota((rows, lanes), 1) // LANE_GROUP)
    result = jnp.zeros((rows, j_here), F32)
    for g in range(groups):
        place = one_hot(iota((j_here, lanes), 0) == g * LANE_GROUP + lane % LANE_GROUP)
        packed = total[g * m_here : (g + 1) * m_here]
        wide = jnp.broadcast_to(packed[:, None, :], (m_here, order, lanes)).reshape(rows, lanes)
        result = result + dot(jnp.where(keep, wide, 0.0).astype(BF16), place, 1, 1)
    out_ref[...] = result.astype(BF16)


def packed_shards(tokens, cotangent, first_factor, second_factor, gate_source, alternate, batch, seq):
    x, cot = tokens[0], cotangent[0]
    rows_here, width = x.shape
    blocks, k_here, order = first_factor.shape
    j_here, m_here, count = second_factor.shape
    groups, lanes = j_here // LANE_GROUP, count * LANE_GROUP
    src = gate_source.reshape(1, width)
    alt = alternate.reshape(1, order)

    flat = jnp.transpose(second_factor, (1, 2, 0)).reshape(m_here * count, j_here)
    vals = {}

    def dep(name, value):
        earlier = [vals[n] for n in CFG['deps'].get(name, ()) if n in vals]
        return after(value, *earlier) if earlier else value

    def keep(name, value):
        vals[name] = value
        return value

    def move(name, value, axis, step, size):
        return keep(name, swap(dep(name, value), axis, step, size))

    (mine,) = call(functools.partial(pack_body, count), [of((groups * m_here, lanes))], [flat])
    packed = {0: mine}
    for d in (3, 2, 1):
        packed[d] = move(f"D{d}", mine, "batch", d, batch)
    (dz,) = call(gate_body, [of((rows_here, width))], [x, cot, src], limit=16 << 20)
    keep("gate", dz)
    first_ready = after(first_factor, dz) if CFG['f2early'] else after(first_factor, dz, *[packed[d] for d in (1, 2, 3)])
    across = move("f2", first_ready, "batch", 2, batch)
    beside = move("f1", first_ready, "batch", 1, batch)
    direct = move("f3", first_ready, "batch", 3, batch) if CFG['direct'] else None
    piece = of((blocks, j_here, width))
    *back, second = call(
        functools.partial(regroup_back_body, batch, seq, count),
        ([of((seq, blocks, j_here, width))] if CFG['a2a'][0] else [piece] * seq) + [of((groups, count, lanes))],
        [*[packed[d] for d in range(batch)], dz],
        [
            pltpu.VMEM((groups, count, lanes), F32),
            pltpu.VMEM((count, j_here, width), BF16),
        ],
    )
    keep("A2", back[0])
    back_got = {0: back[0]}
    if CFG['a2a'][0]:
        back_got[0] = keep("h0", lax.all_to_all(dep("h0", back[0]), "seq", 0, 0, tiled=True))
    else:
        for d in CFG['order'][0]:
            back_got[d] = move(f"h{d}", back[d], "seq", d, seq)
    if direct is None:
        direct = move("fx", across, "batch", 1, batch)
    first = [first_factor, beside, across, direct]
    *regrouped, h = call(
        functools.partial(mix_body, batch, seq),
        [piece] * seq + [of((rows_here, width))],
        [dep("M", first_factor), *first[1:], x, alt, cot, src],
        [
            pltpu.VMEM((order, order), BF16),
            pltpu.VMEM((order, width), BF16),
            pltpu.VMEM((blocks, seq, j_here, width), BF16),
            pltpu.SemaphoreType.DMA((blocks,)),
        ],
    )
    keep("M", regrouped[0])
    got = {0: regrouped[0]}
    if CFG['a2a'][1]:
        got[0] = keep("H0", lax.all_to_all(dep("H0", regrouped[0]), "seq", 0, 0, tiled=True))
    else:
        for d in CFG['order'][1]:
            got[d] = move(f"H{d}", regrouped[d], "seq", d, seq)
    *parts, dmixed = call(
        functools.partial(first_grad_body, batch, seq),
        [of((blocks, k_here, order))] * batch + [of((blocks, order, width))],
        [dep("F1", back_got[0]), *[back_got[d] for d in range(1, seq) if d in back_got], x, alt],
        [pltpu.VMEM((order, order), BF16), pltpu.VMEM((order, width), BF16), pltpu.VMEM((order, order), BF16)],
    )
    keep("F1", dmixed)
    if CFG['rsdirect']:
        others = [move(f"rs{d}", parts[d], "batch", d, batch) for d in (3, 2, 1)]
    else:
        near = move("near", parts[1], "batch", 1, batch)
        far = move("far", parts[3], "batch", 1, batch)
    (dmix_in,) = call(
        functools.partial(mix_back_body, batch),
        [of((rows_here, width))],
        [dep("F2", first_factor), *first[1:], dmixed],
    )
    keep("F2", dmix_in)
    if CFG['rsdirect']:
        (grad_one,) = call(sum_body, [of(parts[0].shape)], [dep("sum", parts[0]), *others])
    else:
        kept, summed = call(
            pair_body, [of(parts[0].shape, F32), of(parts[0].shape)], [dep("pair", parts[0]), parts[2], near, far]
        )
        keep("pair", summed)
        rx = move("rx", summed, "batch", 2, batch)
        (grad_one,) = call(add_body, [of(parts[0].shape)], [kept, rx])
    keep("add", grad_one)
    received = [dep("Z1", after(got[0], dmix_in)), *[got[d] for d in range(1, seq) if d in got]]
    if len(received) == 1:
        received = [received[0].reshape(count, j_here, width)]
    *terms, gathered = call(
        functools.partial(second_grad_body, batch, seq),
        [of((groups * m_here, lanes))] * batch + ([of((count, j_here, width))] if len(received) > 1 else []),
        [*received, dz],
        [pltpu.VMEM((groups, count, lanes), F32)],
    )
    if len(received) == 1:
        terms, gathered = [*terms, gathered], received[0]
    terms_got = [dep("unpack", terms[0])] + [move(f"R{d}", terms[d], "batch", d, batch) for d in (1, 2, 3)]
    (grad_tokens,) = call(
        tokens_body, [of((rows_here, width))], [gathered, second, h, src, dmix_in]
    )
    (grad_flat,) = call(
        functools.partial(unpack_body, count), [of((m_here * count, j_here))], terms_got
    )
    grad_two = jnp.transpose(grad_flat.reshape(m_here, count, j_here), (2, 0, 1))
    return (grad_tokens[None], grad_one, grad_two)


def wide_shards(tokens, cotangent, first_factor, second_factor, gate_source, alternate):
    inputs = tokens[0]
    rows_here = inputs.shape[0]
    width = inputs.shape[1]
    order_len = alternate.shape[0]
    blocks_here = rows_here // order_len
    select = one_hot(lax.broadcasted_iota(jnp.int32, (width, width), 0) == gate_source[None, :])
    gate = jax.nn.sigmoid(jnp.dot(inputs, select, preferred_element_type=F32))
    first_full = lax.all_gather(first_factor, "batch", axis=1, tiled=True)
    second_full = lax.all_gather(second_factor, "batch", axis=1, tiled=True)
    blocked = inputs.reshape(blocks_here, order_len, width)
    mixed = jnp.einsum("ikj,ijc->ikc", first_full, blocked, preferred_element_type=F32).astype(BF16)
    shuffled = jnp.take(mixed, alternate, axis=1)
    piece = lax.all_to_all(shuffled, "seq", split_axis=1, concat_axis=0, tiled=True)
    z_blocks = jnp.einsum("jmi,ijc->jmc", second_full, piece, preferred_element_type=F32)
    j_here, count_second = z_blocks.shape[:2]
    z_out = z_blocks.reshape(rows_here, width)
    cot = cotangent[0].astype(F32)
    dz_out = (cot * gate).astype(BF16)
    dgate = cot * z_out * gate * (1.0 - gate)
    dz_blocks = dz_out.reshape(j_here, count_second, width)
    term_second = jnp.einsum("jmc,ijc->jmi", dz_blocks, piece, preferred_element_type=F32)
    grad_two = lax.psum_scatter(term_second.astype(BF16), "batch", scatter_dimension=1, tiled=True)
    dregrouped = jnp.einsum("jmi,jmc->ijc", second_full, dz_blocks, preferred_element_type=F32).astype(BF16)
    positions = lax.iota(jnp.int32, order_len)
    inverse = jnp.zeros((order_len,), jnp.int32).at[alternate].set(positions)
    restored = jnp.take(
        lax.all_to_all(dregrouped, "seq", split_axis=0, concat_axis=1, tiled=True), inverse, axis=1
    )
    dmix_in = jnp.einsum("ikj,ikc->ijc", first_full, restored, preferred_element_type=F32)
    term_first = jnp.einsum("ikc,ijc->ikj", restored, blocked, preferred_element_type=F32)
    grad_one = lax.psum_scatter(term_first.astype(BF16), "batch", scatter_dimension=1, tiled=True)
    spread = jnp.dot(dgate, select.T.astype(F32), precision=lax.Precision.HIGHEST)
    grad_tokens = (dmix_in.reshape(rows_here, width) + spread).astype(BF16)
    return (grad_tokens[None], grad_one, grad_two)


def solution(mesh):
    batch, seq = mesh.shape["batch"], mesh.shape["seq"]

    def shards(*args):
        j_here, m_here, count = args[3].shape
        if batch == 4 and seq & (seq - 1) == 0 and j_here % LANE_GROUP == 0 and m_here % 8 == 0 and count <= 32:
            return packed_shards(*args, batch, seq)
        return wide_shards(*args)

    in_specs = (
        P("batch", "seq", None),
        P("batch", "seq", None),
        P("seq", "batch", None),
        P("seq", "batch", None),
        P(),
        P(),
    )
    out_specs = (P("batch", "seq", None), P("seq", "batch", None), P("seq", "batch", None))
    return jax.shard_map(shards, mesh=mesh, in_specs=in_specs, out_specs=out_specs, check_vma=False)
```

```python
import functools

import jax
import jax.numpy as jnp
from jax import lax
from jax.experimental import pallas as pl
from jax.experimental.pallas import tpu as pltpu
from jax.sharding import PartitionSpec as P

BF16 = jnp.bfloat16
F32 = jnp.float32
LANE_GROUP = 16
CFG = {'a2a': [False, False], 'cost': {}, 'direct': False, 'rsdirect': True, 'f2early': False, 'order': [[7, 6, 5, 4, 3, 2, 1], [7, 6, 5, 4, 3, 2, 1]], 'deps': {'h3': ['h7'], 'h2': ['h7'], 'h1': ['h7'], 'fx': ['h7', 'h4'], 'F1': ['M', 'H1', 'H2', 'H3', 'fx'], 'pair': ['F2'], 'H1': ['h3'], 'H2': ['M'], 'f2': ['A2'], 'rs1': ['H7', 'H6'], 'rs2': ['H7', 'H6'], 'rs3': ['H7', 'H6'], 'F2': ['rs1']}}


def iota(shape, dim):
    return lax.broadcasted_iota(jnp.int32, shape, dim)


def one_hot(mask):
    return jnp.where(mask, 1.0, 0.0).astype(BF16)


def dot(a, b, da=1, db=0):
    return lax.dot_general(a, b, (((da,), (db,)), ((), ())), preferred_element_type=F32)


def call(body, outs, ins, scratch=(), spaces={}, limit=40 << 20, weight=0, out_space=pltpu.VMEM):
    name = getattr(body, "func", body).__name__
    weight = CFG['cost'].get(name, 0)
    return pl.pallas_call(
        body,
        name=name,
        out_shape=outs,
        in_specs=[pl.BlockSpec(memory_space=spaces.get(n, pltpu.VMEM)) for n in range(len(ins))],
        out_specs=[pl.BlockSpec(memory_space=out_space)] * len(outs),
        scratch_shapes=list(scratch),
        compiler_params=pltpu.CompilerParams(vmem_limit_bytes=limit),
        cost_estimate=pl.CostEstimate(flops=0, bytes_accessed=weight, transcendentals=0),
    )(*ins)


def of(shape, dtype=BF16):
    return jax.ShapeDtypeStruct(shape, dtype)


def swap(value, axis, step, size):
    return lax.ppermute(value, axis, [(p, p ^ step) for p in range(size)])


def after(value, *earlier):
    return lax.optimization_barrier((value, *earlier))[0]


def pack_body(order, s_ref, out_ref):
    rows, j_here = s_ref.shape
    groups = j_here // LANE_GROUP
    lanes = order * LANE_GROUP
    m_here = rows // order
    s = s_ref[...]
    lane = iota((j_here, lanes), 1)
    keep = (iota((rows, lanes), 0) % order) == (iota((rows, lanes), 1) // LANE_GROUP)
    for g in range(groups):
        place = one_hot(iota((j_here, lanes), 0) == g * LANE_GROUP + lane % LANE_GROUP)
        wide = jnp.where(keep, dot(s, place), 0.0)
        packed = jnp.sum(wide.reshape(m_here, order, lanes), axis=1)
        out_ref[g * m_here : (g + 1) * m_here, :] = packed.astype(BF16)


def gate_body(x_ref, cot_ref, src_ref, dz_ref):
    rows, width = x_ref.shape
    step = min(rows, 512)
    select = one_hot(iota((width, width), 0) == src_ref[...])
    for n in range(rows // step):
        part = slice(n * step, (n + 1) * step)
        gate = jax.nn.sigmoid(dot(x_ref[part, :], select))
        dz_ref[part, :] = (cot_ref[part, :].astype(F32) * gate).astype(BF16)


def regroup_back_body(batch, seq, order, *refs):
    pieces, dz_ref = refs[:batch], refs[batch]
    outs, second_ref, d_scr, r_scr = refs[batch + 1 : -3], *refs[-3:]
    me, here = lax.axis_index("batch"), lax.axis_index("seq")
    groups = second_ref.shape[0]
    lanes = order * LANE_GROUP
    m_here = order // batch
    for d in range(batch):
        piece = pieces[d][...].astype(F32)
        first = pl.multiple_of((me ^ d) * m_here, m_here)
        for g in range(groups):
            d_scr[g, pl.ds(first, m_here), :] = piece[g * m_here : (g + 1) * m_here]
    width = dz_ref.shape[1]
    tiled = one_hot((iota((order, lanes), 1) % order) == iota((order, lanes), 0))
    keep = (iota((lanes, lanes), 0) % LANE_GROUP) == (iota((lanes, lanes), 1) // order)
    for g in range(groups):
        packed = d_scr[g].astype(BF16)
        second_ref[g] = packed
        weights = jnp.where(keep, dot(packed, tiled, 0, 0), 0.0).astype(BF16)
        result = dot(weights, dz_ref[g * lanes : (g + 1) * lanes, :]).astype(BF16)
        r_scr[:, g * LANE_GROUP : (g + 1) * LANE_GROUP, :] = result.reshape(order, LANE_GROUP, width)

    blocks = order // seq
    if len(outs) == 1:
        outs[0][...] = r_scr[...].reshape(outs[0].shape)
    else:
        for d in range(seq):
            outs[d][...] = r_scr[pl.ds((here ^ d) * blocks, blocks)]


def mix_body(batch, seq, *refs):
    pieces, x_ref, alt_ref, cot_ref, src_ref = refs[:batch], *refs[batch : batch + 4]
    outs, h_ref, p_scr, mix_scr, reg_scr, sems = refs[batch + 4 : -5], *refs[-5:]
    me, here = lax.axis_index("batch"), lax.axis_index("seq")
    blocks, rows, order = pieces[0].shape
    j_here = order // seq
    width = x_ref.shape[1]
    from_rows = jnp.where(iota((order, order), 0) == alt_ref[...], 1.0, 0.0)
    p_scr[...] = from_rows.T.astype(BF16)
    select = one_hot(iota((width, width), 0) == src_ref[...])

    writes = []
    for i in range(blocks):
        x = x_ref[i * order : (i + 1) * order, :]
        for d in range(batch):
            first = pl.multiple_of((me ^ d) * rows, rows)
            mix_scr[pl.ds(first, rows), :] = dot(pieces[d][i], x).astype(BF16)
        result = dot(p_scr[...], mix_scr[...]).astype(BF16)
        if len(outs) == 1:
            reg_scr[i] = result.reshape(seq, j_here, width)
            writes.append(pltpu.make_async_copy(reg_scr.at[i], outs[0].at[:, i], sems.at[i]))
            writes[i].start()
        else:
            reg_scr[i] = result.reshape(seq, j_here, width)
            for d in range(seq):
                outs[d][i] = reg_scr[i, here ^ d]
        gate = jax.nn.sigmoid(dot(x, select))
        cot = cot_ref[i * order : (i + 1) * order, :].astype(F32)
        h_ref[i * order : (i + 1) * order, :] = (cot * gate * (1.0 - gate)).astype(BF16)
    for write in writes:
        write.wait()


def first_grad_body(batch, seq, *refs):
    count = len(refs) - batch - 6
    pieces, x_ref, alt_ref = refs[:count], refs[count], refs[count + 1]
    outs, dmixed_ref = refs[count + 2 : count + 2 + batch], refs[count + 2 + batch]
    p_scr, reg_scr, part_scr = refs[-3:]
    me, here = lax.axis_index("batch"), lax.axis_index("seq")
    blocks, j_here, width = pieces[0].shape[-3:]
    order = j_here * seq
    rows = order // batch
    p_scr[...] = one_hot(iota((order, order), 0) == alt_ref[...])

    @pl.loop(0, blocks)
    def _(i):
        if count == 1:
            reg_scr[...] = pieces[0][:, i].reshape(order, width)
        else:
            for d in range(seq):
                first = pl.multiple_of((here ^ d) * j_here, j_here)
                reg_scr[pl.ds(first, j_here), :] = pieces[d][i]
        dmixed = dot(p_scr[...], reg_scr[...]).astype(BF16)
        dmixed_ref[i] = dmixed
        x = x_ref[pl.ds(pl.multiple_of(i * order, order), order), :]
        part_scr[...] = dot(dmixed, x, 1, 1).astype(BF16)
        for d in range(batch):
            first = pl.multiple_of((me ^ d) * rows, rows)
            outs[d][i] = part_scr[pl.ds(first, rows), :]


def mix_back_body(batch, *refs):
    pieces, dmixed_ref, out_ref = refs[:batch], *refs[batch:]
    me = lax.axis_index("batch")
    blocks, rows, order = pieces[0].shape

    @pl.loop(0, blocks)
    def _(i):
        total = None
        for d in range(batch):
            first = pl.multiple_of((me ^ d) * rows, rows)
            term = dot(pieces[d][i], dmixed_ref[i, pl.ds(first, rows), :], 0, 0)
            total = term if total is None else total + term
        out_ref[pl.ds(pl.multiple_of(i * order, order), order), :] = total.astype(BF16)


def gather_blocks(seq, pieces, scr):
    here = lax.axis_index("seq")
    blocks = pieces[0].shape[0]
    for d in range(seq):
        scr[pl.ds((here ^ d) * blocks, blocks)] = pieces[d][...]


def second_grad_body(batch, seq, *refs):
    count = len(refs) - batch - 3 if len(refs) > batch + 4 else 1
    if count == 1:
        pieces, dz_ref = refs[:1], refs[1]
        outs, reg_ref, y_scr = refs[2 : 2 + batch], refs[0], refs[-1]
    else:
        pieces, dz_ref = refs[:seq], refs[seq]
        outs, reg_ref, y_scr = refs[seq + 1 : seq + 1 + batch], refs[-2], refs[-1]
    me = lax.axis_index("batch")
    order, j_here, width = reg_ref.shape
    groups, lanes, m_here = j_here // LANE_GROUP, order * LANE_GROUP, order // batch
    if count > 1:
        gather_blocks(seq, pieces, reg_ref)

    @pl.loop(0, groups)
    def _(g):
        js = pl.ds(pl.multiple_of(g * LANE_GROUP, LANE_GROUP), LANE_GROUP)
        reg = reg_ref[:, js, :].reshape(lanes, width)
        dz = dz_ref[pl.ds(pl.multiple_of(g * lanes, lanes), lanes), :]
        wide = dot(dz, reg, 1, 1)
        col = iota((order, lanes), 1) % LANE_GROUP
        packed = wide[:order]
        for jj in range(1, LANE_GROUP):
            packed = jnp.where(col == jj, wide[jj * order : (jj + 1) * order], packed)
        y_scr[g] = packed

    for d in range(batch):
        first = pl.multiple_of((me ^ d) * m_here, m_here)
        rows = [y_scr[g, pl.ds(first, m_here), :] for g in range(groups)]
        outs[d][...] = jnp.concatenate(rows, axis=0).astype(BF16)


def tokens_body(reg_ref, second_ref, h_ref, src_ref, back_ref, out_ref):
    order, j_here, width = reg_ref.shape
    groups, lanes = j_here // LANE_GROUP, order * LANE_GROUP
    select = one_hot(iota((width, width), 0) == src_ref[...])
    col = iota((order, lanes), 1) % LANE_GROUP
    for g in range(groups):
        reg = reg_ref[:, g * LANE_GROUP : (g + 1) * LANE_GROUP, :].reshape(lanes, width)
        packed = second_ref[g].astype(F32)
        weights = jnp.concatenate(
            [jnp.where(col == jj, packed, 0.0).astype(BF16) for jj in range(LANE_GROUP)], axis=0
        )
        rows = slice(g * lanes, (g + 1) * lanes)
        dgate = (dot(weights, reg) * h_ref[rows, :].astype(F32)).astype(BF16)
        out_ref[rows, :] = (back_ref[rows, :].astype(F32) + dot(dgate, select, 1, 1)).astype(BF16)


def pair_body(own_a, own_b, got_a, got_b, out_a, out_b):
    out_a[...] = own_a[...].astype(F32) + got_a[...].astype(F32)
    out_b[...] = (own_b[...].astype(F32) + got_b[...].astype(F32)).astype(BF16)


def sum_body(own, *refs):
    total = own[...].astype(F32)
    for got in refs[:-1]:
        total = total + got[...].astype(F32)
    refs[-1][...] = total.astype(BF16)


def add_body(own, got, out):
    out[...] = (own[...] + got[...].astype(F32)).astype(BF16)


def unpack_body(order, *refs):
    pieces, out_ref = refs[:-1], refs[-1]
    rows, j_here = out_ref.shape
    groups, lanes, m_here = j_here // LANE_GROUP, order * LANE_GROUP, rows // order
    total = pieces[0][...].astype(F32)
    for piece in pieces[1:]:
        total = total + piece[...].astype(F32)
    lane = iota((j_here, lanes), 1)
    keep = (iota((rows, lanes), 0) % order) == (iota((rows, lanes), 1) // LANE_GROUP)
    result = jnp.zeros((rows, j_here), F32)
    for g in range(groups):
        place = one_hot(iota((j_here, lanes), 0) == g * LANE_GROUP + lane % LANE_GROUP)
        packed = total[g * m_here : (g + 1) * m_here]
        wide = jnp.broadcast_to(packed[:, None, :], (m_here, order, lanes)).reshape(rows, lanes)
        result = result + dot(jnp.where(keep, wide, 0.0).astype(BF16), place, 1, 1)
    out_ref[...] = result.astype(BF16)


def packed_shards(tokens, cotangent, first_factor, second_factor, gate_source, alternate, batch, seq):
    x, cot = tokens[0], cotangent[0]
    rows_here, width = x.shape
    blocks, k_here, order = first_factor.shape
    j_here, m_here, count = second_factor.shape
    groups, lanes = j_here // LANE_GROUP, count * LANE_GROUP
    src = gate_source.reshape(1, width)
    alt = alternate.reshape(1, order)

    flat = jnp.transpose(second_factor, (1, 2, 0)).reshape(m_here * count, j_here)
    vals = {}

    def dep(name, value):
        earlier = [vals[n] for n in CFG['deps'].get(name, ()) if n in vals]
        return after(value, *earlier) if earlier else value

    def keep(name, value):
        vals[name] = value
        return value

    def move(name, value, axis, step, size):
        return keep(name, swap(dep(name, value), axis, step, size))

    (mine,) = call(functools.partial(pack_body, count), [of((groups * m_here, lanes))], [flat])
    packed = {0: mine}
    for d in (3, 2, 1):
        packed[d] = move(f"D{d}", mine, "batch", d, batch)
    (dz,) = call(gate_body, [of((rows_here, width))], [x, cot, src], limit=16 << 20)
    keep("gate", dz)
    piece = of((blocks, j_here, width))
    *back, second = call(
        functools.partial(regroup_back_body, batch, seq, count),
        ([of((seq, blocks, j_here, width))] if CFG['a2a'][0] else [piece] * seq) + [of((groups, count, lanes))],
        [*[packed[d] for d in range(batch)], dz],
        [
            pltpu.VMEM((groups, count, lanes), F32),
            pltpu.VMEM((count, j_here, width), BF16),
        ],
    )
    keep("A2", back[0])
    first_ready = after(first_factor, dz) if CFG['f2early'] else after(first_factor, dz, *[packed[d] for d in (1, 2, 3)])
    across = move("f2", first_ready, "batch", 2, batch)
    beside = move("f1", first_ready, "batch", 1, batch)
    direct = move("f3", first_ready, "batch", 3, batch) if CFG['direct'] else None
    back_got = {0: back[0]}
    if CFG['a2a'][0]:
        back_got[0] = keep("h0", lax.all_to_all(dep("h0", back[0]), "seq", 0, 0, tiled=True))
    else:
        for d in CFG['order'][0]:
            back_got[d] = move(f"h{d}", back[d], "seq", d, seq)
    if direct is None:
        direct = move("fx", across, "batch", 1, batch)
    first = [first_factor, beside, across, direct]
    *regrouped, h = call(
        functools.partial(mix_body, batch, seq),
        [piece] * seq + [of((rows_here, width))],
        [dep("M", first_factor), *first[1:], x, alt, cot, src],
        [
            pltpu.VMEM((order, order), BF16),
            pltpu.VMEM((order, width), BF16),
            pltpu.VMEM((blocks, seq, j_here, width), BF16),
            pltpu.SemaphoreType.DMA((blocks,)),
        ],
    )
    keep("M", regrouped[0])
    got = {0: regrouped[0]}
    if CFG['a2a'][1]:
        got[0] = keep("H0", lax.all_to_all(dep("H0", regrouped[0]), "seq", 0, 0, tiled=True))
    else:
        for d in CFG['order'][1]:
            got[d] = move(f"H{d}", regrouped[d], "seq", d, seq)
    *parts, dmixed = call(
        functools.partial(first_grad_body, batch, seq),
        [of((blocks, k_here, order))] * batch + [of((blocks, order, width))],
        [dep("F1", back_got[0]), *[back_got[d] for d in range(1, seq) if d in back_got], x, alt],
        [pltpu.VMEM((order, order), BF16), pltpu.VMEM((order, width), BF16), pltpu.VMEM((order, order), BF16)],
    )
    keep("F1", dmixed)
    if CFG['rsdirect']:
        others = [move(f"rs{d}", parts[d], "batch", d, batch) for d in (3, 2, 1)]
    else:
        near = move("near", parts[1], "batch", 1, batch)
        far = move("far", parts[3], "batch", 1, batch)
    (dmix_in,) = call(
        functools.partial(mix_back_body, batch),
        [of((rows_here, width))],
        [dep("F2", first_factor), *first[1:], dmixed],
    )
    keep("F2", dmix_in)
    if CFG['rsdirect']:
        (grad_one,) = call(sum_body, [of(parts[0].shape)], [dep("sum", parts[0]), *others])
    else:
        kept, summed = call(
            pair_body, [of(parts[0].shape, F32), of(parts[0].shape)], [dep("pair", parts[0]), parts[2], near, far]
        )
        keep("pair", summed)
        rx = move("rx", summed, "batch", 2, batch)
        (grad_one,) = call(add_body, [of(parts[0].shape)], [kept, rx])
    keep("add", grad_one)
    received = [dep("Z1", after(got[0], dmix_in)), *[got[d] for d in range(1, seq) if d in got]]
    if len(received) == 1:
        received = [received[0].reshape(count, j_here, width)]
    *terms, gathered = call(
        functools.partial(second_grad_body, batch, seq),
        [of((groups * m_here, lanes))] * batch + ([of((count, j_here, width))] if len(received) > 1 else []),
        [*received, dz],
        [pltpu.VMEM((groups, count, lanes), F32)],
    )
    if len(received) == 1:
        terms, gathered = [*terms, gathered], received[0]
    terms_got = [dep("unpack", terms[0])] + [move(f"R{d}", terms[d], "batch", d, batch) for d in (1, 2, 3)]
    (grad_tokens,) = call(
        tokens_body, [of((rows_here, width))], [gathered, second, h, src, dmix_in]
    )
    (grad_flat,) = call(
        functools.partial(unpack_body, count), [of((m_here * count, j_here))], terms_got
    )
    grad_two = jnp.transpose(grad_flat.reshape(m_here, count, j_here), (2, 0, 1))
    return (grad_tokens[None], grad_one, grad_two)


def wide_shards(tokens, cotangent, first_factor, second_factor, gate_source, alternate):
    inputs = tokens[0]
    rows_here = inputs.shape[0]
    width = inputs.shape[1]
    order_len = alternate.shape[0]
    blocks_here = rows_here // order_len
    select = one_hot(lax.broadcasted_iota(jnp.int32, (width, width), 0) == gate_source[None, :])
    gate = jax.nn.sigmoid(jnp.dot(inputs, select, preferred_element_type=F32))
    first_full = lax.all_gather(first_factor, "batch", axis=1, tiled=True)
    second_full = lax.all_gather(second_factor, "batch", axis=1, tiled=True)
    blocked = inputs.reshape(blocks_here, order_len, width)
    mixed = jnp.einsum("ikj,ijc->ikc", first_full, blocked, preferred_element_type=F32).astype(BF16)
    shuffled = jnp.take(mixed, alternate, axis=1)
    piece = lax.all_to_all(shuffled, "seq", split_axis=1, concat_axis=0, tiled=True)
    z_blocks = jnp.einsum("jmi,ijc->jmc", second_full, piece, preferred_element_type=F32)
    j_here, count_second = z_blocks.shape[:2]
    z_out = z_blocks.reshape(rows_here, width)
    cot = cotangent[0].astype(F32)
    dz_out = (cot * gate).astype(BF16)
    dgate = cot * z_out * gate * (1.0 - gate)
    dz_blocks = dz_out.reshape(j_here, count_second, width)
    term_second = jnp.einsum("jmc,ijc->jmi", dz_blocks, piece, preferred_element_type=F32)
    grad_two = lax.psum_scatter(term_second.astype(BF16), "batch", scatter_dimension=1, tiled=True)
    dregrouped = jnp.einsum("jmi,jmc->ijc", second_full, dz_blocks, preferred_element_type=F32).astype(BF16)
    positions = lax.iota(jnp.int32, order_len)
    inverse = jnp.zeros((order_len,), jnp.int32).at[alternate].set(positions)
    restored = jnp.take(
        lax.all_to_all(dregrouped, "seq", split_axis=0, concat_axis=1, tiled=True), inverse, axis=1
    )
    dmix_in = jnp.einsum("ikj,ikc->ijc", first_full, restored, preferred_element_type=F32)
    term_first = jnp.einsum("ikc,ijc->ikj", restored, blocked, preferred_element_type=F32)
    grad_one = lax.psum_scatter(term_first.astype(BF16), "batch", scatter_dimension=1, tiled=True)
    spread = jnp.dot(dgate, select.T.astype(F32), precision=lax.Precision.HIGHEST)
    grad_tokens = (dmix_in.reshape(rows_here, width) + spread).astype(BF16)
    return (grad_tokens[None], grad_one, grad_two)


def solution(mesh):
    batch, seq = mesh.shape["batch"], mesh.shape["seq"]

    def shards(*args):
        j_here, m_here, count = args[3].shape
        if batch == 4 and seq & (seq - 1) == 0 and j_here % LANE_GROUP == 0 and m_here % 8 == 0 and count <= 32:
            return packed_shards(*args, batch, seq)
        return wide_shards(*args)

    in_specs = (
        P("batch", "seq", None),
        P("batch", "seq", None),
        P("seq", "batch", None),
        P("seq", "batch", None),
        P(),
        P(),
    )
    out_specs = (P("batch", "seq", None), P("seq", "batch", None), P("seq", "batch", None))
    return jax.shard_map(shards, mesh=mesh, in_specs=in_specs, out_specs=out_specs, check_vma=False)
```

```python
import functools

import jax
import jax.numpy as jnp
from jax import lax
from jax.experimental import pallas as pl
from jax.experimental.pallas import tpu as pltpu
from jax.sharding import PartitionSpec as P

BF16 = jnp.bfloat16
F32 = jnp.float32
LANE_GROUP = 16
CFG = {'a2a': [True, True], 'limit': 62914560, 'cost': {}, 'direct': False, 'rsdirect': False, 'f2early': False, 'order': [[7, 6, 5, 4, 3, 2, 1], [7, 6, 5, 4, 3, 2, 1]], 'deps': {'fx': ['A2'], 'F1': ['M'], 'pair': ['F2'], 'Z1': ['add']}}


def iota(shape, dim):
    return lax.broadcasted_iota(jnp.int32, shape, dim)


def one_hot(mask):
    return jnp.where(mask, 1.0, 0.0).astype(BF16)


def dot(a, b, da=1, db=0):
    return lax.dot_general(a, b, (((da,), (db,)), ((), ())), preferred_element_type=F32)


def call(body, outs, ins, scratch=(), spaces={}, limit=40 << 20, weight=0, far_outs=()):
    name = getattr(body, "func", body).__name__
    weight = CFG['cost'].get(name, 0)
    return pl.pallas_call(
        body,
        name=name,
        out_shape=outs,
        in_specs=[pl.BlockSpec(memory_space=spaces.get(n, pltpu.VMEM)) for n in range(len(ins))],
        out_specs=[
            pl.BlockSpec(memory_space=pltpu.HBM if n in far_outs else pltpu.VMEM) for n in range(len(outs))
        ],
        scratch_shapes=list(scratch),
        compiler_params=pltpu.CompilerParams(vmem_limit_bytes=limit),
        cost_estimate=pl.CostEstimate(flops=0, bytes_accessed=weight, transcendentals=0),
    )(*ins)


def of(shape, dtype=BF16):
    return jax.ShapeDtypeStruct(shape, dtype)


def swap(value, axis, step, size):
    return lax.ppermute(value, axis, [(p, p ^ step) for p in range(size)])


def after(value, *earlier):
    return lax.optimization_barrier((value, *earlier))[0]


def pack_body(order, s_ref, out_ref):
    rows, j_here = s_ref.shape
    groups = j_here // LANE_GROUP
    lanes = order * LANE_GROUP
    m_here = rows // order
    s = s_ref[...]
    lane = iota((j_here, lanes), 1)
    keep = (iota((rows, lanes), 0) % order) == (iota((rows, lanes), 1) // LANE_GROUP)
    for g in range(groups):
        place = one_hot(iota((j_here, lanes), 0) == g * LANE_GROUP + lane % LANE_GROUP)
        wide = jnp.where(keep, dot(s, place), 0.0)
        packed = jnp.sum(wide.reshape(m_here, order, lanes), axis=1)
        out_ref[g * m_here : (g + 1) * m_here, :] = packed.astype(BF16)


def gate_body(x_ref, cot_ref, src_ref, dz_ref):
    rows, width = x_ref.shape
    step = min(rows, 512)
    select = one_hot(iota((width, width), 0) == src_ref[...])
    for n in range(rows // step):
        part = slice(n * step, (n + 1) * step)
        gate = jax.nn.sigmoid(dot(x_ref[part, :], select))
        dz_ref[part, :] = (cot_ref[part, :].astype(F32) * gate).astype(BF16)


def regroup_back_body(batch, seq, order, *refs):
    pieces, dz_ref = refs[:batch], refs[batch]
    outs, second_ref, d_scr, r_scr, sems = refs[batch + 1 : -4], *refs[-4:]
    me, here = lax.axis_index("batch"), lax.axis_index("seq")
    groups = second_ref.shape[0]
    lanes = order * LANE_GROUP
    m_here = order // batch
    for d in range(batch):
        piece = pieces[d][...].astype(F32)
        first = pl.multiple_of((me ^ d) * m_here, m_here)
        for g in range(groups):
            d_scr[g, pl.ds(first, m_here), :] = piece[g * m_here : (g + 1) * m_here]
    width = dz_ref.shape[1]
    tiled = one_hot((iota((order, lanes), 1) % order) == iota((order, lanes), 0))
    keep = (iota((lanes, lanes), 0) % LANE_GROUP) == (iota((lanes, lanes), 1) // order)
    writes = []
    for g in range(groups):
        packed = d_scr[g].astype(BF16)
        second_ref[g] = packed
        weights = jnp.where(keep, dot(packed, tiled, 0, 0), 0.0).astype(BF16)
        result = dot(weights, dz_ref[g * lanes : (g + 1) * lanes, :]).astype(BF16)
        js = slice(g * LANE_GROUP, (g + 1) * LANE_GROUP)
        r_scr[:, js, :] = result.reshape(order, LANE_GROUP, width)
        if len(outs) == 1:
            writes.append(pltpu.make_async_copy(r_scr.at[:, js, :], outs[0].at[:, js, :], sems.at[g]))
            writes[g].start()

    blocks = order // seq
    if len(outs) == 1:
        for write in writes:
            write.wait()
    else:
        for d in range(seq):
            outs[d][...] = r_scr[pl.ds((here ^ d) * blocks, blocks)]


def mix_body(batch, seq, *refs):
    pieces, x_ref, alt_ref, cot_ref, src_ref = refs[:batch], *refs[batch : batch + 4]
    outs, h_ref, p_scr, mix_scr, reg_scr, sems = refs[batch + 4 : -5], *refs[-5:]
    me, here = lax.axis_index("batch"), lax.axis_index("seq")
    blocks, rows, order = pieces[0].shape
    j_here = order // seq
    width = x_ref.shape[1]
    from_rows = jnp.where(iota((order, order), 0) == alt_ref[...], 1.0, 0.0)
    p_scr[...] = from_rows.T.astype(BF16)
    select = one_hot(iota((width, width), 0) == src_ref[...])

    writes = []
    for i in range(blocks):
        x = x_ref[i * order : (i + 1) * order, :]
        for d in range(batch):
            first = pl.multiple_of((me ^ d) * rows, rows)
            mix_scr[pl.ds(first, rows), :] = dot(pieces[d][i], x).astype(BF16)
        result = dot(p_scr[...], mix_scr[...]).astype(BF16)
        if len(outs) == 1:
            reg_scr[i] = result.reshape(seq, j_here, width)
            writes.append(pltpu.make_async_copy(reg_scr.at[i], outs[0].at[:, i], sems.at[i]))
            writes[i].start()
        else:
            reg_scr[i] = result.reshape(seq, j_here, width)
            for d in range(seq):
                outs[d][i] = reg_scr[i, here ^ d]
        gate = jax.nn.sigmoid(dot(x, select))
        cot = cot_ref[i * order : (i + 1) * order, :].astype(F32)
        h_ref[i * order : (i + 1) * order, :] = (cot * gate * (1.0 - gate)).astype(BF16)
    for write in writes:
        write.wait()


def first_grad_body(batch, seq, *refs):
    count = len(refs) - batch - 6
    pieces, x_ref, alt_ref = refs[:count], refs[count], refs[count + 1]
    outs, dmixed_ref = refs[count + 2 : count + 2 + batch], refs[count + 2 + batch]
    p_scr, reg_scr, part_scr = refs[-3:]
    me, here = lax.axis_index("batch"), lax.axis_index("seq")
    blocks, j_here, width = pieces[0].shape[-3:]
    order = j_here * seq
    rows = order // batch
    p_scr[...] = one_hot(iota((order, order), 0) == alt_ref[...])

    @pl.loop(0, blocks)
    def _(i):
        if count == 1:
            reg_scr[...] = pieces[0][:, i].reshape(order, width)
        else:
            for d in range(seq):
                first = pl.multiple_of((here ^ d) * j_here, j_here)
                reg_scr[pl.ds(first, j_here), :] = pieces[d][i]
        dmixed = dot(p_scr[...], reg_scr[...]).astype(BF16)
        dmixed_ref[i] = dmixed
        x = x_ref[pl.ds(pl.multiple_of(i * order, order), order), :]
        part_scr[...] = dot(dmixed, x, 1, 1).astype(BF16)
        for d in range(batch):
            first = pl.multiple_of((me ^ d) * rows, rows)
            outs[d][i] = part_scr[pl.ds(first, rows), :]


def mix_back_body(batch, *refs):
    pieces, dmixed_ref, out_ref = refs[:batch], *refs[batch:]
    me = lax.axis_index("batch")
    blocks, rows, order = pieces[0].shape

    @pl.loop(0, blocks)
    def _(i):
        total = None
        for d in range(batch):
            first = pl.multiple_of((me ^ d) * rows, rows)
            term = dot(pieces[d][i], dmixed_ref[i, pl.ds(first, rows), :], 0, 0)
            total = term if total is None else total + term
        out_ref[pl.ds(pl.multiple_of(i * order, order), order), :] = total.astype(BF16)


def gather_blocks(seq, pieces, scr):
    here = lax.axis_index("seq")
    blocks = pieces[0].shape[0]
    for d in range(seq):
        scr[pl.ds((here ^ d) * blocks, blocks)] = pieces[d][...]


def second_grad_body(batch, seq, *refs):
    count = len(refs) - batch - 3 if len(refs) > batch + 4 else 1
    if count == 1:
        pieces, dz_ref = refs[:1], refs[1]
        outs, reg_ref, y_scr = refs[2 : 2 + batch], refs[0], refs[-1]
    else:
        pieces, dz_ref = refs[:seq], refs[seq]
        outs, reg_ref, y_scr = refs[seq + 1 : seq + 1 + batch], refs[-2], refs[-1]
    me = lax.axis_index("batch")
    order, j_here, width = reg_ref.shape
    groups, lanes, m_here = j_here // LANE_GROUP, order * LANE_GROUP, order // batch
    if count > 1:
        gather_blocks(seq, pieces, reg_ref)

    @pl.loop(0, groups)
    def _(g):
        js = pl.ds(pl.multiple_of(g * LANE_GROUP, LANE_GROUP), LANE_GROUP)
        reg = reg_ref[:, js, :].reshape(lanes, width)
        dz = dz_ref[pl.ds(pl.multiple_of(g * lanes, lanes), lanes), :]
        wide = dot(dz, reg, 1, 1)
        col = iota((order, lanes), 1) % LANE_GROUP
        packed = wide[:order]
        for jj in range(1, LANE_GROUP):
            packed = jnp.where(col == jj, wide[jj * order : (jj + 1) * order], packed)
        y_scr[g] = packed

    for d in range(batch):
        first = pl.multiple_of((me ^ d) * m_here, m_here)
        rows = [y_scr[g, pl.ds(first, m_here), :] for g in range(groups)]
        outs[d][...] = jnp.concatenate(rows, axis=0).astype(BF16)


def tokens_body(reg_ref, second_ref, h_ref, src_ref, back_ref, out_ref):
    order, j_here, width = reg_ref.shape
    groups, lanes = j_here // LANE_GROUP, order * LANE_GROUP
    select = one_hot(iota((width, width), 0) == src_ref[...])
    col = iota((order, lanes), 1) % LANE_GROUP
    for g in range(groups):
        reg = reg_ref[:, g * LANE_GROUP : (g + 1) * LANE_GROUP, :].reshape(lanes, width)
        packed = second_ref[g].astype(F32)
        weights = jnp.concatenate(
            [jnp.where(col == jj, packed, 0.0).astype(BF16) for jj in range(LANE_GROUP)], axis=0
        )
        rows = slice(g * lanes, (g + 1) * lanes)
        dgate = (dot(weights, reg) * h_ref[rows, :].astype(F32)).astype(BF16)
        out_ref[rows, :] = (back_ref[rows, :].astype(F32) + dot(dgate, select, 1, 1)).astype(BF16)


def pair_body(own_a, own_b, got_a, got_b, out_a, out_b):
    out_a[...] = own_a[...].astype(F32) + got_a[...].astype(F32)
    out_b[...] = (own_b[...].astype(F32) + got_b[...].astype(F32)).astype(BF16)


def sum_body(own, *refs):
    total = own[...].astype(F32)
    for got in refs[:-1]:
        total = total + got[...].astype(F32)
    refs[-1][...] = total.astype(BF16)


def add_body(own, got, out):
    out[...] = (own[...] + got[...].astype(F32)).astype(BF16)


def unpack_body(order, *refs):
    pieces, out_ref = refs[:-1], refs[-1]
    rows, j_here = out_ref.shape
    groups, lanes, m_here = j_here // LANE_GROUP, order * LANE_GROUP, rows // order
    total = pieces[0][...].astype(F32)
    for piece in pieces[1:]:
        total = total + piece[...].astype(F32)
    lane = iota((j_here, lanes), 1)
    keep = (iota((rows, lanes), 0) % order) == (iota((rows, lanes), 1) // LANE_GROUP)
    result = jnp.zeros((rows, j_here), F32)
    for g in range(groups):
        place = one_hot(iota((j_here, lanes), 0) == g * LANE_GROUP + lane % LANE_GROUP)
        packed = total[g * m_here : (g + 1) * m_here]
        wide = jnp.broadcast_to(packed[:, None, :], (m_here, order, lanes)).reshape(rows, lanes)
        result = result + dot(jnp.where(keep, wide, 0.0).astype(BF16), place, 1, 1)
    out_ref[...] = result.astype(BF16)


def packed_shards(tokens, cotangent, first_factor, second_factor, gate_source, alternate, batch, seq):
    x, cot = tokens[0], cotangent[0]
    rows_here, width = x.shape
    blocks, k_here, order = first_factor.shape
    j_here, m_here, count = second_factor.shape
    groups, lanes = j_here // LANE_GROUP, count * LANE_GROUP
    src = gate_source.reshape(1, width)
    alt = alternate.reshape(1, order)

    flat = jnp.transpose(second_factor, (1, 2, 0)).reshape(m_here * count, j_here)
    vals = {}

    def dep(name, value):
        earlier = [vals[n] for n in CFG['deps'].get(name, ()) if n in vals]
        return after(value, *earlier) if earlier else value

    def keep(name, value):
        vals[name] = value
        return value

    def move(name, value, axis, step, size):
        return keep(name, swap(dep(name, value), axis, step, size))

    (mine,) = call(functools.partial(pack_body, count), [of((groups * m_here, lanes))], [flat])
    packed = {0: mine}
    for d in (3, 2, 1):
        packed[d] = move(f"D{d}", mine, "batch", d, batch)
    (dz,) = call(gate_body, [of((rows_here, width))], [x, cot, src], limit=16 << 20)
    keep("gate", dz)
    piece = of((blocks, j_here, width))
    *back, second = call(
        functools.partial(regroup_back_body, batch, seq, count),
        ([of((count, j_here, width))] if CFG['a2a'][0] else [piece] * seq) + [of((groups, count, lanes))],
        [*[packed[d] for d in range(batch)], dz],
        [
            pltpu.VMEM((groups, count, lanes), F32),
            pltpu.VMEM((count, j_here, width), BF16),
            pltpu.SemaphoreType.DMA((groups,)),
        ],
        far_outs=(0,) if CFG['a2a'][0] else (),
        limit=24 << 20,
    )
    keep("A2", back[0])
    first_ready = after(first_factor, dz) if CFG['f2early'] else after(first_factor, dz, *[packed[d] for d in (1, 2, 3)])
    across = move("f2", first_ready, "batch", 2, batch)
    beside = move("f1", first_ready, "batch", 1, batch)
    direct = move("f3", first_ready, "batch", 3, batch) if CFG['direct'] else None
    back_got = {0: back[0]}
    if CFG['a2a'][0]:
        back_got[0] = keep("h0", lax.all_to_all(
            dep("h0", back[0]).reshape(seq, blocks, j_here, width), "seq", 0, 0, tiled=True
        ))
    else:
        for d in CFG['order'][0]:
            back_got[d] = move(f"h{d}", back[d], "seq", d, seq)
    if direct is None:
        direct = move("fx", across, "batch", 1, batch)
    first = [first_factor, beside, across, direct]
    *regrouped, h = call(
        functools.partial(mix_body, batch, seq),
        ([of((seq, blocks, j_here, width))] if CFG['a2a'][1] else [piece] * seq) + [of((rows_here, width))],
        [dep("M", first_factor), *first[1:], x, alt, cot, src],
        [
            pltpu.VMEM((order, order), BF16),
            pltpu.VMEM((order, width), BF16),
            pltpu.VMEM((blocks, seq, j_here, width), BF16),
            pltpu.SemaphoreType.DMA((blocks,)),
        ],
        far_outs=(0,) if CFG['a2a'][1] else (),
        limit=CFG['limit'],
    )
    keep("M", regrouped[0])
    got = {0: regrouped[0]}
    if CFG['a2a'][1]:
        got[0] = keep("H0", lax.all_to_all(dep("H0", regrouped[0]), "seq", 0, 0, tiled=True))
    else:
        for d in CFG['order'][1]:
            got[d] = move(f"H{d}", regrouped[d], "seq", d, seq)
    *parts, dmixed = call(
        functools.partial(first_grad_body, batch, seq),
        [of((blocks, k_here, order))] * batch + [of((blocks, order, width))],
        [dep("F1", back_got[0]), *[back_got[d] for d in range(1, seq) if d in back_got], x, alt],
        [pltpu.VMEM((order, order), BF16), pltpu.VMEM((order, width), BF16), pltpu.VMEM((order, order), BF16)],
        limit=CFG['limit'],
    )
    keep("F1", dmixed)
    if CFG['rsdirect']:
        others = [move(f"rs{d}", parts[d], "batch", d, batch) for d in (3, 2, 1)]
    else:
        near = move("near", parts[1], "batch", 1, batch)
        far = move("far", parts[3], "batch", 1, batch)
    (dmix_in,) = call(
        functools.partial(mix_back_body, batch),
        [of((rows_here, width))],
        [dep("F2", first_factor), *first[1:], dmixed],
        limit=CFG['limit'],
    )
    keep("F2", dmix_in)
    if CFG['rsdirect']:
        (grad_one,) = call(sum_body, [of(parts[0].shape)], [dep("sum", parts[0]), *others])
    else:
        kept, summed = call(
            pair_body, [of(parts[0].shape, F32), of(parts[0].shape)], [dep("pair", parts[0]), parts[2], near, far], limit=CFG['limit']
        )
        keep("pair", summed)
        rx = move("rx", summed, "batch", 2, batch)
        (grad_one,) = call(add_body, [of(parts[0].shape)], [kept, rx])
    keep("add", grad_one)
    received = [dep("Z1", after(got[0], dmix_in)), *[got[d] for d in range(1, seq) if d in got]]
    if len(received) == 1:
        received = [received[0].reshape(count, j_here, width)]
    *terms, gathered = call(
        functools.partial(second_grad_body, batch, seq),
        [of((groups * m_here, lanes))] * batch + ([of((count, j_here, width))] if len(received) > 1 else []),
        [*received, dz],
        [pltpu.VMEM((groups, count, lanes), F32)],
    )
    if len(received) == 1:
        terms, gathered = [*terms, gathered], received[0]
    terms_got = [dep("unpack", terms[0])] + [move(f"R{d}", terms[d], "batch", d, batch) for d in (1, 2, 3)]
    (grad_tokens,) = call(
        tokens_body, [of((rows_here, width))], [gathered, second, h, src, dmix_in]
    )
    (grad_flat,) = call(
        functools.partial(unpack_body, count), [of((m_here * count, j_here))], terms_got
    )
    grad_two = jnp.transpose(grad_flat.reshape(m_here, count, j_here), (2, 0, 1))
    return (grad_tokens[None], grad_one, grad_two)


def wide_shards(tokens, cotangent, first_factor, second_factor, gate_source, alternate):
    inputs = tokens[0]
    rows_here = inputs.shape[0]
    width = inputs.shape[1]
    order_len = alternate.shape[0]
    blocks_here = rows_here // order_len
    select = one_hot(lax.broadcasted_iota(jnp.int32, (width, width), 0) == gate_source[None, :])
    gate = jax.nn.sigmoid(jnp.dot(inputs, select, preferred_element_type=F32))
    first_full = lax.all_gather(first_factor, "batch", axis=1, tiled=True)
    second_full = lax.all_gather(second_factor, "batch", axis=1, tiled=True)
    blocked = inputs.reshape(blocks_here, order_len, width)
    mixed = jnp.einsum("ikj,ijc->ikc", first_full, blocked, preferred_element_type=F32).astype(BF16)
    shuffled = jnp.take(mixed, alternate, axis=1)
    piece = lax.all_to_all(shuffled, "seq", split_axis=1, concat_axis=0, tiled=True)
    z_blocks = jnp.einsum("jmi,ijc->jmc", second_full, piece, preferred_element_type=F32)
    j_here, count_second = z_blocks.shape[:2]
    z_out = z_blocks.reshape(rows_here, width)
    cot = cotangent[0].astype(F32)
    dz_out = (cot * gate).astype(BF16)
    dgate = cot * z_out * gate * (1.0 - gate)
    dz_blocks = dz_out.reshape(j_here, count_second, width)
    term_second = jnp.einsum("jmc,ijc->jmi", dz_blocks, piece, preferred_element_type=F32)
    grad_two = lax.psum_scatter(term_second.astype(BF16), "batch", scatter_dimension=1, tiled=True)
    dregrouped = jnp.einsum("jmi,jmc->ijc", second_full, dz_blocks, preferred_element_type=F32).astype(BF16)
    positions = lax.iota(jnp.int32, order_len)
    inverse = jnp.zeros((order_len,), jnp.int32).at[alternate].set(positions)
    restored = jnp.take(
        lax.all_to_all(dregrouped, "seq", split_axis=0, concat_axis=1, tiled=True), inverse, axis=1
    )
    dmix_in = jnp.einsum("ikj,ikc->ijc", first_full, restored, preferred_element_type=F32)
    term_first = jnp.einsum("ikc,ijc->ikj", restored, blocked, preferred_element_type=F32)
    grad_one = lax.psum_scatter(term_first.astype(BF16), "batch", scatter_dimension=1, tiled=True)
    spread = jnp.dot(dgate, select.T.astype(F32), precision=lax.Precision.HIGHEST)
    grad_tokens = (dmix_in.reshape(rows_here, width) + spread).astype(BF16)
    return (grad_tokens[None], grad_one, grad_two)


def solution(mesh):
    batch, seq = mesh.shape["batch"], mesh.shape["seq"]

    def shards(*args):
        j_here, m_here, count = args[3].shape
        if batch == 4 and seq & (seq - 1) == 0 and j_here % LANE_GROUP == 0 and m_here % 8 == 0 and count <= 32:
            return packed_shards(*args, batch, seq)
        return wide_shards(*args)

    in_specs = (
        P("batch", "seq", None),
        P("batch", "seq", None),
        P("seq", "batch", None),
        P("seq", "batch", None),
        P(),
        P(),
    )
    out_specs = (P("batch", "seq", None), P("seq", "batch", None), P("seq", "batch", None))
    return jax.shard_map(shards, mesh=mesh, in_specs=in_specs, out_specs=out_specs, check_vma=False)
```

```python
import functools

import jax
import jax.numpy as jnp
from jax import lax
from jax.experimental import pallas as pl
from jax.experimental.pallas import tpu as pltpu
from jax.sharding import PartitionSpec as P

BF16 = jnp.bfloat16
F32 = jnp.float32
LANE_GROUP = 16
CFG = {'a2a': [True, True], 'limit': 62914560, 'cost': {}, 'direct': False, 'rsdirect': False, 'f2early': False, 'order': [[7, 6, 5, 4, 3, 2, 1], [7, 6, 5, 4, 3, 2, 1]], 'deps': {'fx': ['A2'], 'F1': ['M'], 'F2': ['pair']}}


def iota(shape, dim):
    return lax.broadcasted_iota(jnp.int32, shape, dim)


def one_hot(mask):
    return jnp.where(mask, 1.0, 0.0).astype(BF16)


def dot(a, b, da=1, db=0):
    return lax.dot_general(a, b, (((da,), (db,)), ((), ())), preferred_element_type=F32)


def call(body, outs, ins, scratch=(), spaces={}, limit=40 << 20, weight=0, far_outs=()):
    name = getattr(body, "func", body).__name__
    weight = CFG['cost'].get(name, 0)
    return pl.pallas_call(
        body,
        name=name,
        out_shape=outs,
        in_specs=[pl.BlockSpec(memory_space=spaces.get(n, pltpu.VMEM)) for n in range(len(ins))],
        out_specs=[
            pl.BlockSpec(memory_space=pltpu.HBM if n in far_outs else pltpu.VMEM) for n in range(len(outs))
        ],
        scratch_shapes=list(scratch),
        compiler_params=pltpu.CompilerParams(vmem_limit_bytes=limit),
        cost_estimate=pl.CostEstimate(flops=0, bytes_accessed=weight, transcendentals=0),
    )(*ins)


def of(shape, dtype=BF16):
    return jax.ShapeDtypeStruct(shape, dtype)


def swap(value, axis, step, size):
    return lax.ppermute(value, axis, [(p, p ^ step) for p in range(size)])


def after(value, *earlier):
    return lax.optimization_barrier((value, *earlier))[0]


def pack_body(order, s_ref, out_ref):
    rows, j_here = s_ref.shape
    groups = j_here // LANE_GROUP
    lanes = order * LANE_GROUP
    m_here = rows // order
    s = s_ref[...]
    lane = iota((j_here, lanes), 1)
    keep = (iota((rows, lanes), 0) % order) == (iota((rows, lanes), 1) // LANE_GROUP)
    for g in range(groups):
        place = one_hot(iota((j_here, lanes), 0) == g * LANE_GROUP + lane % LANE_GROUP)
        wide = jnp.where(keep, dot(s, place), 0.0)
        packed = jnp.sum(wide.reshape(m_here, order, lanes), axis=1)
        out_ref[g * m_here : (g + 1) * m_here, :] = packed.astype(BF16)


def gate_body(x_ref, cot_ref, src_ref, dz_ref):
    rows, width = x_ref.shape
    step = min(rows, 512)
    select = one_hot(iota((width, width), 0) == src_ref[...])
    for n in range(rows // step):
        part = slice(n * step, (n + 1) * step)
        gate = jax.nn.sigmoid(dot(x_ref[part, :], select))
        dz_ref[part, :] = (cot_ref[part, :].astype(F32) * gate).astype(BF16)


def regroup_back_body(batch, seq, order, *refs):
    pieces, dz_ref = refs[:batch], refs[batch]
    outs, second_ref, d_scr, r_scr, sems = refs[batch + 1 : -4], *refs[-4:]
    me, here = lax.axis_index("batch"), lax.axis_index("seq")
    groups = second_ref.shape[0]
    lanes = order * LANE_GROUP
    m_here = order // batch
    for d in range(batch):
        piece = pieces[d][...].astype(F32)
        first = pl.multiple_of((me ^ d) * m_here, m_here)
        for g in range(groups):
            d_scr[g, pl.ds(first, m_here), :] = piece[g * m_here : (g + 1) * m_here]
    width = dz_ref.shape[1]
    tiled = one_hot((iota((order, lanes), 1) % order) == iota((order, lanes), 0))
    keep = (iota((lanes, lanes), 0) % LANE_GROUP) == (iota((lanes, lanes), 1) // order)
    writes = []
    for g in range(groups):
        packed = d_scr[g].astype(BF16)
        second_ref[g] = packed
        weights = jnp.where(keep, dot(packed, tiled, 0, 0), 0.0).astype(BF16)
        result = dot(weights, dz_ref[g * lanes : (g + 1) * lanes, :]).astype(BF16)
        js = slice(g * LANE_GROUP, (g + 1) * LANE_GROUP)
        r_scr[:, js, :] = result.reshape(order, LANE_GROUP, width)
        if len(outs) == 1:
            writes.append(pltpu.make_async_copy(r_scr.at[:, js, :], outs[0].at[:, js, :], sems.at[g]))
            writes[g].start()

    blocks = order // seq
    if len(outs) == 1:
        for write in writes:
            write.wait()
    else:
        for d in range(seq):
            outs[d][...] = r_scr[pl.ds((here ^ d) * blocks, blocks)]


def mix_body(batch, seq, *refs):
    pieces, x_ref, alt_ref, cot_ref, src_ref = refs[:batch], *refs[batch : batch + 4]
    outs, h_ref, p_scr, mix_scr, reg_scr, sems = refs[batch + 4 : -5], *refs[-5:]
    me, here = lax.axis_index("batch"), lax.axis_index("seq")
    blocks, rows, order = pieces[0].shape
    j_here = order // seq
    width = x_ref.shape[1]
    from_rows = jnp.where(iota((order, order), 0) == alt_ref[...], 1.0, 0.0)
    p_scr[...] = from_rows.T.astype(BF16)
    select = one_hot(iota((width, width), 0) == src_ref[...])

    writes = []
    for i in range(blocks):
        x = x_ref[i * order : (i + 1) * order, :]
        for d in range(batch):
            first = pl.multiple_of((me ^ d) * rows, rows)
            mix_scr[pl.ds(first, rows), :] = dot(pieces[d][i], x).astype(BF16)
        result = dot(p_scr[...], mix_scr[...]).astype(BF16)
        if len(outs) == 1:
            reg_scr[i] = result.reshape(seq, j_here, width)
            writes.append(pltpu.make_async_copy(reg_scr.at[i], outs[0].at[:, i], sems.at[i]))
            writes[i].start()
        else:
            reg_scr[i] = result.reshape(seq, j_here, width)
            for d in range(seq):
                outs[d][i] = reg_scr[i, here ^ d]
        gate = jax.nn.sigmoid(dot(x, select))
        cot = cot_ref[i * order : (i + 1) * order, :].astype(F32)
        h_ref[i * order : (i + 1) * order, :] = (cot * gate * (1.0 - gate)).astype(BF16)
    for write in writes:
        write.wait()


def first_grad_body(batch, seq, *refs):
    count = len(refs) - batch - 6
    pieces, x_ref, alt_ref = refs[:count], refs[count], refs[count + 1]
    outs, dmixed_ref = refs[count + 2 : count + 2 + batch], refs[count + 2 + batch]
    p_scr, reg_scr, part_scr = refs[-3:]
    me, here = lax.axis_index("batch"), lax.axis_index("seq")
    blocks, j_here, width = pieces[0].shape[-3:]
    order = j_here * seq
    rows = order // batch
    p_scr[...] = one_hot(iota((order, order), 0) == alt_ref[...])

    @pl.loop(0, blocks)
    def _(i):
        if count == 1:
            reg_scr[...] = pieces[0][:, i].reshape(order, width)
        else:
            for d in range(seq):
                first = pl.multiple_of((here ^ d) * j_here, j_here)
                reg_scr[pl.ds(first, j_here), :] = pieces[d][i]
        dmixed = dot(p_scr[...], reg_scr[...]).astype(BF16)
        dmixed_ref[i] = dmixed
        x = x_ref[pl.ds(pl.multiple_of(i * order, order), order), :]
        part_scr[...] = dot(dmixed, x, 1, 1).astype(BF16)
        for d in range(batch):
            first = pl.multiple_of((me ^ d) * rows, rows)
            outs[d][i] = part_scr[pl.ds(first, rows), :]


def mix_back_body(batch, *refs):
    pieces, dmixed_ref, out_ref = refs[:batch], *refs[batch:]
    me = lax.axis_index("batch")
    blocks, rows, order = pieces[0].shape

    @pl.loop(0, blocks)
    def _(i):
        total = None
        for d in range(batch):
            first = pl.multiple_of((me ^ d) * rows, rows)
            term = dot(pieces[d][i], dmixed_ref[i, pl.ds(first, rows), :], 0, 0)
            total = term if total is None else total + term
        out_ref[pl.ds(pl.multiple_of(i * order, order), order), :] = total.astype(BF16)


def gather_blocks(seq, pieces, scr):
    here = lax.axis_index("seq")
    blocks = pieces[0].shape[0]
    for d in range(seq):
        scr[pl.ds((here ^ d) * blocks, blocks)] = pieces[d][...]


def second_grad_body(batch, seq, *refs):
    count = len(refs) - batch - 3 if len(refs) > batch + 4 else 1
    if count == 1:
        pieces, dz_ref = refs[:1], refs[1]
        outs, reg_ref, y_scr = refs[2 : 2 + batch], refs[0], refs[-1]
    else:
        pieces, dz_ref = refs[:seq], refs[seq]
        outs, reg_ref, y_scr = refs[seq + 1 : seq + 1 + batch], refs[-2], refs[-1]
    me = lax.axis_index("batch")
    order, j_here, width = reg_ref.shape
    groups, lanes, m_here = j_here // LANE_GROUP, order * LANE_GROUP, order // batch
    if count > 1:
        gather_blocks(seq, pieces, reg_ref)

    @pl.loop(0, groups)
    def _(g):
        js = pl.ds(pl.multiple_of(g * LANE_GROUP, LANE_GROUP), LANE_GROUP)
        reg = reg_ref[:, js, :].reshape(lanes, width)
        dz = dz_ref[pl.ds(pl.multiple_of(g * lanes, lanes), lanes), :]
        wide = dot(dz, reg, 1, 1)
        col = iota((order, lanes), 1) % LANE_GROUP
        packed = wide[:order]
        for jj in range(1, LANE_GROUP):
            packed = jnp.where(col == jj, wide[jj * order : (jj + 1) * order], packed)
        y_scr[g] = packed

    for d in range(batch):
        first = pl.multiple_of((me ^ d) * m_here, m_here)
        rows = [y_scr[g, pl.ds(first, m_here), :] for g in range(groups)]
        outs[d][...] = jnp.concatenate(rows, axis=0).astype(BF16)


def tokens_body(reg_ref, second_ref, h_ref, src_ref, back_ref, out_hbm, out_ref, sems):
    order, j_here, width = reg_ref.shape
    groups, lanes = j_here // LANE_GROUP, order * LANE_GROUP
    select = one_hot(iota((width, width), 0) == src_ref[...])
    col = iota((order, lanes), 1) % LANE_GROUP
    writes = []
    for g in range(groups):
        reg = reg_ref[:, g * LANE_GROUP : (g + 1) * LANE_GROUP, :].reshape(lanes, width)
        packed = second_ref[g].astype(F32)
        weights = jnp.concatenate(
            [jnp.where(col == jj, packed, 0.0).astype(BF16) for jj in range(LANE_GROUP)], axis=0
        )
        rows = slice(g * lanes, (g + 1) * lanes)
        dgate = (dot(weights, reg) * h_ref[rows, :].astype(F32)).astype(BF16)
        out_ref[rows, :] = (back_ref[rows, :].astype(F32) + dot(dgate, select, 1, 1)).astype(BF16)
        writes.append(pltpu.make_async_copy(out_ref.at[rows, :], out_hbm.at[rows, :], sems.at[g]))
        writes[g].start()
    for write in writes:
        write.wait()


def pair_body(own_a, own_b, got_a, got_b, out_a, out_b):
    out_a[...] = own_a[...].astype(F32) + got_a[...].astype(F32)
    out_b[...] = (own_b[...].astype(F32) + got_b[...].astype(F32)).astype(BF16)


def sum_body(own, *refs):
    total = own[...].astype(F32)
    for got in refs[:-1]:
        total = total + got[...].astype(F32)
    refs[-1][...] = total.astype(BF16)


def add_body(own, got, out):
    out[...] = (own[...] + got[...].astype(F32)).astype(BF16)


def unpack_body(order, *refs):
    pieces, out_ref = refs[:-1], refs[-1]
    rows, j_here = out_ref.shape
    groups, lanes, m_here = j_here // LANE_GROUP, order * LANE_GROUP, rows // order
    total = pieces[0][...].astype(F32)
    for piece in pieces[1:]:
        total = total + piece[...].astype(F32)
    lane = iota((j_here, lanes), 1)
    keep = (iota((rows, lanes), 0) % order) == (iota((rows, lanes), 1) // LANE_GROUP)
    result = jnp.zeros((rows, j_here), F32)
    for g in range(groups):
        place = one_hot(iota((j_here, lanes), 0) == g * LANE_GROUP + lane % LANE_GROUP)
        packed = total[g * m_here : (g + 1) * m_here]
        wide = jnp.broadcast_to(packed[:, None, :], (m_here, order, lanes)).reshape(rows, lanes)
        result = result + dot(jnp.where(keep, wide, 0.0).astype(BF16), place, 1, 1)
    out_ref[...] = result.astype(BF16)


def packed_shards(tokens, cotangent, first_factor, second_factor, gate_source, alternate, batch, seq):
    x, cot = tokens[0], cotangent[0]
    rows_here, width = x.shape
    blocks, k_here, order = first_factor.shape
    j_here, m_here, count = second_factor.shape
    groups, lanes = j_here // LANE_GROUP, count * LANE_GROUP
    src = gate_source.reshape(1, width)
    alt = alternate.reshape(1, order)

    flat = jnp.transpose(second_factor, (1, 2, 0)).reshape(m_here * count, j_here)
    vals = {}

    def dep(name, value):
        earlier = [vals[n] for n in CFG['deps'].get(name, ()) if n in vals]
        return after(value, *earlier) if earlier else value

    def keep(name, value):
        vals[name] = value
        return value

    def move(name, value, axis, step, size):
        return keep(name, swap(dep(name, value), axis, step, size))

    (mine,) = call(functools.partial(pack_body, count), [of((groups * m_here, lanes))], [flat])
    packed = {0: mine}
    for d in (3, 2, 1):
        packed[d] = move(f"D{d}", mine, "batch", d, batch)
    (dz,) = call(gate_body, [of((rows_here, width))], [x, cot, src], limit=16 << 20)
    keep("gate", dz)
    piece = of((blocks, j_here, width))
    *back, second = call(
        functools.partial(regroup_back_body, batch, seq, count),
        ([of((count, j_here, width))] if CFG['a2a'][0] else [piece] * seq) + [of((groups, count, lanes))],
        [*[packed[d] for d in range(batch)], dz],
        [
            pltpu.VMEM((groups, count, lanes), F32),
            pltpu.VMEM((count, j_here, width), BF16),
            pltpu.SemaphoreType.DMA((groups,)),
        ],
        far_outs=(0,) if CFG['a2a'][0] else (),
        limit=24 << 20,
    )
    keep("A2", back[0])
    first_ready = after(first_factor, dz) if CFG['f2early'] else after(first_factor, dz, *[packed[d] for d in (1, 2, 3)])
    across = move("f2", first_ready, "batch", 2, batch)
    beside = move("f1", first_ready, "batch", 1, batch)
    direct = move("f3", first_ready, "batch", 3, batch) if CFG['direct'] else None
    back_got = {0: back[0]}
    if CFG['a2a'][0]:
        back_got[0] = keep("h0", lax.all_to_all(
            dep("h0", back[0]).reshape(seq, blocks, j_here, width), "seq", 0, 0, tiled=True
        ))
    else:
        for d in CFG['order'][0]:
            back_got[d] = move(f"h{d}", back[d], "seq", d, seq)
    if direct is None:
        direct = move("fx", across, "batch", 1, batch)
    first = [first_factor, beside, across, direct]
    *regrouped, h = call(
        functools.partial(mix_body, batch, seq),
        ([of((seq, blocks, j_here, width))] if CFG['a2a'][1] else [piece] * seq) + [of((rows_here, width))],
        [dep("M", first_factor), *first[1:], x, alt, cot, src],
        [
            pltpu.VMEM((order, order), BF16),
            pltpu.VMEM((order, width), BF16),
            pltpu.VMEM((blocks, seq, j_here, width), BF16),
            pltpu.SemaphoreType.DMA((blocks,)),
        ],
        far_outs=(0,) if CFG['a2a'][1] else (),
        limit=CFG['limit'],
    )
    keep("M", regrouped[0])
    got = {0: regrouped[0]}
    if CFG['a2a'][1]:
        got[0] = keep("H0", lax.all_to_all(dep("H0", regrouped[0]), "seq", 0, 0, tiled=True))
    else:
        for d in CFG['order'][1]:
            got[d] = move(f"H{d}", regrouped[d], "seq", d, seq)
    *parts, dmixed = call(
        functools.partial(first_grad_body, batch, seq),
        [of((blocks, k_here, order))] * batch + [of((blocks, order, width))],
        [dep("F1", back_got[0]), *[back_got[d] for d in range(1, seq) if d in back_got], x, alt],
        [pltpu.VMEM((order, order), BF16), pltpu.VMEM((order, width), BF16), pltpu.VMEM((order, order), BF16)],
        limit=40 << 20,
    )
    keep("F1", dmixed)
    if CFG['rsdirect']:
        others = [move(f"rs{d}", parts[d], "batch", d, batch) for d in (3, 2, 1)]
    else:
        near = move("near", parts[1], "batch", 1, batch)
        far = move("far", parts[3], "batch", 1, batch)
    if CFG['rsdirect']:
        (grad_one,) = call(sum_body, [of(parts[0].shape)], [dep("sum", parts[0]), *others])
    else:
        kept, summed = call(
            pair_body, [of(parts[0].shape, F32), of(parts[0].shape)], [dep("pair", parts[0]), parts[2], near, far], limit=40 << 20
        )
        keep("pair", summed)
        rx = move("rx", summed, "batch", 2, batch)
        (grad_one,) = call(add_body, [of(parts[0].shape)], [kept, rx])
    (dmix_in,) = call(
        functools.partial(mix_back_body, batch),
        [of((rows_here, width))],
        [*first, dep("F2", dmixed)],
        limit=CFG['limit'],
    )
    keep("F2", dmix_in)
    keep("add", grad_one)
    received = [dep("Z1", after(got[0], dmix_in)), *[got[d] for d in range(1, seq) if d in got]]
    if len(received) == 1:
        received = [received[0].reshape(count, j_here, width)]
    *terms, gathered = call(
        functools.partial(second_grad_body, batch, seq),
        [of((groups * m_here, lanes))] * batch + ([of((count, j_here, width))] if len(received) > 1 else []),
        [*received, dz],
        [pltpu.VMEM((groups, count, lanes), F32)],
    )
    if len(received) == 1:
        terms, gathered = [*terms, gathered], received[0]
    terms_got = [dep("unpack", terms[0])] + [move(f"R{d}", terms[d], "batch", d, batch) for d in (1, 2, 3)]
    (grad_tokens,) = call(
        tokens_body,
        [of((rows_here, width))],
        [gathered, second, h, src, dmix_in],
        [pltpu.VMEM((rows_here, width), BF16), pltpu.SemaphoreType.DMA((groups,))],
        far_outs=(0,),
    )
    (grad_flat,) = call(
        functools.partial(unpack_body, count), [of((m_here * count, j_here))], terms_got
    )
    grad_two = jnp.transpose(grad_flat.reshape(m_here, count, j_here), (2, 0, 1))
    return (grad_tokens[None], grad_one, grad_two)


def wide_shards(tokens, cotangent, first_factor, second_factor, gate_source, alternate):
    inputs = tokens[0]
    rows_here = inputs.shape[0]
    width = inputs.shape[1]
    order_len = alternate.shape[0]
    blocks_here = rows_here // order_len
    select = one_hot(lax.broadcasted_iota(jnp.int32, (width, width), 0) == gate_source[None, :])
    gate = jax.nn.sigmoid(jnp.dot(inputs, select, preferred_element_type=F32))
    first_full = lax.all_gather(first_factor, "batch", axis=1, tiled=True)
    second_full = lax.all_gather(second_factor, "batch", axis=1, tiled=True)
    blocked = inputs.reshape(blocks_here, order_len, width)
    mixed = jnp.einsum("ikj,ijc->ikc", first_full, blocked, preferred_element_type=F32).astype(BF16)
    shuffled = jnp.take(mixed, alternate, axis=1)
    piece = lax.all_to_all(shuffled, "seq", split_axis=1, concat_axis=0, tiled=True)
    z_blocks = jnp.einsum("jmi,ijc->jmc", second_full, piece, preferred_element_type=F32)
    j_here, count_second = z_blocks.shape[:2]
    z_out = z_blocks.reshape(rows_here, width)
    cot = cotangent[0].astype(F32)
    dz_out = (cot * gate).astype(BF16)
    dgate = cot * z_out * gate * (1.0 - gate)
    dz_blocks = dz_out.reshape(j_here, count_second, width)
    term_second = jnp.einsum("jmc,ijc->jmi", dz_blocks, piece, preferred_element_type=F32)
    grad_two = lax.psum_scatter(term_second.astype(BF16), "batch", scatter_dimension=1, tiled=True)
    dregrouped = jnp.einsum("jmi,jmc->ijc", second_full, dz_blocks, preferred_element_type=F32).astype(BF16)
    positions = lax.iota(jnp.int32, order_len)
    inverse = jnp.zeros((order_len,), jnp.int32).at[alternate].set(positions)
    restored = jnp.take(
        lax.all_to_all(dregrouped, "seq", split_axis=0, concat_axis=1, tiled=True), inverse, axis=1
    )
    dmix_in = jnp.einsum("ikj,ikc->ijc", first_full, restored, preferred_element_type=F32)
    term_first = jnp.einsum("ikc,ijc->ikj", restored, blocked, preferred_element_type=F32)
    grad_one = lax.psum_scatter(term_first.astype(BF16), "batch", scatter_dimension=1, tiled=True)
    spread = jnp.dot(dgate, select.T.astype(F32), precision=lax.Precision.HIGHEST)
    grad_tokens = (dmix_in.reshape(rows_here, width) + spread).astype(BF16)
    return (grad_tokens[None], grad_one, grad_two)


def solution(mesh):
    batch, seq = mesh.shape["batch"], mesh.shape["seq"]

    def shards(*args):
        j_here, m_here, count = args[3].shape
        if batch == 4 and seq & (seq - 1) == 0 and j_here % LANE_GROUP == 0 and m_here % 8 == 0 and count <= 32:
            return packed_shards(*args, batch, seq)
        return wide_shards(*args)

    in_specs = (
        P("batch", "seq", None),
        P("batch", "seq", None),
        P("seq", "batch", None),
        P("seq", "batch", None),
        P(),
        P(),
    )
    out_specs = (P("batch", "seq", None), P("seq", "batch", None), P("seq", "batch", None))
    return jax.shard_map(shards, mesh=mesh, in_specs=in_specs, out_specs=out_specs, check_vma=False)
```

```python
import functools

import jax
import jax.numpy as jnp
from jax import lax
from jax.experimental import pallas as pl
from jax.experimental.pallas import tpu as pltpu
from jax.sharding import PartitionSpec as P

BF16 = jnp.bfloat16
F32 = jnp.float32
LANE_GROUP = 16
CFG = {'a2a': [True, True], 'limit': 62914560, 'cost': {}, 'direct': False, 'rsdirect': False, 'f2early': False, 'order': [[7, 6, 5, 4, 3, 2, 1], [7, 6, 5, 4, 3, 2, 1]], 'deps': {'fx': ['A2'], 'F1': ['M'], 'F2': ['pair'], 'Z1': ['add']}}


def iota(shape, dim):
    return lax.broadcasted_iota(jnp.int32, shape, dim)


def one_hot(mask):
    return jnp.where(mask, 1.0, 0.0).astype(BF16)


def dot(a, b, da=1, db=0):
    return lax.dot_general(a, b, (((da,), (db,)), ((), ())), preferred_element_type=F32)


def call(body, outs, ins, scratch=(), spaces={}, limit=40 << 20, weight=0, far_outs=()):
    name = getattr(body, "func", body).__name__
    weight = CFG['cost'].get(name, 0)
    return pl.pallas_call(
        body,
        name=name,
        out_shape=outs,
        in_specs=[pl.BlockSpec(memory_space=spaces.get(n, pltpu.VMEM)) for n in range(len(ins))],
        out_specs=[
            pl.BlockSpec(memory_space=pltpu.HBM if n in far_outs else pltpu.VMEM) for n in range(len(outs))
        ],
        scratch_shapes=list(scratch),
        compiler_params=pltpu.CompilerParams(vmem_limit_bytes=limit),
        cost_estimate=pl.CostEstimate(flops=0, bytes_accessed=weight, transcendentals=0),
    )(*ins)


def of(shape, dtype=BF16):
    return jax.ShapeDtypeStruct(shape, dtype)


def swap(value, axis, step, size):
    return lax.ppermute(value, axis, [(p, p ^ step) for p in range(size)])


def after(value, *earlier):
    return lax.optimization_barrier((value, *earlier))[0]


def pack_body(order, s_ref, out_ref):
    rows, j_here = s_ref.shape
    groups = j_here // LANE_GROUP
    lanes = order * LANE_GROUP
    m_here = rows // order
    s = s_ref[...]
    lane = iota((j_here, lanes), 1)
    keep = (iota((rows, lanes), 0) % order) == (iota((rows, lanes), 1) // LANE_GROUP)
    for g in range(groups):
        place = one_hot(iota((j_here, lanes), 0) == g * LANE_GROUP + lane % LANE_GROUP)
        wide = jnp.where(keep, dot(s, place), 0.0)
        packed = jnp.sum(wide.reshape(m_here, order, lanes), axis=1)
        out_ref[g * m_here : (g + 1) * m_here, :] = packed.astype(BF16)


def gate_body(x_ref, cot_ref, src_ref, dz_ref):
    rows, width = x_ref.shape
    step = min(rows, 512)
    select = one_hot(iota((width, width), 0) == src_ref[...])
    for n in range(rows // step):
        part = slice(n * step, (n + 1) * step)
        gate = jax.nn.sigmoid(dot(x_ref[part, :], select))
        dz_ref[part, :] = (cot_ref[part, :].astype(F32) * gate).astype(BF16)


def regroup_back_body(batch, seq, order, *refs):
    pieces, dz_ref = refs[:batch], refs[batch]
    outs, second_ref, d_scr, r_scr, sems = refs[batch + 1 : -4], *refs[-4:]
    me, here = lax.axis_index("batch"), lax.axis_index("seq")
    groups = second_ref.shape[0]
    lanes = order * LANE_GROUP
    m_here = order // batch
    for d in range(batch):
        piece = pieces[d][...].astype(F32)
        first = pl.multiple_of((me ^ d) * m_here, m_here)
        for g in range(groups):
            d_scr[g, pl.ds(first, m_here), :] = piece[g * m_here : (g + 1) * m_here]
    width = dz_ref.shape[1]
    tiled = one_hot((iota((order, lanes), 1) % order) == iota((order, lanes), 0))
    keep = (iota((lanes, lanes), 0) % LANE_GROUP) == (iota((lanes, lanes), 1) // order)
    writes = []
    for g in range(groups):
        packed = d_scr[g].astype(BF16)
        second_ref[g] = packed
        weights = jnp.where(keep, dot(packed, tiled, 0, 0), 0.0).astype(BF16)
        result = dot(weights, dz_ref[g * lanes : (g + 1) * lanes, :]).astype(BF16)
        js = slice(g * LANE_GROUP, (g + 1) * LANE_GROUP)
        r_scr[:, js, :] = result.reshape(order, LANE_GROUP, width)
        if len(outs) == 1:
            writes.append(pltpu.make_async_copy(r_scr.at[:, js, :], outs[0].at[:, js, :], sems.at[g]))
            writes[g].start()

    blocks = order // seq
    if len(outs) == 1:
        for write in writes:
            write.wait()
    else:
        for d in range(seq):
            outs[d][...] = r_scr[pl.ds((here ^ d) * blocks, blocks)]


def mix_body(batch, seq, *refs):
    pieces, x_ref, alt_ref, cot_ref, src_ref = refs[:batch], *refs[batch : batch + 4]
    outs, h_ref, p_scr, mix_scr, reg_scr, sems = refs[batch + 4 : -5], *refs[-5:]
    me, here = lax.axis_index("batch"), lax.axis_index("seq")
    blocks, rows, order = pieces[0].shape
    j_here = order // seq
    width = x_ref.shape[1]
    from_rows = jnp.where(iota((order, order), 0) == alt_ref[...], 1.0, 0.0)
    p_scr[...] = from_rows.T.astype(BF16)
    select = one_hot(iota((width, width), 0) == src_ref[...])

    writes = []
    for i in range(blocks):
        x = x_ref[i * order : (i + 1) * order, :]
        for d in range(batch):
            first = pl.multiple_of((me ^ d) * rows, rows)
            mix_scr[pl.ds(first, rows), :] = dot(pieces[d][i], x).astype(BF16)
        result = dot(p_scr[...], mix_scr[...]).astype(BF16)
        if len(outs) == 1:
            reg_scr[i] = result.reshape(seq, j_here, width)
            writes.append(pltpu.make_async_copy(reg_scr.at[i], outs[0].at[:, i], sems.at[i]))
            writes[i].start()
        else:
            reg_scr[i] = result.reshape(seq, j_here, width)
            for d in range(seq):
                outs[d][i] = reg_scr[i, here ^ d]
        gate = jax.nn.sigmoid(dot(x, select))
        cot = cot_ref[i * order : (i + 1) * order, :].astype(F32)
        h_ref[i * order : (i + 1) * order, :] = (cot * gate * (1.0 - gate)).astype(BF16)
    for write in writes:
        write.wait()


def first_grad_body(batch, seq, *refs):
    count = len(refs) - batch - 6
    pieces, x_ref, alt_ref = refs[:count], refs[count], refs[count + 1]
    outs, dmixed_ref = refs[count + 2 : count + 2 + batch], refs[count + 2 + batch]
    p_scr, reg_scr, part_scr = refs[-3:]
    me, here = lax.axis_index("batch"), lax.axis_index("seq")
    blocks, j_here, width = pieces[0].shape[-3:]
    order = j_here * seq
    rows = order // batch
    p_scr[...] = one_hot(iota((order, order), 0) == alt_ref[...])

    @pl.loop(0, blocks)
    def _(i):
        if count == 1:
            reg_scr[...] = pieces[0][:, i].reshape(order, width)
        else:
            for d in range(seq):
                first = pl.multiple_of((here ^ d) * j_here, j_here)
                reg_scr[pl.ds(first, j_here), :] = pieces[d][i]
        dmixed = dot(p_scr[...], reg_scr[...]).astype(BF16)
        dmixed_ref[i] = dmixed
        x = x_ref[pl.ds(pl.multiple_of(i * order, order), order), :]
        part_scr[...] = dot(dmixed, x, 1, 1).astype(BF16)
        for d in range(batch):
            first = pl.multiple_of((me ^ d) * rows, rows)
            outs[d][i] = part_scr[pl.ds(first, rows), :]


def mix_back_body(batch, *refs):
    pieces, dmixed_ref, out_ref = refs[:batch], *refs[batch:]
    me = lax.axis_index("batch")
    blocks, rows, order = pieces[0].shape

    @pl.loop(0, blocks)
    def _(i):
        total = None
        for d in range(batch):
            first = pl.multiple_of((me ^ d) * rows, rows)
            term = dot(pieces[d][i], dmixed_ref[i, pl.ds(first, rows), :], 0, 0)
            total = term if total is None else total + term
        out_ref[pl.ds(pl.multiple_of(i * order, order), order), :] = total.astype(BF16)


def gather_blocks(seq, pieces, scr):
    here = lax.axis_index("seq")
    blocks = pieces[0].shape[0]
    for d in range(seq):
        scr[pl.ds((here ^ d) * blocks, blocks)] = pieces[d][...]


def second_grad_body(batch, seq, *refs):
    count = len(refs) - batch - 3 if len(refs) > batch + 4 else 1
    if count == 1:
        pieces, dz_ref = refs[:1], refs[1]
        outs, reg_ref, y_scr = refs[2 : 2 + batch], refs[0], refs[-1]
    else:
        pieces, dz_ref = refs[:seq], refs[seq]
        outs, reg_ref, y_scr = refs[seq + 1 : seq + 1 + batch], refs[-2], refs[-1]
    me = lax.axis_index("batch")
    order, j_here, width = reg_ref.shape
    groups, lanes, m_here = j_here // LANE_GROUP, order * LANE_GROUP, order // batch
    if count > 1:
        gather_blocks(seq, pieces, reg_ref)

    @pl.loop(0, groups)
    def _(g):
        js = pl.ds(pl.multiple_of(g * LANE_GROUP, LANE_GROUP), LANE_GROUP)
        reg = reg_ref[:, js, :].reshape(lanes, width)
        dz = dz_ref[pl.ds(pl.multiple_of(g * lanes, lanes), lanes), :]
        wide = dot(dz, reg, 1, 1)
        col = iota((order, lanes), 1) % LANE_GROUP
        packed = wide[:order]
        for jj in range(1, LANE_GROUP):
            packed = jnp.where(col == jj, wide[jj * order : (jj + 1) * order], packed)
        y_scr[g] = packed

    for d in range(batch):
        first = pl.multiple_of((me ^ d) * m_here, m_here)
        rows = [y_scr[g, pl.ds(first, m_here), :] for g in range(groups)]
        outs[d][...] = jnp.concatenate(rows, axis=0).astype(BF16)


def tokens_body(reg_ref, second_ref, h_ref, src_ref, back_ref, out_hbm, out_ref, sems):
    order, j_here, width = reg_ref.shape
    groups, lanes = j_here // LANE_GROUP, order * LANE_GROUP
    select = one_hot(iota((width, width), 0) == src_ref[...])
    col = iota((order, lanes), 1) % LANE_GROUP
    writes = []
    for g in range(groups):
        reg = reg_ref[:, g * LANE_GROUP : (g + 1) * LANE_GROUP, :].reshape(lanes, width)
        packed = second_ref[g].astype(F32)
        weights = jnp.concatenate(
            [jnp.where(col == jj, packed, 0.0).astype(BF16) for jj in range(LANE_GROUP)], axis=0
        )
        rows = slice(g * lanes, (g + 1) * lanes)
        dgate = (dot(weights, reg) * h_ref[rows, :].astype(F32)).astype(BF16)
        out_ref[rows, :] = (back_ref[rows, :].astype(F32) + dot(dgate, select, 1, 1)).astype(BF16)
        writes.append(pltpu.make_async_copy(out_ref.at[rows, :], out_hbm.at[rows, :], sems.at[g]))
        writes[g].start()
    for write in writes:
        write.wait()


def pair_body(own_a, own_b, got_a, got_b, out_a, out_b):
    out_a[...] = own_a[...].astype(F32) + got_a[...].astype(F32)
    out_b[...] = (own_b[...].astype(F32) + got_b[...].astype(F32)).astype(BF16)


def sum_body(own, *refs):
    total = own[...].astype(F32)
    for got in refs[:-1]:
        total = total + got[...].astype(F32)
    refs[-1][...] = total.astype(BF16)


def add_body(own, got, out):
    out[...] = (own[...] + got[...].astype(F32)).astype(BF16)


def unpack_body(order, *refs):
    pieces, out_ref = refs[:-1], refs[-1]
    rows, j_here = out_ref.shape
    groups, lanes, m_here = j_here // LANE_GROUP, order * LANE_GROUP, rows // order
    total = pieces[0][...].astype(F32)
    for piece in pieces[1:]:
        total = total + piece[...].astype(F32)
    lane = iota((j_here, lanes), 1)
    keep = (iota((rows, lanes), 0) % order) == (iota((rows, lanes), 1) // LANE_GROUP)
    result = jnp.zeros((rows, j_here), F32)
    for g in range(groups):
        place = one_hot(iota((j_here, lanes), 0) == g * LANE_GROUP + lane % LANE_GROUP)
        packed = total[g * m_here : (g + 1) * m_here]
        wide = jnp.broadcast_to(packed[:, None, :], (m_here, order, lanes)).reshape(rows, lanes)
        result = result + dot(jnp.where(keep, wide, 0.0).astype(BF16), place, 1, 1)
    out_ref[...] = result.astype(BF16)


def packed_shards(tokens, cotangent, first_factor, second_factor, gate_source, alternate, batch, seq):
    x, cot = tokens[0], cotangent[0]
    rows_here, width = x.shape
    blocks, k_here, order = first_factor.shape
    j_here, m_here, count = second_factor.shape
    groups, lanes = j_here // LANE_GROUP, count * LANE_GROUP
    src = gate_source.reshape(1, width)
    alt = alternate.reshape(1, order)

    flat = jnp.transpose(second_factor, (1, 2, 0)).reshape(m_here * count, j_here)
    vals = {}

    def dep(name, value):
        earlier = [vals[n] for n in CFG['deps'].get(name, ()) if n in vals]
        return after(value, *earlier) if earlier else value

    def keep(name, value):
        vals[name] = value
        return value

    def move(name, value, axis, step, size):
        return keep(name, swap(dep(name, value), axis, step, size))

    (mine,) = call(functools.partial(pack_body, count), [of((groups * m_here, lanes))], [flat])
    packed = {0: mine}
    for d in (3, 2, 1):
        packed[d] = move(f"D{d}", mine, "batch", d, batch)
    (dz,) = call(gate_body, [of((rows_here, width))], [x, cot, src], limit=16 << 20)
    keep("gate", dz)
    piece = of((blocks, j_here, width))
    *back, second = call(
        functools.partial(regroup_back_body, batch, seq, count),
        ([of((count, j_here, width))] if CFG['a2a'][0] else [piece] * seq) + [of((groups, count, lanes))],
        [*[packed[d] for d in range(batch)], dz],
        [
            pltpu.VMEM((groups, count, lanes), F32),
            pltpu.VMEM((count, j_here, width), BF16),
            pltpu.SemaphoreType.DMA((groups,)),
        ],
        far_outs=(0,) if CFG['a2a'][0] else (),
        limit=24 << 20,
    )
    keep("A2", back[0])
    first_ready = after(first_factor, dz) if CFG['f2early'] else after(first_factor, dz, *[packed[d] for d in (1, 2, 3)])
    across = move("f2", first_ready, "batch", 2, batch)
    beside = move("f1", first_ready, "batch", 1, batch)
    direct = move("f3", first_ready, "batch", 3, batch) if CFG['direct'] else None
    back_got = {0: back[0]}
    if CFG['a2a'][0]:
        back_got[0] = keep("h0", lax.all_to_all(
            dep("h0", back[0]).reshape(seq, blocks, j_here, width), "seq", 0, 0, tiled=True
        ))
    else:
        for d in CFG['order'][0]:
            back_got[d] = move(f"h{d}", back[d], "seq", d, seq)
    if direct is None:
        direct = move("fx", across, "batch", 1, batch)
    first = [first_factor, beside, across, direct]
    *regrouped, h = call(
        functools.partial(mix_body, batch, seq),
        ([of((seq, blocks, j_here, width))] if CFG['a2a'][1] else [piece] * seq) + [of((rows_here, width))],
        [dep("M", first_factor), *first[1:], x, alt, cot, src],
        [
            pltpu.VMEM((order, order), BF16),
            pltpu.VMEM((order, width), BF16),
            pltpu.VMEM((blocks, seq, j_here, width), BF16),
            pltpu.SemaphoreType.DMA((blocks,)),
        ],
        far_outs=(0,) if CFG['a2a'][1] else (),
        limit=CFG['limit'],
    )
    keep("M", regrouped[0])
    got = {0: regrouped[0]}
    if CFG['a2a'][1]:
        got[0] = keep("H0", lax.all_to_all(dep("H0", regrouped[0]), "seq", 0, 0, tiled=True))
    else:
        for d in CFG['order'][1]:
            got[d] = move(f"H{d}", regrouped[d], "seq", d, seq)
    *parts, dmixed = call(
        functools.partial(first_grad_body, batch, seq),
        [of((blocks, k_here, order))] * batch + [of((blocks, order, width))],
        [dep("F1", back_got[0]), *[back_got[d] for d in range(1, seq) if d in back_got], x, alt],
        [pltpu.VMEM((order, order), BF16), pltpu.VMEM((order, width), BF16), pltpu.VMEM((order, order), BF16)],
        limit=40 << 20,
    )
    keep("F1", dmixed)
    if CFG['rsdirect']:
        others = [move(f"rs{d}", parts[d], "batch", d, batch) for d in (3, 2, 1)]
    else:
        near = move("near", parts[1], "batch", 1, batch)
        far = move("far", parts[3], "batch", 1, batch)
    if CFG['rsdirect']:
        (grad_one,) = call(sum_body, [of(parts[0].shape)], [dep("sum", parts[0]), *others])
    else:
        kept, summed = call(
            pair_body, [of(parts[0].shape, F32), of(parts[0].shape)], [dep("pair", parts[0]), parts[2], near, far], limit=40 << 20
        )
        keep("pair", summed)
        rx = move("rx", summed, "batch", 2, batch)
        (grad_one,) = call(add_body, [of(parts[0].shape)], [kept, rx])
    (dmix_in,) = call(
        functools.partial(mix_back_body, batch),
        [of((rows_here, width))],
        [*first, dep("F2", dmixed)],
        limit=CFG['limit'],
    )
    keep("F2", dmix_in)
    keep("add", grad_one)
    received = [dep("Z1", after(got[0], dmix_in)), *[got[d] for d in range(1, seq) if d in got]]
    if len(received) == 1:
        received = [received[0].reshape(count, j_here, width)]
    *terms, gathered = call(
        functools.partial(second_grad_body, batch, seq),
        [of((groups * m_here, lanes))] * batch + ([of((count, j_here, width))] if len(received) > 1 else []),
        [*received, dz],
        [pltpu.VMEM((groups, count, lanes), F32)],
    )
    if len(received) == 1:
        terms, gathered = [*terms, gathered], received[0]
    terms_got = [dep("unpack", terms[0])] + [move(f"R{d}", terms[d], "batch", d, batch) for d in (1, 2, 3)]
    (grad_tokens,) = call(
        tokens_body,
        [of((rows_here, width))],
        [gathered, second, h, src, dmix_in],
        [pltpu.VMEM((rows_here, width), BF16), pltpu.SemaphoreType.DMA((groups,))],
        far_outs=(0,),
    )
    (grad_flat,) = call(
        functools.partial(unpack_body, count), [of((m_here * count, j_here))], terms_got
    )
    grad_two = jnp.transpose(grad_flat.reshape(m_here, count, j_here), (2, 0, 1))
    return (grad_tokens[None], grad_one, grad_two)


def wide_shards(tokens, cotangent, first_factor, second_factor, gate_source, alternate):
    inputs = tokens[0]
    rows_here = inputs.shape[0]
    width = inputs.shape[1]
    order_len = alternate.shape[0]
    blocks_here = rows_here // order_len
    select = one_hot(lax.broadcasted_iota(jnp.int32, (width, width), 0) == gate_source[None, :])
    gate = jax.nn.sigmoid(jnp.dot(inputs, select, preferred_element_type=F32))
    first_full = lax.all_gather(first_factor, "batch", axis=1, tiled=True)
    second_full = lax.all_gather(second_factor, "batch", axis=1, tiled=True)
    blocked = inputs.reshape(blocks_here, order_len, width)
    mixed = jnp.einsum("ikj,ijc->ikc", first_full, blocked, preferred_element_type=F32).astype(BF16)
    shuffled = jnp.take(mixed, alternate, axis=1)
    piece = lax.all_to_all(shuffled, "seq", split_axis=1, concat_axis=0, tiled=True)
    z_blocks = jnp.einsum("jmi,ijc->jmc", second_full, piece, preferred_element_type=F32)
    j_here, count_second = z_blocks.shape[:2]
    z_out = z_blocks.reshape(rows_here, width)
    cot = cotangent[0].astype(F32)
    dz_out = (cot * gate).astype(BF16)
    dgate = cot * z_out * gate * (1.0 - gate)
    dz_blocks = dz_out.reshape(j_here, count_second, width)
    term_second = jnp.einsum("jmc,ijc->jmi", dz_blocks, piece, preferred_element_type=F32)
    grad_two = lax.psum_scatter(term_second.astype(BF16), "batch", scatter_dimension=1, tiled=True)
    dregrouped = jnp.einsum("jmi,jmc->ijc", second_full, dz_blocks, preferred_element_type=F32).astype(BF16)
    positions = lax.iota(jnp.int32, order_len)
    inverse = jnp.zeros((order_len,), jnp.int32).at[alternate].set(positions)
    restored = jnp.take(
        lax.all_to_all(dregrouped, "seq", split_axis=0, concat_axis=1, tiled=True), inverse, axis=1
    )
    dmix_in = jnp.einsum("ikj,ikc->ijc", first_full, restored, preferred_element_type=F32)
    term_first = jnp.einsum("ikc,ijc->ikj", restored, blocked, preferred_element_type=F32)
    grad_one = lax.psum_scatter(term_first.astype(BF16), "batch", scatter_dimension=1, tiled=True)
    spread = jnp.dot(dgate, select.T.astype(F32), precision=lax.Precision.HIGHEST)
    grad_tokens = (dmix_in.reshape(rows_here, width) + spread).astype(BF16)
    return (grad_tokens[None], grad_one, grad_two)


def solution(mesh):
    batch, seq = mesh.shape["batch"], mesh.shape["seq"]

    def shards(*args):
        j_here, m_here, count = args[3].shape
        if batch == 4 and seq & (seq - 1) == 0 and j_here % LANE_GROUP == 0 and m_here % 8 == 0 and count <= 32:
            return packed_shards(*args, batch, seq)
        return wide_shards(*args)

    in_specs = (
        P("batch", "seq", None),
        P("batch", "seq", None),
        P("seq", "batch", None),
        P("seq", "batch", None),
        P(),
        P(),
    )
    out_specs = (P("batch", "seq", None), P("seq", "batch", None), P("seq", "batch", None))
    return jax.shard_map(shards, mesh=mesh, in_specs=in_specs, out_specs=out_specs, check_vma=False)
```

```python
import functools

import jax
import jax.numpy as jnp
from jax import lax
from jax.experimental import pallas as pl
from jax.experimental.pallas import tpu as pltpu
from jax.sharding import PartitionSpec as P

BF16 = jnp.bfloat16
F32 = jnp.float32
LANE_GROUP = 16
CFG = {'cost': {}, 'direct': False, 'rsdirect': False, 'f2early': False, 'order': [[7, 6, 5, 4, 3, 2, 1], [3, 6, 7, 5, 4, 2, 1]], 'deps': {'h3': ['h7', 'D2'], 'h2': ['h7'], 'h1': ['h7'], 'fx': ['h7', 'h4'], 'F1': ['M', 'H1', 'H2', 'H3', 'fx', 'H6'], 'near': ['H7', 'H6'], 'far': ['h3', 'H3'], 'pair': ['F2'], 'H1': [], 'H2': ['M'], 'Z1': ['add'], 'H6': ['M']}, 'a2a': [False, False]}


def iota(shape, dim):
    return lax.broadcasted_iota(jnp.int32, shape, dim)


def one_hot(mask):
    return jnp.where(mask, 1.0, 0.0).astype(BF16)


def dot(a, b, da=1, db=0):
    return lax.dot_general(a, b, (((da,), (db,)), ((), ())), preferred_element_type=F32)


def call(body, outs, ins, scratch=(), spaces={}, limit=40 << 20, weight=0, far_outs=()):
    name = getattr(body, "func", body).__name__
    weight = CFG['cost'].get(name, 0)
    return pl.pallas_call(
        body,
        name=name,
        out_shape=outs,
        in_specs=[pl.BlockSpec(memory_space=spaces.get(n, pltpu.VMEM)) for n in range(len(ins))],
        out_specs=[
            pl.BlockSpec(memory_space=pltpu.HBM if n in far_outs else pltpu.VMEM) for n in range(len(outs))
        ],
        scratch_shapes=list(scratch),
        compiler_params=pltpu.CompilerParams(vmem_limit_bytes=limit),
        cost_estimate=pl.CostEstimate(flops=0, bytes_accessed=weight, transcendentals=0),
    )(*ins)


def of(shape, dtype=BF16):
    return jax.ShapeDtypeStruct(shape, dtype)


def swap(value, axis, step, size):
    return lax.ppermute(value, axis, [(p, p ^ step) for p in range(size)])


def after(value, *earlier):
    return lax.optimization_barrier((value, *earlier))[0]


def pack_body(order, s_ref, out_ref):
    rows, j_here = s_ref.shape
    groups = j_here // LANE_GROUP
    lanes = order * LANE_GROUP
    m_here = rows // order
    s = s_ref[...]
    lane = iota((j_here, lanes), 1)
    keep = (iota((rows, lanes), 0) % order) == (iota((rows, lanes), 1) // LANE_GROUP)
    for g in range(groups):
        place = one_hot(iota((j_here, lanes), 0) == g * LANE_GROUP + lane % LANE_GROUP)
        wide = jnp.where(keep, dot(s, place), 0.0)
        packed = jnp.sum(wide.reshape(m_here, order, lanes), axis=1)
        out_ref[g * m_here : (g + 1) * m_here, :] = packed.astype(BF16)


def gate_body(x_ref, cot_ref, src_ref, dz_ref):
    rows, width = x_ref.shape
    step = min(rows, 512)
    select = one_hot(iota((width, width), 0) == src_ref[...])
    for n in range(rows // step):
        part = slice(n * step, (n + 1) * step)
        gate = jax.nn.sigmoid(dot(x_ref[part, :], select))
        dz_ref[part, :] = (cot_ref[part, :].astype(F32) * gate).astype(BF16)


def regroup_back_body(batch, seq, order, *refs):
    pieces, dz_ref = refs[:batch], refs[batch]
    outs, second_ref, d_scr, r_scr = refs[batch + 1 : -3], *refs[-3:]
    me, here = lax.axis_index("batch"), lax.axis_index("seq")
    groups = second_ref.shape[0]
    lanes = order * LANE_GROUP
    m_here = order // batch
    for d in range(batch):
        piece = pieces[d][...].astype(F32)
        first = pl.multiple_of((me ^ d) * m_here, m_here)
        for g in range(groups):
            d_scr[g, pl.ds(first, m_here), :] = piece[g * m_here : (g + 1) * m_here]
    width = dz_ref.shape[1]
    tiled = one_hot((iota((order, lanes), 1) % order) == iota((order, lanes), 0))
    keep = (iota((lanes, lanes), 0) % LANE_GROUP) == (iota((lanes, lanes), 1) // order)
    for g in range(groups):
        packed = d_scr[g].astype(BF16)
        second_ref[g] = packed
        weights = jnp.where(keep, dot(packed, tiled, 0, 0), 0.0).astype(BF16)
        result = dot(weights, dz_ref[g * lanes : (g + 1) * lanes, :]).astype(BF16)
        r_scr[:, g * LANE_GROUP : (g + 1) * LANE_GROUP, :] = result.reshape(order, LANE_GROUP, width)

    blocks = order // seq
    if len(outs) == 1:
        outs[0][...] = r_scr[...].reshape(outs[0].shape)
    else:
        for d in range(seq):
            outs[d][...] = r_scr[pl.ds((here ^ d) * blocks, blocks)]


def mix_body(batch, seq, *refs):
    pieces, x_ref, alt_ref, cot_ref, src_ref = refs[:batch], *refs[batch : batch + 4]
    outs, h_ref, p_scr, mix_scr, reg_scr, sems = refs[batch + 4 : -5], *refs[-5:]
    me, here = lax.axis_index("batch"), lax.axis_index("seq")
    blocks, rows, order = pieces[0].shape
    j_here = order // seq
    width = x_ref.shape[1]
    from_rows = jnp.where(iota((order, order), 0) == alt_ref[...], 1.0, 0.0)
    p_scr[...] = from_rows.T.astype(BF16)
    select = one_hot(iota((width, width), 0) == src_ref[...])

    writes = []
    for i in range(blocks):
        x = x_ref[i * order : (i + 1) * order, :]
        for d in range(batch):
            first = pl.multiple_of((me ^ d) * rows, rows)
            mix_scr[pl.ds(first, rows), :] = dot(pieces[d][i], x).astype(BF16)
        result = dot(p_scr[...], mix_scr[...]).astype(BF16)
        if len(outs) == 1:
            reg_scr[i] = result.reshape(seq, j_here, width)
            writes.append(pltpu.make_async_copy(reg_scr.at[i], outs[0].at[:, i], sems.at[i]))
            writes[i].start()
        else:
            reg_scr[i] = result.reshape(seq, j_here, width)
            for d in range(seq):
                outs[d][i] = reg_scr[i, here ^ d]
        gate = jax.nn.sigmoid(dot(x, select))
        cot = cot_ref[i * order : (i + 1) * order, :].astype(F32)
        h_ref[i * order : (i + 1) * order, :] = (cot * gate * (1.0 - gate)).astype(BF16)
    for write in writes:
        write.wait()


def first_grad_body(batch, seq, *refs):
    count = len(refs) - batch - 6
    pieces, x_ref, alt_ref = refs[:count], refs[count], refs[count + 1]
    outs, dmixed_ref = refs[count + 2 : count + 2 + batch], refs[count + 2 + batch]
    p_scr, reg_scr, part_scr = refs[-3:]
    me, here = lax.axis_index("batch"), lax.axis_index("seq")
    blocks, j_here, width = pieces[0].shape[-3:]
    order = j_here * seq
    rows = order // batch
    p_scr[...] = one_hot(iota((order, order), 0) == alt_ref[...])

    @pl.loop(0, blocks)
    def _(i):
        if count == 1:
            reg_scr[...] = pieces[0][:, i].reshape(order, width)
        else:
            for d in range(seq):
                first = pl.multiple_of((here ^ d) * j_here, j_here)
                reg_scr[pl.ds(first, j_here), :] = pieces[d][i]
        dmixed = dot(p_scr[...], reg_scr[...]).astype(BF16)
        dmixed_ref[i] = dmixed
        x = x_ref[pl.ds(pl.multiple_of(i * order, order), order), :]
        part_scr[...] = dot(dmixed, x, 1, 1).astype(BF16)
        for d in range(batch):
            first = pl.multiple_of((me ^ d) * rows, rows)
            outs[d][i] = part_scr[pl.ds(first, rows), :]


def mix_back_body(batch, *refs):
    pieces, dmixed_ref, out_ref = refs[:batch], *refs[batch:]
    me = lax.axis_index("batch")
    blocks, rows, order = pieces[0].shape

    @pl.loop(0, blocks)
    def _(i):
        total = None
        for d in range(batch):
            first = pl.multiple_of((me ^ d) * rows, rows)
            term = dot(pieces[d][i], dmixed_ref[i, pl.ds(first, rows), :], 0, 0)
            total = term if total is None else total + term
        out_ref[pl.ds(pl.multiple_of(i * order, order), order), :] = total.astype(BF16)


def gather_blocks(seq, pieces, scr):
    here = lax.axis_index("seq")
    blocks = pieces[0].shape[0]
    for d in range(seq):
        scr[pl.ds((here ^ d) * blocks, blocks)] = pieces[d][...]


def second_grad_body(batch, seq, *refs):
    count = len(refs) - batch - 3 if len(refs) > batch + 4 else 1
    if count == 1:
        pieces, dz_ref = refs[:1], refs[1]
        outs, reg_ref, y_scr = refs[2 : 2 + batch], refs[0], refs[-1]
    else:
        pieces, dz_ref = refs[:seq], refs[seq]
        outs, reg_ref, y_scr = refs[seq + 1 : seq + 1 + batch], refs[-2], refs[-1]
    me = lax.axis_index("batch")
    order, j_here, width = reg_ref.shape
    groups, lanes, m_here = j_here // LANE_GROUP, order * LANE_GROUP, order // batch
    if count > 1:
        gather_blocks(seq, pieces, reg_ref)

    @pl.loop(0, groups)
    def _(g):
        js = pl.ds(pl.multiple_of(g * LANE_GROUP, LANE_GROUP), LANE_GROUP)
        reg = reg_ref[:, js, :].reshape(lanes, width)
        dz = dz_ref[pl.ds(pl.multiple_of(g * lanes, lanes), lanes), :]
        wide = dot(dz, reg, 1, 1)
        col = iota((order, lanes), 1) % LANE_GROUP
        packed = wide[:order]
        for jj in range(1, LANE_GROUP):
            packed = jnp.where(col == jj, wide[jj * order : (jj + 1) * order], packed)
        y_scr[g] = packed

    for d in range(batch):
        first = pl.multiple_of((me ^ d) * m_here, m_here)
        rows = [y_scr[g, pl.ds(first, m_here), :] for g in range(groups)]
        outs[d][...] = jnp.concatenate(rows, axis=0).astype(BF16)


def tokens_body(reg_ref, second_ref, h_ref, src_ref, back_ref, out_hbm, out_ref, sems):
    order, j_here, width = reg_ref.shape
    groups, lanes = j_here // LANE_GROUP, order * LANE_GROUP
    select = one_hot(iota((width, width), 0) == src_ref[...])
    col = iota((order, lanes), 1) % LANE_GROUP
    writes = []
    for g in range(groups):
        reg = reg_ref[:, g * LANE_GROUP : (g + 1) * LANE_GROUP, :].reshape(lanes, width)
        packed = second_ref[g].astype(F32)
        weights = jnp.concatenate(
            [jnp.where(col == jj, packed, 0.0).astype(BF16) for jj in range(LANE_GROUP)], axis=0
        )
        rows = slice(g * lanes, (g + 1) * lanes)
        dgate = (dot(weights, reg) * h_ref[rows, :].astype(F32)).astype(BF16)
        out_ref[rows, :] = (back_ref[rows, :].astype(F32) + dot(dgate, select, 1, 1)).astype(BF16)
        writes.append(pltpu.make_async_copy(out_ref.at[rows, :], out_hbm.at[rows, :], sems.at[g]))
        writes[g].start()
    for write in writes:
        write.wait()


def pair_body(own_a, own_b, got_a, got_b, out_a, out_b):
    out_a[...] = own_a[...].astype(F32) + got_a[...].astype(F32)
    out_b[...] = (own_b[...].astype(F32) + got_b[...].astype(F32)).astype(BF16)


def sum_body(own, *refs):
    total = own[...].astype(F32)
    for got in refs[:-1]:
        total = total + got[...].astype(F32)
    refs[-1][...] = total.astype(BF16)


def add_body(own, got, out):
    out[...] = (own[...] + got[...].astype(F32)).astype(BF16)


def unpack_body(order, *refs):
    pieces, out_ref = refs[:-1], refs[-1]
    rows, j_here = out_ref.shape
    groups, lanes, m_here = j_here // LANE_GROUP, order * LANE_GROUP, rows // order
    total = pieces[0][...].astype(F32)
    for piece in pieces[1:]:
        total = total + piece[...].astype(F32)
    lane = iota((j_here, lanes), 1)
    keep = (iota((rows, lanes), 0) % order) == (iota((rows, lanes), 1) // LANE_GROUP)
    result = jnp.zeros((rows, j_here), F32)
    for g in range(groups):
        place = one_hot(iota((j_here, lanes), 0) == g * LANE_GROUP + lane % LANE_GROUP)
        packed = total[g * m_here : (g + 1) * m_here]
        wide = jnp.broadcast_to(packed[:, None, :], (m_here, order, lanes)).reshape(rows, lanes)
        result = result + dot(jnp.where(keep, wide, 0.0).astype(BF16), place, 1, 1)
    out_ref[...] = result.astype(BF16)


def packed_shards(tokens, cotangent, first_factor, second_factor, gate_source, alternate, batch, seq):
    x, cot = tokens[0], cotangent[0]
    rows_here, width = x.shape
    blocks, k_here, order = first_factor.shape
    j_here, m_here, count = second_factor.shape
    groups, lanes = j_here // LANE_GROUP, count * LANE_GROUP
    src = gate_source.reshape(1, width)
    alt = alternate.reshape(1, order)

    flat = jnp.transpose(second_factor, (1, 2, 0)).reshape(m_here * count, j_here)
    vals = {}

    def dep(name, value):
        earlier = [vals[n] for n in CFG['deps'].get(name, ()) if n in vals]
        return after(value, *earlier) if earlier else value

    def keep(name, value):
        vals[name] = value
        return value

    def move(name, value, axis, step, size):
        return keep(name, swap(dep(name, value), axis, step, size))

    (mine,) = call(functools.partial(pack_body, count), [of((groups * m_here, lanes))], [flat])
    packed = {0: mine}
    for d in (3, 2, 1):
        packed[d] = move(f"D{d}", mine, "batch", d, batch)
    (dz,) = call(gate_body, [of((rows_here, width))], [x, cot, src], limit=16 << 20)
    keep("gate", dz)
    piece = of((blocks, j_here, width))
    *back, second = call(
        functools.partial(regroup_back_body, batch, seq, count),
        ([of((seq, blocks, j_here, width))] if CFG['a2a'][0] else [piece] * seq) + [of((groups, count, lanes))],
        [*[packed[d] for d in range(batch)], dz],
        [
            pltpu.VMEM((groups, count, lanes), F32),
            pltpu.VMEM((count, j_here, width), BF16),
        ],
    )
    keep("A2", back[0])
    first_ready = after(first_factor, dz) if CFG['f2early'] else after(first_factor, dz, *[packed[d] for d in (1, 2, 3)])
    across = move("f2", first_ready, "batch", 2, batch)
    beside = move("f1", first_ready, "batch", 1, batch)
    direct = move("f3", first_ready, "batch", 3, batch) if CFG['direct'] else None
    back_got = {0: back[0]}
    if CFG['a2a'][0]:
        back_got[0] = keep("h0", lax.all_to_all(dep("h0", back[0]), "seq", 0, 0, tiled=True))
    else:
        for d in CFG['order'][0]:
            back_got[d] = move(f"h{d}", back[d], "seq", d, seq)
    if direct is None:
        direct = move("fx", across, "batch", 1, batch)
    first = [first_factor, beside, across, direct]
    *regrouped, h = call(
        functools.partial(mix_body, batch, seq),
        [piece] * seq + [of((rows_here, width))],
        [dep("M", first_factor), *first[1:], x, alt, cot, src],
        [
            pltpu.VMEM((order, order), BF16),
            pltpu.VMEM((order, width), BF16),
            pltpu.VMEM((blocks, seq, j_here, width), BF16),
            pltpu.SemaphoreType.DMA((blocks,)),
        ],
    )
    keep("M", regrouped[0])
    got = {0: regrouped[0]}
    if CFG['a2a'][1]:
        got[0] = keep("H0", lax.all_to_all(dep("H0", regrouped[0]), "seq", 0, 0, tiled=True))
    else:
        for d in CFG['order'][1]:
            got[d] = move(f"H{d}", regrouped[d], "seq", d, seq)
    *parts, dmixed = call(
        functools.partial(first_grad_body, batch, seq),
        [of((blocks, k_here, order))] * batch + [of((blocks, order, width))],
        [dep("F1", back_got[0]), *[back_got[d] for d in range(1, seq) if d in back_got], x, alt],
        [pltpu.VMEM((order, order), BF16), pltpu.VMEM((order, width), BF16), pltpu.VMEM((order, order), BF16)],
    )
    keep("F1", dmixed)
    if CFG['rsdirect']:
        others = [move(f"rs{d}", parts[d], "batch", d, batch) for d in (3, 2, 1)]
    else:
        near = move("near", parts[1], "batch", 1, batch)
        far = move("far", parts[3], "batch", 1, batch)
    (dmix_in,) = call(
        functools.partial(mix_back_body, batch),
        [of((rows_here, width))],
        [dep("F2", first_factor), *first[1:], dmixed],
    )
    keep("F2", dmix_in)
    if CFG['rsdirect']:
        (grad_one,) = call(sum_body, [of(parts[0].shape)], [dep("sum", parts[0]), *others])
    else:
        kept, summed = call(
            pair_body, [of(parts[0].shape, F32), of(parts[0].shape)], [dep("pair", parts[0]), parts[2], near, far]
        )
        keep("pair", summed)
        rx = move("rx", summed, "batch", 2, batch)
        (grad_one,) = call(add_body, [of(parts[0].shape)], [kept, rx])
    keep("add", grad_one)
    received = [dep("Z1", after(got[0], dmix_in)), *[got[d] for d in range(1, seq) if d in got]]
    if len(received) == 1:
        received = [received[0].reshape(count, j_here, width)]
    *terms, gathered = call(
        functools.partial(second_grad_body, batch, seq),
        [of((groups * m_here, lanes))] * batch + ([of((count, j_here, width))] if len(received) > 1 else []),
        [*received, dz],
        [pltpu.VMEM((groups, count, lanes), F32)],
    )
    if len(received) == 1:
        terms, gathered = [*terms, gathered], received[0]
    terms_got = [dep("unpack", terms[0])] + [move(f"R{d}", terms[d], "batch", d, batch) for d in (1, 2, 3)]
    (grad_tokens,) = call(
        tokens_body,
        [of((rows_here, width))],
        [gathered, second, h, src, dmix_in],
        [pltpu.VMEM((rows_here, width), BF16), pltpu.SemaphoreType.DMA((groups,))],
        far_outs=(0,),
    )
    (grad_flat,) = call(
        functools.partial(unpack_body, count), [of((m_here * count, j_here))], terms_got
    )
    grad_two = jnp.transpose(grad_flat.reshape(m_here, count, j_here), (2, 0, 1))
    return (grad_tokens[None], grad_one, grad_two)


def wide_shards(tokens, cotangent, first_factor, second_factor, gate_source, alternate):
    inputs = tokens[0]
    rows_here = inputs.shape[0]
    width = inputs.shape[1]
    order_len = alternate.shape[0]
    blocks_here = rows_here // order_len
    select = one_hot(lax.broadcasted_iota(jnp.int32, (width, width), 0) == gate_source[None, :])
    gate = jax.nn.sigmoid(jnp.dot(inputs, select, preferred_element_type=F32))
    first_full = lax.all_gather(first_factor, "batch", axis=1, tiled=True)
    second_full = lax.all_gather(second_factor, "batch", axis=1, tiled=True)
    blocked = inputs.reshape(blocks_here, order_len, width)
    mixed = jnp.einsum("ikj,ijc->ikc", first_full, blocked, preferred_element_type=F32).astype(BF16)
    shuffled = jnp.take(mixed, alternate, axis=1)
    piece = lax.all_to_all(shuffled, "seq", split_axis=1, concat_axis=0, tiled=True)
    z_blocks = jnp.einsum("jmi,ijc->jmc", second_full, piece, preferred_element_type=F32)
    j_here, count_second = z_blocks.shape[:2]
    z_out = z_blocks.reshape(rows_here, width)
    cot = cotangent[0].astype(F32)
    dz_out = (cot * gate).astype(BF16)
    dgate = cot * z_out * gate * (1.0 - gate)
    dz_blocks = dz_out.reshape(j_here, count_second, width)
    term_second = jnp.einsum("jmc,ijc->jmi", dz_blocks, piece, preferred_element_type=F32)
    grad_two = lax.psum_scatter(term_second.astype(BF16), "batch", scatter_dimension=1, tiled=True)
    dregrouped = jnp.einsum("jmi,jmc->ijc", second_full, dz_blocks, preferred_element_type=F32).astype(BF16)
    positions = lax.iota(jnp.int32, order_len)
    inverse = jnp.zeros((order_len,), jnp.int32).at[alternate].set(positions)
    restored = jnp.take(
        lax.all_to_all(dregrouped, "seq", split_axis=0, concat_axis=1, tiled=True), inverse, axis=1
    )
    dmix_in = jnp.einsum("ikj,ikc->ijc", first_full, restored, preferred_element_type=F32)
    term_first = jnp.einsum("ikc,ijc->ikj", restored, blocked, preferred_element_type=F32)
    grad_one = lax.psum_scatter(term_first.astype(BF16), "batch", scatter_dimension=1, tiled=True)
    spread = jnp.dot(dgate, select.T.astype(F32), precision=lax.Precision.HIGHEST)
    grad_tokens = (dmix_in.reshape(rows_here, width) + spread).astype(BF16)
    return (grad_tokens[None], grad_one, grad_two)


def solution(mesh):
    batch, seq = mesh.shape["batch"], mesh.shape["seq"]

    def shards(*args):
        j_here, m_here, count = args[3].shape
        if batch == 4 and seq & (seq - 1) == 0 and j_here % LANE_GROUP == 0 and m_here % 8 == 0 and count <= 32:
            return packed_shards(*args, batch, seq)
        return wide_shards(*args)

    in_specs = (
        P("batch", "seq", None),
        P("batch", "seq", None),
        P("seq", "batch", None),
        P("seq", "batch", None),
        P(),
        P(),
    )
    out_specs = (P("batch", "seq", None), P("seq", "batch", None), P("seq", "batch", None))
    return jax.shard_map(shards, mesh=mesh, in_specs=in_specs, out_specs=out_specs, check_vma=False)
```

```python
import functools

import jax
import jax.numpy as jnp
from jax import lax
from jax.experimental import pallas as pl
from jax.experimental.pallas import tpu as pltpu
from jax.sharding import PartitionSpec as P

BF16 = jnp.bfloat16
F32 = jnp.float32
LANE_GROUP = 16
CFG = {'a2a': [True, True], 'limit': 62914560, 'cost': {'add_body': 18000000, 'mix_back_body': 18000000}, 'direct': False, 'rsdirect': False, 'f2early': False, 'order': [[7, 6, 5, 4, 3, 2, 1], [7, 6, 5, 4, 3, 2, 1]], 'deps': {'fx': ['A2'], 'F1': ['M'], 'F2': ['pair'], 'Z1': ['add']}}


def iota(shape, dim):
    return lax.broadcasted_iota(jnp.int32, shape, dim)


def one_hot(mask):
    return jnp.where(mask, 1.0, 0.0).astype(BF16)


def dot(a, b, da=1, db=0):
    return lax.dot_general(a, b, (((da,), (db,)), ((), ())), preferred_element_type=F32)


def call(body, outs, ins, scratch=(), spaces={}, limit=40 << 20, weight=0, far_outs=()):
    name = getattr(body, "func", body).__name__
    weight = CFG['cost'].get(name, 0)
    return pl.pallas_call(
        body,
        name=name,
        out_shape=outs,
        in_specs=[pl.BlockSpec(memory_space=spaces.get(n, pltpu.VMEM)) for n in range(len(ins))],
        out_specs=[
            pl.BlockSpec(memory_space=pltpu.HBM if n in far_outs else pltpu.VMEM) for n in range(len(outs))
        ],
        scratch_shapes=list(scratch),
        compiler_params=pltpu.CompilerParams(vmem_limit_bytes=limit),
        cost_estimate=pl.CostEstimate(flops=0, bytes_accessed=weight, transcendentals=0),
    )(*ins)


def of(shape, dtype=BF16):
    return jax.ShapeDtypeStruct(shape, dtype)


def swap(value, axis, step, size):
    return lax.ppermute(value, axis, [(p, p ^ step) for p in range(size)])


def after(value, *earlier):
    return lax.optimization_barrier((value, *earlier))[0]


def pack_body(order, s_ref, out_ref):
    rows, j_here = s_ref.shape
    groups = j_here // LANE_GROUP
    lanes = order * LANE_GROUP
    m_here = rows // order
    s = s_ref[...]
    lane = iota((j_here, lanes), 1)
    keep = (iota((rows, lanes), 0) % order) == (iota((rows, lanes), 1) // LANE_GROUP)
    for g in range(groups):
        place = one_hot(iota((j_here, lanes), 0) == g * LANE_GROUP + lane % LANE_GROUP)
        wide = jnp.where(keep, dot(s, place), 0.0)
        packed = jnp.sum(wide.reshape(m_here, order, lanes), axis=1)
        out_ref[g * m_here : (g + 1) * m_here, :] = packed.astype(BF16)


def gate_body(x_ref, cot_ref, src_ref, dz_ref):
    rows, width = x_ref.shape
    step = min(rows, 512)
    select = one_hot(iota((width, width), 0) == src_ref[...])
    for n in range(rows // step):
        part = slice(n * step, (n + 1) * step)
        gate = jax.nn.sigmoid(dot(x_ref[part, :], select))
        dz_ref[part, :] = (cot_ref[part, :].astype(F32) * gate).astype(BF16)


def regroup_back_body(batch, seq, order, *refs):
    pieces, dz_ref = refs[:batch], refs[batch]
    outs, second_ref, d_scr, r_scr, sems = refs[batch + 1 : -4], *refs[-4:]
    me, here = lax.axis_index("batch"), lax.axis_index("seq")
    groups = second_ref.shape[0]
    lanes = order * LANE_GROUP
    m_here = order // batch
    for d in range(batch):
        piece = pieces[d][...].astype(F32)
        first = pl.multiple_of((me ^ d) * m_here, m_here)
        for g in range(groups):
            d_scr[g, pl.ds(first, m_here), :] = piece[g * m_here : (g + 1) * m_here]
    width = dz_ref.shape[1]
    tiled = one_hot((iota((order, lanes), 1) % order) == iota((order, lanes), 0))
    keep = (iota((lanes, lanes), 0) % LANE_GROUP) == (iota((lanes, lanes), 1) // order)
    writes = []
    for g in range(groups):
        packed = d_scr[g].astype(BF16)
        second_ref[g] = packed
        weights = jnp.where(keep, dot(packed, tiled, 0, 0), 0.0).astype(BF16)
        result = dot(weights, dz_ref[g * lanes : (g + 1) * lanes, :]).astype(BF16)
        js = slice(g * LANE_GROUP, (g + 1) * LANE_GROUP)
        r_scr[:, js, :] = result.reshape(order, LANE_GROUP, width)
        if len(outs) == 1:
            writes.append(pltpu.make_async_copy(r_scr.at[:, js, :], outs[0].at[:, js, :], sems.at[g]))
            writes[g].start()

    blocks = order // seq
    if len(outs) == 1:
        for write in writes:
            write.wait()
    else:
        for d in range(seq):
            outs[d][...] = r_scr[pl.ds((here ^ d) * blocks, blocks)]


def mix_body(batch, seq, *refs):
    pieces, x_ref, alt_ref, cot_ref, src_ref = refs[:batch], *refs[batch : batch + 4]
    outs, h_ref, p_scr, mix_scr, reg_scr, sems = refs[batch + 4 : -5], *refs[-5:]
    me, here = lax.axis_index("batch"), lax.axis_index("seq")
    blocks, rows, order = pieces[0].shape
    j_here = order // seq
    width = x_ref.shape[1]
    from_rows = jnp.where(iota((order, order), 0) == alt_ref[...], 1.0, 0.0)
    p_scr[...] = from_rows.T.astype(BF16)
    select = one_hot(iota((width, width), 0) == src_ref[...])

    writes = []
    for i in range(blocks):
        x = x_ref[i * order : (i + 1) * order, :]
        for d in range(batch):
            first = pl.multiple_of((me ^ d) * rows, rows)
            mix_scr[pl.ds(first, rows), :] = dot(pieces[d][i], x).astype(BF16)
        result = dot(p_scr[...], mix_scr[...]).astype(BF16)
        if len(outs) == 1:
            reg_scr[i] = result.reshape(seq, j_here, width)
            writes.append(pltpu.make_async_copy(reg_scr.at[i], outs[0].at[:, i], sems.at[i]))
            writes[i].start()
        else:
            reg_scr[i] = result.reshape(seq, j_here, width)
            for d in range(seq):
                outs[d][i] = reg_scr[i, here ^ d]
        gate = jax.nn.sigmoid(dot(x, select))
        cot = cot_ref[i * order : (i + 1) * order, :].astype(F32)
        h_ref[i * order : (i + 1) * order, :] = (cot * gate * (1.0 - gate)).astype(BF16)
    for write in writes:
        write.wait()


def first_grad_body(batch, seq, *refs):
    count = len(refs) - batch - 6
    pieces, x_ref, alt_ref = refs[:count], refs[count], refs[count + 1]
    outs, dmixed_ref = refs[count + 2 : count + 2 + batch], refs[count + 2 + batch]
    p_scr, reg_scr, part_scr = refs[-3:]
    me, here = lax.axis_index("batch"), lax.axis_index("seq")
    blocks, j_here, width = pieces[0].shape[-3:]
    order = j_here * seq
    rows = order // batch
    p_scr[...] = one_hot(iota((order, order), 0) == alt_ref[...])

    @pl.loop(0, blocks)
    def _(i):
        if count == 1:
            reg_scr[...] = pieces[0][:, i].reshape(order, width)
        else:
            for d in range(seq):
                first = pl.multiple_of((here ^ d) * j_here, j_here)
                reg_scr[pl.ds(first, j_here), :] = pieces[d][i]
        dmixed = dot(p_scr[...], reg_scr[...]).astype(BF16)
        dmixed_ref[i] = dmixed
        x = x_ref[pl.ds(pl.multiple_of(i * order, order), order), :]
        part_scr[...] = dot(dmixed, x, 1, 1).astype(BF16)
        for d in range(batch):
            first = pl.multiple_of((me ^ d) * rows, rows)
            outs[d][i] = part_scr[pl.ds(first, rows), :]


def mix_back_body(batch, *refs):
    pieces, dmixed_ref, out_ref = refs[:batch], *refs[batch:]
    me = lax.axis_index("batch")
    blocks, rows, order = pieces[0].shape

    @pl.loop(0, blocks)
    def _(i):
        total = None
        for d in range(batch):
            first = pl.multiple_of((me ^ d) * rows, rows)
            term = dot(pieces[d][i], dmixed_ref[i, pl.ds(first, rows), :], 0, 0)
            total = term if total is None else total + term
        out_ref[pl.ds(pl.multiple_of(i * order, order), order), :] = total.astype(BF16)


def gather_blocks(seq, pieces, scr):
    here = lax.axis_index("seq")
    blocks = pieces[0].shape[0]
    for d in range(seq):
        scr[pl.ds((here ^ d) * blocks, blocks)] = pieces[d][...]


def second_grad_body(batch, seq, *refs):
    count = len(refs) - batch - 3 if len(refs) > batch + 4 else 1
    if count == 1:
        pieces, dz_ref = refs[:1], refs[1]
        outs, reg_ref, y_scr = refs[2 : 2 + batch], refs[0], refs[-1]
    else:
        pieces, dz_ref = refs[:seq], refs[seq]
        outs, reg_ref, y_scr = refs[seq + 1 : seq + 1 + batch], refs[-2], refs[-1]
    me = lax.axis_index("batch")
    order, j_here, width = reg_ref.shape
    groups, lanes, m_here = j_here // LANE_GROUP, order * LANE_GROUP, order // batch
    if count > 1:
        gather_blocks(seq, pieces, reg_ref)

    @pl.loop(0, groups)
    def _(g):
        js = pl.ds(pl.multiple_of(g * LANE_GROUP, LANE_GROUP), LANE_GROUP)
        reg = reg_ref[:, js, :].reshape(lanes, width)
        dz = dz_ref[pl.ds(pl.multiple_of(g * lanes, lanes), lanes), :]
        wide = dot(dz, reg, 1, 1)
        col = iota((order, lanes), 1) % LANE_GROUP
        packed = wide[:order]
        for jj in range(1, LANE_GROUP):
            packed = jnp.where(col == jj, wide[jj * order : (jj + 1) * order], packed)
        y_scr[g] = packed

    for d in range(batch):
        first = pl.multiple_of((me ^ d) * m_here, m_here)
        rows = [y_scr[g, pl.ds(first, m_here), :] for g in range(groups)]
        outs[d][...] = jnp.concatenate(rows, axis=0).astype(BF16)


def tokens_body(reg_ref, second_ref, h_ref, src_ref, back_ref, out_hbm, out_ref, sems):
    order, j_here, width = reg_ref.shape
    groups, lanes = j_here // LANE_GROUP, order * LANE_GROUP
    select = one_hot(iota((width, width), 0) == src_ref[...])
    col = iota((order, lanes), 1) % LANE_GROUP
    writes = []
    for g in range(groups):
        reg = reg_ref[:, g * LANE_GROUP : (g + 1) * LANE_GROUP, :].reshape(lanes, width)
        packed = second_ref[g].astype(F32)
        weights = jnp.concatenate(
            [jnp.where(col == jj, packed, 0.0).astype(BF16) for jj in range(LANE_GROUP)], axis=0
        )
        rows = slice(g * lanes, (g + 1) * lanes)
        dgate = (dot(weights, reg) * h_ref[rows, :].astype(F32)).astype(BF16)
        out_ref[rows, :] = (back_ref[rows, :].astype(F32) + dot(dgate, select, 1, 1)).astype(BF16)
        writes.append(pltpu.make_async_copy(out_ref.at[rows, :], out_hbm.at[rows, :], sems.at[g]))
        writes[g].start()
    for write in writes:
        write.wait()


def pair_body(own_a, own_b, got_a, got_b, out_a, out_b):
    out_a[...] = own_a[...].astype(F32) + got_a[...].astype(F32)
    out_b[...] = (own_b[...].astype(F32) + got_b[...].astype(F32)).astype(BF16)


def sum_body(own, *refs):
    total = own[...].astype(F32)
    for got in refs[:-1]:
        total = total + got[...].astype(F32)
    refs[-1][...] = total.astype(BF16)


def add_body(own, got, out):
    out[...] = (own[...] + got[...].astype(F32)).astype(BF16)


def unpack_body(order, *refs):
    pieces, out_ref = refs[:-1], refs[-1]
    rows, j_here = out_ref.shape
    groups, lanes, m_here = j_here // LANE_GROUP, order * LANE_GROUP, rows // order
    total = pieces[0][...].astype(F32)
    for piece in pieces[1:]:
        total = total + piece[...].astype(F32)
    lane = iota((j_here, lanes), 1)
    keep = (iota((rows, lanes), 0) % order) == (iota((rows, lanes), 1) // LANE_GROUP)
    result = jnp.zeros((rows, j_here), F32)
    for g in range(groups):
        place = one_hot(iota((j_here, lanes), 0) == g * LANE_GROUP + lane % LANE_GROUP)
        packed = total[g * m_here : (g + 1) * m_here]
        wide = jnp.broadcast_to(packed[:, None, :], (m_here, order, lanes)).reshape(rows, lanes)
        result = result + dot(jnp.where(keep, wide, 0.0).astype(BF16), place, 1, 1)
    out_ref[...] = result.astype(BF16)


def packed_shards(tokens, cotangent, first_factor, second_factor, gate_source, alternate, batch, seq):
    x, cot = tokens[0], cotangent[0]
    rows_here, width = x.shape
    blocks, k_here, order = first_factor.shape
    j_here, m_here, count = second_factor.shape
    groups, lanes = j_here // LANE_GROUP, count * LANE_GROUP
    src = gate_source.reshape(1, width)
    alt = alternate.reshape(1, order)

    flat = jnp.transpose(second_factor, (1, 2, 0)).reshape(m_here * count, j_here)
    vals = {}

    def dep(name, value):
        earlier = [vals[n] for n in CFG['deps'].get(name, ()) if n in vals]
        return after(value, *earlier) if earlier else value

    def keep(name, value):
        vals[name] = value
        return value

    def move(name, value, axis, step, size):
        return keep(name, swap(dep(name, value), axis, step, size))

    (mine,) = call(functools.partial(pack_body, count), [of((groups * m_here, lanes))], [flat])
    packed = {0: mine}
    for d in (3, 2, 1):
        packed[d] = move(f"D{d}", mine, "batch", d, batch)
    (dz,) = call(gate_body, [of((rows_here, width))], [x, cot, src], limit=16 << 20)
    keep("gate", dz)
    piece = of((blocks, j_here, width))
    *back, second = call(
        functools.partial(regroup_back_body, batch, seq, count),
        ([of((count, j_here, width))] if CFG['a2a'][0] else [piece] * seq) + [of((groups, count, lanes))],
        [*[packed[d] for d in range(batch)], dz],
        [
            pltpu.VMEM((groups, count, lanes), F32),
            pltpu.VMEM((count, j_here, width), BF16),
            pltpu.SemaphoreType.DMA((groups,)),
        ],
        far_outs=(0,) if CFG['a2a'][0] else (),
        limit=24 << 20,
    )
    keep("A2", back[0])
    first_ready = after(first_factor, dz) if CFG['f2early'] else after(first_factor, dz, *[packed[d] for d in (1, 2, 3)])
    across = move("f2", first_ready, "batch", 2, batch)
    beside = move("f1", first_ready, "batch", 1, batch)
    direct = move("f3", first_ready, "batch", 3, batch) if CFG['direct'] else None
    back_got = {0: back[0]}
    if CFG['a2a'][0]:
        back_got[0] = keep("h0", lax.all_to_all(
            dep("h0", back[0]).reshape(seq, blocks, j_here, width), "seq", 0, 0, tiled=True
        ))
    else:
        for d in CFG['order'][0]:
            back_got[d] = move(f"h{d}", back[d], "seq", d, seq)
    if direct is None:
        direct = move("fx", across, "batch", 1, batch)
    first = [first_factor, beside, across, direct]
    *regrouped, h = call(
        functools.partial(mix_body, batch, seq),
        ([of((seq, blocks, j_here, width))] if CFG['a2a'][1] else [piece] * seq) + [of((rows_here, width))],
        [dep("M", first_factor), *first[1:], x, alt, cot, src],
        [
            pltpu.VMEM((order, order), BF16),
            pltpu.VMEM((order, width), BF16),
            pltpu.VMEM((blocks, seq, j_here, width), BF16),
            pltpu.SemaphoreType.DMA((blocks,)),
        ],
        far_outs=(0,) if CFG['a2a'][1] else (),
        limit=CFG['limit'],
    )
    keep("M", regrouped[0])
    got = {0: regrouped[0]}
    if CFG['a2a'][1]:
        got[0] = keep("H0", lax.all_to_all(dep("H0", regrouped[0]), "seq", 0, 0, tiled=True))
    else:
        for d in CFG['order'][1]:
            got[d] = move(f"H{d}", regrouped[d], "seq", d, seq)
    *parts, dmixed = call(
        functools.partial(first_grad_body, batch, seq),
        [of((blocks, k_here, order))] * batch + [of((blocks, order, width))],
        [dep("F1", back_got[0]), *[back_got[d] for d in range(1, seq) if d in back_got], x, alt],
        [pltpu.VMEM((order, order), BF16), pltpu.VMEM((order, width), BF16), pltpu.VMEM((order, order), BF16)],
        limit=40 << 20,
    )
    keep("F1", dmixed)
    if CFG['rsdirect']:
        others = [move(f"rs{d}", parts[d], "batch", d, batch) for d in (3, 2, 1)]
    else:
        near = move("near", parts[1], "batch", 1, batch)
        far = move("far", parts[3], "batch", 1, batch)
    if CFG['rsdirect']:
        (grad_one,) = call(sum_body, [of(parts[0].shape)], [dep("sum", parts[0]), *others])
    else:
        kept, summed = call(
            pair_body, [of(parts[0].shape, F32), of(parts[0].shape)], [dep("pair", parts[0]), parts[2], near, far], limit=40 << 20
        )
        keep("pair", summed)
        rx = move("rx", summed, "batch", 2, batch)
        (grad_one,) = call(add_body, [of(parts[0].shape)], [kept, rx])
    (dmix_in,) = call(
        functools.partial(mix_back_body, batch),
        [of((rows_here, width))],
        [*first, dep("F2", dmixed)],
        limit=CFG['limit'],
    )
    keep("F2", dmix_in)
    keep("add", grad_one)
    received = [dep("Z1", after(got[0], dmix_in)), *[got[d] for d in range(1, seq) if d in got]]
    if len(received) == 1:
        received = [received[0].reshape(count, j_here, width)]
    *terms, gathered = call(
        functools.partial(second_grad_body, batch, seq),
        [of((groups * m_here, lanes))] * batch + ([of((count, j_here, width))] if len(received) > 1 else []),
        [*received, dz],
        [pltpu.VMEM((groups, count, lanes), F32)],
    )
    if len(received) == 1:
        terms, gathered = [*terms, gathered], received[0]
    terms_got = [dep("unpack", terms[0])] + [move(f"R{d}", terms[d], "batch", d, batch) for d in (1, 2, 3)]
    (grad_tokens,) = call(
        tokens_body,
        [of((rows_here, width))],
        [gathered, second, h, src, dmix_in],
        [pltpu.VMEM((rows_here, width), BF16), pltpu.SemaphoreType.DMA((groups,))],
        far_outs=(0,),
    )
    (grad_flat,) = call(
        functools.partial(unpack_body, count), [of((m_here * count, j_here))], terms_got
    )
    grad_two = jnp.transpose(grad_flat.reshape(m_here, count, j_here), (2, 0, 1))
    return (grad_tokens[None], grad_one, grad_two)


def wide_shards(tokens, cotangent, first_factor, second_factor, gate_source, alternate):
    inputs = tokens[0]
    rows_here = inputs.shape[0]
    width = inputs.shape[1]
    order_len = alternate.shape[0]
    blocks_here = rows_here // order_len
    select = one_hot(lax.broadcasted_iota(jnp.int32, (width, width), 0) == gate_source[None, :])
    gate = jax.nn.sigmoid(jnp.dot(inputs, select, preferred_element_type=F32))
    first_full = lax.all_gather(first_factor, "batch", axis=1, tiled=True)
    second_full = lax.all_gather(second_factor, "batch", axis=1, tiled=True)
    blocked = inputs.reshape(blocks_here, order_len, width)
    mixed = jnp.einsum("ikj,ijc->ikc", first_full, blocked, preferred_element_type=F32).astype(BF16)
    shuffled = jnp.take(mixed, alternate, axis=1)
    piece = lax.all_to_all(shuffled, "seq", split_axis=1, concat_axis=0, tiled=True)
    z_blocks = jnp.einsum("jmi,ijc->jmc", second_full, piece, preferred_element_type=F32)
    j_here, count_second = z_blocks.shape[:2]
    z_out = z_blocks.reshape(rows_here, width)
    cot = cotangent[0].astype(F32)
    dz_out = (cot * gate).astype(BF16)
    dgate = cot * z_out * gate * (1.0 - gate)
    dz_blocks = dz_out.reshape(j_here, count_second, width)
    term_second = jnp.einsum("jmc,ijc->jmi", dz_blocks, piece, preferred_element_type=F32)
    grad_two = lax.psum_scatter(term_second.astype(BF16), "batch", scatter_dimension=1, tiled=True)
    dregrouped = jnp.einsum("jmi,jmc->ijc", second_full, dz_blocks, preferred_element_type=F32).astype(BF16)
    positions = lax.iota(jnp.int32, order_len)
    inverse = jnp.zeros((order_len,), jnp.int32).at[alternate].set(positions)
    restored = jnp.take(
        lax.all_to_all(dregrouped, "seq", split_axis=0, concat_axis=1, tiled=True), inverse, axis=1
    )
    dmix_in = jnp.einsum("ikj,ikc->ijc", first_full, restored, preferred_element_type=F32)
    term_first = jnp.einsum("ikc,ijc->ikj", restored, blocked, preferred_element_type=F32)
    grad_one = lax.psum_scatter(term_first.astype(BF16), "batch", scatter_dimension=1, tiled=True)
    spread = jnp.dot(dgate, select.T.astype(F32), precision=lax.Precision.HIGHEST)
    grad_tokens = (dmix_in.reshape(rows_here, width) + spread).astype(BF16)
    return (grad_tokens[None], grad_one, grad_two)


def solution(mesh):
    batch, seq = mesh.shape["batch"], mesh.shape["seq"]

    def shards(*args):
        j_here, m_here, count = args[3].shape
        if batch == 4 and seq & (seq - 1) == 0 and j_here % LANE_GROUP == 0 and m_here % 8 == 0 and count <= 32:
            return packed_shards(*args, batch, seq)
        return wide_shards(*args)

    in_specs = (
        P("batch", "seq", None),
        P("batch", "seq", None),
        P("seq", "batch", None),
        P("seq", "batch", None),
        P(),
        P(),
    )
    out_specs = (P("batch", "seq", None), P("seq", "batch", None), P("seq", "batch", None))
    return jax.shard_map(shards, mesh=mesh, in_specs=in_specs, out_specs=out_specs, check_vma=False)
```

```python
import functools

import jax
import jax.numpy as jnp
from jax import lax
from jax.experimental import pallas as pl
from jax.experimental.pallas import tpu as pltpu
from jax.sharding import PartitionSpec as P

BF16 = jnp.bfloat16
F32 = jnp.float32
LANE_GROUP = 16
CFG = {'a2a': [True, True], 'limit': 62914560, 'cost': {}, 'direct': False, 'rsdirect': False, 'f2early': False, 'order': [[7, 6, 5, 4, 3, 2, 1], [7, 6, 5, 4, 3, 2, 1]], 'deps': {'fx': ['A2'], 'F1': ['M'], 'F2': ['pair'], 'Z1': ['add']}}


def iota(shape, dim):
    return lax.broadcasted_iota(jnp.int32, shape, dim)


def one_hot(mask):
    return jnp.where(mask, 1.0, 0.0).astype(BF16)


def dot(a, b, da=1, db=0):
    return lax.dot_general(a, b, (((da,), (db,)), ((), ())), preferred_element_type=F32)


def call(body, outs, ins, scratch=(), spaces={}, limit=40 << 20, weight=0, far_outs=()):
    name = getattr(body, "func", body).__name__
    weight = CFG['cost'].get(name, 0)
    return pl.pallas_call(
        body,
        name=name,
        out_shape=outs,
        in_specs=[pl.BlockSpec(memory_space=spaces.get(n, pltpu.VMEM)) for n in range(len(ins))],
        out_specs=[
            pl.BlockSpec(memory_space=pltpu.HBM if n in far_outs else pltpu.VMEM) for n in range(len(outs))
        ],
        scratch_shapes=list(scratch),
        compiler_params=pltpu.CompilerParams(vmem_limit_bytes=limit),
        cost_estimate=pl.CostEstimate(flops=0, bytes_accessed=weight, transcendentals=0),
    )(*ins)


def of(shape, dtype=BF16):
    return jax.ShapeDtypeStruct(shape, dtype)


def swap(value, axis, step, size):
    return lax.ppermute(value, axis, [(p, p ^ step) for p in range(size)])


def after(value, *earlier):
    return lax.optimization_barrier((value, *earlier))[0]


def pack_body(order, s_ref, out_ref):
    rows, j_here = s_ref.shape
    groups = j_here // LANE_GROUP
    lanes = order * LANE_GROUP
    m_here = rows // order
    s = s_ref[...]
    lane = iota((j_here, lanes), 1)
    keep = (iota((rows, lanes), 0) % order) == (iota((rows, lanes), 1) // LANE_GROUP)
    for g in range(groups):
        place = one_hot(iota((j_here, lanes), 0) == g * LANE_GROUP + lane % LANE_GROUP)
        wide = jnp.where(keep, dot(s, place), 0.0)
        packed = jnp.sum(wide.reshape(m_here, order, lanes), axis=1)
        out_ref[g * m_here : (g + 1) * m_here, :] = packed.astype(BF16)


def gate_body(x_ref, cot_ref, src_ref, dz_ref):
    rows, width = x_ref.shape
    step = min(rows, 512)
    select = one_hot(iota((width, width), 0) == src_ref[...])
    for n in range(rows // step):
        part = slice(n * step, (n + 1) * step)
        gate = jax.nn.sigmoid(dot(x_ref[part, :], select))
        dz_ref[part, :] = (cot_ref[part, :].astype(F32) * gate).astype(BF16)


def regroup_back_body(batch, seq, order, *refs):
    pieces, dz_ref = refs[:batch], refs[batch]
    outs, second_ref, d_scr, r_scr, sems = refs[batch + 1 : -4], *refs[-4:]
    me, here = lax.axis_index("batch"), lax.axis_index("seq")
    groups = second_ref.shape[0]
    lanes = order * LANE_GROUP
    m_here = order // batch
    for d in range(batch):
        piece = pieces[d][...].astype(F32)
        first = pl.multiple_of((me ^ d) * m_here, m_here)
        for g in range(groups):
            d_scr[g, pl.ds(first, m_here), :] = piece[g * m_here : (g + 1) * m_here]
    width = dz_ref.shape[1]
    tiled = one_hot((iota((order, lanes), 1) % order) == iota((order, lanes), 0))
    keep = (iota((lanes, lanes), 0) % LANE_GROUP) == (iota((lanes, lanes), 1) // order)
    writes = []
    for g in range(groups):
        packed = d_scr[g].astype(BF16)
        second_ref[g] = packed
        weights = jnp.where(keep, dot(packed, tiled, 0, 0), 0.0).astype(BF16)
        result = dot(weights, dz_ref[g * lanes : (g + 1) * lanes, :]).astype(BF16)
        js = slice(g * LANE_GROUP, (g + 1) * LANE_GROUP)
        r_scr[:, js, :] = result.reshape(order, LANE_GROUP, width)
        if len(outs) == 1:
            writes.append(pltpu.make_async_copy(r_scr.at[:, js, :], outs[0].at[:, js, :], sems.at[g]))
            writes[g].start()

    blocks = order // seq
    if len(outs) == 1:
        for write in writes:
            write.wait()
    else:
        for d in range(seq):
            outs[d][...] = r_scr[pl.ds((here ^ d) * blocks, blocks)]


def mix_body(batch, seq, *refs):
    pieces, x_ref, alt_ref, cot_ref, src_ref = refs[:batch], *refs[batch : batch + 4]
    outs, h_ref, p_scr, mix_scr, reg_scr, sems = refs[batch + 4 : -5], *refs[-5:]
    me, here = lax.axis_index("batch"), lax.axis_index("seq")
    blocks, rows, order = pieces[0].shape
    j_here = order // seq
    width = x_ref.shape[1]
    from_rows = jnp.where(iota((order, order), 0) == alt_ref[...], 1.0, 0.0)
    p_scr[...] = from_rows.T.astype(BF16)
    select = one_hot(iota((width, width), 0) == src_ref[...])

    writes = []
    for i in range(blocks):
        x = x_ref[i * order : (i + 1) * order, :]
        for d in range(batch):
            first = pl.multiple_of((me ^ d) * rows, rows)
            mix_scr[pl.ds(first, rows), :] = dot(pieces[d][i], x).astype(BF16)
        result = dot(p_scr[...], mix_scr[...]).astype(BF16)
        if len(outs) == 1:
            reg_scr[i] = result.reshape(seq, j_here, width)
            writes.append(pltpu.make_async_copy(reg_scr.at[i], outs[0].at[:, i], sems.at[i]))
            writes[i].start()
        else:
            reg_scr[i] = result.reshape(seq, j_here, width)
            for d in range(seq):
                outs[d][i] = reg_scr[i, here ^ d]
        gate = jax.nn.sigmoid(dot(x, select))
        cot = cot_ref[i * order : (i + 1) * order, :].astype(F32)
        h_ref[i * order : (i + 1) * order, :] = (cot * gate * (1.0 - gate)).astype(BF16)
    for write in writes:
        write.wait()


def first_grad_body(batch, seq, *refs):
    count = len(refs) - batch - 6
    pieces, x_ref, alt_ref = refs[:count], refs[count], refs[count + 1]
    outs, dmixed_ref = refs[count + 2 : count + 2 + batch], refs[count + 2 + batch]
    p_scr, reg_scr, part_scr = refs[-3:]
    me, here = lax.axis_index("batch"), lax.axis_index("seq")
    blocks, j_here, width = pieces[0].shape[-3:]
    order = j_here * seq
    rows = order // batch
    p_scr[...] = one_hot(iota((order, order), 0) == alt_ref[...])

    @pl.loop(0, blocks)
    def _(i):
        if count == 1:
            reg_scr[...] = pieces[0][:, i].reshape(order, width)
        else:
            for d in range(seq):
                first = pl.multiple_of((here ^ d) * j_here, j_here)
                reg_scr[pl.ds(first, j_here), :] = pieces[d][i]
        dmixed = dot(p_scr[...], reg_scr[...]).astype(BF16)
        dmixed_ref[i] = dmixed
        x = x_ref[pl.ds(pl.multiple_of(i * order, order), order), :]
        part_scr[...] = dot(dmixed, x, 1, 1).astype(BF16)
        for d in range(batch):
            first = pl.multiple_of((me ^ d) * rows, rows)
            outs[d][i] = part_scr[pl.ds(first, rows), :]


def mix_back_body(batch, *refs):
    pieces, dmixed_ref, out_ref = refs[:batch], *refs[batch:]
    me = lax.axis_index("batch")
    blocks, rows, order = pieces[0].shape

    @pl.loop(0, blocks)
    def _(i):
        total = None
        for d in range(batch):
            first = pl.multiple_of((me ^ d) * rows, rows)
            term = dot(pieces[d][i], dmixed_ref[i, pl.ds(first, rows), :], 0, 0)
            total = term if total is None else total + term
        out_ref[pl.ds(pl.multiple_of(i * order, order), order), :] = total.astype(BF16)


def gather_blocks(seq, pieces, scr):
    here = lax.axis_index("seq")
    blocks = pieces[0].shape[0]
    for d in range(seq):
        scr[pl.ds((here ^ d) * blocks, blocks)] = pieces[d][...]


def second_grad_body(batch, seq, *refs):
    count = len(refs) - batch - 3 if len(refs) > batch + 4 else 1
    if count == 1:
        pieces, dz_ref = refs[:1], refs[1]
        outs, reg_ref, y_scr = refs[2 : 2 + batch], refs[0], refs[-1]
    else:
        pieces, dz_ref = refs[:seq], refs[seq]
        outs, reg_ref, y_scr = refs[seq + 1 : seq + 1 + batch], refs[-2], refs[-1]
    me = lax.axis_index("batch")
    order, j_here, width = reg_ref.shape
    groups, lanes, m_here = j_here // LANE_GROUP, order * LANE_GROUP, order // batch
    if count > 1:
        gather_blocks(seq, pieces, reg_ref)

    @pl.loop(0, groups)
    def _(g):
        js = pl.ds(pl.multiple_of(g * LANE_GROUP, LANE_GROUP), LANE_GROUP)
        reg = reg_ref[:, js, :].reshape(lanes, width)
        dz = dz_ref[pl.ds(pl.multiple_of(g * lanes, lanes), lanes), :]
        wide = dot(dz, reg, 1, 1)
        col = iota((order, lanes), 1) % LANE_GROUP
        packed = wide[:order]
        for jj in range(1, LANE_GROUP):
            packed = jnp.where(col == jj, wide[jj * order : (jj + 1) * order], packed)
        y_scr[g] = packed

    for d in range(batch):
        first = pl.multiple_of((me ^ d) * m_here, m_here)
        rows = [y_scr[g, pl.ds(first, m_here), :] for g in range(groups)]
        outs[d][...] = jnp.concatenate(rows, axis=0).astype(BF16)


def tokens_body(reg_ref, second_ref, h_ref, src_ref, back_ref, out_hbm, out_ref, sems):
    order, j_here, width = reg_ref.shape
    groups, lanes = j_here // LANE_GROUP, order * LANE_GROUP
    select = one_hot(iota((width, width), 0) == src_ref[...])
    col = iota((order, lanes), 1) % LANE_GROUP
    writes = []
    for g in range(groups):
        reg = reg_ref[:, g * LANE_GROUP : (g + 1) * LANE_GROUP, :].reshape(lanes, width)
        packed = second_ref[g].astype(F32)
        weights = jnp.concatenate(
            [jnp.where(col == jj, packed, 0.0).astype(BF16) for jj in range(LANE_GROUP)], axis=0
        )
        rows = slice(g * lanes, (g + 1) * lanes)
        dgate = (dot(weights, reg) * h_ref[rows, :].astype(F32)).astype(BF16)
        out_ref[rows, :] = (back_ref[rows, :].astype(F32) + dot(dgate, select, 1, 1)).astype(BF16)
        writes.append(pltpu.make_async_copy(out_ref.at[rows, :], out_hbm.at[rows, :], sems.at[g]))
        writes[g].start()
    for write in writes:
        write.wait()


def pair_body(own_a, own_b, got_a, got_b, out_a, *outs_b):
    out_a[...] = own_a[...].astype(F32) + got_a[...].astype(F32)
    for n, out_b in enumerate(outs_b):
        out_b[...] = (own_b[n].astype(F32) + got_b[n].astype(F32)).astype(BF16)


def sum_body(own, *refs):
    total = own[...].astype(F32)
    for got in refs[:-1]:
        total = total + got[...].astype(F32)
    refs[-1][...] = total.astype(BF16)


def add_body(own, *refs):
    for n, got in enumerate(refs[:-1]):
        refs[-1][n] = (own[n] + got[...].astype(F32)).astype(BF16)


def unpack_body(order, *refs):
    pieces, out_ref = refs[:-1], refs[-1]
    rows, j_here = out_ref.shape
    groups, lanes, m_here = j_here // LANE_GROUP, order * LANE_GROUP, rows // order
    total = pieces[0][...].astype(F32)
    for piece in pieces[1:]:
        total = total + piece[...].astype(F32)
    lane = iota((j_here, lanes), 1)
    keep = (iota((rows, lanes), 0) % order) == (iota((rows, lanes), 1) // LANE_GROUP)
    result = jnp.zeros((rows, j_here), F32)
    for g in range(groups):
        place = one_hot(iota((j_here, lanes), 0) == g * LANE_GROUP + lane % LANE_GROUP)
        packed = total[g * m_here : (g + 1) * m_here]
        wide = jnp.broadcast_to(packed[:, None, :], (m_here, order, lanes)).reshape(rows, lanes)
        result = result + dot(jnp.where(keep, wide, 0.0).astype(BF16), place, 1, 1)
    out_ref[...] = result.astype(BF16)


def packed_shards(tokens, cotangent, first_factor, second_factor, gate_source, alternate, batch, seq):
    x, cot = tokens[0], cotangent[0]
    rows_here, width = x.shape
    blocks, k_here, order = first_factor.shape
    j_here, m_here, count = second_factor.shape
    groups, lanes = j_here // LANE_GROUP, count * LANE_GROUP
    src = gate_source.reshape(1, width)
    alt = alternate.reshape(1, order)

    flat = jnp.transpose(second_factor, (1, 2, 0)).reshape(m_here * count, j_here)
    vals = {}

    def dep(name, value):
        earlier = [vals[n] for n in CFG['deps'].get(name, ()) if n in vals]
        return after(value, *earlier) if earlier else value

    def keep(name, value):
        vals[name] = value
        return value

    def move(name, value, axis, step, size):
        return keep(name, swap(dep(name, value), axis, step, size))

    (mine,) = call(functools.partial(pack_body, count), [of((groups * m_here, lanes))], [flat])
    packed = {0: mine}
    for d in (3, 2, 1):
        packed[d] = move(f"D{d}", mine, "batch", d, batch)
    (dz,) = call(gate_body, [of((rows_here, width))], [x, cot, src], limit=16 << 20)
    keep("gate", dz)
    piece = of((blocks, j_here, width))
    *back, second = call(
        functools.partial(regroup_back_body, batch, seq, count),
        ([of((count, j_here, width))] if CFG['a2a'][0] else [piece] * seq) + [of((groups, count, lanes))],
        [*[packed[d] for d in range(batch)], dz],
        [
            pltpu.VMEM((groups, count, lanes), F32),
            pltpu.VMEM((count, j_here, width), BF16),
            pltpu.SemaphoreType.DMA((groups,)),
        ],
        far_outs=(0,) if CFG['a2a'][0] else (),
        limit=24 << 20,
    )
    keep("A2", back[0])
    first_ready = after(first_factor, dz) if CFG['f2early'] else after(first_factor, dz, *[packed[d] for d in (1, 2, 3)])
    across = move("f2", first_ready, "batch", 2, batch)
    beside = move("f1", first_ready, "batch", 1, batch)
    direct = move("f3", first_ready, "batch", 3, batch) if CFG['direct'] else None
    back_got = {0: back[0]}
    if CFG['a2a'][0]:
        back_got[0] = keep("h0", lax.all_to_all(
            dep("h0", back[0]).reshape(seq, blocks, j_here, width), "seq", 0, 0, tiled=True
        ))
    else:
        for d in CFG['order'][0]:
            back_got[d] = move(f"h{d}", back[d], "seq", d, seq)
    if direct is None:
        direct = move("fx", across, "batch", 1, batch)
    first = [first_factor, beside, across, direct]
    *regrouped, h = call(
        functools.partial(mix_body, batch, seq),
        ([of((seq, blocks, j_here, width))] if CFG['a2a'][1] else [piece] * seq) + [of((rows_here, width))],
        [dep("M", first_factor), *first[1:], x, alt, cot, src],
        [
            pltpu.VMEM((order, order), BF16),
            pltpu.VMEM((order, width), BF16),
            pltpu.VMEM((blocks, seq, j_here, width), BF16),
            pltpu.SemaphoreType.DMA((blocks,)),
        ],
        far_outs=(0,) if CFG['a2a'][1] else (),
        limit=CFG['limit'],
    )
    keep("M", regrouped[0])
    got = {0: regrouped[0]}
    if CFG['a2a'][1]:
        got[0] = keep("H0", lax.all_to_all(dep("H0", regrouped[0]), "seq", 0, 0, tiled=True))
    else:
        for d in CFG['order'][1]:
            got[d] = move(f"H{d}", regrouped[d], "seq", d, seq)
    *parts, dmixed = call(
        functools.partial(first_grad_body, batch, seq),
        [of((blocks, k_here, order))] * batch + [of((blocks, order, width))],
        [dep("F1", back_got[0]), *[back_got[d] for d in range(1, seq) if d in back_got], x, alt],
        [pltpu.VMEM((order, order), BF16), pltpu.VMEM((order, width), BF16), pltpu.VMEM((order, order), BF16)],
        limit=40 << 20,
    )
    keep("F1", dmixed)
    if CFG['rsdirect']:
        others = [move(f"rs{d}", parts[d], "batch", d, batch) for d in (3, 2, 1)]
    else:
        near = move("near", parts[1], "batch", 1, batch)
        far = move("far", parts[3], "batch", 1, batch)
    if CFG['rsdirect']:
        (grad_one,) = call(sum_body, [of(parts[0].shape)], [dep("sum", parts[0]), *others])
    else:
        kept, *summed = call(
            pair_body,
            [of(parts[0].shape, F32)] + [of((k_here, order))] * blocks,
            [dep("pair", parts[0]), parts[2], near, far],
            limit=40 << 20,
        )
        keep("pair", summed[0])
        across_sums = [move(f"rx{n}", summed[n], "batch", 2, batch) for n in range(blocks)]
        (grad_one,) = call(add_body, [of(parts[0].shape)], [kept, *across_sums])
    (dmix_in,) = call(
        functools.partial(mix_back_body, batch),
        [of((rows_here, width))],
        [*first, dep("F2", dmixed)],
        limit=CFG['limit'],
    )
    keep("F2", dmix_in)
    keep("add", grad_one)
    received = [dep("Z1", after(got[0], dmix_in)), *[got[d] for d in range(1, seq) if d in got]]
    if len(received) == 1:
        received = [received[0].reshape(count, j_here, width)]
    *terms, gathered = call(
        functools.partial(second_grad_body, batch, seq),
        [of((groups * m_here, lanes))] * batch + ([of((count, j_here, width))] if len(received) > 1 else []),
        [*received, dz],
        [pltpu.VMEM((groups, count, lanes), F32)],
    )
    if len(received) == 1:
        terms, gathered = [*terms, gathered], received[0]
    terms_got = [dep("unpack", terms[0])] + [move(f"R{d}", terms[d], "batch", d, batch) for d in (1, 2, 3)]
    (grad_tokens,) = call(
        tokens_body,
        [of((rows_here, width))],
        [gathered, second, h, src, dmix_in],
        [pltpu.VMEM((rows_here, width), BF16), pltpu.SemaphoreType.DMA((groups,))],
        far_outs=(0,),
    )
    (grad_flat,) = call(
        functools.partial(unpack_body, count), [of((m_here * count, j_here))], terms_got
    )
    grad_two = jnp.transpose(grad_flat.reshape(m_here, count, j_here), (2, 0, 1))
    return (grad_tokens[None], grad_one, grad_two)


def wide_shards(tokens, cotangent, first_factor, second_factor, gate_source, alternate):
    inputs = tokens[0]
    rows_here = inputs.shape[0]
    width = inputs.shape[1]
    order_len = alternate.shape[0]
    blocks_here = rows_here // order_len
    select = one_hot(lax.broadcasted_iota(jnp.int32, (width, width), 0) == gate_source[None, :])
    gate = jax.nn.sigmoid(jnp.dot(inputs, select, preferred_element_type=F32))
    first_full = lax.all_gather(first_factor, "batch", axis=1, tiled=True)
    second_full = lax.all_gather(second_factor, "batch", axis=1, tiled=True)
    blocked = inputs.reshape(blocks_here, order_len, width)
    mixed = jnp.einsum("ikj,ijc->ikc", first_full, blocked, preferred_element_type=F32).astype(BF16)
    shuffled = jnp.take(mixed, alternate, axis=1)
    piece = lax.all_to_all(shuffled, "seq", split_axis=1, concat_axis=0, tiled=True)
    z_blocks = jnp.einsum("jmi,ijc->jmc", second_full, piece, preferred_element_type=F32)
    j_here, count_second = z_blocks.shape[:2]
    z_out = z_blocks.reshape(rows_here, width)
    cot = cotangent[0].astype(F32)
    dz_out = (cot * gate).astype(BF16)
    dgate = cot * z_out * gate * (1.0 - gate)
    dz_blocks = dz_out.reshape(j_here, count_second, width)
    term_second = jnp.einsum("jmc,ijc->jmi", dz_blocks, piece, preferred_element_type=F32)
    grad_two = lax.psum_scatter(term_second.astype(BF16), "batch", scatter_dimension=1, tiled=True)
    dregrouped = jnp.einsum("jmi,jmc->ijc", second_full, dz_blocks, preferred_element_type=F32).astype(BF16)
    positions = lax.iota(jnp.int32, order_len)
    inverse = jnp.zeros((order_len,), jnp.int32).at[alternate].set(positions)
    restored = jnp.take(
        lax.all_to_all(dregrouped, "seq", split_axis=0, concat_axis=1, tiled=True), inverse, axis=1
    )
    dmix_in = jnp.einsum("ikj,ikc->ijc", first_full, restored, preferred_element_type=F32)
    term_first = jnp.einsum("ikc,ijc->ikj", restored, blocked, preferred_element_type=F32)
    grad_one = lax.psum_scatter(term_first.astype(BF16), "batch", scatter_dimension=1, tiled=True)
    spread = jnp.dot(dgate, select.T.astype(F32), precision=lax.Precision.HIGHEST)
    grad_tokens = (dmix_in.reshape(rows_here, width) + spread).astype(BF16)
    return (grad_tokens[None], grad_one, grad_two)


def solution(mesh):
    batch, seq = mesh.shape["batch"], mesh.shape["seq"]

    def shards(*args):
        j_here, m_here, count = args[3].shape
        if batch == 4 and seq & (seq - 1) == 0 and j_here % LANE_GROUP == 0 and m_here % 8 == 0 and count <= 32:
            return packed_shards(*args, batch, seq)
        return wide_shards(*args)

    in_specs = (
        P("batch", "seq", None),
        P("batch", "seq", None),
        P("seq", "batch", None),
        P("seq", "batch", None),
        P(),
        P(),
    )
    out_specs = (P("batch", "seq", None), P("seq", "batch", None), P("seq", "batch", None))
    return jax.shard_map(shards, mesh=mesh, in_specs=in_specs, out_specs=out_specs, check_vma=False)
```

```python
import functools

import jax
import jax.numpy as jnp
from jax import lax
from jax.experimental import pallas as pl
from jax.experimental.pallas import tpu as pltpu
from jax.sharding import PartitionSpec as P

BF16 = jnp.bfloat16
F32 = jnp.float32
LANE_GROUP = 16
CFG = {'a2a': [True, True], 'limit': 62914560, 'cost': {}, 'direct': False, 'rsdirect': False, 'f2early': False, 'order': [[7, 6, 5, 4, 3, 2, 1], [7, 6, 5, 4, 3, 2, 1]], 'deps': {'fx': ['A2'], 'F1': ['M'], 'F2': ['pair'], 'Z1': ['add']}}


def iota(shape, dim):
    return lax.broadcasted_iota(jnp.int32, shape, dim)


def one_hot(mask):
    return jnp.where(mask, 1.0, 0.0).astype(BF16)


def dot(a, b, da=1, db=0):
    return lax.dot_general(a, b, (((da,), (db,)), ((), ())), preferred_element_type=F32)


def call(body, outs, ins, scratch=(), spaces={}, limit=40 << 20, weight=0, far_outs=()):
    name = getattr(body, "func", body).__name__
    weight = CFG['cost'].get(name, 0)
    return pl.pallas_call(
        body,
        name=name,
        out_shape=outs,
        in_specs=[pl.BlockSpec(memory_space=spaces.get(n, pltpu.VMEM)) for n in range(len(ins))],
        out_specs=[
            pl.BlockSpec(memory_space=pltpu.HBM if n in far_outs else pltpu.VMEM) for n in range(len(outs))
        ],
        scratch_shapes=list(scratch),
        compiler_params=pltpu.CompilerParams(vmem_limit_bytes=limit),
        cost_estimate=pl.CostEstimate(flops=0, bytes_accessed=weight, transcendentals=0),
    )(*ins)


def of(shape, dtype=BF16):
    return jax.ShapeDtypeStruct(shape, dtype)


def swap(value, axis, step, size):
    return lax.ppermute(value, axis, [(p, p ^ step) for p in range(size)])


def ring_at(place, size):
    return jnp.where(place < size // 2, 2 * place, 2 * size - 1 - 2 * place)


def ring_of(size):
    return [2 * p if p < size // 2 else 2 * size - 1 - 2 * p for p in range(size)]


def after(value, *earlier):
    return lax.optimization_barrier((value, *earlier))[0]


def pack_body(order, s_ref, out_ref):
    rows, j_here = s_ref.shape
    groups = j_here // LANE_GROUP
    lanes = order * LANE_GROUP
    m_here = rows // order
    s = s_ref[...]
    lane = iota((j_here, lanes), 1)
    keep = (iota((rows, lanes), 0) % order) == (iota((rows, lanes), 1) // LANE_GROUP)
    for g in range(groups):
        place = one_hot(iota((j_here, lanes), 0) == g * LANE_GROUP + lane % LANE_GROUP)
        wide = jnp.where(keep, dot(s, place), 0.0)
        packed = jnp.sum(wide.reshape(m_here, order, lanes), axis=1)
        out_ref[g * m_here : (g + 1) * m_here, :] = packed.astype(BF16)


def gate_body(x_ref, cot_ref, src_ref, dz_ref):
    rows, width = x_ref.shape
    step = min(rows, 512)
    select = one_hot(iota((width, width), 0) == src_ref[...])
    for n in range(rows // step):
        part = slice(n * step, (n + 1) * step)
        gate = jax.nn.sigmoid(dot(x_ref[part, :], select))
        dz_ref[part, :] = (cot_ref[part, :].astype(F32) * gate).astype(BF16)


def regroup_back_body(batch, seq, order, *refs):
    pieces, dz_ref = refs[:batch], refs[batch]
    outs, second_ref, d_scr, r_scr, sems = refs[batch + 1 : -4], *refs[-4:]
    me, here = lax.axis_index("batch"), lax.axis_index("seq")
    groups = second_ref.shape[0]
    lanes = order * LANE_GROUP
    m_here = order // batch
    for d in range(batch):
        piece = pieces[d][...].astype(F32)
        first = pl.multiple_of((me ^ d) * m_here, m_here)
        for g in range(groups):
            d_scr[g, pl.ds(first, m_here), :] = piece[g * m_here : (g + 1) * m_here]
    width = dz_ref.shape[1]
    tiled = one_hot((iota((order, lanes), 1) % order) == iota((order, lanes), 0))
    keep = (iota((lanes, lanes), 0) % LANE_GROUP) == (iota((lanes, lanes), 1) // order)
    writes = []
    blocks = order // seq
    part = lanes // seq
    for g in range(groups):
        wide = d_scr[g]
        packed = wide.astype(BF16)
        ringed = [wide[:, there * part : (there + 1) * part] for there in ring_of(seq)]
        second_ref[g] = jnp.concatenate(ringed, axis=1).astype(BF16)
        weights = jnp.where(keep, dot(packed, tiled, 0, 0), 0.0).astype(BF16)
        result = dot(weights, dz_ref[g * lanes : (g + 1) * lanes, :]).astype(BF16)
        js = slice(g * LANE_GROUP, (g + 1) * LANE_GROUP)
        r_scr[:, js, :] = result.reshape(order, LANE_GROUP, width)
        if len(outs) == 1:
            for p, there in enumerate(ring_of(seq)):
                source, target = pl.ds(there * blocks, blocks), pl.ds(p * blocks, blocks)
                write = pltpu.make_async_copy(
                    r_scr.at[source, js, :], outs[0].at[target, js, :], sems.at[g, p]
                )
                write.start()
                writes.append(write)

    if len(outs) == 1:
        for write in writes:
            write.wait()
    else:
        for d in range(seq):
            outs[d][...] = r_scr[pl.ds((here ^ d) * blocks, blocks)]


def mix_body(batch, seq, *refs):
    pieces, x_ref, alt_ref, cot_ref, src_ref = refs[:batch], *refs[batch : batch + 4]
    outs, h_ref, p_scr, mix_scr, reg_scr, sems = refs[batch + 4 : -5], *refs[-5:]
    me, here = lax.axis_index("batch"), lax.axis_index("seq")
    blocks, rows, order = pieces[0].shape
    j_here = order // seq
    width = x_ref.shape[1]
    from_rows = jnp.where(iota((order, order), 0) == alt_ref[...], 1.0, 0.0)
    p_scr[...] = from_rows.T.astype(BF16)
    select = one_hot(iota((width, width), 0) == src_ref[...])

    writes = []
    for i in range(blocks):
        x = x_ref[i * order : (i + 1) * order, :]
        for d in range(batch):
            first = pl.multiple_of((me ^ d) * rows, rows)
            mix_scr[pl.ds(first, rows), :] = dot(pieces[d][i], x).astype(BF16)
        result = dot(p_scr[...], mix_scr[...]).astype(BF16)
        if len(outs) == 1:
            reg_scr[i] = result.reshape(seq, j_here, width)
            for p, there in enumerate(ring_of(seq)):
                write = pltpu.make_async_copy(reg_scr.at[i, there], outs[0].at[p, i], sems.at[i, p])
                write.start()
                writes.append(write)
        else:
            reg_scr[i] = result.reshape(seq, j_here, width)
            for d in range(seq):
                outs[d][i] = reg_scr[i, here ^ d]
        gate = jax.nn.sigmoid(dot(x, select))
        cot = cot_ref[i * order : (i + 1) * order, :].astype(F32)
        h_ref[i * order : (i + 1) * order, :] = (cot * gate * (1.0 - gate)).astype(BF16)
    for write in writes:
        write.wait()


def first_grad_body(batch, seq, *refs):
    count = len(refs) - batch - 6
    pieces, x_ref, alt_ref = refs[:count], refs[count], refs[count + 1]
    outs, dmixed_ref = refs[count + 2 : count + 2 + batch], refs[count + 2 + batch]
    p_scr, reg_scr, part_scr = refs[-3:]
    me, here = lax.axis_index("batch"), lax.axis_index("seq")
    blocks, j_here, width = pieces[0].shape[-3:]
    order = j_here * seq
    rows = order // batch
    p_scr[...] = one_hot(iota((order, order), 0) == alt_ref[...])

    @pl.loop(0, blocks)
    def _(i):
        if count == 1:
            for p, there in enumerate(ring_of(seq)):
                reg_scr[there * j_here : (there + 1) * j_here, :] = pieces[0][p, i]
        else:
            for d in range(seq):
                first = pl.multiple_of((here ^ d) * j_here, j_here)
                reg_scr[pl.ds(first, j_here), :] = pieces[d][i]
        dmixed = dot(p_scr[...], reg_scr[...]).astype(BF16)
        dmixed_ref[i] = dmixed
        x = x_ref[pl.ds(pl.multiple_of(i * order, order), order), :]
        part_scr[...] = dot(dmixed, x, 1, 1).astype(BF16)
        for d in range(batch):
            first = pl.multiple_of((me ^ d) * rows, rows)
            outs[d][i] = part_scr[pl.ds(first, rows), :]


def mix_back_body(batch, *refs):
    pieces, dmixed_ref, out_ref = refs[:batch], *refs[batch:]
    me = lax.axis_index("batch")
    blocks, rows, order = pieces[0].shape

    @pl.loop(0, blocks)
    def _(i):
        total = None
        for d in range(batch):
            first = pl.multiple_of((me ^ d) * rows, rows)
            term = dot(pieces[d][i], dmixed_ref[i, pl.ds(first, rows), :], 0, 0)
            total = term if total is None else total + term
        out_ref[pl.ds(pl.multiple_of(i * order, order), order), :] = total.astype(BF16)


def gather_blocks(seq, pieces, scr):
    here = lax.axis_index("seq")
    blocks = pieces[0].shape[0]
    for d in range(seq):
        scr[pl.ds((here ^ d) * blocks, blocks)] = pieces[d][...]


def second_grad_body(batch, seq, *refs):
    count = len(refs) - batch - 3 if len(refs) > batch + 4 else 1
    if count == 1:
        pieces, dz_ref = refs[:1], refs[1]
        outs, reg_ref, y_scr = refs[2 : 2 + batch], refs[0], refs[-1]
    else:
        pieces, dz_ref = refs[:seq], refs[seq]
        outs, reg_ref, y_scr = refs[seq + 1 : seq + 1 + batch], refs[-2], refs[-1]
    me = lax.axis_index("batch")
    order, j_here, width = reg_ref.shape
    groups, lanes, m_here = j_here // LANE_GROUP, order * LANE_GROUP, order // batch
    if count > 1:
        gather_blocks(seq, pieces, reg_ref)

    @pl.loop(0, groups)
    def _(g):
        js = pl.ds(pl.multiple_of(g * LANE_GROUP, LANE_GROUP), LANE_GROUP)
        reg = reg_ref[:, js, :].reshape(lanes, width)
        dz = dz_ref[pl.ds(pl.multiple_of(g * lanes, lanes), lanes), :]
        wide = dot(dz, reg, 1, 1)
        col = iota((order, lanes), 1) % LANE_GROUP
        packed = wide[:order]
        for jj in range(1, LANE_GROUP):
            packed = jnp.where(col == jj, wide[jj * order : (jj + 1) * order], packed)
        y_scr[g] = packed

    for d in range(batch):
        first = pl.multiple_of((me ^ d) * m_here, m_here)
        rows = [y_scr[g, pl.ds(first, m_here), :] for g in range(groups)]
        outs[d][...] = jnp.concatenate(rows, axis=0).astype(BF16)


def tokens_body(reg_ref, second_ref, h_ref, src_ref, back_ref, out_hbm, out_ref, sems):
    order, j_here, width = reg_ref.shape
    groups, lanes = j_here // LANE_GROUP, order * LANE_GROUP
    select = one_hot(iota((width, width), 0) == src_ref[...])
    col = iota((order, lanes), 1) % LANE_GROUP
    masks = [one_hot(col == jj) for jj in range(LANE_GROUP)]
    writes = []
    for g in range(groups):
        reg = reg_ref[:, g * LANE_GROUP : (g + 1) * LANE_GROUP, :].reshape(lanes, width)
        packed = second_ref[g]
        weights = jnp.concatenate([packed * mask for mask in masks], axis=0)
        rows = slice(g * lanes, (g + 1) * lanes)
        dgate = (dot(weights, reg) * h_ref[rows, :].astype(F32)).astype(BF16)
        out_ref[rows, :] = (back_ref[rows, :].astype(F32) + dot(dgate, select, 1, 1)).astype(BF16)
        writes.append(pltpu.make_async_copy(out_ref.at[rows, :], out_hbm.at[rows, :], sems.at[g]))
        writes[g].start()
    for write in writes:
        write.wait()


def pair_body(own_a, own_b, got_a, got_b, out_a, *outs_b):
    out_a[...] = own_a[...].astype(F32) + got_a[...].astype(F32)
    for n, out_b in enumerate(outs_b):
        out_b[...] = (own_b[n].astype(F32) + got_b[n].astype(F32)).astype(BF16)


def sum_body(own, *refs):
    total = own[...].astype(F32)
    for got in refs[:-1]:
        total = total + got[...].astype(F32)
    refs[-1][...] = total.astype(BF16)


def add_body(own, *refs):
    for n, got in enumerate(refs[:-1]):
        refs[-1][n] = (own[n] + got[...].astype(F32)).astype(BF16)


def unpack_body(order, seq, *refs):
    pieces, out_ref = refs[:-1], refs[-1]
    rows, j_here = out_ref.shape
    groups, lanes, m_here = j_here // LANE_GROUP, order * LANE_GROUP, rows // order
    total = pieces[0][...].astype(F32)
    for piece in pieces[1:]:
        total = total + piece[...].astype(F32)
    lane = iota((j_here, lanes), 1)
    blocks = order // seq
    place_i = iota((rows, lanes), 1) // LANE_GROUP
    keep = (iota((rows, lanes), 0) % order) == ring_at(place_i // blocks, seq) * blocks + place_i % blocks
    result = jnp.zeros((rows, j_here), F32)
    for g in range(groups):
        place = one_hot(iota((j_here, lanes), 0) == g * LANE_GROUP + lane % LANE_GROUP)
        packed = total[g * m_here : (g + 1) * m_here]
        wide = jnp.broadcast_to(packed[:, None, :], (m_here, order, lanes)).reshape(rows, lanes)
        result = result + dot(jnp.where(keep, wide, 0.0).astype(BF16), place, 1, 1)
    out_ref[...] = result.astype(BF16)


def packed_shards(tokens, cotangent, first_factor, second_factor, gate_source, alternate, batch, seq):
    x, cot = tokens[0], cotangent[0]
    rows_here, width = x.shape
    blocks, k_here, order = first_factor.shape
    j_here, m_here, count = second_factor.shape
    groups, lanes = j_here // LANE_GROUP, count * LANE_GROUP
    src = gate_source.reshape(1, width)
    alt = alternate.reshape(1, order)

    flat = jnp.transpose(second_factor, (1, 2, 0)).reshape(m_here * count, j_here)
    vals = {}

    def dep(name, value):
        earlier = [vals[n] for n in CFG['deps'].get(name, ()) if n in vals]
        return after(value, *earlier) if earlier else value

    def keep(name, value):
        vals[name] = value
        return value

    def move(name, value, axis, step, size):
        return keep(name, swap(dep(name, value), axis, step, size))

    (mine,) = call(functools.partial(pack_body, count), [of((groups * m_here, lanes))], [flat])
    packed = {0: mine}
    for d in (3, 2, 1):
        packed[d] = move(f"D{d}", mine, "batch", d, batch)
    (dz,) = call(gate_body, [of((rows_here, width))], [x, cot, src], limit=16 << 20)
    keep("gate", dz)
    piece = of((blocks, j_here, width))
    *back, second = call(
        functools.partial(regroup_back_body, batch, seq, count),
        ([of((count, j_here, width))] if CFG['a2a'][0] else [piece] * seq) + [of((groups, count, lanes))],
        [*[packed[d] for d in range(batch)], dz],
        [
            pltpu.VMEM((groups, count, lanes), F32),
            pltpu.VMEM((count, j_here, width), BF16),
            pltpu.SemaphoreType.DMA((groups, seq)),
        ],
        far_outs=(0,) if CFG['a2a'][0] else (),
        limit=24 << 20,
    )
    keep("A2", back[0])
    first_ready = after(first_factor, dz) if CFG['f2early'] else after(first_factor, dz, *[packed[d] for d in (1, 2, 3)])
    across = move("f2", first_ready, "batch", 2, batch)
    beside = move("f1", first_ready, "batch", 1, batch)
    direct = move("f3", first_ready, "batch", 3, batch) if CFG['direct'] else None
    back_got = {0: back[0]}
    if CFG['a2a'][0]:
        back_got[0] = keep("h0", lax.all_to_all(
            dep("h0", back[0]).reshape(seq, blocks, j_here, width), "seq", 0, 0, axis_index_groups=[ring_of(seq)], tiled=True
        ))
    else:
        for d in CFG['order'][0]:
            back_got[d] = move(f"h{d}", back[d], "seq", d, seq)
    if direct is None:
        direct = move("fx", across, "batch", 1, batch)
    first = [first_factor, beside, across, direct]
    *regrouped, h = call(
        functools.partial(mix_body, batch, seq),
        ([of((seq, blocks, j_here, width))] if CFG['a2a'][1] else [piece] * seq) + [of((rows_here, width))],
        [dep("M", first_factor), *first[1:], x, alt, cot, src],
        [
            pltpu.VMEM((order, order), BF16),
            pltpu.VMEM((order, width), BF16),
            pltpu.VMEM((blocks, seq, j_here, width), BF16),
            pltpu.SemaphoreType.DMA((blocks, seq)),
        ],
        far_outs=(0,) if CFG['a2a'][1] else (),
        limit=CFG['limit'],
    )
    keep("M", regrouped[0])
    got = {0: regrouped[0]}
    if CFG['a2a'][1]:
        got[0] = keep("H0", lax.all_to_all(
            dep("H0", regrouped[0]), "seq", 0, 0, axis_index_groups=[ring_of(seq)], tiled=True
        ))
    else:
        for d in CFG['order'][1]:
            got[d] = move(f"H{d}", regrouped[d], "seq", d, seq)
    *parts, dmixed = call(
        functools.partial(first_grad_body, batch, seq),
        [of((blocks, k_here, order))] * batch + [of((blocks, order, width))],
        [dep("F1", back_got[0]), *[back_got[d] for d in range(1, seq) if d in back_got], x, alt],
        [pltpu.VMEM((order, order), BF16), pltpu.VMEM((order, width), BF16), pltpu.VMEM((order, order), BF16)],
        limit=40 << 20,
    )
    keep("F1", dmixed)
    if CFG['rsdirect']:
        others = [move(f"rs{d}", parts[d], "batch", d, batch) for d in (3, 2, 1)]
    else:
        near = move("near", parts[1], "batch", 1, batch)
        far = move("far", parts[3], "batch", 1, batch)
    if CFG['rsdirect']:
        (grad_one,) = call(sum_body, [of(parts[0].shape)], [dep("sum", parts[0]), *others])
    else:
        kept, *summed = call(
            pair_body,
            [of(parts[0].shape, F32)] + [of((k_here, order))] * blocks,
            [dep("pair", parts[0]), parts[2], near, far],
            limit=40 << 20,
        )
        keep("pair", summed[0])
        across_sums = [move(f"rx{n}", summed[n], "batch", 2, batch) for n in range(blocks)]
        (grad_one,) = call(add_body, [of(parts[0].shape)], [kept, *across_sums])
    (dmix_in,) = call(
        functools.partial(mix_back_body, batch),
        [of((rows_here, width))],
        [*first, dep("F2", dmixed)],
        limit=CFG['limit'],
    )
    keep("F2", dmix_in)
    keep("add", grad_one)
    received = [dep("Z1", after(got[0], dmix_in)), *[got[d] for d in range(1, seq) if d in got]]
    if len(received) == 1:
        received = [received[0].reshape(count, j_here, width)]
    *terms, gathered = call(
        functools.partial(second_grad_body, batch, seq),
        [of((groups * m_here, lanes))] * batch + ([of((count, j_here, width))] if len(received) > 1 else []),
        [*received, dz],
        [pltpu.VMEM((groups, count, lanes), F32)],
    )
    if len(received) == 1:
        terms, gathered = [*terms, gathered], received[0]
    terms_got = [dep("unpack", terms[0])] + [move(f"R{d}", terms[d], "batch", d, batch) for d in (1, 2, 3)]
    (grad_tokens,) = call(
        tokens_body,
        [of((rows_here, width))],
        [gathered, second, h, src, dmix_in],
        [pltpu.VMEM((rows_here, width), BF16), pltpu.SemaphoreType.DMA((groups,))],
        far_outs=(0,),
    )
    (grad_flat,) = call(
        functools.partial(unpack_body, count, seq), [of((m_here * count, j_here))], terms_got
    )
    grad_two = jnp.transpose(grad_flat.reshape(m_here, count, j_here), (2, 0, 1))
    return (grad_tokens[None], grad_one, grad_two)


def wide_shards(tokens, cotangent, first_factor, second_factor, gate_source, alternate):
    inputs = tokens[0]
    rows_here = inputs.shape[0]
    width = inputs.shape[1]
    order_len = alternate.shape[0]
    blocks_here = rows_here // order_len
    select = one_hot(lax.broadcasted_iota(jnp.int32, (width, width), 0) == gate_source[None, :])
    gate = jax.nn.sigmoid(jnp.dot(inputs, select, preferred_element_type=F32))
    first_full = lax.all_gather(first_factor, "batch", axis=1, tiled=True)
    second_full = lax.all_gather(second_factor, "batch", axis=1, tiled=True)
    blocked = inputs.reshape(blocks_here, order_len, width)
    mixed = jnp.einsum("ikj,ijc->ikc", first_full, blocked, preferred_element_type=F32).astype(BF16)
    shuffled = jnp.take(mixed, alternate, axis=1)
    piece = lax.all_to_all(shuffled, "seq", split_axis=1, concat_axis=0, tiled=True)
    z_blocks = jnp.einsum("jmi,ijc->jmc", second_full, piece, preferred_element_type=F32)
    j_here, count_second = z_blocks.shape[:2]
    z_out = z_blocks.reshape(rows_here, width)
    cot = cotangent[0].astype(F32)
    dz_out = (cot * gate).astype(BF16)
    dgate = cot * z_out * gate * (1.0 - gate)
    dz_blocks = dz_out.reshape(j_here, count_second, width)
    term_second = jnp.einsum("jmc,ijc->jmi", dz_blocks, piece, preferred_element_type=F32)
    grad_two = lax.psum_scatter(term_second.astype(BF16), "batch", scatter_dimension=1, tiled=True)
    dregrouped = jnp.einsum("jmi,jmc->ijc", second_full, dz_blocks, preferred_element_type=F32).astype(BF16)
    positions = lax.iota(jnp.int32, order_len)
    inverse = jnp.zeros((order_len,), jnp.int32).at[alternate].set(positions)
    restored = jnp.take(
        lax.all_to_all(dregrouped, "seq", split_axis=0, concat_axis=1, tiled=True), inverse, axis=1
    )
    dmix_in = jnp.einsum("ikj,ikc->ijc", first_full, restored, preferred_element_type=F32)
    term_first = jnp.einsum("ikc,ijc->ikj", restored, blocked, preferred_element_type=F32)
    grad_one = lax.psum_scatter(term_first.astype(BF16), "batch", scatter_dimension=1, tiled=True)
    spread = jnp.dot(dgate, select.T.astype(F32), precision=lax.Precision.HIGHEST)
    grad_tokens = (dmix_in.reshape(rows_here, width) + spread).astype(BF16)
    return (grad_tokens[None], grad_one, grad_two)


def solution(mesh):
    batch, seq = mesh.shape["batch"], mesh.shape["seq"]

    def shards(*args):
        j_here, m_here, count = args[3].shape
        if batch == 4 and seq & (seq - 1) == 0 and j_here % LANE_GROUP == 0 and m_here % 8 == 0 and count <= 32:
            return packed_shards(*args, batch, seq)
        return wide_shards(*args)

    in_specs = (
        P("batch", "seq", None),
        P("batch", "seq", None),
        P("seq", "batch", None),
        P("seq", "batch", None),
        P(),
        P(),
    )
    out_specs = (P("batch", "seq", None), P("seq", "batch", None), P("seq", "batch", None))
    return jax.shard_map(shards, mesh=mesh, in_specs=in_specs, out_specs=out_specs, check_vma=False)
```

```python
import functools

import jax
import jax.numpy as jnp
from jax import lax
from jax.experimental import pallas as pl
from jax.experimental.pallas import tpu as pltpu
from jax.sharding import PartitionSpec as P

BF16 = jnp.bfloat16
F32 = jnp.float32
LANE_GROUP = 16
CFG = {'a2a': [True, True], 'limit': 62914560, 'cost': {}, 'direct': False, 'rsdirect': False, 'f2early': False, 'order': [[7, 6, 5, 4, 3, 2, 1], [7, 6, 5, 4, 3, 2, 1]], 'deps': {'fx': ['A2'], 'F1': ['M'], 'F2': ['pair'], 'Z1': ['add']}}


def iota(shape, dim):
    return lax.broadcasted_iota(jnp.int32, shape, dim)


def one_hot(mask):
    return jnp.where(mask, 1.0, 0.0).astype(BF16)


def dot(a, b, da=1, db=0):
    return lax.dot_general(a, b, (((da,), (db,)), ((), ())), preferred_element_type=F32)


def call(body, outs, ins, scratch=(), spaces={}, limit=40 << 20, weight=0, far_outs=()):
    name = getattr(body, "func", body).__name__
    weight = CFG['cost'].get(name, 0)
    return pl.pallas_call(
        body,
        name=name,
        out_shape=outs,
        in_specs=[pl.BlockSpec(memory_space=spaces.get(n, pltpu.VMEM)) for n in range(len(ins))],
        out_specs=[
            pl.BlockSpec(memory_space=pltpu.HBM if n in far_outs else pltpu.VMEM) for n in range(len(outs))
        ],
        scratch_shapes=list(scratch),
        compiler_params=pltpu.CompilerParams(vmem_limit_bytes=limit),
        cost_estimate=pl.CostEstimate(flops=0, bytes_accessed=weight, transcendentals=0),
    )(*ins)


def of(shape, dtype=BF16):
    return jax.ShapeDtypeStruct(shape, dtype)


def swap(value, axis, step, size):
    return lax.ppermute(value, axis, [(p, p ^ step) for p in range(size)])


def ring_at(place, size):
    return jnp.where(place < size // 2, 2 * place, 2 * size - 1 - 2 * place)


def ring_of(size):
    return [2 * p if p < size // 2 else 2 * size - 1 - 2 * p for p in range(size)]


def after(value, *earlier):
    return lax.optimization_barrier((value, *earlier))[0]


def pack_body(order, s_ref, out_ref):
    rows, j_here = s_ref.shape
    groups = j_here // LANE_GROUP
    lanes = order * LANE_GROUP
    m_here = rows // order
    s = s_ref[...]
    lane = iota((j_here, lanes), 1)
    keep = (iota((rows, lanes), 0) % order) == (iota((rows, lanes), 1) // LANE_GROUP)
    for g in range(groups):
        place = one_hot(iota((j_here, lanes), 0) == g * LANE_GROUP + lane % LANE_GROUP)
        wide = jnp.where(keep, dot(s, place), 0.0)
        packed = jnp.sum(wide.reshape(m_here, order, lanes), axis=1)
        out_ref[g * m_here : (g + 1) * m_here, :] = packed.astype(BF16)


def gate_body(x_ref, cot_ref, src_ref, dz_ref):
    rows, width = x_ref.shape
    step = min(rows, 512)
    select = one_hot(iota((width, width), 0) == src_ref[...])
    for n in range(rows // step):
        part = slice(n * step, (n + 1) * step)
        gate = jax.nn.sigmoid(dot(x_ref[part, :], select))
        dz_ref[part, :] = (cot_ref[part, :].astype(F32) * gate).astype(BF16)


def regroup_back_body(batch, seq, order, *refs):
    pieces, dz_ref = refs[:batch], refs[batch]
    outs, second_ref, d_scr, r_scr, sems = refs[batch + 1 : -4], *refs[-4:]
    me, here = lax.axis_index("batch"), lax.axis_index("seq")
    groups = second_ref.shape[0]
    lanes = order * LANE_GROUP
    m_here = order // batch
    for d in range(batch):
        piece = pieces[d][...].astype(F32)
        first = pl.multiple_of((me ^ d) * m_here, m_here)
        for g in range(groups):
            d_scr[g, pl.ds(first, m_here), :] = piece[g * m_here : (g + 1) * m_here]
    width = dz_ref.shape[1]
    tiled = one_hot((iota((order, lanes), 1) % order) == iota((order, lanes), 0))
    keep = (iota((lanes, lanes), 0) % LANE_GROUP) == (iota((lanes, lanes), 1) // order)
    writes = []
    blocks = order // seq
    part = lanes // seq
    for g in range(groups):
        wide = d_scr[g]
        packed = wide.astype(BF16)
        ringed = [wide[:, there * part : (there + 1) * part] for there in ring_of(seq)]
        second_ref[g] = jnp.concatenate(ringed, axis=1).astype(BF16)
        weights = jnp.where(keep, dot(packed, tiled, 0, 0), 0.0).astype(BF16)
        result = dot(weights, dz_ref[g * lanes : (g + 1) * lanes, :]).astype(BF16)
        js = slice(g * LANE_GROUP, (g + 1) * LANE_GROUP)
        r_scr[:, js, :] = result.reshape(order, LANE_GROUP, width)
        if len(outs) == 1:
            for p, there in enumerate(ring_of(seq)):
                source, target = pl.ds(there * blocks, blocks), pl.ds(p * blocks, blocks)
                write = pltpu.make_async_copy(
                    r_scr.at[source, js, :], outs[0].at[target, js, :], sems.at[g, p]
                )
                write.start()
                writes.append(write)

    if len(outs) == 1:
        for write in writes:
            write.wait()
    else:
        for d in range(seq):
            outs[d][...] = r_scr[pl.ds((here ^ d) * blocks, blocks)]


def mix_body(batch, seq, *refs):
    pieces, x_hbm, alt_ref, out_hbm = refs[:batch], *refs[batch : batch + 3]
    f_scr, x_scr, p_scr, mix_scr, reg_scr, read_sems, write_sems = refs[batch + 3 :]
    me = lax.axis_index("batch")
    blocks, rows, order = pieces[0].shape
    j_here = order // seq
    width = x_scr.shape[1]
    reads, writes = [], []
    for i in range(blocks):
        part = pl.ds(i * order, order)
        reads.append([pltpu.make_async_copy(x_hbm.at[part, :], x_scr.at[part, :], read_sems.at[i, batch])])
        for d in range(batch):
            reads[i].append(pltpu.make_async_copy(pieces[d].at[i], f_scr.at[d, i], read_sems.at[i, d]))
        for read in reads[i]:
            read.start()
    p_scr[...] = jnp.where(iota((order, order), 0) == alt_ref[...], 1.0, 0.0).T.astype(BF16)
    for i in range(blocks):
        for read in reads[i]:
            read.wait()
        x = x_scr[i * order : (i + 1) * order, :]
        for d in range(batch):
            first = pl.multiple_of((me ^ d) * rows, rows)
            mix_scr[pl.ds(first, rows), :] = dot(f_scr[d, i], x).astype(BF16)
        reg_scr[i] = dot(p_scr[...], mix_scr[...]).astype(BF16).reshape(seq, j_here, width)
        for p, there in enumerate(ring_of(seq)):
            write = pltpu.make_async_copy(reg_scr.at[i, there], out_hbm.at[p, i], write_sems.at[i, p])
            write.start()
            writes.append(write)
    for write in writes:
        write.wait()


def first_grad_body(batch, seq, *refs):
    count = len(refs) - batch - 8
    pieces, x_ref, alt_ref = refs[:count], refs[count], refs[count + 1]
    outs, dmixed_hbm = refs[count + 2 : count + 2 + batch], refs[count + 2 + batch]
    p_scr, reg_scr, part_scr, dmixed_ref, sems = refs[-5:]
    me, here = lax.axis_index("batch"), lax.axis_index("seq")
    blocks, j_here, width = pieces[0].shape[-3:]
    order = j_here * seq
    rows = order // batch
    p_scr[...] = one_hot(iota((order, order), 0) == alt_ref[...])

    writes = []
    for i in range(blocks):
        if count == 1:
            for p, there in enumerate(ring_of(seq)):
                reg_scr[there * j_here : (there + 1) * j_here, :] = pieces[0][p, i]
        else:
            for d in range(seq):
                first = pl.multiple_of((here ^ d) * j_here, j_here)
                reg_scr[pl.ds(first, j_here), :] = pieces[d][i]
        dmixed = dot(p_scr[...], reg_scr[...]).astype(BF16)
        dmixed_ref[i] = dmixed
        writes.append(pltpu.make_async_copy(dmixed_ref.at[i], dmixed_hbm.at[i], sems.at[i]))
        writes[i].start()
        x = x_ref[i * order : (i + 1) * order, :]
        part_scr[...] = dot(dmixed, x, 1, 1).astype(BF16)
        for d in range(batch):
            first = pl.multiple_of((me ^ d) * rows, rows)
            outs[d][i] = part_scr[pl.ds(first, rows), :]
    for write in writes:
        write.wait()


def mix_back_body(batch, *refs):
    pieces, dmixed_ref, x_ref, cot_ref, src_ref, out_ref, h_ref = refs[:batch], *refs[batch:]
    me = lax.axis_index("batch")
    blocks, rows, order = pieces[0].shape
    width = x_ref.shape[1]
    select = one_hot(iota((width, width), 0) == src_ref[...])

    @pl.loop(0, blocks)
    def _(i):
        part = pl.ds(pl.multiple_of(i * order, order), order)
        total = None
        for d in range(batch):
            first = pl.multiple_of((me ^ d) * rows, rows)
            term = dot(pieces[d][i], dmixed_ref[i, pl.ds(first, rows), :], 0, 0)
            total = term if total is None else total + term
        out_ref[part, :] = total.astype(BF16)
        gate = jax.nn.sigmoid(dot(x_ref[part, :], select))
        h_ref[part, :] = (cot_ref[part, :].astype(F32) * gate * (1.0 - gate)).astype(BF16)


def gather_blocks(seq, pieces, scr):
    here = lax.axis_index("seq")
    blocks = pieces[0].shape[0]
    for d in range(seq):
        scr[pl.ds((here ^ d) * blocks, blocks)] = pieces[d][...]


def second_grad_body(batch, seq, *refs):
    count = len(refs) - batch - 3 if len(refs) > batch + 4 else 1
    if count == 1:
        pieces, dz_ref = refs[:1], refs[1]
        outs, reg_ref, y_scr = refs[2 : 2 + batch], refs[0], refs[-1]
    else:
        pieces, dz_ref = refs[:seq], refs[seq]
        outs, reg_ref, y_scr = refs[seq + 1 : seq + 1 + batch], refs[-2], refs[-1]
    me = lax.axis_index("batch")
    order, j_here, width = reg_ref.shape
    groups, lanes, m_here = j_here // LANE_GROUP, order * LANE_GROUP, order // batch
    if count > 1:
        gather_blocks(seq, pieces, reg_ref)

    @pl.loop(0, groups)
    def _(g):
        js = pl.ds(pl.multiple_of(g * LANE_GROUP, LANE_GROUP), LANE_GROUP)
        reg = reg_ref[:, js, :].reshape(lanes, width)
        dz = dz_ref[pl.ds(pl.multiple_of(g * lanes, lanes), lanes), :]
        wide = dot(dz, reg, 1, 1)
        col = iota((order, lanes), 1) % LANE_GROUP
        packed = wide[:order]
        for jj in range(1, LANE_GROUP):
            packed = jnp.where(col == jj, wide[jj * order : (jj + 1) * order], packed)
        y_scr[g] = packed

    for d in range(batch):
        first = pl.multiple_of((me ^ d) * m_here, m_here)
        rows = [y_scr[g, pl.ds(first, m_here), :] for g in range(groups)]
        outs[d][...] = jnp.concatenate(rows, axis=0).astype(BF16)


def tokens_body(reg_ref, second_ref, h_ref, src_ref, back_ref, out_hbm, out_ref, sems):
    order, j_here, width = reg_ref.shape
    groups, lanes = j_here // LANE_GROUP, order * LANE_GROUP
    select = one_hot(iota((width, width), 0) == src_ref[...])
    col = iota((order, lanes), 1) % LANE_GROUP
    masks = [one_hot(col == jj) for jj in range(LANE_GROUP)]
    writes = []
    for g in range(groups):
        reg = reg_ref[:, g * LANE_GROUP : (g + 1) * LANE_GROUP, :].reshape(lanes, width)
        packed = second_ref[g]
        weights = jnp.concatenate([packed * mask for mask in masks], axis=0)
        rows = slice(g * lanes, (g + 1) * lanes)
        dgate = (dot(weights, reg) * h_ref[rows, :].astype(F32)).astype(BF16)
        out_ref[rows, :] = (back_ref[rows, :].astype(F32) + dot(dgate, select, 1, 1)).astype(BF16)
        writes.append(pltpu.make_async_copy(out_ref.at[rows, :], out_hbm.at[rows, :], sems.at[g]))
        writes[g].start()
    for write in writes:
        write.wait()


def pair_body(own_a, own_b, got_a, got_b, out_a, *outs_b):
    out_a[...] = own_a[...].astype(F32) + got_a[...].astype(F32)
    step = outs_b[0].shape[0]
    for n, out_b in enumerate(outs_b):
        part = slice(n * step, (n + 1) * step)
        out_b[...] = (own_b[part].astype(F32) + got_b[part].astype(F32)).astype(BF16)


def sum_body(own, *refs):
    total = own[...].astype(F32)
    for got in refs[:-1]:
        total = total + got[...].astype(F32)
    refs[-1][...] = total.astype(BF16)


def add_body(own, *refs):
    step = refs[0].shape[0]
    for n, got in enumerate(refs[:-1]):
        part = slice(n * step, (n + 1) * step)
        refs[-1][part] = (own[part] + got[...].astype(F32)).astype(BF16)


def unpack_body(order, seq, *refs):
    pieces, out_ref = refs[:-1], refs[-1]
    rows, j_here = out_ref.shape
    groups, lanes, m_here = j_here // LANE_GROUP, order * LANE_GROUP, rows // order
    total = pieces[0][...].astype(F32)
    for piece in pieces[1:]:
        total = total + piece[...].astype(F32)
    lane = iota((j_here, lanes), 1)
    blocks = order // seq
    place_i = iota((rows, lanes), 1) // LANE_GROUP
    keep = (iota((rows, lanes), 0) % order) == ring_at(place_i // blocks, seq) * blocks + place_i % blocks
    result = jnp.zeros((rows, j_here), F32)
    for g in range(groups):
        place = one_hot(iota((j_here, lanes), 0) == g * LANE_GROUP + lane % LANE_GROUP)
        packed = total[g * m_here : (g + 1) * m_here]
        wide = jnp.broadcast_to(packed[:, None, :], (m_here, order, lanes)).reshape(rows, lanes)
        result = result + dot(jnp.where(keep, wide, 0.0).astype(BF16), place, 1, 1)
    out_ref[...] = result.astype(BF16)


def packed_shards(tokens, cotangent, first_factor, second_factor, gate_source, alternate, batch, seq):
    x, cot = tokens[0], cotangent[0]
    rows_here, width = x.shape
    blocks, k_here, order = first_factor.shape
    j_here, m_here, count = second_factor.shape
    groups, lanes = j_here // LANE_GROUP, count * LANE_GROUP
    src = gate_source.reshape(1, width)
    alt = alternate.reshape(1, order)

    flat = jnp.transpose(second_factor, (1, 2, 0)).reshape(m_here * count, j_here)
    vals = {}

    def dep(name, value):
        earlier = [vals[n] for n in CFG['deps'].get(name, ()) if n in vals]
        return after(value, *earlier) if earlier else value

    def keep(name, value):
        vals[name] = value
        return value

    def move(name, value, axis, step, size):
        return keep(name, swap(dep(name, value), axis, step, size))

    (mine,) = call(functools.partial(pack_body, count), [of((groups * m_here, lanes))], [flat])
    packed = {0: mine}
    for d in (3, 2, 1):
        packed[d] = move(f"D{d}", mine, "batch", d, batch)
    (dz,) = call(gate_body, [of((rows_here, width))], [x, cot, src], limit=16 << 20)
    keep("gate", dz)
    piece = of((blocks, j_here, width))
    *back, second = call(
        functools.partial(regroup_back_body, batch, seq, count),
        ([of((count, j_here, width))] if CFG['a2a'][0] else [piece] * seq) + [of((groups, count, lanes))],
        [*[packed[d] for d in range(batch)], dz],
        [
            pltpu.VMEM((groups, count, lanes), F32),
            pltpu.VMEM((count, j_here, width), BF16),
            pltpu.SemaphoreType.DMA((groups, seq)),
        ],
        far_outs=(0,) if CFG['a2a'][0] else (),
        limit=24 << 20,
    )
    keep("A2", back[0])
    first_ready = after(first_factor, dz) if CFG['f2early'] else after(first_factor, dz, *[packed[d] for d in (1, 2, 3)])
    across = move("f2", first_ready, "batch", 2, batch)
    beside = move("f1", first_ready, "batch", 1, batch)
    direct = move("f3", first_ready, "batch", 3, batch) if CFG['direct'] else None
    back_got = {0: back[0]}
    if CFG['a2a'][0]:
        back_got[0] = keep("h0", lax.all_to_all(
            dep("h0", back[0]).reshape(seq, blocks, j_here, width), "seq", 0, 0, axis_index_groups=[ring_of(seq)], tiled=True
        ))
    else:
        for d in CFG['order'][0]:
            back_got[d] = move(f"h{d}", back[d], "seq", d, seq)
    if direct is None:
        direct = move("fx", across, "batch", 1, batch)
    first = [first_factor, beside, across, direct]
    regrouped = call(
        functools.partial(mix_body, batch, seq),
        [of((seq, blocks, j_here, width))],
        [dep("M", first_factor), *first[1:], x, alt],
        [
            pltpu.VMEM((batch, blocks, k_here, order), BF16),
            pltpu.VMEM((rows_here, width), BF16),
            pltpu.VMEM((order, order), BF16),
            pltpu.VMEM((order, width), BF16),
            pltpu.VMEM((blocks, seq, j_here, width), BF16),
            pltpu.SemaphoreType.DMA((blocks, batch + 1)),
            pltpu.SemaphoreType.DMA((blocks, seq)),
        ],
        spaces={n: pltpu.HBM for n in range(batch + 1)},
        far_outs=(0,),
        limit=CFG['limit'],
    )
    keep("M", regrouped[0])
    got = {0: regrouped[0]}
    if CFG['a2a'][1]:
        got[0] = keep("H0", lax.all_to_all(
            dep("H0", regrouped[0]), "seq", 0, 0, axis_index_groups=[ring_of(seq)], tiled=True
        ))
    else:
        for d in CFG['order'][1]:
            got[d] = move(f"H{d}", regrouped[d], "seq", d, seq)
    *parts, dmixed = call(
        functools.partial(first_grad_body, batch, seq),
        [of((blocks, k_here, order))] * batch + [of((blocks, order, width))],
        [dep("F1", back_got[0]), *[back_got[d] for d in range(1, seq) if d in back_got], x, alt],
        [
            pltpu.VMEM((order, order), BF16),
            pltpu.VMEM((order, width), BF16),
            pltpu.VMEM((order, order), BF16),
            pltpu.VMEM((blocks, order, width), BF16),
            pltpu.SemaphoreType.DMA((blocks,)),
        ],
        far_outs=(batch,),
        limit=40 << 20,
    )
    keep("F1", dmixed)
    if CFG['rsdirect']:
        others = [move(f"rs{d}", parts[d], "batch", d, batch) for d in (3, 2, 1)]
    else:
        near = move("near", parts[1], "batch", 1, batch)
        far = move("far", parts[3], "batch", 1, batch)
    if CFG['rsdirect']:
        (grad_one,) = call(sum_body, [of(parts[0].shape)], [dep("sum", parts[0]), *others])
    else:
        halves = 4 if blocks % 4 == 0 else 1
        kept, *summed = call(
            pair_body,
            [of(parts[0].shape, F32)] + [of((blocks // halves, k_here, order))] * halves,
            [dep("pair", parts[0]), parts[2], near, far],
            limit=40 << 20,
        )
        keep("pair", summed[0])
        across_sums = [move(f"rx{n}", summed[n], "batch", 2, batch) for n in range(halves)]
        (grad_one,) = call(add_body, [of(parts[0].shape)], [kept, *across_sums])
    dmix_in, h = call(
        functools.partial(mix_back_body, batch),
        [of((rows_here, width))] * 2,
        [*first, dep("F2", dmixed), x, cot, src],
        limit=CFG['limit'],
    )
    keep("F2", dmix_in)
    keep("add", grad_one)
    received = [dep("Z1", after(got[0], dmix_in)), *[got[d] for d in range(1, seq) if d in got]]
    if len(received) == 1:
        received = [received[0].reshape(count, j_here, width)]
    *terms, gathered = call(
        functools.partial(second_grad_body, batch, seq),
        [of((groups * m_here, lanes))] * batch + ([of((count, j_here, width))] if len(received) > 1 else []),
        [*received, dz],
        [pltpu.VMEM((groups, count, lanes), F32)],
    )
    if len(received) == 1:
        terms, gathered = [*terms, gathered], received[0]
    terms_got = [dep("unpack", terms[0])] + [move(f"R{d}", terms[d], "batch", d, batch) for d in (1, 2, 3)]
    (grad_tokens,) = call(
        tokens_body,
        [of((rows_here, width))],
        [gathered, second, h, src, dmix_in],
        [pltpu.VMEM((rows_here, width), BF16), pltpu.SemaphoreType.DMA((groups,))],
        far_outs=(0,),
    )
    (grad_flat,) = call(
        functools.partial(unpack_body, count, seq), [of((m_here * count, j_here))], terms_got
    )
    grad_two = jnp.transpose(grad_flat.reshape(m_here, count, j_here), (2, 0, 1))
    return (grad_tokens[None], grad_one, grad_two)


def wide_shards(tokens, cotangent, first_factor, second_factor, gate_source, alternate):
    inputs = tokens[0]
    rows_here = inputs.shape[0]
    width = inputs.shape[1]
    order_len = alternate.shape[0]
    blocks_here = rows_here // order_len
    select = one_hot(lax.broadcasted_iota(jnp.int32, (width, width), 0) == gate_source[None, :])
    gate = jax.nn.sigmoid(jnp.dot(inputs, select, preferred_element_type=F32))
    first_full = lax.all_gather(first_factor, "batch", axis=1, tiled=True)
    second_full = lax.all_gather(second_factor, "batch", axis=1, tiled=True)
    blocked = inputs.reshape(blocks_here, order_len, width)
    mixed = jnp.einsum("ikj,ijc->ikc", first_full, blocked, preferred_element_type=F32).astype(BF16)
    shuffled = jnp.take(mixed, alternate, axis=1)
    piece = lax.all_to_all(shuffled, "seq", split_axis=1, concat_axis=0, tiled=True)
    z_blocks = jnp.einsum("jmi,ijc->jmc", second_full, piece, preferred_element_type=F32)
    j_here, count_second = z_blocks.shape[:2]
    z_out = z_blocks.reshape(rows_here, width)
    cot = cotangent[0].astype(F32)
    dz_out = (cot * gate).astype(BF16)
    dgate = cot * z_out * gate * (1.0 - gate)
    dz_blocks = dz_out.reshape(j_here, count_second, width)
    term_second = jnp.einsum("jmc,ijc->jmi", dz_blocks, piece, preferred_element_type=F32)
    grad_two = lax.psum_scatter(term_second.astype(BF16), "batch", scatter_dimension=1, tiled=True)
    dregrouped = jnp.einsum("jmi,jmc->ijc", second_full, dz_blocks, preferred_element_type=F32).astype(BF16)
    positions = lax.iota(jnp.int32, order_len)
    inverse = jnp.zeros((order_len,), jnp.int32).at[alternate].set(positions)
    restored = jnp.take(
        lax.all_to_all(dregrouped, "seq", split_axis=0, concat_axis=1, tiled=True), inverse, axis=1
    )
    dmix_in = jnp.einsum("ikj,ikc->ijc", first_full, restored, preferred_element_type=F32)
    term_first = jnp.einsum("ikc,ijc->ikj", restored, blocked, preferred_element_type=F32)
    grad_one = lax.psum_scatter(term_first.astype(BF16), "batch", scatter_dimension=1, tiled=True)
    spread = jnp.dot(dgate, select.T.astype(F32), precision=lax.Precision.HIGHEST)
    grad_tokens = (dmix_in.reshape(rows_here, width) + spread).astype(BF16)
    return (grad_tokens[None], grad_one, grad_two)


def solution(mesh):
    batch, seq = mesh.shape["batch"], mesh.shape["seq"]

    def shards(*args):
        j_here, m_here, count = args[3].shape
        if batch == 4 and seq & (seq - 1) == 0 and j_here % LANE_GROUP == 0 and m_here % 8 == 0 and count <= 32:
            return packed_shards(*args, batch, seq)
        return wide_shards(*args)

    in_specs = (
        P("batch", "seq", None),
        P("batch", "seq", None),
        P("seq", "batch", None),
        P("seq", "batch", None),
        P(),
        P(),
    )
    out_specs = (P("batch", "seq", None), P("seq", "batch", None), P("seq", "batch", None))
    return jax.shard_map(shards, mesh=mesh, in_specs=in_specs, out_specs=out_specs, check_vma=False)
```

```python
import functools

import jax
import jax.numpy as jnp
from jax import lax
from jax.experimental import pallas as pl
from jax.experimental.pallas import tpu as pltpu
from jax.sharding import PartitionSpec as P

BF16 = jnp.bfloat16
F32 = jnp.float32
LANE_GROUP = 16
CFG = {'a2a': [True, True], 'limit': 62914560, 'cost': {}, 'direct': False, 'rsdirect': False, 'f2early': False, 'order': [[7, 6, 5, 4, 3, 2, 1], [7, 6, 5, 4, 3, 2, 1]], 'deps': {'fx': ['A2'], 'F1': ['M'], 'F2': ['pair'], 'Z1': ['add']}}


def iota(shape, dim):
    return lax.broadcasted_iota(jnp.int32, shape, dim)


def one_hot(mask):
    return jnp.where(mask, 1.0, 0.0).astype(BF16)


def dot(a, b, da=1, db=0):
    return lax.dot_general(a, b, (((da,), (db,)), ((), ())), preferred_element_type=F32)


def call(body, outs, ins, scratch=(), spaces={}, limit=40 << 20, weight=0, far_outs=()):
    name = getattr(body, "func", body).__name__
    weight = CFG['cost'].get(name, 0)
    return pl.pallas_call(
        body,
        name=name,
        out_shape=outs,
        in_specs=[pl.BlockSpec(memory_space=spaces.get(n, pltpu.VMEM)) for n in range(len(ins))],
        out_specs=[
            pl.BlockSpec(memory_space=pltpu.HBM if n in far_outs else pltpu.VMEM) for n in range(len(outs))
        ],
        scratch_shapes=list(scratch),
        compiler_params=pltpu.CompilerParams(vmem_limit_bytes=limit),
        cost_estimate=pl.CostEstimate(flops=0, bytes_accessed=weight, transcendentals=0),
    )(*ins)


def of(shape, dtype=BF16):
    return jax.ShapeDtypeStruct(shape, dtype)


def swap(value, axis, step, size):
    return lax.ppermute(value, axis, [(p, p ^ step) for p in range(size)])


def ring_of(size):
    low, high = list(range(0, size // 2, 2)), list(range(size // 2, size, 2))
    up = [v for pair in zip(low, high) for v in pair]
    down = [v + 1 for pair in zip(low[::-1], high[::-1]) for v in pair]
    return up + down


def after(value, *earlier):
    return lax.optimization_barrier((value, *earlier))[0]


def pack_body(order, s_ref, out_ref):
    rows, j_here = s_ref.shape
    groups = j_here // LANE_GROUP
    lanes = order * LANE_GROUP
    m_here = rows // order
    s = s_ref[...]
    lane = iota((j_here, lanes), 1)
    keep = (iota((rows, lanes), 0) % order) == (iota((rows, lanes), 1) // LANE_GROUP)
    for g in range(groups):
        place = one_hot(iota((j_here, lanes), 0) == g * LANE_GROUP + lane % LANE_GROUP)
        wide = jnp.where(keep, dot(s, place), 0.0)
        packed = jnp.sum(wide.reshape(m_here, order, lanes), axis=1)
        out_ref[g * m_here : (g + 1) * m_here, :] = packed.astype(BF16)


def gate_body(x_ref, cot_ref, src_ref, dz_ref):
    rows, width = x_ref.shape
    step = min(rows, 512)
    select = one_hot(iota((width, width), 0) == src_ref[...])
    for n in range(rows // step):
        part = slice(n * step, (n + 1) * step)
        gate = jax.nn.sigmoid(dot(x_ref[part, :], select))
        dz_ref[part, :] = (cot_ref[part, :].astype(F32) * gate).astype(BF16)


def regroup_back_body(batch, seq, order, *refs):
    pieces, dz_ref = refs[:batch], refs[batch]
    outs, second_ref, d_scr, r_scr, sems = refs[batch + 1 : -4], *refs[-4:]
    me, here = lax.axis_index("batch"), lax.axis_index("seq")
    groups = second_ref.shape[0]
    lanes = order * LANE_GROUP
    m_here = order // batch
    for d in range(batch):
        piece = pieces[d][...].astype(F32)
        first = pl.multiple_of((me ^ d) * m_here, m_here)
        for g in range(groups):
            d_scr[g, pl.ds(first, m_here), :] = piece[g * m_here : (g + 1) * m_here]
    width = dz_ref.shape[1]
    tiled = one_hot((iota((order, lanes), 1) % order) == iota((order, lanes), 0))
    keep = (iota((lanes, lanes), 0) % LANE_GROUP) == (iota((lanes, lanes), 1) // order)
    writes = []
    blocks = order // seq
    part = lanes // seq
    for g in range(groups):
        wide = d_scr[g]
        packed = wide.astype(BF16)
        ringed = [wide[:, there * part : (there + 1) * part] for there in ring_of(seq)]
        second_ref[g] = jnp.concatenate(ringed, axis=1).astype(BF16)
        weights = jnp.where(keep, dot(packed, tiled, 0, 0), 0.0).astype(BF16)
        result = dot(weights, dz_ref[g * lanes : (g + 1) * lanes, :]).astype(BF16)
        js = slice(g * LANE_GROUP, (g + 1) * LANE_GROUP)
        r_scr[:, js, :] = result.reshape(order, LANE_GROUP, width)
        if len(outs) == 1:
            for p, there in enumerate(ring_of(seq)):
                source, target = pl.ds(there * blocks, blocks), pl.ds(p * blocks, blocks)
                write = pltpu.make_async_copy(
                    r_scr.at[source, js, :], outs[0].at[target, js, :], sems.at[g, p]
                )
                write.start()
                writes.append(write)

    if len(outs) == 1:
        for write in writes:
            write.wait()
    else:
        for d in range(seq):
            outs[d][...] = r_scr[pl.ds((here ^ d) * blocks, blocks)]


def mix_body(batch, seq, *refs):
    pieces, x_hbm, alt_ref, out_hbm = refs[:batch], *refs[batch : batch + 3]
    f_scr, x_scr, p_scr, mix_scr, reg_scr, read_sems, write_sems = refs[batch + 3 :]
    me = lax.axis_index("batch")
    blocks, rows, order = pieces[0].shape
    j_here = order // seq
    width = x_scr.shape[1]
    reads, writes = [], []
    for i in range(blocks):
        part = pl.ds(i * order, order)
        reads.append([pltpu.make_async_copy(x_hbm.at[part, :], x_scr.at[part, :], read_sems.at[i, batch])])
        for d in range(batch):
            reads[i].append(pltpu.make_async_copy(pieces[d].at[i], f_scr.at[d, i], read_sems.at[i, d]))
        for read in reads[i]:
            read.start()
    p_scr[...] = jnp.where(iota((order, order), 0) == alt_ref[...], 1.0, 0.0).T.astype(BF16)
    for i in range(blocks):
        for read in reads[i]:
            read.wait()
        x = x_scr[i * order : (i + 1) * order, :]
        for d in range(batch):
            first = pl.multiple_of((me ^ d) * rows, rows)
            mix_scr[pl.ds(first, rows), :] = dot(f_scr[d, i], x).astype(BF16)
        reg_scr[i] = dot(p_scr[...], mix_scr[...]).astype(BF16).reshape(seq, j_here, width)
        for p, there in enumerate(ring_of(seq)):
            write = pltpu.make_async_copy(reg_scr.at[i, there], out_hbm.at[p, i], write_sems.at[i, p])
            write.start()
            writes.append(write)
    for write in writes:
        write.wait()


def first_grad_body(batch, seq, *refs):
    count = len(refs) - batch - 8
    pieces, x_ref, alt_ref = refs[:count], refs[count], refs[count + 1]
    outs, dmixed_hbm = refs[count + 2 : count + 2 + batch], refs[count + 2 + batch]
    p_scr, reg_scr, part_scr, dmixed_ref, sems = refs[-5:]
    me, here = lax.axis_index("batch"), lax.axis_index("seq")
    blocks, j_here, width = pieces[0].shape[-3:]
    order = j_here * seq
    rows = order // batch
    p_scr[...] = one_hot(iota((order, order), 0) == alt_ref[...])

    writes = []
    for i in range(blocks):
        if count == 1:
            for p, there in enumerate(ring_of(seq)):
                reg_scr[there * j_here : (there + 1) * j_here, :] = pieces[0][p, i]
        else:
            for d in range(seq):
                first = pl.multiple_of((here ^ d) * j_here, j_here)
                reg_scr[pl.ds(first, j_here), :] = pieces[d][i]
        dmixed = dot(p_scr[...], reg_scr[...]).astype(BF16)
        dmixed_ref[i] = dmixed
        writes.append(pltpu.make_async_copy(dmixed_ref.at[i], dmixed_hbm.at[i], sems.at[i]))
        writes[i].start()
        x = x_ref[i * order : (i + 1) * order, :]
        part_scr[...] = dot(dmixed, x, 1, 1).astype(BF16)
        for d in range(batch):
            first = pl.multiple_of((me ^ d) * rows, rows)
            outs[d][i] = part_scr[pl.ds(first, rows), :]
    for write in writes:
        write.wait()


def mix_back_body(batch, *refs):
    pieces, dmixed_ref, x_ref, cot_ref, src_ref, out_ref, h_ref = refs[:batch], *refs[batch:]
    me = lax.axis_index("batch")
    blocks, rows, order = pieces[0].shape
    width = x_ref.shape[1]
    select = one_hot(iota((width, width), 0) == src_ref[...])

    @pl.loop(0, blocks)
    def _(i):
        part = pl.ds(pl.multiple_of(i * order, order), order)
        total = None
        for d in range(batch):
            first = pl.multiple_of((me ^ d) * rows, rows)
            term = dot(pieces[d][i], dmixed_ref[i, pl.ds(first, rows), :], 0, 0)
            total = term if total is None else total + term
        out_ref[part, :] = total.astype(BF16)
        gate = jax.nn.sigmoid(dot(x_ref[part, :], select))
        h_ref[part, :] = (cot_ref[part, :].astype(F32) * gate * (1.0 - gate)).astype(BF16)


def gather_blocks(seq, pieces, scr):
    here = lax.axis_index("seq")
    blocks = pieces[0].shape[0]
    for d in range(seq):
        scr[pl.ds((here ^ d) * blocks, blocks)] = pieces[d][...]


def second_grad_body(batch, seq, *refs):
    count = len(refs) - batch - 3 if len(refs) > batch + 4 else 1
    if count == 1:
        pieces, dz_ref = refs[:1], refs[1]
        outs, reg_ref, y_scr = refs[2 : 2 + batch], refs[0], refs[-1]
    else:
        pieces, dz_ref = refs[:seq], refs[seq]
        outs, reg_ref, y_scr = refs[seq + 1 : seq + 1 + batch], refs[-2], refs[-1]
    me = lax.axis_index("batch")
    order, j_here, width = reg_ref.shape
    groups, lanes, m_here = j_here // LANE_GROUP, order * LANE_GROUP, order // batch
    if count > 1:
        gather_blocks(seq, pieces, reg_ref)

    @pl.loop(0, groups)
    def _(g):
        js = pl.ds(pl.multiple_of(g * LANE_GROUP, LANE_GROUP), LANE_GROUP)
        reg = reg_ref[:, js, :].reshape(lanes, width)
        dz = dz_ref[pl.ds(pl.multiple_of(g * lanes, lanes), lanes), :]
        wide = dot(dz, reg, 1, 1)
        col = iota((order, lanes), 1) % LANE_GROUP
        packed = wide[:order]
        for jj in range(1, LANE_GROUP):
            packed = jnp.where(col == jj, wide[jj * order : (jj + 1) * order], packed)
        y_scr[g] = packed

    for d in range(batch):
        first = pl.multiple_of((me ^ d) * m_here, m_here)
        rows = [y_scr[g, pl.ds(first, m_here), :] for g in range(groups)]
        outs[d][...] = jnp.concatenate(rows, axis=0).astype(BF16)


def tokens_body(reg_ref, second_ref, h_ref, src_ref, back_ref, out_hbm, out_ref, sems):
    order, j_here, width = reg_ref.shape
    groups, lanes = j_here // LANE_GROUP, order * LANE_GROUP
    select = one_hot(iota((width, width), 0) == src_ref[...])
    col = iota((order, lanes), 1) % LANE_GROUP
    masks = [one_hot(col == jj) for jj in range(LANE_GROUP)]
    writes = []
    for g in range(groups):
        reg = reg_ref[:, g * LANE_GROUP : (g + 1) * LANE_GROUP, :].reshape(lanes, width)
        packed = second_ref[g]
        weights = jnp.concatenate([packed * mask for mask in masks], axis=0)
        rows = slice(g * lanes, (g + 1) * lanes)
        dgate = (dot(weights, reg) * h_ref[rows, :].astype(F32)).astype(BF16)
        out_ref[rows, :] = (back_ref[rows, :].astype(F32) + dot(dgate, select, 1, 1)).astype(BF16)
        writes.append(pltpu.make_async_copy(out_ref.at[rows, :], out_hbm.at[rows, :], sems.at[g]))
        writes[g].start()
    for write in writes:
        write.wait()


def pair_body(own_a, own_b, got_a, got_b, out_a, *outs_b):
    out_a[...] = own_a[...].astype(F32) + got_a[...].astype(F32)
    step = outs_b[0].shape[0]
    for n, out_b in enumerate(outs_b):
        part = slice(n * step, (n + 1) * step)
        out_b[...] = (own_b[part].astype(F32) + got_b[part].astype(F32)).astype(BF16)


def sum_body(own, *refs):
    total = own[...].astype(F32)
    for got in refs[:-1]:
        total = total + got[...].astype(F32)
    refs[-1][...] = total.astype(BF16)


def add_body(own, *refs):
    step = refs[0].shape[0]
    for n, got in enumerate(refs[:-1]):
        part = slice(n * step, (n + 1) * step)
        refs[-1][part] = (own[part] + got[...].astype(F32)).astype(BF16)


def unpack_body(order, seq, *refs):
    pieces, out_ref = refs[:-1], refs[-1]
    rows, j_here = out_ref.shape
    groups, lanes, m_here = j_here // LANE_GROUP, order * LANE_GROUP, rows // order
    total = pieces[0][...].astype(F32)
    for piece in pieces[1:]:
        total = total + piece[...].astype(F32)
    lane = iota((j_here, lanes), 1)
    blocks = order // seq
    place_i = iota((1, lanes), 1) // LANE_GROUP
    actual = place_i % blocks
    for p, there in enumerate(ring_of(seq)):
        actual = jnp.where(place_i // blocks == p, actual + there * blocks, actual)
    keep = (iota((rows, lanes), 0) % order) == actual
    result = jnp.zeros((rows, j_here), F32)
    for g in range(groups):
        place = one_hot(iota((j_here, lanes), 0) == g * LANE_GROUP + lane % LANE_GROUP)
        packed = total[g * m_here : (g + 1) * m_here]
        wide = jnp.broadcast_to(packed[:, None, :], (m_here, order, lanes)).reshape(rows, lanes)
        result = result + dot(jnp.where(keep, wide, 0.0).astype(BF16), place, 1, 1)
    out_ref[...] = result.astype(BF16)


def packed_shards(tokens, cotangent, first_factor, second_factor, gate_source, alternate, batch, seq):
    x, cot = tokens[0], cotangent[0]
    rows_here, width = x.shape
    blocks, k_here, order = first_factor.shape
    j_here, m_here, count = second_factor.shape
    groups, lanes = j_here // LANE_GROUP, count * LANE_GROUP
    src = gate_source.reshape(1, width)
    alt = alternate.reshape(1, order)

    flat = jnp.transpose(second_factor, (1, 2, 0)).reshape(m_here * count, j_here)
    vals = {}

    def dep(name, value):
        earlier = [vals[n] for n in CFG['deps'].get(name, ()) if n in vals]
        return after(value, *earlier) if earlier else value

    def keep(name, value):
        vals[name] = value
        return value

    def move(name, value, axis, step, size):
        return keep(name, swap(dep(name, value), axis, step, size))

    (mine,) = call(functools.partial(pack_body, count), [of((groups * m_here, lanes))], [flat])
    packed = {0: mine}
    for d in (3, 2, 1):
        packed[d] = move(f"D{d}", mine, "batch", d, batch)
    (dz,) = call(gate_body, [of((rows_here, width))], [x, cot, src], limit=16 << 20)
    keep("gate", dz)
    piece = of((blocks, j_here, width))
    *back, second = call(
        functools.partial(regroup_back_body, batch, seq, count),
        ([of((count, j_here, width))] if CFG['a2a'][0] else [piece] * seq) + [of((groups, count, lanes))],
        [*[packed[d] for d in range(batch)], dz],
        [
            pltpu.VMEM((groups, count, lanes), F32),
            pltpu.VMEM((count, j_here, width), BF16),
            pltpu.SemaphoreType.DMA((groups, seq)),
        ],
        far_outs=(0,) if CFG['a2a'][0] else (),
        limit=24 << 20,
    )
    keep("A2", back[0])
    first_ready = after(first_factor, dz) if CFG['f2early'] else after(first_factor, dz, *[packed[d] for d in (1, 2, 3)])
    across = move("f2", first_ready, "batch", 2, batch)
    beside = move("f1", first_ready, "batch", 1, batch)
    direct = move("f3", first_ready, "batch", 3, batch) if CFG['direct'] else None
    back_got = {0: back[0]}
    if CFG['a2a'][0]:
        back_got[0] = keep("h0", lax.all_to_all(
            dep("h0", back[0]).reshape(seq, blocks, j_here, width), "seq", 0, 0, axis_index_groups=[ring_of(seq)], tiled=True
        ))
    else:
        for d in CFG['order'][0]:
            back_got[d] = move(f"h{d}", back[d], "seq", d, seq)
    if direct is None:
        direct = move("fx", across, "batch", 1, batch)
    first = [first_factor, beside, across, direct]
    regrouped = call(
        functools.partial(mix_body, batch, seq),
        [of((seq, blocks, j_here, width))],
        [dep("M", first_factor), *first[1:], x, alt],
        [
            pltpu.VMEM((batch, blocks, k_here, order), BF16),
            pltpu.VMEM((rows_here, width), BF16),
            pltpu.VMEM((order, order), BF16),
            pltpu.VMEM((order, width), BF16),
            pltpu.VMEM((blocks, seq, j_here, width), BF16),
            pltpu.SemaphoreType.DMA((blocks, batch + 1)),
            pltpu.SemaphoreType.DMA((blocks, seq)),
        ],
        spaces={n: pltpu.HBM for n in range(batch + 1)},
        far_outs=(0,),
        limit=CFG['limit'],
    )
    keep("M", regrouped[0])
    got = {0: regrouped[0]}
    if CFG['a2a'][1]:
        got[0] = keep("H0", lax.all_to_all(
            dep("H0", regrouped[0]), "seq", 0, 0, axis_index_groups=[ring_of(seq)], tiled=True
        ))
    else:
        for d in CFG['order'][1]:
            got[d] = move(f"H{d}", regrouped[d], "seq", d, seq)
    *parts, dmixed = call(
        functools.partial(first_grad_body, batch, seq),
        [of((blocks, k_here, order))] * batch + [of((blocks, order, width))],
        [dep("F1", back_got[0]), *[back_got[d] for d in range(1, seq) if d in back_got], x, alt],
        [
            pltpu.VMEM((order, order), BF16),
            pltpu.VMEM((order, width), BF16),
            pltpu.VMEM((order, order), BF16),
            pltpu.VMEM((blocks, order, width), BF16),
            pltpu.SemaphoreType.DMA((blocks,)),
        ],
        far_outs=(batch,),
        limit=40 << 20,
    )
    keep("F1", dmixed)
    if CFG['rsdirect']:
        others = [move(f"rs{d}", parts[d], "batch", d, batch) for d in (3, 2, 1)]
    else:
        near = move("near", parts[1], "batch", 1, batch)
        far = move("far", parts[3], "batch", 1, batch)
    if CFG['rsdirect']:
        (grad_one,) = call(sum_body, [of(parts[0].shape)], [dep("sum", parts[0]), *others])
    else:
        halves = 4 if blocks % 4 == 0 else 1
        kept, *summed = call(
            pair_body,
            [of(parts[0].shape, F32)] + [of((blocks // halves, k_here, order))] * halves,
            [dep("pair", parts[0]), parts[2], near, far],
            limit=40 << 20,
        )
        keep("pair", summed[0])
        across_sums = [move(f"rx{n}", summed[n], "batch", 2, batch) for n in range(halves)]
        (grad_one,) = call(add_body, [of(parts[0].shape)], [kept, *across_sums])
    dmix_in, h = call(
        functools.partial(mix_back_body, batch),
        [of((rows_here, width))] * 2,
        [*first, dep("F2", dmixed), x, cot, src],
        limit=CFG['limit'],
    )
    keep("F2", dmix_in)
    keep("add", grad_one)
    received = [dep("Z1", after(got[0], dmix_in)), *[got[d] for d in range(1, seq) if d in got]]
    if len(received) == 1:
        received = [received[0].reshape(count, j_here, width)]
    *terms, gathered = call(
        functools.partial(second_grad_body, batch, seq),
        [of((groups * m_here, lanes))] * batch + ([of((count, j_here, width))] if len(received) > 1 else []),
        [*received, dz],
        [pltpu.VMEM((groups, count, lanes), F32)],
    )
    if len(received) == 1:
        terms, gathered = [*terms, gathered], received[0]
    terms_got = [dep("unpack", terms[0])] + [move(f"R{d}", terms[d], "batch", d, batch) for d in (1, 2, 3)]
    (grad_tokens,) = call(
        tokens_body,
        [of((rows_here, width))],
        [gathered, second, h, src, dmix_in],
        [pltpu.VMEM((rows_here, width), BF16), pltpu.SemaphoreType.DMA((groups,))],
        far_outs=(0,),
    )
    (grad_flat,) = call(
        functools.partial(unpack_body, count, seq), [of((m_here * count, j_here))], terms_got
    )
    grad_two = jnp.transpose(grad_flat.reshape(m_here, count, j_here), (2, 0, 1))
    return (grad_tokens[None], grad_one, grad_two)


def wide_shards(tokens, cotangent, first_factor, second_factor, gate_source, alternate):
    inputs = tokens[0]
    rows_here = inputs.shape[0]
    width = inputs.shape[1]
    order_len = alternate.shape[0]
    blocks_here = rows_here // order_len
    select = one_hot(lax.broadcasted_iota(jnp.int32, (width, width), 0) == gate_source[None, :])
    gate = jax.nn.sigmoid(jnp.dot(inputs, select, preferred_element_type=F32))
    first_full = lax.all_gather(first_factor, "batch", axis=1, tiled=True)
    second_full = lax.all_gather(second_factor, "batch", axis=1, tiled=True)
    blocked = inputs.reshape(blocks_here, order_len, width)
    mixed = jnp.einsum("ikj,ijc->ikc", first_full, blocked, preferred_element_type=F32).astype(BF16)
    shuffled = jnp.take(mixed, alternate, axis=1)
    piece = lax.all_to_all(shuffled, "seq", split_axis=1, concat_axis=0, tiled=True)
    z_blocks = jnp.einsum("jmi,ijc->jmc", second_full, piece, preferred_element_type=F32)
    j_here, count_second = z_blocks.shape[:2]
    z_out = z_blocks.reshape(rows_here, width)
    cot = cotangent[0].astype(F32)
    dz_out = (cot * gate).astype(BF16)
    dgate = cot * z_out * gate * (1.0 - gate)
    dz_blocks = dz_out.reshape(j_here, count_second, width)
    term_second = jnp.einsum("jmc,ijc->jmi", dz_blocks, piece, preferred_element_type=F32)
    grad_two = lax.psum_scatter(term_second.astype(BF16), "batch", scatter_dimension=1, tiled=True)
    dregrouped = jnp.einsum("jmi,jmc->ijc", second_full, dz_blocks, preferred_element_type=F32).astype(BF16)
    positions = lax.iota(jnp.int32, order_len)
    inverse = jnp.zeros((order_len,), jnp.int32).at[alternate].set(positions)
    restored = jnp.take(
        lax.all_to_all(dregrouped, "seq", split_axis=0, concat_axis=1, tiled=True), inverse, axis=1
    )
    dmix_in = jnp.einsum("ikj,ikc->ijc", first_full, restored, preferred_element_type=F32)
    term_first = jnp.einsum("ikc,ijc->ikj", restored, blocked, preferred_element_type=F32)
    grad_one = lax.psum_scatter(term_first.astype(BF16), "batch", scatter_dimension=1, tiled=True)
    spread = jnp.dot(dgate, select.T.astype(F32), precision=lax.Precision.HIGHEST)
    grad_tokens = (dmix_in.reshape(rows_here, width) + spread).astype(BF16)
    return (grad_tokens[None], grad_one, grad_two)


def solution(mesh):
    batch, seq = mesh.shape["batch"], mesh.shape["seq"]

    def shards(*args):
        j_here, m_here, count = args[3].shape
        if batch == 4 and seq & (seq - 1) == 0 and seq % 4 == 0 and j_here % LANE_GROUP == 0 and m_here % 8 == 0 and count <= 32:
            return packed_shards(*args, batch, seq)
        return wide_shards(*args)

    in_specs = (
        P("batch", "seq", None),
        P("batch", "seq", None),
        P("seq", "batch", None),
        P("seq", "batch", None),
        P(),
        P(),
    )
    out_specs = (P("batch", "seq", None), P("seq", "batch", None), P("seq", "batch", None))
    return jax.shard_map(shards, mesh=mesh, in_specs=in_specs, out_specs=out_specs, check_vma=False)
```

```python
import functools

import jax
import jax.numpy as jnp
from jax import lax
from jax.experimental import pallas as pl
from jax.experimental.pallas import tpu as pltpu
from jax.sharding import PartitionSpec as P

BF16 = jnp.bfloat16
F32 = jnp.float32
LANE_GROUP = 16
CFG = {'a2a': [True, True], 'limit': 62914560, 'cost': {}, 'direct': False, 'rsdirect': False, 'f2early': False, 'order': [[7, 6, 5, 4, 3, 2, 1], [7, 6, 5, 4, 3, 2, 1]], 'deps': {'fx': ['A2'], 'F1': ['M'], 'F2': ['pair'], 'Z1': ['add']}}


def iota(shape, dim):
    return lax.broadcasted_iota(jnp.int32, shape, dim)


def one_hot(mask):
    return jnp.where(mask, 1.0, 0.0).astype(BF16)


def dot(a, b, da=1, db=0):
    return lax.dot_general(a, b, (((da,), (db,)), ((), ())), preferred_element_type=F32)


def call(body, outs, ins, scratch=(), spaces={}, limit=40 << 20, weight=0, far_outs=()):
    name = getattr(body, "func", body).__name__
    weight = CFG['cost'].get(name, 0)
    return pl.pallas_call(
        body,
        name=name,
        out_shape=outs,
        in_specs=[pl.BlockSpec(memory_space=spaces.get(n, pltpu.VMEM)) for n in range(len(ins))],
        out_specs=[
            pl.BlockSpec(memory_space=pltpu.HBM if n in far_outs else pltpu.VMEM) for n in range(len(outs))
        ],
        scratch_shapes=list(scratch),
        compiler_params=pltpu.CompilerParams(vmem_limit_bytes=limit),
        cost_estimate=pl.CostEstimate(flops=0, bytes_accessed=weight, transcendentals=0),
    )(*ins)


def of(shape, dtype=BF16):
    return jax.ShapeDtypeStruct(shape, dtype)


def swap(value, axis, step, size):
    return lax.ppermute(value, axis, [(p, p ^ step) for p in range(size)])


def ring_at(place, size):
    return jnp.where(place < size // 2, 2 * place, 2 * size - 1 - 2 * place)


def ring_of(size):
    return [2 * p if p < size // 2 else 2 * size - 1 - 2 * p for p in range(size)]


def after(value, *earlier):
    return lax.optimization_barrier((value, *earlier))[0]


def pack_body(order, s_ref, out_ref):
    rows, j_here = s_ref.shape
    groups = j_here // LANE_GROUP
    lanes = order * LANE_GROUP
    m_here = rows // order
    s = s_ref[...]
    lane = iota((j_here, lanes), 1)
    keep = (iota((rows, lanes), 0) % order) == (iota((rows, lanes), 1) // LANE_GROUP)
    for g in range(groups):
        place = one_hot(iota((j_here, lanes), 0) == g * LANE_GROUP + lane % LANE_GROUP)
        wide = jnp.where(keep, dot(s, place), 0.0)
        packed = jnp.sum(wide.reshape(m_here, order, lanes), axis=1)
        out_ref[g * m_here : (g + 1) * m_here, :] = packed.astype(BF16)


def gate_body(x_ref, cot_ref, src_ref, dz_ref):
    rows, width = x_ref.shape
    step = min(rows, 512)
    select = one_hot(iota((width, width), 0) == src_ref[...])
    for n in range(rows // step):
        part = slice(n * step, (n + 1) * step)
        gate = jax.nn.sigmoid(dot(x_ref[part, :], select))
        dz_ref[part, :] = (cot_ref[part, :].astype(F32) * gate).astype(BF16)


def regroup_back_body(batch, seq, order, *refs):
    pieces, dz_ref = refs[:batch], refs[batch]
    outs, second_ref, d_scr, r_scr, sems = refs[batch + 1 : -4], *refs[-4:]
    me = lax.axis_index("batch")
    groups = second_ref.shape[0]
    lanes = order * LANE_GROUP
    m_here = order // batch
    for d in range(batch):
        piece = pieces[d][...].astype(F32)
        first = pl.multiple_of((me ^ d) * m_here, m_here)
        for g in range(groups):
            d_scr[g, pl.ds(first, m_here), :] = piece[g * m_here : (g + 1) * m_here]
    width = dz_ref.shape[1]
    tiled = one_hot((iota((order, lanes), 1) % order) == iota((order, lanes), 0))
    keep = (iota((lanes, lanes), 0) % LANE_GROUP) == (iota((lanes, lanes), 1) // order)
    writes = []
    part = lanes // seq
    for g in range(groups):
        wide = d_scr[g]
        ringed = [wide[:, there * part : (there + 1) * part] for there in ring_of(seq)]
        packed = jnp.concatenate(ringed, axis=1).astype(BF16)
        second_ref[g] = packed
        weights = jnp.where(keep, dot(packed, tiled, 0, 0), 0.0).astype(BF16)
        result = dot(weights, dz_ref[g * lanes : (g + 1) * lanes, :]).astype(BF16)
        js = slice(g * LANE_GROUP, (g + 1) * LANE_GROUP)
        r_scr[:, js, :] = result.reshape(order, LANE_GROUP, width)
        writes.append(pltpu.make_async_copy(r_scr.at[:, js, :], outs[0].at[:, js, :], sems.at[g]))
        writes[g].start()
    for write in writes:
        write.wait()


def mix_body(batch, seq, *refs):
    pieces, x_hbm, alt_ref, out_hbm = refs[:batch], *refs[batch : batch + 3]
    f_scr, x_scr, p_scr, mix_scr, reg_scr, read_sems, write_sems = refs[batch + 3 :]
    me = lax.axis_index("batch")
    blocks, rows, order = pieces[0].shape
    j_here = order // seq
    width = x_scr.shape[1]
    reads, writes = [], []
    for i in range(blocks):
        part = pl.ds(i * order, order)
        reads.append([pltpu.make_async_copy(x_hbm.at[part, :], x_scr.at[part, :], read_sems.at[i, batch])])
        for d in range(batch):
            reads[i].append(pltpu.make_async_copy(pieces[d].at[i], f_scr.at[d, i], read_sems.at[i, d]))
        for read in reads[i]:
            read.start()
    p_scr[...] = jnp.where(iota((order, order), 0) == alt_ref[...], 1.0, 0.0).T.astype(BF16)
    for i in range(blocks):
        for read in reads[i]:
            read.wait()
        x = x_scr[i * order : (i + 1) * order, :]
        for d in range(batch):
            first = pl.multiple_of((me ^ d) * rows, rows)
            mix_scr[pl.ds(first, rows), :] = dot(f_scr[d, i], x).astype(BF16)
        reg_scr[i] = dot(p_scr[...], mix_scr[...]).astype(BF16).reshape(seq, j_here, width)
        for p, there in enumerate(ring_of(seq)):
            write = pltpu.make_async_copy(reg_scr.at[i, there], out_hbm.at[p, i], write_sems.at[i, p])
            write.start()
            writes.append(write)
    for write in writes:
        write.wait()


def first_grad_body(batch, seq, *refs):
    count = len(refs) - batch - 8
    pieces, x_ref, alt_ref = refs[:count], refs[count], refs[count + 1]
    outs, dmixed_hbm = refs[count + 2 : count + 2 + batch], refs[count + 2 + batch]
    p_scr, reg_scr, part_scr, dmixed_ref, sems = refs[-5:]
    me, here = lax.axis_index("batch"), lax.axis_index("seq")
    blocks, j_here, width = pieces[0].shape[-3:]
    order = j_here * seq
    rows = order // batch
    p_scr[...] = one_hot(iota((order, order), 0) == alt_ref[...])

    writes = []
    for i in range(blocks):
        if count == 1:
            for p, there in enumerate(ring_of(seq)):
                reg_scr[there * j_here : (there + 1) * j_here, :] = pieces[0][p, i]
        else:
            for d in range(seq):
                first = pl.multiple_of((here ^ d) * j_here, j_here)
                reg_scr[pl.ds(first, j_here), :] = pieces[d][i]
        dmixed = dot(p_scr[...], reg_scr[...]).astype(BF16)
        dmixed_ref[i] = dmixed
        writes.append(pltpu.make_async_copy(dmixed_ref.at[i], dmixed_hbm.at[i], sems.at[i]))
        writes[i].start()
        x = x_ref[i * order : (i + 1) * order, :]
        part_scr[...] = dot(dmixed, x, 1, 1).astype(BF16)
        for d in range(batch):
            first = pl.multiple_of((me ^ d) * rows, rows)
            outs[d][i] = part_scr[pl.ds(first, rows), :]
    for write in writes:
        write.wait()


def mix_back_body(batch, *refs):
    pieces, dmixed_ref, x_ref, cot_ref, src_ref, out_ref, h_ref = refs[:batch], *refs[batch:]
    me = lax.axis_index("batch")
    blocks, rows, order = pieces[0].shape
    width = x_ref.shape[1]
    select = one_hot(iota((width, width), 0) == src_ref[...])

    @pl.loop(0, blocks)
    def _(i):
        part = pl.ds(pl.multiple_of(i * order, order), order)
        total = None
        for d in range(batch):
            first = pl.multiple_of((me ^ d) * rows, rows)
            term = dot(pieces[d][i], dmixed_ref[i, pl.ds(first, rows), :], 0, 0)
            total = term if total is None else total + term
        out_ref[part, :] = total.astype(BF16)
        gate = jax.nn.sigmoid(dot(x_ref[part, :], select))
        h_ref[part, :] = (cot_ref[part, :].astype(F32) * gate * (1.0 - gate)).astype(BF16)


def gather_blocks(seq, pieces, scr):
    here = lax.axis_index("seq")
    blocks = pieces[0].shape[0]
    for d in range(seq):
        scr[pl.ds((here ^ d) * blocks, blocks)] = pieces[d][...]


def second_grad_body(batch, seq, *refs):
    count = len(refs) - batch - 3 if len(refs) > batch + 4 else 1
    if count == 1:
        pieces, dz_ref = refs[:1], refs[1]
        outs, reg_ref, y_scr = refs[2 : 2 + batch], refs[0], refs[-1]
    else:
        pieces, dz_ref = refs[:seq], refs[seq]
        outs, reg_ref, y_scr = refs[seq + 1 : seq + 1 + batch], refs[-2], refs[-1]
    me = lax.axis_index("batch")
    order, j_here, width = reg_ref.shape
    groups, lanes, m_here = j_here // LANE_GROUP, order * LANE_GROUP, order // batch
    if count > 1:
        gather_blocks(seq, pieces, reg_ref)

    @pl.loop(0, groups)
    def _(g):
        js = pl.ds(pl.multiple_of(g * LANE_GROUP, LANE_GROUP), LANE_GROUP)
        reg = reg_ref[:, js, :].reshape(lanes, width)
        dz = dz_ref[pl.ds(pl.multiple_of(g * lanes, lanes), lanes), :]
        wide = dot(dz, reg, 1, 1)
        col = iota((order, lanes), 1) % LANE_GROUP
        packed = wide[:order]
        for jj in range(1, LANE_GROUP):
            packed = jnp.where(col == jj, wide[jj * order : (jj + 1) * order], packed)
        y_scr[g] = packed

    for d in range(batch):
        first = pl.multiple_of((me ^ d) * m_here, m_here)
        rows = [y_scr[g, pl.ds(first, m_here), :] for g in range(groups)]
        outs[d][...] = jnp.concatenate(rows, axis=0).astype(BF16)


def tokens_body(reg_ref, second_ref, h_ref, src_ref, back_ref, out_hbm, out_ref, sems):
    order, j_here, width = reg_ref.shape
    groups, lanes = j_here // LANE_GROUP, order * LANE_GROUP
    select = one_hot(iota((width, width), 0) == src_ref[...])
    col = iota((order, lanes), 1) % LANE_GROUP
    masks = [one_hot(col == jj) for jj in range(LANE_GROUP)]
    writes = []
    for g in range(groups):
        reg = reg_ref[:, g * LANE_GROUP : (g + 1) * LANE_GROUP, :].reshape(lanes, width)
        packed = second_ref[g]
        weights = jnp.concatenate([packed * mask for mask in masks], axis=0)
        rows = slice(g * lanes, (g + 1) * lanes)
        dgate = (dot(weights, reg) * h_ref[rows, :].astype(F32)).astype(BF16)
        out_ref[rows, :] = (back_ref[rows, :].astype(F32) + dot(dgate, select, 1, 1)).astype(BF16)
        writes.append(pltpu.make_async_copy(out_ref.at[rows, :], out_hbm.at[rows, :], sems.at[g]))
        writes[g].start()
    for write in writes:
        write.wait()


def pair_body(own_a, own_b, got_a, got_b, out_a, *outs_b):
    out_a[...] = own_a[...].astype(F32) + got_a[...].astype(F32)
    step = outs_b[0].shape[0]
    for n, out_b in enumerate(outs_b):
        part = slice(n * step, (n + 1) * step)
        out_b[...] = (own_b[part].astype(F32) + got_b[part].astype(F32)).astype(BF16)


def sum_body(own, *refs):
    total = own[...].astype(F32)
    for got in refs[:-1]:
        total = total + got[...].astype(F32)
    refs[-1][...] = total.astype(BF16)


def add_body(own, *refs):
    step = refs[0].shape[0]
    for n, got in enumerate(refs[:-1]):
        part = slice(n * step, (n + 1) * step)
        refs[-1][part] = (own[part] + got[...].astype(F32)).astype(BF16)


def unpack_body(order, seq, *refs):
    pieces, out_ref = refs[:-1], refs[-1]
    rows, j_here = out_ref.shape
    groups, lanes, m_here = j_here // LANE_GROUP, order * LANE_GROUP, rows // order
    total = pieces[0][...].astype(F32)
    for piece in pieces[1:]:
        total = total + piece[...].astype(F32)
    lane = iota((j_here, lanes), 1)
    blocks = order // seq
    place_i = iota((rows, lanes), 1) // LANE_GROUP
    keep = (iota((rows, lanes), 0) % order) == ring_at(place_i // blocks, seq) * blocks + place_i % blocks
    result = jnp.zeros((rows, j_here), F32)
    for g in range(groups):
        place = one_hot(iota((j_here, lanes), 0) == g * LANE_GROUP + lane % LANE_GROUP)
        packed = total[g * m_here : (g + 1) * m_here]
        wide = jnp.broadcast_to(packed[:, None, :], (m_here, order, lanes)).reshape(rows, lanes)
        result = result + dot(jnp.where(keep, wide, 0.0).astype(BF16), place, 1, 1)
    out_ref[...] = result.astype(BF16)


def packed_shards(tokens, cotangent, first_factor, second_factor, gate_source, alternate, batch, seq):
    x, cot = tokens[0], cotangent[0]
    rows_here, width = x.shape
    blocks, k_here, order = first_factor.shape
    j_here, m_here, count = second_factor.shape
    groups, lanes = j_here // LANE_GROUP, count * LANE_GROUP
    src = gate_source.reshape(1, width)
    alt = alternate.reshape(1, order)

    flat = jnp.transpose(second_factor, (1, 2, 0)).reshape(m_here * count, j_here)
    vals = {}

    def dep(name, value):
        earlier = [vals[n] for n in CFG['deps'].get(name, ()) if n in vals]
        return after(value, *earlier) if earlier else value

    def keep(name, value):
        vals[name] = value
        return value

    def move(name, value, axis, step, size):
        return keep(name, swap(dep(name, value), axis, step, size))

    (mine,) = call(functools.partial(pack_body, count), [of((groups * m_here, lanes))], [flat])
    packed = {0: mine}
    for d in (3, 2, 1):
        packed[d] = move(f"D{d}", mine, "batch", d, batch)
    (dz,) = call(gate_body, [of((rows_here, width))], [x, cot, src], limit=16 << 20)
    keep("gate", dz)
    piece = of((blocks, j_here, width))
    *back, second = call(
        functools.partial(regroup_back_body, batch, seq, count),
        ([of((count, j_here, width))] if CFG['a2a'][0] else [piece] * seq) + [of((groups, count, lanes))],
        [*[packed[d] for d in range(batch)], dz],
        [
            pltpu.VMEM((groups, count, lanes), F32),
            pltpu.VMEM((count, j_here, width), BF16),
            pltpu.SemaphoreType.DMA((groups,)),
        ],
        far_outs=(0,) if CFG['a2a'][0] else (),
        limit=24 << 20,
    )
    keep("A2", back[0])
    first_ready = after(first_factor, dz) if CFG['f2early'] else after(first_factor, dz, *[packed[d] for d in (1, 2, 3)])
    across = move("f2", first_ready, "batch", 2, batch)
    beside = move("f1", first_ready, "batch", 1, batch)
    direct = move("f3", first_ready, "batch", 3, batch) if CFG['direct'] else None
    back_got = {0: back[0]}
    if CFG['a2a'][0]:
        back_got[0] = keep("h0", lax.all_to_all(
            dep("h0", back[0]).reshape(seq, blocks, j_here, width), "seq", 0, 0, axis_index_groups=[ring_of(seq)], tiled=True
        ))
    else:
        for d in CFG['order'][0]:
            back_got[d] = move(f"h{d}", back[d], "seq", d, seq)
    if direct is None:
        direct = move("fx", across, "batch", 1, batch)
    first = [first_factor, beside, across, direct]
    regrouped = call(
        functools.partial(mix_body, batch, seq),
        [of((seq, blocks, j_here, width))],
        [dep("M", first_factor), *first[1:], x, alt],
        [
            pltpu.VMEM((batch, blocks, k_here, order), BF16),
            pltpu.VMEM((rows_here, width), BF16),
            pltpu.VMEM((order, order), BF16),
            pltpu.VMEM((order, width), BF16),
            pltpu.VMEM((blocks, seq, j_here, width), BF16),
            pltpu.SemaphoreType.DMA((blocks, batch + 1)),
            pltpu.SemaphoreType.DMA((blocks, seq)),
        ],
        spaces={n: pltpu.HBM for n in range(batch + 1)},
        far_outs=(0,),
        limit=CFG['limit'],
    )
    keep("M", regrouped[0])
    got = {0: regrouped[0]}
    if CFG['a2a'][1]:
        got[0] = keep("H0", lax.all_to_all(
            dep("H0", regrouped[0]), "seq", 0, 0, axis_index_groups=[ring_of(seq)], tiled=True
        ))
    else:
        for d in CFG['order'][1]:
            got[d] = move(f"H{d}", regrouped[d], "seq", d, seq)
    *parts, dmixed = call(
        functools.partial(first_grad_body, batch, seq),
        [of((blocks, k_here, order))] * batch + [of((blocks, order, width))],
        [dep("F1", back_got[0]), *[back_got[d] for d in range(1, seq) if d in back_got], x, alt],
        [
            pltpu.VMEM((order, order), BF16),
            pltpu.VMEM((order, width), BF16),
            pltpu.VMEM((order, order), BF16),
            pltpu.VMEM((blocks, order, width), BF16),
            pltpu.SemaphoreType.DMA((blocks,)),
        ],
        far_outs=(batch,),
        limit=40 << 20,
    )
    keep("F1", dmixed)
    if CFG['rsdirect']:
        others = [move(f"rs{d}", parts[d], "batch", d, batch) for d in (3, 2, 1)]
    else:
        near = move("near", parts[1], "batch", 1, batch)
        far = move("far", parts[3], "batch", 1, batch)
    if CFG['rsdirect']:
        (grad_one,) = call(sum_body, [of(parts[0].shape)], [dep("sum", parts[0]), *others])
    else:
        halves = 4 if blocks % 4 == 0 else 1
        kept, *summed = call(
            pair_body,
            [of(parts[0].shape, F32)] + [of((blocks // halves, k_here, order))] * halves,
            [dep("pair", parts[0]), parts[2], near, far],
            limit=40 << 20,
        )
        keep("pair", summed[0])
        across_sums = [move(f"rx{n}", summed[n], "batch", 2, batch) for n in range(halves)]
        (grad_one,) = call(add_body, [of(parts[0].shape)], [kept, *across_sums])
    dmix_in, h = call(
        functools.partial(mix_back_body, batch),
        [of((rows_here, width))] * 2,
        [*first, dep("F2", dmixed), x, cot, src],
        limit=CFG['limit'],
    )
    keep("F2", dmix_in)
    keep("add", grad_one)
    received = [dep("Z1", after(got[0], dmix_in)), *[got[d] for d in range(1, seq) if d in got]]
    if len(received) == 1:
        received = [received[0].reshape(count, j_here, width)]
    *terms, gathered = call(
        functools.partial(second_grad_body, batch, seq),
        [of((groups * m_here, lanes))] * batch + ([of((count, j_here, width))] if len(received) > 1 else []),
        [*received, dz],
        [pltpu.VMEM((groups, count, lanes), F32)],
    )
    if len(received) == 1:
        terms, gathered = [*terms, gathered], received[0]
    terms_got = [dep("unpack", terms[0])] + [move(f"R{d}", terms[d], "batch", d, batch) for d in (1, 2, 3)]
    (grad_tokens,) = call(
        tokens_body,
        [of((rows_here, width))],
        [gathered, second, h, src, dmix_in],
        [pltpu.VMEM((rows_here, width), BF16), pltpu.SemaphoreType.DMA((groups,))],
        far_outs=(0,),
    )
    (grad_flat,) = call(
        functools.partial(unpack_body, count, seq), [of((m_here * count, j_here))], terms_got
    )
    grad_two = jnp.transpose(grad_flat.reshape(m_here, count, j_here), (2, 0, 1))
    return (grad_tokens[None], grad_one, grad_two)


def wide_shards(tokens, cotangent, first_factor, second_factor, gate_source, alternate):
    inputs = tokens[0]
    rows_here = inputs.shape[0]
    width = inputs.shape[1]
    order_len = alternate.shape[0]
    blocks_here = rows_here // order_len
    select = one_hot(lax.broadcasted_iota(jnp.int32, (width, width), 0) == gate_source[None, :])
    gate = jax.nn.sigmoid(jnp.dot(inputs, select, preferred_element_type=F32))
    first_full = lax.all_gather(first_factor, "batch", axis=1, tiled=True)
    second_full = lax.all_gather(second_factor, "batch", axis=1, tiled=True)
    blocked = inputs.reshape(blocks_here, order_len, width)
    mixed = jnp.einsum("ikj,ijc->ikc", first_full, blocked, preferred_element_type=F32).astype(BF16)
    shuffled = jnp.take(mixed, alternate, axis=1)
    piece = lax.all_to_all(shuffled, "seq", split_axis=1, concat_axis=0, tiled=True)
    z_blocks = jnp.einsum("jmi,ijc->jmc", second_full, piece, preferred_element_type=F32)
    j_here, count_second = z_blocks.shape[:2]
    z_out = z_blocks.reshape(rows_here, width)
    cot = cotangent[0].astype(F32)
    dz_out = (cot * gate).astype(BF16)
    dgate = cot * z_out * gate * (1.0 - gate)
    dz_blocks = dz_out.reshape(j_here, count_second, width)
    term_second = jnp.einsum("jmc,ijc->jmi", dz_blocks, piece, preferred_element_type=F32)
    grad_two = lax.psum_scatter(term_second.astype(BF16), "batch", scatter_dimension=1, tiled=True)
    dregrouped = jnp.einsum("jmi,jmc->ijc", second_full, dz_blocks, preferred_element_type=F32).astype(BF16)
    positions = lax.iota(jnp.int32, order_len)
    inverse = jnp.zeros((order_len,), jnp.int32).at[alternate].set(positions)
    restored = jnp.take(
        lax.all_to_all(dregrouped, "seq", split_axis=0, concat_axis=1, tiled=True), inverse, axis=1
    )
    dmix_in = jnp.einsum("ikj,ikc->ijc", first_full, restored, preferred_element_type=F32)
    term_first = jnp.einsum("ikc,ijc->ikj", restored, blocked, preferred_element_type=F32)
    grad_one = lax.psum_scatter(term_first.astype(BF16), "batch", scatter_dimension=1, tiled=True)
    spread = jnp.dot(dgate, select.T.astype(F32), precision=lax.Precision.HIGHEST)
    grad_tokens = (dmix_in.reshape(rows_here, width) + spread).astype(BF16)
    return (grad_tokens[None], grad_one, grad_two)


def solution(mesh):
    batch, seq = mesh.shape["batch"], mesh.shape["seq"]

    def shards(*args):
        j_here, m_here, count = args[3].shape
        if batch == 4 and seq & (seq - 1) == 0 and j_here % LANE_GROUP == 0 and m_here % 8 == 0 and count <= 32:
            return packed_shards(*args, batch, seq)
        return wide_shards(*args)

    in_specs = (
        P("batch", "seq", None),
        P("batch", "seq", None),
        P("seq", "batch", None),
        P("seq", "batch", None),
        P(),
        P(),
    )
    out_specs = (P("batch", "seq", None), P("seq", "batch", None), P("seq", "batch", None))
    return jax.shard_map(shards, mesh=mesh, in_specs=in_specs, out_specs=out_specs, check_vma=False)
```

```python
import functools

import jax
import jax.numpy as jnp
from jax import lax
from jax.experimental import pallas as pl
from jax.experimental.pallas import tpu as pltpu
from jax.sharding import PartitionSpec as P

BF16 = jnp.bfloat16
F32 = jnp.float32
LANE_GROUP = 16
CFG = {'a2a': [True, True], 'limit': 62914560, 'cost': {}, 'direct': False, 'rsdirect': False, 'f2early': False, 'order': [[7, 6, 5, 4, 3, 2, 1], [7, 6, 5, 4, 3, 2, 1]], 'deps': {'fx': ['A2'], 'F1': ['M'], 'F2': ['pair'], 'Z1': ['add']}}


def iota(shape, dim):
    return lax.broadcasted_iota(jnp.int32, shape, dim)


def one_hot(mask):
    return jnp.where(mask, 1.0, 0.0).astype(BF16)


def dot(a, b, da=1, db=0):
    return lax.dot_general(a, b, (((da,), (db,)), ((), ())), preferred_element_type=F32)


def call(body, outs, ins, scratch=(), spaces={}, limit=40 << 20, weight=0, far_outs=()):
    name = getattr(body, "func", body).__name__
    weight = CFG['cost'].get(name, 0)
    return pl.pallas_call(
        body,
        name=name,
        out_shape=outs,
        in_specs=[pl.BlockSpec(memory_space=spaces.get(n, pltpu.VMEM)) for n in range(len(ins))],
        out_specs=[
            pl.BlockSpec(memory_space=pltpu.HBM if n in far_outs else pltpu.VMEM) for n in range(len(outs))
        ],
        scratch_shapes=list(scratch),
        compiler_params=pltpu.CompilerParams(vmem_limit_bytes=limit),
        cost_estimate=pl.CostEstimate(flops=0, bytes_accessed=weight, transcendentals=0),
    )(*ins)


def of(shape, dtype=BF16):
    return jax.ShapeDtypeStruct(shape, dtype)


def swap(value, axis, step, size):
    return lax.ppermute(value, axis, [(p, p ^ step) for p in range(size)])


def ring_at(place, size):
    return jnp.where(place < size // 2, 2 * place + 1, 2 * size - 2 - 2 * place)


def ring_of(size):
    return [2 * p + 1 if p < size // 2 else 2 * size - 2 - 2 * p for p in range(size)]


def after(value, *earlier):
    return lax.optimization_barrier((value, *earlier))[0]


def pack_body(order, s_ref, out_ref):
    rows, j_here = s_ref.shape
    groups = j_here // LANE_GROUP
    lanes = order * LANE_GROUP
    m_here = rows // order
    s = s_ref[...]
    lane = iota((j_here, lanes), 1)
    keep = (iota((rows, lanes), 0) % order) == (iota((rows, lanes), 1) // LANE_GROUP)
    for g in range(groups):
        place = one_hot(iota((j_here, lanes), 0) == g * LANE_GROUP + lane % LANE_GROUP)
        wide = jnp.where(keep, dot(s, place), 0.0)
        packed = jnp.sum(wide.reshape(m_here, order, lanes), axis=1)
        out_ref[g * m_here : (g + 1) * m_here, :] = packed.astype(BF16)


def gate_body(x_ref, cot_ref, src_ref, dz_ref):
    rows, width = x_ref.shape
    step = min(rows, 512)
    select = one_hot(iota((width, width), 0) == src_ref[...])
    for n in range(rows // step):
        part = slice(n * step, (n + 1) * step)
        gate = jax.nn.sigmoid(dot(x_ref[part, :], select))
        dz_ref[part, :] = (cot_ref[part, :].astype(F32) * gate).astype(BF16)


def regroup_back_body(batch, seq, order, *refs):
    pieces, dz_ref = refs[:batch], refs[batch]
    outs, second_ref, d_scr, r_scr, sems = refs[batch + 1 : -4], *refs[-4:]
    me = lax.axis_index("batch")
    groups = second_ref.shape[0]
    lanes = order * LANE_GROUP
    m_here = order // batch
    for d in range(batch):
        piece = pieces[d][...].astype(F32)
        first = pl.multiple_of((me ^ d) * m_here, m_here)
        for g in range(groups):
            d_scr[g, pl.ds(first, m_here), :] = piece[g * m_here : (g + 1) * m_here]
    width = dz_ref.shape[1]
    tiled = one_hot((iota((order, lanes), 1) % order) == iota((order, lanes), 0))
    keep = (iota((lanes, lanes), 0) % LANE_GROUP) == (iota((lanes, lanes), 1) // order)
    writes = []
    part = lanes // seq
    for g in range(groups):
        wide = d_scr[g]
        ringed = [wide[:, there * part : (there + 1) * part] for there in ring_of(seq)]
        packed = jnp.concatenate(ringed, axis=1).astype(BF16)
        second_ref[g] = packed
        weights = jnp.where(keep, dot(packed, tiled, 0, 0), 0.0).astype(BF16)
        result = dot(weights, dz_ref[g * lanes : (g + 1) * lanes, :]).astype(BF16)
        js = slice(g * LANE_GROUP, (g + 1) * LANE_GROUP)
        r_scr[:, js, :] = result.reshape(order, LANE_GROUP, width)
        writes.append(pltpu.make_async_copy(r_scr.at[:, js, :], outs[0].at[:, js, :], sems.at[g]))
        writes[g].start()
    for write in writes:
        write.wait()


def mix_body(batch, seq, *refs):
    pieces, x_hbm, alt_ref, out_hbm = refs[:batch], *refs[batch : batch + 3]
    f_scr, x_scr, p_scr, mix_scr, reg_scr, read_sems, write_sems = refs[batch + 3 :]
    me = lax.axis_index("batch")
    blocks, rows, order = pieces[0].shape
    j_here = order // seq
    width = x_scr.shape[1]
    reads, writes = [], []
    for i in range(blocks):
        part = pl.ds(i * order, order)
        reads.append([pltpu.make_async_copy(x_hbm.at[part, :], x_scr.at[part, :], read_sems.at[i, batch])])
        for d in range(batch):
            reads[i].append(pltpu.make_async_copy(pieces[d].at[i], f_scr.at[d, i], read_sems.at[i, d]))
        for read in reads[i]:
            read.start()
    p_scr[...] = jnp.where(iota((order, order), 0) == alt_ref[...], 1.0, 0.0).T.astype(BF16)
    for i in range(blocks):
        for read in reads[i]:
            read.wait()
        x = x_scr[i * order : (i + 1) * order, :]
        for d in range(batch):
            first = pl.multiple_of((me ^ d) * rows, rows)
            mix_scr[pl.ds(first, rows), :] = dot(f_scr[d, i], x).astype(BF16)
        reg_scr[i] = dot(p_scr[...], mix_scr[...]).astype(BF16).reshape(seq, j_here, width)
        for p, there in enumerate(ring_of(seq)):
            write = pltpu.make_async_copy(reg_scr.at[i, there], out_hbm.at[p, i], write_sems.at[i, p])
            write.start()
            writes.append(write)
    for write in writes:
        write.wait()


def first_grad_body(batch, seq, *refs):
    count = len(refs) - batch - 8
    pieces, x_ref, alt_ref = refs[:count], refs[count], refs[count + 1]
    outs, dmixed_hbm = refs[count + 2 : count + 2 + batch], refs[count + 2 + batch]
    p_scr, reg_scr, part_scr, dmixed_ref, sems = refs[-5:]
    me, here = lax.axis_index("batch"), lax.axis_index("seq")
    blocks, j_here, width = pieces[0].shape[-3:]
    order = j_here * seq
    rows = order // batch
    p_scr[...] = one_hot(iota((order, order), 0) == alt_ref[...])

    writes = []
    for i in range(blocks):
        if count == 1:
            for p, there in enumerate(ring_of(seq)):
                reg_scr[there * j_here : (there + 1) * j_here, :] = pieces[0][p, i]
        else:
            for d in range(seq):
                first = pl.multiple_of((here ^ d) * j_here, j_here)
                reg_scr[pl.ds(first, j_here), :] = pieces[d][i]
        dmixed = dot(p_scr[...], reg_scr[...]).astype(BF16)
        dmixed_ref[i] = dmixed
        writes.append(pltpu.make_async_copy(dmixed_ref.at[i], dmixed_hbm.at[i], sems.at[i]))
        writes[i].start()
        x = x_ref[i * order : (i + 1) * order, :]
        part_scr[...] = dot(dmixed, x, 1, 1).astype(BF16)
        for d in range(batch):
            first = pl.multiple_of((me ^ d) * rows, rows)
            outs[d][i] = part_scr[pl.ds(first, rows), :]
    for write in writes:
        write.wait()


def mix_back_body(batch, *refs):
    pieces, dmixed_ref, x_ref, cot_ref, src_ref, out_ref, h_ref = refs[:batch], *refs[batch:]
    me = lax.axis_index("batch")
    blocks, rows, order = pieces[0].shape
    width = x_ref.shape[1]
    select = one_hot(iota((width, width), 0) == src_ref[...])

    @pl.loop(0, blocks)
    def _(i):
        part = pl.ds(pl.multiple_of(i * order, order), order)
        total = None
        for d in range(batch):
            first = pl.multiple_of((me ^ d) * rows, rows)
            term = dot(pieces[d][i], dmixed_ref[i, pl.ds(first, rows), :], 0, 0)
            total = term if total is None else total + term
        out_ref[part, :] = total.astype(BF16)
        gate = jax.nn.sigmoid(dot(x_ref[part, :], select))
        h_ref[part, :] = (cot_ref[part, :].astype(F32) * gate * (1.0 - gate)).astype(BF16)


def gather_blocks(seq, pieces, scr):
    here = lax.axis_index("seq")
    blocks = pieces[0].shape[0]
    for d in range(seq):
        scr[pl.ds((here ^ d) * blocks, blocks)] = pieces[d][...]


def second_grad_body(batch, seq, *refs):
    count = len(refs) - batch - 3 if len(refs) > batch + 4 else 1
    if count == 1:
        pieces, dz_ref = refs[:1], refs[1]
        outs, reg_ref, y_scr = refs[2 : 2 + batch], refs[0], refs[-1]
    else:
        pieces, dz_ref = refs[:seq], refs[seq]
        outs, reg_ref, y_scr = refs[seq + 1 : seq + 1 + batch], refs[-2], refs[-1]
    me = lax.axis_index("batch")
    order, j_here, width = reg_ref.shape
    groups, lanes, m_here = j_here // LANE_GROUP, order * LANE_GROUP, order // batch
    if count > 1:
        gather_blocks(seq, pieces, reg_ref)

    @pl.loop(0, groups)
    def _(g):
        js = pl.ds(pl.multiple_of(g * LANE_GROUP, LANE_GROUP), LANE_GROUP)
        reg = reg_ref[:, js, :].reshape(lanes, width)
        dz = dz_ref[pl.ds(pl.multiple_of(g * lanes, lanes), lanes), :]
        wide = dot(dz, reg, 1, 1)
        col = iota((order, lanes), 1) % LANE_GROUP
        packed = wide[:order]
        for jj in range(1, LANE_GROUP):
            packed = jnp.where(col == jj, wide[jj * order : (jj + 1) * order], packed)
        y_scr[g] = packed

    for d in range(batch):
        first = pl.multiple_of((me ^ d) * m_here, m_here)
        rows = [y_scr[g, pl.ds(first, m_here), :] for g in range(groups)]
        outs[d][...] = jnp.concatenate(rows, axis=0).astype(BF16)


def tokens_body(reg_ref, second_ref, h_ref, src_ref, back_ref, out_hbm, out_ref, sems):
    order, j_here, width = reg_ref.shape
    groups, lanes = j_here // LANE_GROUP, order * LANE_GROUP
    select = one_hot(iota((width, width), 0) == src_ref[...])
    col = iota((order, lanes), 1) % LANE_GROUP
    masks = [one_hot(col == jj) for jj in range(LANE_GROUP)]
    writes = []
    for g in range(groups):
        reg = reg_ref[:, g * LANE_GROUP : (g + 1) * LANE_GROUP, :].reshape(lanes, width)
        packed = second_ref[g]
        weights = jnp.concatenate([packed * mask for mask in masks], axis=0)
        rows = slice(g * lanes, (g + 1) * lanes)
        dgate = (dot(weights, reg) * h_ref[rows, :].astype(F32)).astype(BF16)
        out_ref[rows, :] = (back_ref[rows, :].astype(F32) + dot(dgate, select, 1, 1)).astype(BF16)
        writes.append(pltpu.make_async_copy(out_ref.at[rows, :], out_hbm.at[rows, :], sems.at[g]))
        writes[g].start()
    for write in writes:
        write.wait()


def pair_body(own_a, own_b, got_a, got_b, out_a, *outs_b):
    out_a[...] = own_a[...].astype(F32) + got_a[...].astype(F32)
    step = outs_b[0].shape[0]
    for n, out_b in enumerate(outs_b):
        part = slice(n * step, (n + 1) * step)
        out_b[...] = (own_b[part].astype(F32) + got_b[part].astype(F32)).astype(BF16)


def sum_body(own, *refs):
    total = own[...].astype(F32)
    for got in refs[:-1]:
        total = total + got[...].astype(F32)
    refs[-1][...] = total.astype(BF16)


def add_body(own, *refs):
    step = refs[0].shape[0]
    for n, got in enumerate(refs[:-1]):
        part = slice(n * step, (n + 1) * step)
        refs[-1][part] = (own[part] + got[...].astype(F32)).astype(BF16)


def unpack_body(order, seq, *refs):
    pieces, out_ref = refs[:-1], refs[-1]
    rows, j_here = out_ref.shape
    groups, lanes, m_here = j_here // LANE_GROUP, order * LANE_GROUP, rows // order
    total = pieces[0][...].astype(F32)
    for piece in pieces[1:]:
        total = total + piece[...].astype(F32)
    lane = iota((j_here, lanes), 1)
    blocks = order // seq
    place_i = iota((rows, lanes), 1) // LANE_GROUP
    keep = (iota((rows, lanes), 0) % order) == ring_at(place_i // blocks, seq) * blocks + place_i % blocks
    result = jnp.zeros((rows, j_here), F32)
    for g in range(groups):
        place = one_hot(iota((j_here, lanes), 0) == g * LANE_GROUP + lane % LANE_GROUP)
        packed = total[g * m_here : (g + 1) * m_here]
        wide = jnp.broadcast_to(packed[:, None, :], (m_here, order, lanes)).reshape(rows, lanes)
        result = result + dot(jnp.where(keep, wide, 0.0).astype(BF16), place, 1, 1)
    out_ref[...] = result.astype(BF16)


def packed_shards(tokens, cotangent, first_factor, second_factor, gate_source, alternate, batch, seq):
    x, cot = tokens[0], cotangent[0]
    rows_here, width = x.shape
    blocks, k_here, order = first_factor.shape
    j_here, m_here, count = second_factor.shape
    groups, lanes = j_here // LANE_GROUP, count * LANE_GROUP
    src = gate_source.reshape(1, width)
    alt = alternate.reshape(1, order)

    flat = jnp.transpose(second_factor, (1, 2, 0)).reshape(m_here * count, j_here)
    vals = {}

    def dep(name, value):
        earlier = [vals[n] for n in CFG['deps'].get(name, ()) if n in vals]
        return after(value, *earlier) if earlier else value

    def keep(name, value):
        vals[name] = value
        return value

    def move(name, value, axis, step, size):
        return keep(name, swap(dep(name, value), axis, step, size))

    (mine,) = call(functools.partial(pack_body, count), [of((groups * m_here, lanes))], [flat])
    packed = {0: mine}
    for d in (3, 2, 1):
        packed[d] = move(f"D{d}", mine, "batch", d, batch)
    (dz,) = call(gate_body, [of((rows_here, width))], [x, cot, src], limit=16 << 20)
    keep("gate", dz)
    piece = of((blocks, j_here, width))
    *back, second = call(
        functools.partial(regroup_back_body, batch, seq, count),
        ([of((count, j_here, width))] if CFG['a2a'][0] else [piece] * seq) + [of((groups, count, lanes))],
        [*[packed[d] for d in range(batch)], dz],
        [
            pltpu.VMEM((groups, count, lanes), F32),
            pltpu.VMEM((count, j_here, width), BF16),
            pltpu.SemaphoreType.DMA((groups,)),
        ],
        far_outs=(0,) if CFG['a2a'][0] else (),
        limit=24 << 20,
    )
    keep("A2", back[0])
    first_ready = after(first_factor, dz) if CFG['f2early'] else after(first_factor, dz, *[packed[d] for d in (1, 2, 3)])
    across = move("f2", first_ready, "batch", 2, batch)
    beside = move("f1", first_ready, "batch", 1, batch)
    direct = move("f3", first_ready, "batch", 3, batch) if CFG['direct'] else None
    back_got = {0: back[0]}
    if CFG['a2a'][0]:
        back_got[0] = keep("h0", lax.all_to_all(
            dep("h0", back[0]).reshape(seq, blocks, j_here, width), "seq", 0, 0, axis_index_groups=[ring_of(seq)], tiled=True
        ))
    else:
        for d in CFG['order'][0]:
            back_got[d] = move(f"h{d}", back[d], "seq", d, seq)
    if direct is None:
        direct = move("fx", across, "batch", 1, batch)
    first = [first_factor, beside, across, direct]
    regrouped = call(
        functools.partial(mix_body, batch, seq),
        [of((seq, blocks, j_here, width))],
        [dep("M", first_factor), *first[1:], x, alt],
        [
            pltpu.VMEM((batch, blocks, k_here, order), BF16),
            pltpu.VMEM((rows_here, width), BF16),
            pltpu.VMEM((order, order), BF16),
            pltpu.VMEM((order, width), BF16),
            pltpu.VMEM((blocks, seq, j_here, width), BF16),
            pltpu.SemaphoreType.DMA((blocks, batch + 1)),
            pltpu.SemaphoreType.DMA((blocks, seq)),
        ],
        spaces={n: pltpu.HBM for n in range(batch + 1)},
        far_outs=(0,),
        limit=CFG['limit'],
    )
    keep("M", regrouped[0])
    got = {0: regrouped[0]}
    if CFG['a2a'][1]:
        got[0] = keep("H0", lax.all_to_all(
            dep("H0", regrouped[0]), "seq", 0, 0, axis_index_groups=[ring_of(seq)], tiled=True
        ))
    else:
        for d in CFG['order'][1]:
            got[d] = move(f"H{d}", regrouped[d], "seq", d, seq)
    *parts, dmixed = call(
        functools.partial(first_grad_body, batch, seq),
        [of((blocks, k_here, order))] * batch + [of((blocks, order, width))],
        [dep("F1", back_got[0]), *[back_got[d] for d in range(1, seq) if d in back_got], x, alt],
        [
            pltpu.VMEM((order, order), BF16),
            pltpu.VMEM((order, width), BF16),
            pltpu.VMEM((order, order), BF16),
            pltpu.VMEM((blocks, order, width), BF16),
            pltpu.SemaphoreType.DMA((blocks,)),
        ],
        far_outs=(batch,),
        limit=40 << 20,
    )
    keep("F1", dmixed)
    if CFG['rsdirect']:
        others = [move(f"rs{d}", parts[d], "batch", d, batch) for d in (3, 2, 1)]
    else:
        near = move("near", parts[1], "batch", 1, batch)
        far = move("far", parts[3], "batch", 1, batch)
    if CFG['rsdirect']:
        (grad_one,) = call(sum_body, [of(parts[0].shape)], [dep("sum", parts[0]), *others])
    else:
        halves = 4 if blocks % 4 == 0 else 1
        kept, *summed = call(
            pair_body,
            [of(parts[0].shape, F32)] + [of((blocks // halves, k_here, order))] * halves,
            [dep("pair", parts[0]), parts[2], near, far],
            limit=40 << 20,
        )
        keep("pair", summed[0])
        across_sums = [move(f"rx{n}", summed[n], "batch", 2, batch) for n in range(halves)]
        (grad_one,) = call(add_body, [of(parts[0].shape)], [kept, *across_sums])
    dmix_in, h = call(
        functools.partial(mix_back_body, batch),
        [of((rows_here, width))] * 2,
        [*first, dep("F2", dmixed), x, cot, src],
        limit=CFG['limit'],
    )
    keep("F2", dmix_in)
    keep("add", grad_one)
    received = [dep("Z1", after(got[0], dmix_in)), *[got[d] for d in range(1, seq) if d in got]]
    if len(received) == 1:
        received = [received[0].reshape(count, j_here, width)]
    *terms, gathered = call(
        functools.partial(second_grad_body, batch, seq),
        [of((groups * m_here, lanes))] * batch + ([of((count, j_here, width))] if len(received) > 1 else []),
        [*received, dz],
        [pltpu.VMEM((groups, count, lanes), F32)],
    )
    if len(received) == 1:
        terms, gathered = [*terms, gathered], received[0]
    terms_got = [dep("unpack", terms[0])] + [move(f"R{d}", terms[d], "batch", d, batch) for d in (1, 2, 3)]
    (grad_tokens,) = call(
        tokens_body,
        [of((rows_here, width))],
        [gathered, second, h, src, dmix_in],
        [pltpu.VMEM((rows_here, width), BF16), pltpu.SemaphoreType.DMA((groups,))],
        far_outs=(0,),
    )
    (grad_flat,) = call(
        functools.partial(unpack_body, count, seq), [of((m_here * count, j_here))], terms_got
    )
    grad_two = jnp.transpose(grad_flat.reshape(m_here, count, j_here), (2, 0, 1))
    return (grad_tokens[None], grad_one, grad_two)


def wide_shards(tokens, cotangent, first_factor, second_factor, gate_source, alternate):
    inputs = tokens[0]
    rows_here = inputs.shape[0]
    width = inputs.shape[1]
    order_len = alternate.shape[0]
    blocks_here = rows_here // order_len
    select = one_hot(lax.broadcasted_iota(jnp.int32, (width, width), 0) == gate_source[None, :])
    gate = jax.nn.sigmoid(jnp.dot(inputs, select, preferred_element_type=F32))
    first_full = lax.all_gather(first_factor, "batch", axis=1, tiled=True)
    second_full = lax.all_gather(second_factor, "batch", axis=1, tiled=True)
    blocked = inputs.reshape(blocks_here, order_len, width)
    mixed = jnp.einsum("ikj,ijc->ikc", first_full, blocked, preferred_element_type=F32).astype(BF16)
    shuffled = jnp.take(mixed, alternate, axis=1)
    piece = lax.all_to_all(shuffled, "seq", split_axis=1, concat_axis=0, tiled=True)
    z_blocks = jnp.einsum("jmi,ijc->jmc", second_full, piece, preferred_element_type=F32)
    j_here, count_second = z_blocks.shape[:2]
    z_out = z_blocks.reshape(rows_here, width)
    cot = cotangent[0].astype(F32)
    dz_out = (cot * gate).astype(BF16)
    dgate = cot * z_out * gate * (1.0 - gate)
    dz_blocks = dz_out.reshape(j_here, count_second, width)
    term_second = jnp.einsum("jmc,ijc->jmi", dz_blocks, piece, preferred_element_type=F32)
    grad_two = lax.psum_scatter(term_second.astype(BF16), "batch", scatter_dimension=1, tiled=True)
    dregrouped = jnp.einsum("jmi,jmc->ijc", second_full, dz_blocks, preferred_element_type=F32).astype(BF16)
    positions = lax.iota(jnp.int32, order_len)
    inverse = jnp.zeros((order_len,), jnp.int32).at[alternate].set(positions)
    restored = jnp.take(
        lax.all_to_all(dregrouped, "seq", split_axis=0, concat_axis=1, tiled=True), inverse, axis=1
    )
    dmix_in = jnp.einsum("ikj,ikc->ijc", first_full, restored, preferred_element_type=F32)
    term_first = jnp.einsum("ikc,ijc->ikj", restored, blocked, preferred_element_type=F32)
    grad_one = lax.psum_scatter(term_first.astype(BF16), "batch", scatter_dimension=1, tiled=True)
    spread = jnp.dot(dgate, select.T.astype(F32), precision=lax.Precision.HIGHEST)
    grad_tokens = (dmix_in.reshape(rows_here, width) + spread).astype(BF16)
    return (grad_tokens[None], grad_one, grad_two)


def solution(mesh):
    batch, seq = mesh.shape["batch"], mesh.shape["seq"]

    def shards(*args):
        j_here, m_here, count = args[3].shape
        if batch == 4 and seq & (seq - 1) == 0 and j_here % LANE_GROUP == 0 and m_here % 8 == 0 and count <= 32:
            return packed_shards(*args, batch, seq)
        return wide_shards(*args)

    in_specs = (
        P("batch", "seq", None),
        P("batch", "seq", None),
        P("seq", "batch", None),
        P("seq", "batch", None),
        P(),
        P(),
    )
    out_specs = (P("batch", "seq", None), P("seq", "batch", None), P("seq", "batch", None))
    return jax.shard_map(shards, mesh=mesh, in_specs=in_specs, out_specs=out_specs, check_vma=False)
```
